32 devices in a mesh: date: 16 (over z, x, core), row: 2 (over y).
Axes of the slice: x: 2, y: 2, z: 4, core: 2. Of those that a mesh axis runs over, the one named last changes fastest.
Arguments:
- tokens: bfloat16 [32, 32, 16, 384], P('date', 'row'), may hold values from -6 to 6
- clear_flags: int32 [32, 32, 16], P('date', 'row'), may hold values 0 or 1
- date_numbers: int32 [32], P('date'), may hold values from 0 to 255, as said below
- decay_slopes: float32 [12], replicated, may hold values from 0.001953125 to 0.03
- time_project: bfloat16 [384, 1152], replicated, may hold values from -0.35 to 0.35
- time_output: bfloat16 [384, 384], replicated, may hold values from -0.3125 to 0.3125
- column_project: bfloat16 [384, 1152], replicated, may hold values from -0.35 to 0.35
- column_output: bfloat16 [384, 384], replicated, may hold values from -0.3125 to 0.3125
- cotangent: bfloat16 [32, 32, 16, 384], P('date', 'row'), may hold values from -6 to 6
Outputs:
- mixed_tokens: bfloat16 [32, 32, 16, 384], P('date', 'row')
- column_project_grad: float32 [384, 1152], P('row', 'date')
- column_output_grad: float32 [384, 384], P('row', 'date')
The draws below stay inside these ranges and needn't reach their ends.
Inputs may be any that keep to these rules, and one draw needn't show every extreme that they name: `date_numbers`: strictly increasing; consecutive dates lie 1 to 15 days apart.
All inputs are finite; a program needn't handle non-finite values. No bound on the sum of `clear_flags` on one device may be relied on, other than what follows from the above.
Results may differ from the reference program's by a relative error of at most 0.018.
The reference program's roundings to bfloat16 on the way count: a program that leaves them out, or rounds other values in their place, can miss the bound.
Values may be sent and summed in bfloat16 or wider, within the bound.
No kernel may reach another device: no remote copies, remote signals or barrier semaphores. Data moves between devices by JAX's collectives and lax.ppermute only.
A program may use at most 64 MiB of HBM per device.

```python
import math
import jax
import jax.numpy as jnp
from jax import lax

D = 384
HEADS = 12
COLS = 16
DATES = 32
ROWS = 32


def draw_date_numbers(key, part):
    jitter = jax.random.randint(jax.random.fold_in(key, 17), (DATES,), 0, 8)
    positions = jnp.arange(DATES, dtype=jnp.int32)
    jitter = jnp.where(positions == 0, 0, jnp.where(positions == DATES - 1, 7, jitter))
    return (positions * 8 + jitter).astype(jnp.int32)


def draw_tokens(key, part):
    noise = jax.random.truncated_normal(jax.random.fold_in(key, 31), -6.0, 6.0, (DATES, ROWS, COLS, D), jnp.float32)
    return noise.astype(jnp.bfloat16)


def projection_draw(key, salt):
    base = jax.random.truncated_normal(jax.random.fold_in(key, salt), -6.0, 6.0, (D, 3 * D), jnp.float32) * D ** (-0.5)
    return jnp.clip(base, -0.35, 0.35)


def draw_time_project(key, part):
    return projection_draw(key, 101).astype(jnp.bfloat16)


def draw_column_project(key, part):
    return projection_draw(key, 202).astype(jnp.bfloat16)


def place_ends(values, stream_key, low, high):
    longest = values.shape.index(max(values.shape))
    spots = []
    for shift in (0, 1):
        where = [jax.random.randint(jax.random.fold_in(stream_key, axis), (), 0, length) for axis, length in enumerate(values.shape)]
        where[longest] = (where[longest] + shift) % values.shape[longest]
        spots.append(tuple(where))
    return values.at[spots[0]].set(low).at[spots[1]].set(high)


def steps_of(own_key, extent, pieces, least, top_value):
    def one(dim, blocks):
        steps = jax.random.uniform(jax.random.fold_in(jax.random.fold_in(own_key, 6), dim), (blocks,), jnp.float32, least / len(pieces), top_value / len(pieces))
        return jnp.repeat(jnp.exp(steps), extent[dim] // blocks).reshape((-1,) + (1,) * (len(extent) - dim - 1))

    loudness = one(*pieces[0])
    for cut in pieces[1:]:
        loudness = loudness * one(*cut)
    return loudness


def bell_draw(key, extent, width, most, split=(), kind=jnp.bfloat16):
    values = width * jax.random.normal(key, extent, jnp.float32)
    if split:
        values = values * steps_of(key, extent, split, -0.22, 0.18)
    return jnp.clip(values, -most, most).astype(kind)


def setup_inputs(seed: int = 0) -> dict:
    arg_keys = jax.random.split(jax.random.key(seed), 10)
    return {
        "tokens": draw_tokens(jax.random.fold_in(arg_keys[9], 71), 0),
        "clear_flags": place_ends((jax.random.randint(arg_keys[1], (DATES, ROWS, COLS), 0, 4) < 3).astype(jnp.int32), jax.random.fold_in(arg_keys[1], 1), 0, 1),
        "date_numbers": draw_date_numbers(jax.random.fold_in(arg_keys[9], 71), 0),
        "decay_slopes": jnp.clip(jnp.exp(jax.random.uniform(arg_keys[3], (HEADS,), jnp.float32, math.log(0.001953125), math.log(0.03))), 0.001953125, 0.03),
        "time_project": draw_time_project(jax.random.fold_in(arg_keys[9], 71), 0),
        "time_output": bell_draw(arg_keys[5], (D, D), D ** -0.5, 0.3125),
        "column_project": draw_column_project(jax.random.fold_in(arg_keys[9], 71), 0),
        "column_output": bell_draw(arg_keys[7], (D, D), D ** -0.5, 0.3125),
        "cotangent": bell_draw(arg_keys[8], (DATES, ROWS, COLS, D), 1.0, 6.0, ((0, 16), (1, 2))),
    }


epsilon = 1e-06
masked_score = -1e+30

def rms_norm(values):
    widened = values.astype(jnp.float32)
    factor = lax.rsqrt(lax.optimization_barrier(jnp.mean(widened * widened, axis=-1, keepdims=True)) + epsilon)
    return (widened * factor).astype(jnp.bfloat16)

def softmax_rows(scores):
    top_score = lax.optimization_barrier(jnp.max(scores, axis=-1, keepdims=True))
    raised = jnp.exp(scores - top_score)
    return raised / lax.optimization_barrier(jnp.sum(raised, axis=-1, keepdims=True))

def lowered(values):
    return lax.optimization_barrier(values.astype(jnp.bfloat16)).astype(jnp.float32)

def reference(tokens, clear_flags, date_numbers, decay_slopes, time_project, time_output, column_project, column_output, cotangent):
    head_size = D // HEADS
    inverse_root = 1.0 / math.sqrt(head_size)
    gap_days = jnp.abs(date_numbers[:, None] - date_numbers[None, :]).astype(jnp.float32)
    time_bias = -decay_slopes[:, None, None] * gap_days[None, :, :]
    positions = jnp.arange(DATES)
    same_date = positions[:, None] == positions[None, :]
    patch_tokens = jnp.transpose(tokens.reshape(DATES, ROWS * COLS, D), (1, 0, 2))
    patch_flags = jnp.transpose(clear_flags.reshape(DATES, ROWS * COLS), (1, 0))

    def time_patch(inputs):
        series, flags = inputs
        normed = rms_norm(series)
        projected = lowered(jnp.dot(normed, time_project, preferred_element_type=jnp.float32))
        projected = projected.reshape(DATES, 3, HEADS, head_size)
        scores = jnp.einsum('qhe,khe->hqk', projected[:, 0], projected[:, 1]) * inverse_root + time_bias
        allowed = (flags[None, :] > 0) | same_date
        scores = jnp.where(allowed[None], scores, masked_score)
        weights_low = lowered(softmax_rows(scores))
        time_heads = jnp.einsum('hqk,khe->qhe', weights_low, projected[:, 2]).astype(jnp.bfloat16)
        update = jnp.dot(time_heads.reshape(DATES, D), time_output, preferred_element_type=jnp.float32)
        return (series.astype(jnp.float32) + update).astype(jnp.bfloat16)
    hidden = lax.map(time_patch, (patch_tokens, patch_flags))
    hidden = jnp.transpose(hidden, (1, 0, 2)).reshape(DATES, ROWS, COLS, D)

    def column_date(totals, inputs):
        plane, plane_grad = inputs
        normed = rms_norm(plane).reshape(ROWS * COLS, D)
        projected = lowered(jnp.dot(normed, column_project, preferred_element_type=jnp.float32))
        projected = projected.reshape(ROWS, COLS, 3, HEADS, head_size)
        queries = projected[:, :, 0]
        key_block = projected[:, :, 1]
        value_block = projected[:, :, 2]
        scores = jnp.einsum('ache,bche->chab', queries, key_block) * inverse_root
        weights = softmax_rows(scores)
        weights_low = lowered(weights)
        column_heads = jnp.einsum('chab,bche->ache', weights_low, value_block).astype(jnp.bfloat16)
        heads_flat = column_heads.reshape(ROWS * COLS, D)
        update = jnp.dot(heads_flat, column_output, preferred_element_type=jnp.float32)
        result = (plane.reshape(ROWS * COLS, D).astype(jnp.float32) + update).astype(jnp.bfloat16)
        grad_flat = plane_grad.reshape(ROWS * COLS, D)
        output_term = jnp.dot(heads_flat.T, grad_flat, preferred_element_type=jnp.float32)
        heads_grad = lowered(jnp.dot(grad_flat, column_output.T, preferred_element_type=jnp.float32))
        heads_grad = heads_grad.reshape(ROWS, COLS, HEADS, head_size)
        product_grad = jnp.einsum('ache,bche->chab', heads_grad, value_block)
        score_grad = weights * (product_grad - lax.optimization_barrier(jnp.sum(weights * product_grad, axis=-1, keepdims=True)))
        score_low = lowered(score_grad)
        query_grad = lowered(jnp.einsum('chab,bche->ache', score_low, key_block) * inverse_root)
        key_grad = lowered(jnp.einsum('chab,ache->bche', score_low, queries) * inverse_root)
        value_grad = lowered(jnp.einsum('chab,ache->bche', weights_low, heads_grad))
        qkv_grad = jnp.stack([query_grad, key_grad, value_grad], axis=2).reshape(ROWS * COLS, 3 * D).astype(jnp.bfloat16)
        project_term = jnp.dot(normed.T, qkv_grad, preferred_element_type=jnp.float32)
        return ((totals[0] + project_term, totals[1] + output_term), result.reshape(ROWS, COLS, D))
    start = (jnp.zeros((D, 3 * D), jnp.float32), jnp.zeros((D, D), jnp.float32))
    totals, mixed_tokens = lax.scan(column_date, start, (hidden, cotangent))
    return (mixed_tokens, totals[0], totals[1])
```

```python
import functools
import math

import jax
import jax.numpy as jnp
from jax import lax
from jax.experimental import pallas as pl
from jax.experimental.pallas import tpu as pltpu
from jax.sharding import PartitionSpec as P

epsilon = 1e-06
masked_score = -1e30
vmem_limit = 48 * 1024 * 1024
low = jnp.bfloat16
wide = jnp.float32


def rms_norm(values):
    factor = lax.rsqrt(jnp.mean(values * values, axis=-1, keepdims=True) + epsilon)
    return (values * factor).astype(low)


def matmul(left, right):
    return jnp.dot(left, right, preferred_element_type=wide)


def contract_rows(left, right):
    return lax.dot_general(left, right, (((0,), (0,)), ((), ())), preferred_element_type=wide)


def contract_last(left, right):
    return lax.dot_general(left, right, (((1,), (1,)), ((), ())), preferred_element_type=wide)


def block_mask(length, packed, head_size):
    shape = (packed * length, packed * head_size)
    rows = lax.broadcasted_iota(jnp.int32, shape, 0) // length
    lanes = lax.broadcasted_iota(jnp.int32, shape, 1) // head_size
    return rows == lanes


def spread(values, mask, packed):
    tiled = jnp.concatenate([values] * packed, axis=0)
    return jnp.where(mask, tiled, jnp.zeros_like(tiled))


def own_blocks(full, length, packed, head_size):
    lanes = lax.broadcasted_iota(jnp.int32, (length, packed * head_size), 1) // head_size
    out = full[:length]
    for head in range(1, packed):
        out = jnp.where(lanes == head, full[head * length : (head + 1) * length], out)
    return out


def softmax_first(scores):
    raised = jnp.exp(scores - jnp.max(scores, axis=0, keepdims=True))
    return raised * (1.0 / jnp.sum(raised, axis=0, keepdims=True))


def put_tiles(scratch, rows, values):
    tiles, _, lanes = scratch.shape
    for tile in range(tiles):
        scratch[tile, rows, :] = values[:, tile * lanes : (tile + 1) * lanes]


def get_tiles(scratch, rows):
    return jnp.concatenate([scratch[tile, rows, :] for tile in range(scratch.shape[0])], axis=-1)


def time_kernel(
    sizes, slopes_ref, block_ref, project_ref, output_ref, out_ref, seq_scr, token_scr, qkv_scr, heads_scr
):
    sources, dates_each, groups, head_count, packed, columns_each = sizes
    width = block_ref.shape[2]
    head_size = width // head_count
    lanes = packed * head_size
    length = sources * dates_each
    token_rows = dates_each * groups
    inverse_root = 1.0 / math.sqrt(head_size)
    info = []
    for source in range(sources):
        plane = block_ref[source].astype(wide)
        put_tiles(
            seq_scr, slice(source * token_rows, (source + 1) * token_rows), plane[:token_rows]
        )
        info.append(plane[token_rows : token_rows + dates_each])
    info = jnp.concatenate(info, axis=0)
    for group in range(groups):
        token_scr[group * length : (group + 1) * length, :] = get_tiles(
            seq_scr, pl.ds(group, length, stride=groups)
        )
    tokens = token_scr[...]
    qkv_scr[...] = matmul(rms_norm(tokens), project_ref[...]).astype(low)
    numbers = info[:, groups : groups + 1] * 32.0 + info[:, groups + 1 : groups + 2]
    key_at = lax.broadcasted_iota(jnp.int32, (length, packed * length), 0)
    column_at = lax.broadcasted_iota(jnp.int32, (length, packed * length), 1)
    same_date = key_at == column_at % length
    query_numbers = jnp.sum(jnp.where(same_date, numbers, 0.0), axis=0, keepdims=True)
    gap_days = jnp.abs(numbers - query_numbers)
    head_at = column_at // length
    mask = block_mask(length, packed, head_size)
    biases = []
    for first in range(0, head_count, packed):
        slope = jnp.full((length, packed * length), slopes_ref[first], wide)
        for head in range(1, packed):
            slope = jnp.where(head_at == head, slopes_ref[first + head], slope)
        biases.append(-slope * gap_days)
    for group in range(groups):
        rows = slice(group * length, (group + 1) * length)
        allowed = (info[:, group : group + 1] > 0) | same_date
        for part in range(head_count // packed):
            start = part * lanes
            query = qkv_scr[rows, start : start + lanes]
            key = qkv_scr[rows, width + start : width + start + lanes]
            value = qkv_scr[rows, 2 * width + start : 2 * width + start + lanes]
            scores = contract_last(key, spread(query, mask, packed)) * inverse_root + biases[part]
            weights = softmax_first(jnp.where(allowed, scores, masked_score)).astype(low)
            full = contract_rows(weights, value)
            heads_scr[rows, start : start + lanes] = own_blocks(
                full, length, packed, head_size
            ).astype(low)
    hidden = token_scr[...] + matmul(heads_scr[...], output_ref[...])
    for group in range(groups):
        first = (group // columns_each) * (length * columns_each) + group % columns_each
        put_tiles(
            seq_scr,
            pl.ds(first, length, stride=columns_each),
            hidden[group * length : (group + 1) * length],
        )
    out_ref[...] = get_tiles(seq_scr, slice(None)).astype(low)


def column_kernel(
    sizes,
    hidden_ref,
    cotangent_ref,
    project_ref,
    output_ref,
    mixed_ref,
    project_grad_ref,
    output_grad_ref,
    seq_scr,
    grad_scr,
    plane_scr,
    normed_scr,
    qkv_scr,
    grad_low_scr,
    heads_grad_scr,
    heads_scr,
    qkv_grad_scr,
):
    dates_each, row_parts, rows_each, columns_each, head_count, packed, row_major = sizes
    width = hidden_ref.shape[1]
    head_size = width // head_count
    lanes = packed * head_size
    length = row_parts * rows_each
    groups = dates_each * columns_each
    inverse_root = 1.0 / math.sqrt(head_size)
    put_tiles(seq_scr, slice(None), hidden_ref[...].astype(wide))
    put_tiles(grad_scr, slice(None), cotangent_ref[...].astype(wide))
    for group in range(groups):
        rows = slice(group * length, (group + 1) * length)
        first = (group // columns_each) * (length * columns_each) + group % columns_each
        if row_major:
            plane_scr[rows, :] = get_tiles(seq_scr, pl.ds(group, length, stride=groups))
        else:
            plane_scr[rows, :] = get_tiles(seq_scr, pl.ds(first, length, stride=columns_each))
        grad_low_scr[rows, :] = get_tiles(
            grad_scr, pl.ds(first, length, stride=columns_each)
        ).astype(low)
    normed_scr[...] = rms_norm(plane_scr[...])
    qkv_scr[...] = matmul(normed_scr[...], project_ref[...]).astype(low)
    heads_grad_scr[...] = contract_last(grad_low_scr[...], output_ref[...]).astype(low)
    mask = block_mask(length, packed, head_size)
    for group in range(groups):
        rows = slice(group * length, (group + 1) * length)
        for part in range(head_count // packed):
            start = part * lanes
            at_query = slice(start, start + lanes)
            at_key = slice(width + start, width + start + lanes)
            at_value = slice(2 * width + start, 2 * width + start + lanes)
            query = spread(qkv_scr[rows, at_query], mask, packed)
            key = qkv_scr[rows, at_key]
            value = qkv_scr[rows, at_value]
            heads_grad = spread(heads_grad_scr[rows, at_query], mask, packed)
            weights = softmax_first(contract_last(key, query) * inverse_root)
            weights_low = weights.astype(low)
            heads_scr[rows, at_query] = own_blocks(
                contract_rows(weights_low, value), length, packed, head_size
            ).astype(low)
            product_grad = contract_last(value, heads_grad)
            score_grad = weights * (
                product_grad - jnp.sum(weights * product_grad, axis=0, keepdims=True)
            )
            score_low = score_grad.astype(low)
            query_grad = own_blocks(contract_rows(score_low, key), length, packed, head_size)
            qkv_grad_scr[rows, at_query] = (query_grad * inverse_root).astype(low)
            qkv_grad_scr[rows, at_key] = (matmul(score_low, query) * inverse_root).astype(low)
            qkv_grad_scr[rows, at_value] = matmul(weights_low, heads_grad).astype(low)
    mixed = plane_scr[...] + matmul(heads_scr[...], output_ref[...])
    part_rows = dates_each * rows_each * columns_each
    for group in range(groups):
        inner = (group // columns_each) * (rows_each * columns_each) + group % columns_each
        for part in range(row_parts):
            begin = group * length + part * rows_each
            put_tiles(
                seq_scr,
                pl.ds(part * part_rows + inner, rows_each, stride=columns_each),
                mixed[begin : begin + rows_each],
            )
    mixed_ref[...] = get_tiles(seq_scr, slice(None)).astype(low)
    project_grad_ref[...] = contract_rows(qkv_grad_scr[...], normed_scr[...])
    output_grad_ref[...] = contract_rows(grad_low_scr[...], heads_scr[...])


def body(
    row_size,
    date_size,
    tokens,
    clear_flags,
    date_numbers,
    decay_slopes,
    time_project,
    time_output,
    column_project,
    column_output,
    cotangent,
):
    date_local, row_local, column_count, width = tokens.shape
    head_count = decay_slopes.shape[0]
    head_size = width // head_count
    packed = max(1, 128 // head_size)
    local_patches = row_local * column_count
    patches_each = local_patches // date_size
    columns_each = column_count // row_size
    row_count = row_local * row_size
    date_count = date_local * date_size
    direct = patches_each == column_count

    cotangent_planes = lax.all_to_all(cotangent, "row", split_axis=2, concat_axis=1, tiled=True)
    token_rows = date_local * patches_each
    block_rows = -(-(token_rows + date_local) // 8) * 8
    flags = jnp.transpose(
        clear_flags.reshape(date_local, date_size, patches_each), (1, 0, 2)
    ).astype(low)
    numbers = jnp.stack([date_numbers // 32, date_numbers % 32], axis=-1).astype(low)
    numbers = jnp.broadcast_to(numbers[None], (date_size, date_local, 2))
    info = jnp.concatenate([flags, numbers], axis=-1)
    info = jnp.pad(
        info, ((0, 0), (0, block_rows - token_rows - date_local), (0, width - patches_each - 2))
    )
    outgoing = jnp.transpose(
        tokens.reshape(date_local, date_size, patches_each, width), (1, 0, 2, 3)
    ).reshape(date_size, token_rows, width)
    outgoing = jnp.concatenate([outgoing, info], axis=1)
    incoming = lax.all_to_all(outgoing, "date", split_axis=0, concat_axis=0, tiled=True)

    time_tokens = date_count * patches_each
    hidden = pl.pallas_call(
        functools.partial(
            time_kernel,
            (
                date_size,
                date_local,
                patches_each,
                head_count,
                packed,
                columns_each if direct else patches_each,
            ),
        ),
        out_shape=jax.ShapeDtypeStruct((time_tokens, width), low),
        in_specs=[pl.BlockSpec(memory_space=pltpu.SMEM)]
        + [pl.BlockSpec(memory_space=pltpu.VMEM)] * 3,
        out_specs=pl.BlockSpec(memory_space=pltpu.VMEM),
        scratch_shapes=[
            pltpu.VMEM((width // 128, time_tokens, 128), wide),
            pltpu.VMEM((time_tokens, width), wide),
            pltpu.VMEM((time_tokens, 3 * width), low),
            pltpu.VMEM((time_tokens, width), low),
        ],
        compiler_params=pltpu.CompilerParams(vmem_limit_bytes=vmem_limit),
        name="time_attention",
    )(decay_slopes, incoming, time_project, time_output)

    column_tokens = date_local * row_count * columns_each
    if direct:
        parts = hidden.reshape(row_size * date_size, date_local * columns_each, width)
        plane = lax.all_to_all(parts, ("row", "date"), split_axis=0, concat_axis=0, tiled=True)
    else:
        parts = hidden.reshape(date_size, date_local, patches_each, width)
        back = lax.all_to_all(parts, "date", split_axis=0, concat_axis=0, tiled=True)
        back = jnp.transpose(back, (1, 0, 2, 3)).reshape(
            date_local, row_local, column_count, width
        )
        plane = lax.all_to_all(back, "row", split_axis=2, concat_axis=1, tiled=True)
    plane = plane.reshape(column_tokens, width)
    mixed, project_grad, output_grad = pl.pallas_call(
        functools.partial(
            column_kernel,
            (date_local, row_size, row_local, columns_each, head_count, packed, direct),
        ),
        out_shape=(
            jax.ShapeDtypeStruct((column_tokens, width), low),
            jax.ShapeDtypeStruct((3 * width, width), wide),
            jax.ShapeDtypeStruct((width, width), wide),
        ),
        scratch_shapes=[
            pltpu.VMEM((width // 128, column_tokens, 128), wide),
            pltpu.VMEM((width // 128, column_tokens, 128), wide),
            pltpu.VMEM((column_tokens, width), wide),
            pltpu.VMEM((column_tokens, width), low),
            pltpu.VMEM((column_tokens, 3 * width), low),
            pltpu.VMEM((column_tokens, width), low),
            pltpu.VMEM((column_tokens, width), low),
            pltpu.VMEM((column_tokens, width), low),
            pltpu.VMEM((column_tokens, 3 * width), low),
        ],
        compiler_params=pltpu.CompilerParams(vmem_limit_bytes=vmem_limit),
        name="column_attention",
    )(plane, cotangent_planes.reshape(column_tokens, width), column_project, column_output)

    project_each = 3 * width // date_size
    output_each = width // date_size
    lane_each = width // row_size
    grads = jnp.concatenate(
        [
            project_grad.reshape(date_size, project_each, row_size, lane_each),
            output_grad.reshape(date_size, output_each, row_size, lane_each),
        ],
        axis=1,
    ).astype(low)
    grads = jnp.transpose(grads, (2, 0, 1, 3)).reshape(
        row_size * date_size, project_each + output_each, lane_each
    )
    terms = lax.all_to_all(grads, ("row", "date"), split_axis=0, concat_axis=0, tiled=True)
    owned = jnp.sum(terms.astype(wide), axis=0)

    mixed = mixed.reshape(row_size, date_local, row_local, columns_each, width)
    mixed = lax.all_to_all(mixed, "row", split_axis=0, concat_axis=0, tiled=True)
    mixed = jnp.transpose(mixed, (1, 2, 0, 3, 4)).reshape(
        date_local, row_local, column_count, width
    )
    owned_project = jnp.transpose(owned[:project_each])
    owned_output = jnp.transpose(owned[project_each:])
    return (mixed, owned_project, owned_output)


def solution(mesh):
    return jax.shard_map(
        functools.partial(body, mesh.shape["row"], mesh.shape["date"]),
        mesh=mesh,
        in_specs=(
            P("date", "row", None, None),
            P("date", "row", None),
            P("date"),
            P(),
            P(),
            P(),
            P(),
            P(),
            P("date", "row", None, None),
        ),
        out_specs=(P("date", "row", None, None), P("row", "date"), P("row", "date")),
        check_vma=False,
    )
```

```python
import functools
import math

import jax
import jax.numpy as jnp
from jax import lax
from jax.experimental import pallas as pl
from jax.experimental.pallas import tpu as pltpu
from jax.sharding import PartitionSpec as P

epsilon = 1e-06
masked_score = -1e30
units_each = 6
dates = ("outer", "pair")
vmem_limit = 48 * 1024 * 1024
low = jnp.bfloat16
wide = jnp.float32


def rms_norm(values):
    factor = lax.rsqrt(jnp.mean(values * values, axis=-1, keepdims=True) + epsilon)
    return (values * factor).astype(low)


def matmul(left, right):
    return jnp.dot(left, right, preferred_element_type=wide)


def contract_rows(left, right):
    return lax.dot_general(left, right, (((0,), (0,)), ((), ())), preferred_element_type=wide)


def contract_last(left, right):
    return lax.dot_general(left, right, (((1,), (1,)), ((), ())), preferred_element_type=wide)


def block_mask(length, packed, head_size):
    shape = (packed * length, packed * head_size)
    rows = lax.broadcasted_iota(jnp.int32, shape, 0) // length
    lanes = lax.broadcasted_iota(jnp.int32, shape, 1) // head_size
    return jnp.where(rows == lanes, 1.0, 0.0).astype(low)


def spread(values, mask, packed):
    return jnp.concatenate([values] * packed, axis=0) * mask


def batches(groups, parts, each):
    units = [(group, part) for group in range(groups) for part in range(parts)]
    return [units[first : first + each] for first in range(0, len(units), each)]


def own_blocks(full, length, packed, head_size):
    lanes = lax.broadcasted_iota(jnp.int32, (length, packed * head_size), 1) // head_size
    out = full[:length]
    for head in range(1, packed):
        out = jnp.where(lanes == head, full[head * length : (head + 1) * length], out)
    return out


def softmax_first(scores):
    raised = jnp.exp(scores - jnp.max(scores, axis=0, keepdims=True))
    return raised * (1.0 / jnp.sum(raised, axis=0, keepdims=True))


def put_tiles(scratch, rows, values):
    tiles, _, lanes = scratch.shape
    for tile in range(tiles):
        scratch[tile, rows, :] = values[:, tile * lanes : (tile + 1) * lanes]


def get_tiles(scratch, rows):
    return jnp.concatenate([scratch[tile, rows, :] for tile in range(scratch.shape[0])], axis=-1)


def time_kernel(
    sizes, slopes_ref, block_ref, project_ref, output_ref, out_ref, seq_scr, token_scr, qkv_scr, heads_scr
):
    sources, dates_each, groups, head_count, packed, columns_each = sizes
    width = block_ref.shape[2]
    head_size = width // head_count
    lanes = packed * head_size
    length = sources * dates_each
    token_rows = dates_each * groups
    inverse_root = 1.0 / math.sqrt(head_size)
    info = []
    for source in range(sources):
        plane = block_ref[source].astype(wide)
        put_tiles(
            seq_scr, slice(source * token_rows, (source + 1) * token_rows), plane[:token_rows]
        )
        info.append(plane[token_rows : token_rows + dates_each])
    info = jnp.concatenate(info, axis=0)
    for group in range(groups):
        token_scr[group * length : (group + 1) * length, :] = get_tiles(
            seq_scr, pl.ds(group, length, stride=groups)
        )
    tokens = token_scr[...]
    qkv_scr[...] = matmul(rms_norm(tokens), project_ref[...]).astype(low)
    numbers = info[:, groups : groups + 1] * 32.0 + info[:, groups + 1 : groups + 2]
    key_at = lax.broadcasted_iota(jnp.int32, (length, packed * length), 0)
    column_at = lax.broadcasted_iota(jnp.int32, (length, packed * length), 1)
    same_date = key_at == column_at % length
    query_numbers = jnp.sum(jnp.where(same_date, numbers, 0.0), axis=0, keepdims=True)
    gap_days = jnp.abs(numbers - query_numbers)
    head_at = column_at // length
    mask = block_mask(length, packed, head_size)
    biases = []
    for first in range(0, head_count, packed):
        slope = jnp.full((length, packed * length), slopes_ref[first], wide)
        for head in range(1, packed):
            slope = jnp.where(head_at == head, slopes_ref[first + head], slope)
        biases.append(-slope * gap_days)
    for units in batches(groups, head_count // packed, units_each):
        all_scores = []
        for group, part in units:
            rows = slice(group * length, (group + 1) * length)
            start = part * lanes
            query = qkv_scr[rows, start : start + lanes]
            key = qkv_scr[rows, width + start : width + start + lanes]
            all_scores.append(contract_last(key, spread(query, mask, packed)))
        all_weights = []
        for (group, part), scores in zip(units, all_scores):
            allowed = (info[:, group : group + 1] > 0) | same_date
            scores = jnp.where(allowed, scores * inverse_root + biases[part], masked_score)
            all_weights.append(softmax_first(scores).astype(low))
        all_heads = []
        for (group, part), weights in zip(units, all_weights):
            rows = slice(group * length, (group + 1) * length)
            start = 2 * width + part * lanes
            all_heads.append(contract_rows(weights, qkv_scr[rows, start : start + lanes]))
        for (group, part), full in zip(units, all_heads):
            rows = slice(group * length, (group + 1) * length)
            heads_scr[rows, part * lanes : (part + 1) * lanes] = own_blocks(
                full, length, packed, head_size
            ).astype(low)
    hidden = token_scr[...] + matmul(heads_scr[...], output_ref[...])
    for group in range(groups):
        first = (group // columns_each) * (length * columns_each) + group % columns_each
        put_tiles(
            seq_scr,
            pl.ds(first, length, stride=columns_each),
            hidden[group * length : (group + 1) * length],
        )
    out_ref[...] = get_tiles(seq_scr, slice(None)).astype(low)


def column_kernel(
    sizes,
    pair_ref,
    hidden_ref,
    cotangent_ref,
    project_ref,
    output_ref,
    mixed_ref,
    first_grad_ref,
    second_grad_ref,
    seq_scr,
    grad_scr,
    plane_scr,
    normed_scr,
    qkv_scr,
    grad_low_scr,
    heads_grad_scr,
    heads_scr,
    qkv_grad_scr,
):
    dates_each, row_parts, rows_each, columns_each, head_count, packed, row_major, date_size = sizes
    width = hidden_ref.shape[1]
    head_size = width // head_count
    lanes = packed * head_size
    length = row_parts * rows_each
    groups = dates_each * columns_each
    inverse_root = 1.0 / math.sqrt(head_size)
    put_tiles(seq_scr, slice(None), hidden_ref[...].astype(wide))
    put_tiles(grad_scr, slice(None), cotangent_ref[...].astype(wide))
    for group in range(groups):
        rows = slice(group * length, (group + 1) * length)
        first = (group // columns_each) * (length * columns_each) + group % columns_each
        if row_major:
            plane_scr[rows, :] = get_tiles(seq_scr, pl.ds(group, length, stride=groups))
        else:
            plane_scr[rows, :] = get_tiles(seq_scr, pl.ds(first, length, stride=columns_each))
        grad_low_scr[rows, :] = get_tiles(
            grad_scr, pl.ds(first, length, stride=columns_each)
        ).astype(low)
    normed_scr[...] = rms_norm(plane_scr[...])
    qkv_scr[...] = matmul(normed_scr[...], project_ref[...]).astype(low)
    heads_grad_scr[...] = contract_last(grad_low_scr[...], output_ref[...]).astype(low)
    mask = block_mask(length, packed, head_size)
    for units in batches(groups, head_count // packed, units_each):
        places = []
        for group, part in units:
            start = part * lanes
            places.append(
                (
                    slice(group * length, (group + 1) * length),
                    slice(start, start + lanes),
                    slice(width + start, width + start + lanes),
                    slice(2 * width + start, 2 * width + start + lanes),
                )
            )
        all_scores = []
        for rows, at_query, at_key, at_value in places:
            query = spread(qkv_scr[rows, at_query], mask, packed)
            heads_grad = spread(heads_grad_scr[rows, at_query], mask, packed)
            all_scores.append(
                (
                    contract_last(qkv_scr[rows, at_key], query),
                    contract_last(qkv_scr[rows, at_value], heads_grad),
                )
            )
        all_weights = []
        for scores, product_grad in all_scores:
            weights = softmax_first(scores * inverse_root)
            score_grad = weights * (
                product_grad - jnp.sum(weights * product_grad, axis=0, keepdims=True)
            )
            all_weights.append((weights.astype(low), score_grad.astype(low)))
        all_full = []
        for (rows, at_query, at_key, at_value), (weights, score_low) in zip(places, all_weights):
            all_full.append(
                (
                    contract_rows(weights, qkv_scr[rows, at_value]),
                    contract_rows(score_low, qkv_scr[rows, at_key]),
                )
            )
            query = spread(qkv_scr[rows, at_query], mask, packed)
            heads_grad = spread(heads_grad_scr[rows, at_query], mask, packed)
            key_grad = matmul(score_low, query) * inverse_root
            qkv_grad_scr[rows, at_key] = key_grad.astype(low)
            qkv_grad_scr[rows, at_value] = matmul(weights, heads_grad).astype(low)
        for (rows, at_query, _, _), (heads_full, query_full) in zip(places, all_full):
            heads = own_blocks(heads_full, length, packed, head_size)
            heads_scr[rows, at_query] = heads.astype(low)
            query_grad = own_blocks(query_full, length, packed, head_size) * inverse_root
            qkv_grad_scr[rows, at_query] = query_grad.astype(low)
    mixed = plane_scr[...] + matmul(heads_scr[...], output_ref[...])
    part_rows = dates_each * rows_each * columns_each
    for group in range(groups):
        inner = (group // columns_each) * (rows_each * columns_each) + group % columns_each
        for part in range(row_parts):
            begin = group * length + part * rows_each
            put_tiles(
                seq_scr,
                pl.ds(part * part_rows + inner, rows_each, stride=columns_each),
                mixed[begin : begin + rows_each],
            )
    mixed_ref[...] = get_tiles(seq_scr, slice(None)).astype(low)
    project_grad = contract_rows(qkv_grad_scr[...], normed_scr[...])
    output_grad = contract_rows(grad_low_scr[...], heads_scr[...])
    if date_size is None:
        first_grad_ref[...] = project_grad
        second_grad_ref[...] = output_grad
        return
    keep_ref, send_ref = first_grad_ref, second_grad_ref
    even = pair_ref[0] == 0
    project_each = project_grad.shape[0] // date_size
    output_each = output_grad.shape[0] // date_size
    half = (project_each + output_each) // 2
    lower = lax.broadcasted_iota(jnp.int32, (half, 128), 1) < 64
    for outer in range(date_size // 2):
        pair = []
        for part in (2 * outer, 2 * outer + 1):
            block = jnp.concatenate(
                [
                    project_grad[part * project_each : (part + 1) * project_each],
                    output_grad[part * output_each : (part + 1) * output_each],
                ],
                axis=0,
            )
            top, bottom = block[:half, 128:256], block[half:, 128:256]
            pair.append(
                (
                    (block[:, :128], jnp.where(lower, top, pltpu.roll(bottom, 64, 1))),
                    (block[:, 256:], jnp.where(lower, pltpu.roll(top, 64, 1), bottom)),
                )
            )
        for row_part in range(2):
            for first, one, two in zip((0, 2 * half), pair[0][row_part], pair[1][row_part]):
                at = slice(first, first + one.shape[0])
                keep_ref[row_part, outer, at, :] = jnp.where(even, one, two).astype(low)
                send_ref[row_part, outer, at, :] = jnp.where(even, two, one).astype(low)


def finish_kernel(project_each, row_ref, terms_ref, project_ref, output_ref):
    total = terms_ref[0].astype(wide)
    for source in range(1, terms_ref.shape[0]):
        total = total + terms_ref[source].astype(wide)
    whole = 2 * total.shape[0] // 3
    main = jnp.transpose(total[:whole])
    tail = jnp.transpose(total[whole:])
    tail = jnp.concatenate([tail[:64], tail[64:]], axis=1)
    first = row_ref[0] == 0
    front = jnp.concatenate([main, tail], axis=0)
    back = jnp.concatenate([tail, main], axis=0)
    owned = jnp.where(first, front, back)
    project_ref[...] = owned[:, :project_each]
    output_ref[...] = owned[:, project_each:]


def body(
    row_size,
    date_size,
    pair_size,
    tokens,
    clear_flags,
    date_numbers,
    decay_slopes,
    time_project,
    time_output,
    column_project,
    column_output,
    cotangent,
):
    date_local, row_local, column_count, width = tokens.shape
    head_count = decay_slopes.shape[0]
    head_size = width // head_count
    packed = max(1, 128 // head_size)
    local_patches = row_local * column_count
    patches_each = local_patches // date_size
    columns_each = column_count // row_size
    row_count = row_local * row_size
    date_count = date_local * date_size
    direct = patches_each == column_count

    cotangent_planes = lax.all_to_all(cotangent, "row", split_axis=2, concat_axis=1, tiled=True)
    token_rows = date_local * patches_each
    block_rows = -(-(token_rows + date_local) // 8) * 8
    flags = jnp.transpose(
        clear_flags.reshape(date_local, date_size, patches_each), (1, 0, 2)
    ).astype(low)
    numbers = jnp.stack([date_numbers // 32, date_numbers % 32], axis=-1).astype(low)
    numbers = jnp.broadcast_to(numbers[None], (date_size, date_local, 2))
    info = jnp.concatenate([flags, numbers], axis=-1)
    info = jnp.pad(
        info, ((0, 0), (0, block_rows - token_rows - date_local), (0, width - patches_each - 2))
    )
    outgoing = jnp.transpose(
        tokens.reshape(date_local, date_size, patches_each, width), (1, 0, 2, 3)
    ).reshape(date_size, token_rows, width)
    outgoing = jnp.concatenate([outgoing, info], axis=1)
    incoming = lax.all_to_all(outgoing, dates, split_axis=0, concat_axis=0, tiled=True)

    time_tokens = date_count * patches_each
    hidden = pl.pallas_call(
        functools.partial(
            time_kernel,
            (
                date_size,
                date_local,
                patches_each,
                head_count,
                packed,
                columns_each if direct else patches_each,
            ),
        ),
        out_shape=jax.ShapeDtypeStruct((time_tokens, width), low),
        in_specs=[pl.BlockSpec(memory_space=pltpu.SMEM)]
        + [pl.BlockSpec(memory_space=pltpu.VMEM)] * 3,
        out_specs=pl.BlockSpec(memory_space=pltpu.VMEM),
        scratch_shapes=[
            pltpu.VMEM((width // 128, time_tokens, 128), wide),
            pltpu.VMEM((time_tokens, width), wide),
            pltpu.VMEM((time_tokens, 3 * width), low),
            pltpu.VMEM((time_tokens, width), low),
        ],
        compiler_params=pltpu.CompilerParams(vmem_limit_bytes=vmem_limit),
        name="time_attention",
    )(decay_slopes, incoming, time_project, time_output)

    column_tokens = date_local * row_count * columns_each
    if direct:
        parts = hidden.reshape(row_size * date_size, date_local * columns_each, width)
        plane = lax.all_to_all(parts, ("row", *dates), split_axis=0, concat_axis=0, tiled=True)
    else:
        parts = hidden.reshape(date_size, date_local, patches_each, width)
        back = lax.all_to_all(parts, dates, split_axis=0, concat_axis=0, tiled=True)
        back = jnp.transpose(back, (1, 0, 2, 3)).reshape(
            date_local, row_local, column_count, width
        )
        plane = lax.all_to_all(back, "row", split_axis=2, concat_axis=1, tiled=True)
    plane = plane.reshape(column_tokens, width)
    project_each = 3 * width // date_size
    output_each = width // date_size
    lane_each = width // row_size
    paired = (
        pair_size == 2
        and row_size == 2
        and lane_each == 192
        and project_each % 8 == 0
        and output_each % 8 == 0
        and (project_each + output_each) % 32 == 0
    )
    pair_at = lax.axis_index("pair")
    if paired:
        packed_rows = (project_each + output_each) * 3 // 2
        grad_shapes = (
            jax.ShapeDtypeStruct((row_size, date_size // 2, packed_rows, 128), low),
        ) * 2
    else:
        grad_shapes = (
            jax.ShapeDtypeStruct((3 * width, width), wide),
            jax.ShapeDtypeStruct((width, width), wide),
        )
    mixed, first_grad, second_grad = pl.pallas_call(
        functools.partial(
            column_kernel,
            (
                date_local,
                row_size,
                row_local,
                columns_each,
                head_count,
                packed,
                direct,
                date_size if paired else None,
            ),
        ),
        out_shape=(jax.ShapeDtypeStruct((column_tokens, width), low), *grad_shapes),
        in_specs=[pl.BlockSpec(memory_space=pltpu.SMEM)]
        + [pl.BlockSpec(memory_space=pltpu.VMEM)] * 4,
        scratch_shapes=[
            pltpu.VMEM((width // 128, column_tokens, 128), wide),
            pltpu.VMEM((width // 128, column_tokens, 128), wide),
            pltpu.VMEM((column_tokens, width), wide),
            pltpu.VMEM((column_tokens, width), low),
            pltpu.VMEM((column_tokens, 3 * width), low),
            pltpu.VMEM((column_tokens, width), low),
            pltpu.VMEM((column_tokens, width), low),
            pltpu.VMEM((column_tokens, width), low),
            pltpu.VMEM((column_tokens, 3 * width), low),
        ],
        compiler_params=pltpu.CompilerParams(vmem_limit_bytes=vmem_limit),
        name="column_attention",
    )(
        pair_at.reshape(1),
        plane,
        cotangent_planes.reshape(column_tokens, width),
        column_project,
        column_output,
    )


    if paired:
        arrived = lax.ppermute(second_grad, "pair", [(0, 1), (1, 0)])
        halves = (first_grad.astype(wide) + arrived.astype(wide)).astype(low)
        halves = halves.reshape(row_size * date_size // 2, packed_rows, 128)
        terms = lax.all_to_all(halves, ("row", "outer"), split_axis=0, concat_axis=0, tiled=True)
        owned_project, owned_output = pl.pallas_call(
            functools.partial(finish_kernel, project_each),
            out_shape=(
                jax.ShapeDtypeStruct((lane_each, project_each), wide),
                jax.ShapeDtypeStruct((lane_each, output_each), wide),
            ),
            in_specs=[
                pl.BlockSpec(memory_space=pltpu.SMEM),
                pl.BlockSpec(memory_space=pltpu.VMEM),
            ],
            name="gradient_sum",
        )(lax.axis_index("row").reshape(1), terms)
    else:
        grads = jnp.concatenate(
            [
                first_grad.reshape(date_size, project_each, row_size, lane_each),
                second_grad.reshape(date_size, output_each, row_size, lane_each),
            ],
            axis=1,
        ).astype(low)
        grads = jnp.transpose(grads, (2, 0, 1, 3)).reshape(
            row_size * date_size, project_each + output_each, lane_each
        )
        terms = lax.all_to_all(grads, ("row", *dates), split_axis=0, concat_axis=0, tiled=True)
        owned = jnp.sum(terms.astype(wide), axis=0)
        owned_project = jnp.transpose(owned[:project_each])
        owned_output = jnp.transpose(owned[project_each:])

    mixed = mixed.reshape(row_size, date_local, row_local, columns_each, width)
    mixed = lax.all_to_all(mixed, "row", split_axis=0, concat_axis=0, tiled=True)
    mixed = jnp.transpose(mixed, (1, 2, 0, 3, 4)).reshape(
        date_local, row_local, column_count, width
    )
    return (mixed, owned_project, owned_output)


def solution(mesh):
    date_size, row_size = mesh.shape["date"], mesh.shape["row"]
    pair_size = 2 if date_size % 2 == 0 else 1
    split = jax.sharding.Mesh(
        mesh.devices.reshape(date_size // pair_size, pair_size, row_size),
        ("outer", "pair", "row"),
    )
    return jax.shard_map(
        functools.partial(body, row_size, date_size, pair_size),
        mesh=split,
        in_specs=(
            P(dates, "row", None, None),
            P(dates, "row", None),
            P(dates),
            P(),
            P(),
            P(),
            P(),
            P(),
            P(dates, "row", None, None),
        ),
        out_specs=(P(dates, "row", None, None), P("row", dates), P("row", dates)),
        check_vma=False,
    )
```

```python
import functools
import math

import jax
import jax.numpy as jnp
from jax import lax
from jax.experimental import pallas as pl
from jax.experimental.pallas import tpu as pltpu
from jax.sharding import PartitionSpec as P

epsilon = 1e-06
masked_score = -1e30
units_each = 6
dates = ("outer", "pair")
vmem_limit = 48 * 1024 * 1024
low = jnp.bfloat16
wide = jnp.float32


def rms_norm(values):
    factor = lax.rsqrt(jnp.mean(values * values, axis=-1, keepdims=True) + epsilon)
    return (values * factor).astype(low)


def matmul(left, right):
    return jnp.dot(left, right, preferred_element_type=wide)


def contract_rows(left, right):
    return lax.dot_general(left, right, (((0,), (0,)), ((), ())), preferred_element_type=wide)


def contract_last(left, right):
    return lax.dot_general(left, right, (((1,), (1,)), ((), ())), preferred_element_type=wide)


def block_mask(length, packed, head_size):
    shape = (packed * length, packed * head_size)
    rows = lax.broadcasted_iota(jnp.int32, shape, 0) // length
    lanes = lax.broadcasted_iota(jnp.int32, shape, 1) // head_size
    return jnp.where(rows == lanes, 1.0, 0.0).astype(low)


def spread(values, mask, packed):
    return jnp.concatenate([values] * packed, axis=0) * mask


def batches(groups, parts, each):
    units = [(group, part) for group in range(groups) for part in range(parts)]
    return [units[first : first + each] for first in range(0, len(units), each)]


def own_blocks(full, length, packed, head_size):
    lanes = lax.broadcasted_iota(jnp.int32, (length, packed * head_size), 1) // head_size
    out = full[:length]
    for head in range(1, packed):
        out = jnp.where(lanes == head, full[head * length : (head + 1) * length], out)
    return out


def softmax_first(scores):
    raised = jnp.exp(scores - jnp.max(scores, axis=0, keepdims=True))
    return raised * (1.0 / jnp.sum(raised, axis=0, keepdims=True))


def put_tiles(scratch, rows, values):
    tiles, _, lanes = scratch.shape
    for tile in range(tiles):
        scratch[tile, rows, :] = values[:, tile * lanes : (tile + 1) * lanes]


def get_tiles(scratch, rows):
    return jnp.concatenate([scratch[tile, rows, :] for tile in range(scratch.shape[0])], axis=-1)


def pack_kernel(numbers_ref, tokens_ref, flags_ref, out_ref):
    dates_each, parts, patches, width = tokens_ref.shape
    spare = out_ref.shape[1] - dates_each * patches
    place = lax.broadcasted_iota(jnp.int32, (patches, width), 0)
    lane = lax.broadcasted_iota(jnp.int32, (patches, width), 1)
    place = jnp.where(place == lane, 1.0, 0.0).astype(low)
    lane = lax.broadcasted_iota(jnp.int32, (parts, width), 1)
    infos = []
    for date in range(dates_each):
        number = numbers_ref[date]
        upper = (number // 32).astype(wide)
        under = (number % 32).astype(wide)
        info = matmul(flags_ref[date].astype(wide).astype(low), place)
        info = jnp.where(lane == patches, upper, info)
        infos.append(jnp.where(lane == patches + 1, under, info))
    row = lax.broadcasted_iota(jnp.int32, (spare, width), 0)
    for part in range(parts):
        pieces = [tokens_ref[date, part].astype(wide) for date in range(dates_each)]
        extra = jnp.zeros((spare, width), wide)
        for date in range(dates_each):
            extra = jnp.where(row == date, infos[date][part : part + 1], extra)
        out_ref[part] = jnp.concatenate(pieces + [extra], axis=0).astype(low)


def time_kernel(
    sizes, slopes_ref, block_ref, project_ref, output_ref, out_ref, seq_scr, token_scr, qkv_scr, heads_scr
):
    sources, dates_each, groups, head_count, packed, columns_each = sizes
    width = block_ref.shape[2]
    head_size = width // head_count
    lanes = packed * head_size
    length = sources * dates_each
    token_rows = dates_each * groups
    inverse_root = 1.0 / math.sqrt(head_size)
    info = []
    for source in range(sources):
        plane = block_ref[source].astype(wide)
        put_tiles(
            seq_scr, slice(source * token_rows, (source + 1) * token_rows), plane[:token_rows]
        )
        info.append(plane[token_rows : token_rows + dates_each])
    info = jnp.concatenate(info, axis=0)
    for group in range(groups):
        token_scr[group * length : (group + 1) * length, :] = get_tiles(
            seq_scr, pl.ds(group, length, stride=groups)
        )
    tokens = token_scr[...]
    qkv_scr[...] = matmul(rms_norm(tokens), project_ref[...]).astype(low)
    numbers = info[:, groups : groups + 1] * 32.0 + info[:, groups + 1 : groups + 2]
    key_at = lax.broadcasted_iota(jnp.int32, (length, packed * length), 0)
    column_at = lax.broadcasted_iota(jnp.int32, (length, packed * length), 1)
    same_date = key_at == column_at % length
    query_numbers = jnp.sum(jnp.where(same_date, numbers, 0.0), axis=0, keepdims=True)
    gap_days = jnp.abs(numbers - query_numbers)
    head_at = column_at // length
    mask = block_mask(length, packed, head_size)
    biases = []
    for first in range(0, head_count, packed):
        slope = jnp.full((length, packed * length), slopes_ref[first], wide)
        for head in range(1, packed):
            slope = jnp.where(head_at == head, slopes_ref[first + head], slope)
        biases.append(-slope * gap_days)
    for units in batches(groups, head_count // packed, units_each):
        all_scores = []
        for group, part in units:
            rows = slice(group * length, (group + 1) * length)
            start = part * lanes
            query = qkv_scr[rows, start : start + lanes]
            key = qkv_scr[rows, width + start : width + start + lanes]
            all_scores.append(contract_last(key, spread(query, mask, packed)))
        all_weights = []
        for (group, part), scores in zip(units, all_scores):
            allowed = (info[:, group : group + 1] > 0) | same_date
            scores = jnp.where(allowed, scores * inverse_root + biases[part], masked_score)
            all_weights.append(softmax_first(scores).astype(low))
        all_heads = []
        for (group, part), weights in zip(units, all_weights):
            rows = slice(group * length, (group + 1) * length)
            start = 2 * width + part * lanes
            all_heads.append(contract_rows(weights, qkv_scr[rows, start : start + lanes]))
        for (group, part), full in zip(units, all_heads):
            rows = slice(group * length, (group + 1) * length)
            heads_scr[rows, part * lanes : (part + 1) * lanes] = own_blocks(
                full, length, packed, head_size
            ).astype(low)
    hidden = token_scr[...] + matmul(heads_scr[...], output_ref[...])
    for group in range(groups):
        first = (group // columns_each) * (length * columns_each) + group % columns_each
        put_tiles(
            seq_scr,
            pl.ds(first, length, stride=columns_each),
            hidden[group * length : (group + 1) * length],
        )
    out_ref[...] = get_tiles(seq_scr, slice(None)).astype(low)


def column_kernel(sizes, *refs):
    dates_each, row_parts, rows_each, columns_each, head_count, packed, date_size, direct = sizes
    if direct:
        row_ref, pair_ref, hidden_ref, own_ref, other_ref, project_ref, output_ref = refs[:7]
        kept_ref, sent_ref, first_grad_ref, second_grad_ref = refs[7:11]
    else:
        hidden_ref, cotangent_ref, project_ref, output_ref = refs[:4]
        mixed_ref, first_grad_ref, second_grad_ref = refs[4:7]
    (
        seq_scr,
        grad_scr,
        plane_scr,
        normed_scr,
        qkv_scr,
        grad_low_scr,
        heads_grad_scr,
        heads_scr,
        qkv_grad_scr,
    ) = refs[-9:]
    width = hidden_ref.shape[1]
    head_size = width // head_count
    lanes = packed * head_size
    length = row_parts * rows_each
    groups = dates_each * columns_each
    part_rows = rows_each * groups
    inverse_root = 1.0 / math.sqrt(head_size)
    if direct:
        row_at = row_ref[0]
        for part in range(row_parts):
            source = pl.multiple_of(((row_at + part) % row_parts) * part_rows, part_rows)
            put_tiles(
                seq_scr,
                slice(part * part_rows, (part + 1) * part_rows),
                hidden_ref[pl.ds(source, part_rows), :].astype(wide),
            )
        own_rows = dates_each * rows_each
        own = own_ref[...].astype(wide)
        own = own.reshape(own_rows, row_parts, columns_each, width)
        own = jnp.where(row_at == 0, own[:, 0], own[:, 1]).reshape(part_rows, width)
        put_tiles(grad_scr, slice(0, part_rows), own)
        put_tiles(grad_scr, slice(part_rows, 2 * part_rows), other_ref[...].astype(wide))
    else:
        put_tiles(seq_scr, slice(None), hidden_ref[...].astype(wide))
        put_tiles(grad_scr, slice(None), cotangent_ref[...].astype(wide))
    for group in range(groups):
        rows = slice(group * length, (group + 1) * length)
        if direct:
            inner = (group // columns_each) * (rows_each * columns_each) + group % columns_each
            plane_scr[rows, :] = get_tiles(seq_scr, pl.ds(group, length, stride=groups))
            pieces = [
                get_tiles(
                    grad_scr, pl.ds(part * part_rows + inner, rows_each, stride=columns_each)
                )
                for part in range(row_parts)
            ]
            grad_low_scr[rows, :] = jnp.concatenate(pieces, axis=0).astype(low)
        else:
            first = (group // columns_each) * (length * columns_each) + group % columns_each
            at = pl.ds(first, length, stride=columns_each)
            plane_scr[rows, :] = get_tiles(seq_scr, at)
            grad_low_scr[rows, :] = get_tiles(grad_scr, at).astype(low)
    normed_scr[...] = rms_norm(plane_scr[...])
    qkv_scr[...] = matmul(normed_scr[...], project_ref[...]).astype(low)
    heads_grad_scr[...] = contract_last(grad_low_scr[...], output_ref[...]).astype(low)
    mask = block_mask(length, packed, head_size)
    for units in batches(groups, head_count // packed, units_each):
        places = []
        for group, part in units:
            start = part * lanes
            places.append(
                (
                    slice(group * length, (group + 1) * length),
                    slice(start, start + lanes),
                    slice(width + start, width + start + lanes),
                    slice(2 * width + start, 2 * width + start + lanes),
                )
            )
        all_scores = []
        for rows, at_query, at_key, at_value in places:
            query = spread(qkv_scr[rows, at_query], mask, packed)
            heads_grad = spread(heads_grad_scr[rows, at_query], mask, packed)
            all_scores.append(
                (
                    contract_last(qkv_scr[rows, at_key], query),
                    contract_last(qkv_scr[rows, at_value], heads_grad),
                )
            )
        all_weights = []
        for scores, product_grad in all_scores:
            weights = softmax_first(scores * inverse_root)
            score_grad = weights * (
                product_grad - jnp.sum(weights * product_grad, axis=0, keepdims=True)
            )
            all_weights.append((weights.astype(low), score_grad.astype(low)))
        all_full = []
        for (rows, at_query, at_key, at_value), (weights, score_low) in zip(places, all_weights):
            all_full.append(
                (
                    contract_rows(weights, qkv_scr[rows, at_value]),
                    contract_rows(score_low, qkv_scr[rows, at_key]),
                )
            )
            query = spread(qkv_scr[rows, at_query], mask, packed)
            heads_grad = spread(heads_grad_scr[rows, at_query], mask, packed)
            key_grad = matmul(score_low, query) * inverse_root
            qkv_grad_scr[rows, at_key] = key_grad.astype(low)
            qkv_grad_scr[rows, at_value] = matmul(weights, heads_grad).astype(low)
        for (rows, at_query, _, _), (heads_full, query_full) in zip(places, all_full):
            heads = own_blocks(heads_full, length, packed, head_size)
            heads_scr[rows, at_query] = heads.astype(low)
            query_grad = own_blocks(query_full, length, packed, head_size) * inverse_root
            qkv_grad_scr[rows, at_query] = query_grad.astype(low)
    mixed = plane_scr[...] + matmul(heads_scr[...], output_ref[...])
    for group in range(groups):
        inner = (group // columns_each) * (rows_each * columns_each) + group % columns_each
        for part in range(row_parts):
            begin = group * length + part * rows_each
            put_tiles(
                seq_scr,
                pl.ds(part * part_rows + inner, rows_each, stride=columns_each),
                mixed[begin : begin + rows_each],
            )
    if direct:
        kept_ref[...] = get_tiles(seq_scr, slice(0, part_rows)).astype(low)
        sent_ref[...] = get_tiles(seq_scr, slice(part_rows, 2 * part_rows)).astype(low)
    else:
        mixed_ref[...] = get_tiles(seq_scr, slice(None)).astype(low)
    project_grad = contract_rows(qkv_grad_scr[...], normed_scr[...])
    output_grad = contract_rows(grad_low_scr[...], heads_scr[...])
    if not direct:
        first_grad_ref[...] = project_grad
        second_grad_ref[...] = output_grad
        return
    keep_ref, send_ref = first_grad_ref, second_grad_ref
    even = pair_ref[0] == 0
    project_each = project_grad.shape[0] // date_size
    output_each = output_grad.shape[0] // date_size
    half = (project_each + output_each) // 2
    lower = lax.broadcasted_iota(jnp.int32, (half, 128), 1) < 64
    for outer in range(date_size // 2):
        pair = []
        for part in (2 * outer, 2 * outer + 1):
            block = jnp.concatenate(
                [
                    project_grad[part * project_each : (part + 1) * project_each],
                    output_grad[part * output_each : (part + 1) * output_each],
                ],
                axis=0,
            )
            top, bottom = block[:half, 128:256], block[half:, 128:256]
            pair.append(
                (
                    (block[:, :128], jnp.where(lower, top, pltpu.roll(bottom, 64, 1))),
                    (block[:, 256:], jnp.where(lower, pltpu.roll(top, 64, 1), bottom)),
                )
            )
        for row_part in range(2):
            for first, one, two in zip((0, 2 * half), pair[0][row_part], pair[1][row_part]):
                at = slice(first, first + one.shape[0])
                keep_ref[row_part, outer, at, :] = jnp.where(even, one, two).astype(low)
                send_ref[row_part, outer, at, :] = jnp.where(even, two, one).astype(low)


def finish_kernel(project_each, row_ref, terms_ref, project_ref, output_ref):
    total = terms_ref[0].astype(wide)
    for source in range(1, terms_ref.shape[0]):
        total = total + terms_ref[source].astype(wide)
    whole = 2 * total.shape[0] // 3
    main = total[:whole]
    tail = total[whole:]
    swapped = pltpu.roll(tail, 64, 1)
    lower = lax.broadcasted_iota(jnp.int32, (whole, 128), 1) < 64
    tail_first = jnp.concatenate([tail, swapped], axis=0)
    turned = pltpu.roll(main, 64, 1)
    front = jnp.concatenate([main, tail_first[:, :64]], axis=1)
    back = jnp.concatenate([jnp.where(lower, tail_first, turned), turned[:, :64]], axis=1)
    owned = jnp.where(row_ref[0] == 0, front, back)
    project_ref[...] = owned[:project_each]
    output_ref[...] = owned[project_each:]


def body(
    row_size,
    date_size,
    pair_size,
    tokens,
    clear_flags,
    date_numbers,
    decay_slopes,
    time_project,
    time_output,
    column_project,
    column_output,
    cotangent,
):
    date_local, row_local, column_count, width = tokens.shape
    head_count = decay_slopes.shape[0]
    head_size = width // head_count
    packed = max(1, 128 // head_size)
    local_patches = row_local * column_count
    patches_each = local_patches // date_size
    columns_each = column_count // row_size
    row_count = row_local * row_size
    date_count = date_local * date_size
    project_each = 3 * width // date_size
    output_each = width // date_size
    lane_each = width // row_size
    direct = (
        patches_each == column_count
        and column_count % 16 == 0
        and pair_size == 2
        and row_size == 2
        and lane_each == 192
        and project_each % 8 == 0
        and output_each % 8 == 0
        and (project_each + output_each) % 32 == 0
    )
    token_rows = date_local * patches_each
    block_rows = -(-(token_rows + date_local) // 8) * 8
    params = pltpu.CompilerParams(vmem_limit_bytes=vmem_limit)
    in_vmem = pl.BlockSpec(memory_space=pltpu.VMEM)
    in_smem = pl.BlockSpec(memory_space=pltpu.SMEM)
    if direct:
        outgoing = pl.pallas_call(
            pack_kernel,
            out_shape=jax.ShapeDtypeStruct((date_size, block_rows, width), low),
            in_specs=[in_smem, in_vmem, in_vmem],
            compiler_params=params,
            name="pack_tokens",
        )(date_numbers, tokens, clear_flags)
        row_at = lax.axis_index("row")
        halves = cotangent.reshape(date_local, row_local, row_size, columns_each, width)
        leaving = lax.dynamic_index_in_dim(halves, 1 - row_at, 2, keepdims=False)
        other_grad = lax.ppermute(leaving, "row", [(0, 1), (1, 0)])
    else:
        flags = jnp.transpose(
            clear_flags.reshape(date_local, date_size, patches_each), (1, 0, 2)
        ).astype(low)
        numbers = jnp.stack([date_numbers // 32, date_numbers % 32], axis=-1).astype(low)
        numbers = jnp.broadcast_to(numbers[None], (date_size, date_local, 2))
        info = jnp.concatenate([flags, numbers], axis=-1)
        info = jnp.pad(
            info, ((0, 0), (0, block_rows - token_rows - date_local), (0, width - patches_each - 2))
        )
        outgoing = jnp.transpose(
            tokens.reshape(date_local, date_size, patches_each, width), (1, 0, 2, 3)
        ).reshape(date_size, token_rows, width)
        outgoing = jnp.concatenate([outgoing, info], axis=1)
    incoming = lax.all_to_all(outgoing, dates, split_axis=0, concat_axis=0, tiled=True)

    time_tokens = date_count * patches_each
    hidden = pl.pallas_call(
        functools.partial(
            time_kernel,
            (
                date_size,
                date_local,
                patches_each,
                head_count,
                packed,
                columns_each if direct else patches_each,
            ),
        ),
        out_shape=jax.ShapeDtypeStruct((time_tokens, width), low),
        in_specs=[in_smem, in_vmem, in_vmem, in_vmem],
        scratch_shapes=[
            pltpu.VMEM((width // 128, time_tokens, 128), wide),
            pltpu.VMEM((time_tokens, width), wide),
            pltpu.VMEM((time_tokens, 3 * width), low),
            pltpu.VMEM((time_tokens, width), low),
        ],
        compiler_params=params,
        name="time_attention",
    )(decay_slopes, incoming, time_project, time_output)

    column_tokens = date_local * row_count * columns_each
    if direct:
        parts = hidden.reshape(row_size * date_size, date_local * columns_each, width)
        plane = lax.all_to_all(parts, ("row", *dates), split_axis=0, concat_axis=0, tiled=True)
    else:
        parts = hidden.reshape(date_size, date_local, patches_each, width)
        back = lax.all_to_all(parts, dates, split_axis=0, concat_axis=0, tiled=True)
        back = jnp.transpose(back, (1, 0, 2, 3)).reshape(
            date_local, row_local, column_count, width
        )
        plane = lax.all_to_all(back, "row", split_axis=2, concat_axis=1, tiled=True)
    plane = plane.reshape(column_tokens, width)
    half_tokens = column_tokens // row_size
    half_shape = jax.ShapeDtypeStruct((half_tokens, width), low)
    packed_rows = (project_each + output_each) * 3 // 2
    if direct:
        operands = (
            row_at.reshape(1),
            lax.axis_index("pair").reshape(1),
            plane,
            cotangent.reshape(local_patches * date_local, width),
            other_grad.reshape(half_tokens, width),
        )
        half_grads = jax.ShapeDtypeStruct((row_size, date_size // 2, packed_rows, 128), low)
        out_shape = (half_shape, half_shape, half_grads, half_grads)
        in_specs = [in_smem] * 2 + [in_vmem] * 5
    else:
        operands = (
            plane,
            lax.all_to_all(cotangent, "row", split_axis=2, concat_axis=1, tiled=True).reshape(
                column_tokens, width
            ),
        )
        out_shape = (
            jax.ShapeDtypeStruct((column_tokens, width), low),
            jax.ShapeDtypeStruct((3 * width, width), wide),
            jax.ShapeDtypeStruct((width, width), wide),
        )
        in_specs = [in_vmem] * 4
    results = pl.pallas_call(
        functools.partial(
            column_kernel,
            (
                date_local,
                row_size,
                row_local,
                columns_each,
                head_count,
                packed,
                date_size,
                direct,
            ),
        ),
        out_shape=out_shape,
        in_specs=in_specs,
        scratch_shapes=[
            pltpu.VMEM((width // 128, column_tokens, 128), wide),
            pltpu.VMEM((width // 128, column_tokens, 128), wide),
            pltpu.VMEM((column_tokens, width), wide),
            pltpu.VMEM((column_tokens, width), low),
            pltpu.VMEM((column_tokens, 3 * width), low),
            pltpu.VMEM((column_tokens, width), low),
            pltpu.VMEM((column_tokens, width), low),
            pltpu.VMEM((column_tokens, width), low),
            pltpu.VMEM((column_tokens, 3 * width), low),
        ],
        compiler_params=params,
        name="column_attention",
    )(*operands, column_project, column_output)

    if direct:
        kept, sent, kept_grad, sent_grad = results
        arrived_grad = lax.ppermute(sent_grad, "pair", [(0, 1), (1, 0)])
        arrived = lax.ppermute(sent, "row", [(0, 1), (1, 0)])
        pair_sum = (kept_grad.astype(wide) + arrived_grad.astype(wide)).astype(low)
        pair_sum = pair_sum.reshape(row_size * date_size // 2, packed_rows, 128)
        terms = lax.all_to_all(pair_sum, ("row", "outer"), split_axis=0, concat_axis=0, tiled=True)
        owned_project, owned_output = pl.pallas_call(
            functools.partial(finish_kernel, project_each),
            out_shape=(
                jax.ShapeDtypeStruct((project_each, lane_each), wide),
                jax.ShapeDtypeStruct((output_each, lane_each), wide),
            ),
            in_specs=[in_smem, in_vmem],
            compiler_params=params,
            name="gradient_sum",
        )(row_at.reshape(1), terms)
        quarter = (date_local, row_local, 1, columns_each, width)
        kept, arrived = kept.reshape(quarter), arrived.reshape(quarter)
        mixed = jnp.concatenate(
            [jnp.where(row_at == 0, kept, arrived), jnp.where(row_at == 0, arrived, kept)], axis=2
        )
    else:
        mixed, project_grad, output_grad = results
        grads = jnp.concatenate(
            [
                project_grad.reshape(date_size, project_each, row_size, lane_each),
                output_grad.reshape(date_size, output_each, row_size, lane_each),
            ],
            axis=1,
        ).astype(low)
        grads = jnp.transpose(grads, (2, 0, 1, 3)).reshape(
            row_size * date_size, project_each + output_each, lane_each
        )
        terms = lax.all_to_all(grads, ("row", *dates), split_axis=0, concat_axis=0, tiled=True)
        owned = jnp.sum(terms.astype(wide), axis=0)
        owned_project, owned_output = owned[:project_each], owned[project_each:]
        mixed = mixed.reshape(row_size, date_local, row_local, columns_each, width)
        mixed = lax.all_to_all(mixed, "row", split_axis=0, concat_axis=0, tiled=True)
        mixed = jnp.transpose(mixed, (1, 2, 0, 3, 4))
    mixed = mixed.reshape(date_local, row_local, column_count, width)
    return (mixed, jnp.transpose(owned_project), jnp.transpose(owned_output))


def solution(mesh):
    date_size, row_size = mesh.shape["date"], mesh.shape["row"]
    pair_size = 2 if date_size % 2 == 0 else 1
    split = jax.sharding.Mesh(
        mesh.devices.reshape(date_size // pair_size, pair_size, row_size),
        ("outer", "pair", "row"),
    )
    return jax.shard_map(
        functools.partial(body, row_size, date_size, pair_size),
        mesh=split,
        in_specs=(
            P(dates, "row", None, None),
            P(dates, "row", None),
            P(dates),
            P(),
            P(),
            P(),
            P(),
            P(),
            P(dates, "row", None, None),
        ),
        out_specs=(P(dates, "row", None, None), P("row", dates), P("row", dates)),
        check_vma=False,
    )
```

```python
import functools
import math

import jax
import jax.numpy as jnp
from jax import lax
from jax.experimental import pallas as pl
from jax.experimental.pallas import tpu as pltpu
from jax.sharding import PartitionSpec as P

epsilon = 1e-06
masked_score = -1e30
units_each = 6
dates = ("outer", "mid", "pair")
vmem_limit = 48 * 1024 * 1024
low = jnp.bfloat16
wide = jnp.float32


def rms_norm(values):
    factor = lax.rsqrt(jnp.mean(values * values, axis=-1, keepdims=True) + epsilon)
    return (values * factor).astype(low)


def matmul(left, right):
    return jnp.dot(left, right, preferred_element_type=wide)


def contract_rows(left, right):
    return lax.dot_general(left, right, (((0,), (0,)), ((), ())), preferred_element_type=wide)


def contract_last(left, right):
    return lax.dot_general(left, right, (((1,), (1,)), ((), ())), preferred_element_type=wide)


def block_mask(length, packed, head_size):
    shape = (packed * length, packed * head_size)
    rows = lax.broadcasted_iota(jnp.int32, shape, 0) // length
    lanes = lax.broadcasted_iota(jnp.int32, shape, 1) // head_size
    return jnp.where(rows == lanes, 1.0, 0.0).astype(low)


def spread(values, mask, packed):
    return jnp.concatenate([values] * packed, axis=0) * mask


def batches(groups, parts, each):
    units = [(group, part) for group in range(groups) for part in range(parts)]
    return [units[first : first + each] for first in range(0, len(units), each)]


def own_blocks(full, length, packed, head_size):
    lanes = lax.broadcasted_iota(jnp.int32, (length, packed * head_size), 1) // head_size
    out = full[:length]
    for head in range(1, packed):
        out = jnp.where(lanes == head, full[head * length : (head + 1) * length], out)
    return out


def softmax_first(scores):
    raised = jnp.exp(scores - jnp.max(scores, axis=0, keepdims=True))
    return raised * (1.0 / jnp.sum(raised, axis=0, keepdims=True))


def put_tiles(scratch, rows, values):
    tiles, _, lanes = scratch.shape
    for tile in range(tiles):
        scratch[tile, rows, :] = values[:, tile * lanes : (tile + 1) * lanes]


def get_tiles(scratch, rows):
    return jnp.concatenate([scratch[tile, rows, :] for tile in range(scratch.shape[0])], axis=-1)


def pack_kernel(
    numbers_ref, tokens_ref, flags_ref, out_ref, numbers_scr, tokens_scr, flags_scr, copied
):
    copies = [
        pltpu.make_async_copy(tokens_ref, tokens_scr, copied.at[0]),
        pltpu.make_async_copy(flags_ref, flags_scr, copied.at[1]),
        pltpu.make_async_copy(numbers_ref, numbers_scr, copied.at[2]),
    ]
    for copy in copies:
        copy.start()
    dates_each, parts, patches, width = tokens_ref.shape
    lanes = out_ref.shape[2]
    tiles = width // lanes
    spare = out_ref.shape[1] - tiles * dates_each * patches
    place = lax.broadcasted_iota(jnp.int32, (patches, lanes), 0)
    lane = lax.broadcasted_iota(jnp.int32, (patches, lanes), 1)
    place = jnp.where(place == lane, 1.0, 0.0).astype(low)
    lane = lax.broadcasted_iota(jnp.int32, (parts, lanes), 1)
    row = lax.broadcasted_iota(jnp.int32, (spare, lanes), 0)
    copies[1].wait()
    copies[2].wait()
    infos = []
    for date in range(dates_each):
        number = numbers_scr[date]
        upper = (number // 32).astype(wide)
        under = (number % 32).astype(wide)
        info = matmul(flags_scr[date].astype(wide).astype(low), place)
        info = jnp.where(lane == patches, upper, info)
        infos.append(jnp.where(lane == patches + 1, under, info))
    copies[0].wait()
    for part in range(parts):
        tokens = jnp.concatenate(
            [tokens_scr[date, part].astype(wide) for date in range(dates_each)], axis=0
        )
        extra = jnp.zeros((spare, lanes), wide)
        for date in range(dates_each):
            extra = jnp.where(row == date, infos[date][part : part + 1], extra)
        pieces = [tokens[:, tile * lanes : (tile + 1) * lanes] for tile in range(tiles)]
        out_ref[part] = jnp.concatenate(pieces + [extra], axis=0).astype(low)


def time_kernel(
    sizes,
    slopes_ref,
    block_ref,
    project_ref,
    output_ref,
    earlier_ref,
    out_ref,
    seq_scr,
    token_scr,
    qkv_scr,
    heads_scr,
):
    sources, dates_each, groups, head_count, packed, columns_each = sizes
    width = project_ref.shape[0]
    tile_lanes = block_ref.shape[2]
    tiles = width // tile_lanes
    head_size = width // head_count
    lanes = packed * head_size
    length = sources * dates_each
    token_rows = dates_each * groups
    inverse_root = 1.0 / math.sqrt(head_size)
    info = []
    for source in range(sources):
        plane = block_ref[source].astype(wide)
        rows = slice(source * token_rows, (source + 1) * token_rows)
        for tile in range(tiles):
            at = slice(tile * token_rows, (tile + 1) * token_rows)
            if tiles == 1:
                put_tiles(seq_scr, rows, plane[at])
            else:
                seq_scr[tile, rows, :] = plane[at]
        info.append(plane[tiles * token_rows : tiles * token_rows + dates_each])
    info = jnp.concatenate(info, axis=0)
    for group in range(groups):
        token_scr[group * length : (group + 1) * length, :] = get_tiles(
            seq_scr, pl.ds(group, length, stride=groups)
        )
    tokens = token_scr[...]
    qkv_scr[...] = matmul(rms_norm(tokens), project_ref[...]).astype(low)
    numbers = info[:, groups : groups + 1] * 32.0 + info[:, groups + 1 : groups + 2]
    key_at = lax.broadcasted_iota(jnp.int32, (length, packed * length), 0)
    column_at = lax.broadcasted_iota(jnp.int32, (length, packed * length), 1)
    same_date = key_at == column_at % length
    query_numbers = jnp.sum(jnp.where(same_date, numbers, 0.0), axis=0, keepdims=True)
    gap_days = jnp.abs(numbers - query_numbers)
    head_at = column_at // length
    mask = block_mask(length, packed, head_size)
    biases = []
    for first in range(0, head_count, packed):
        slope = jnp.full((length, packed * length), slopes_ref[first], wide)
        for head in range(1, packed):
            slope = jnp.where(head_at == head, slopes_ref[first + head], slope)
        biases.append(-slope * gap_days)
    for units in batches(groups, head_count // packed, units_each):
        all_scores = []
        for group, part in units:
            rows = slice(group * length, (group + 1) * length)
            start = part * lanes
            query = qkv_scr[rows, start : start + lanes]
            key = qkv_scr[rows, width + start : width + start + lanes]
            all_scores.append(contract_last(key, spread(query, mask, packed)))
        all_weights = []
        for (group, part), scores in zip(units, all_scores):
            allowed = (info[:, group : group + 1] > 0) | same_date
            scores = jnp.where(allowed, scores * inverse_root + biases[part], masked_score)
            all_weights.append(softmax_first(scores).astype(low))
        all_heads = []
        for (group, part), weights in zip(units, all_weights):
            rows = slice(group * length, (group + 1) * length)
            start = 2 * width + part * lanes
            all_heads.append(contract_rows(weights, qkv_scr[rows, start : start + lanes]))
        for (group, part), full in zip(units, all_heads):
            rows = slice(group * length, (group + 1) * length)
            heads_scr[rows, part * lanes : (part + 1) * lanes] = own_blocks(
                full, length, packed, head_size
            ).astype(low)
    hidden = token_scr[...] + matmul(heads_scr[...], output_ref[...])
    for group in range(groups):
        first = (group // columns_each) * (length * columns_each) + group % columns_each
        put_tiles(
            seq_scr,
            pl.ds(first, length, stride=columns_each),
            hidden[group * length : (group + 1) * length],
        )
    out_ref[...] = get_tiles(seq_scr, slice(None)).astype(low)


def cotangent_kernel(sizes, *refs):
    dates_each, row_parts, rows_each, columns_each, direct = sizes
    output_ref, grad_low_ref, heads_grad_ref, grad_scr = refs[-4:]
    width = output_ref.shape[0]
    length = row_parts * rows_each
    groups = dates_each * columns_each
    part_rows = rows_each * groups
    if direct:
        row_ref, own_ref, other_ref = refs[:3]
        own = own_ref[...].astype(wide)
        own = own.reshape(dates_each * rows_each, row_parts, columns_each, width)
        own = jnp.where(row_ref[0] == 0, own[:, 0], own[:, 1]).reshape(part_rows, width)
        put_tiles(grad_scr, slice(0, part_rows), own)
        put_tiles(grad_scr, slice(part_rows, 2 * part_rows), other_ref[...].astype(wide))
    else:
        put_tiles(grad_scr, slice(None), refs[0][...].astype(wide))
    for group in range(groups):
        if direct:
            inner = (group // columns_each) * (rows_each * columns_each) + group % columns_each
            pieces = [
                get_tiles(
                    grad_scr, pl.ds(part * part_rows + inner, rows_each, stride=columns_each)
                )
                for part in range(row_parts)
            ]
            values = jnp.concatenate(pieces, axis=0)
        else:
            first = (group // columns_each) * (length * columns_each) + group % columns_each
            values = get_tiles(grad_scr, pl.ds(first, length, stride=columns_each))
        grad_low_ref[group * length : (group + 1) * length, :] = values.astype(low)
    heads_grad_ref[...] = contract_last(grad_low_ref[...], output_ref[...]).astype(low)


def column_kernel(sizes, *refs):
    dates_each, row_parts, rows_each, columns_each, head_count, packed, date_size, direct = sizes
    if direct:
        row_ref, pair_ref, *refs = refs
        kept_ref, sent_ref, first_grad_ref, second_grad_ref = refs[5:9]
    else:
        mixed_ref, first_grad_ref, second_grad_ref = refs[5:8]
    hidden_ref, grad_low_scr, heads_grad_scr, project_ref, output_ref = refs[:5]
    seq_scr, plane_scr, normed_scr, qkv_scr, heads_scr, qkv_grad_scr = refs[-6:]
    width = hidden_ref.shape[1]
    head_size = width // head_count
    lanes = packed * head_size
    length = row_parts * rows_each
    groups = dates_each * columns_each
    part_rows = rows_each * groups
    inverse_root = 1.0 / math.sqrt(head_size)
    if direct:
        for part in range(row_parts):
            source = pl.multiple_of(((row_ref[0] + part) % row_parts) * part_rows, part_rows)
            put_tiles(
                seq_scr,
                slice(part * part_rows, (part + 1) * part_rows),
                hidden_ref[pl.ds(source, part_rows), :].astype(wide),
            )
    else:
        put_tiles(seq_scr, slice(None), hidden_ref[...].astype(wide))
    for group in range(groups):
        rows = slice(group * length, (group + 1) * length)
        if direct:
            at = pl.ds(group, length, stride=groups)
        else:
            first = (group // columns_each) * (length * columns_each) + group % columns_each
            at = pl.ds(first, length, stride=columns_each)
        plane_scr[rows, :] = get_tiles(seq_scr, at)
    normed_scr[...] = rms_norm(plane_scr[...])
    qkv_scr[...] = matmul(normed_scr[...], project_ref[...]).astype(low)
    mask = block_mask(length, packed, head_size)
    for units in batches(groups, head_count // packed, units_each):
        places = []
        for group, part in units:
            start = part * lanes
            places.append(
                (
                    slice(group * length, (group + 1) * length),
                    slice(start, start + lanes),
                    slice(width + start, width + start + lanes),
                    slice(2 * width + start, 2 * width + start + lanes),
                )
            )
        all_scores = []
        for rows, at_query, at_key, at_value in places:
            query = spread(qkv_scr[rows, at_query], mask, packed)
            heads_grad = spread(heads_grad_scr[rows, at_query], mask, packed)
            all_scores.append(
                (
                    contract_last(qkv_scr[rows, at_key], query),
                    contract_last(qkv_scr[rows, at_value], heads_grad),
                )
            )
        all_weights = []
        for scores, product_grad in all_scores:
            weights = softmax_first(scores * inverse_root)
            score_grad = weights * (
                product_grad - jnp.sum(weights * product_grad, axis=0, keepdims=True)
            )
            all_weights.append((weights.astype(low), score_grad.astype(low)))
        all_full = []
        for (rows, at_query, at_key, at_value), (weights, score_low) in zip(places, all_weights):
            all_full.append(
                (
                    contract_rows(weights, qkv_scr[rows, at_value]),
                    contract_rows(score_low, qkv_scr[rows, at_key]),
                )
            )
            query = spread(qkv_scr[rows, at_query], mask, packed)
            heads_grad = spread(heads_grad_scr[rows, at_query], mask, packed)
            key_grad = matmul(score_low, query) * inverse_root
            qkv_grad_scr[rows, at_key] = key_grad.astype(low)
            qkv_grad_scr[rows, at_value] = matmul(weights, heads_grad).astype(low)
        for (rows, at_query, _, _), (heads_full, query_full) in zip(places, all_full):
            heads = own_blocks(heads_full, length, packed, head_size)
            heads_scr[rows, at_query] = heads.astype(low)
            query_grad = own_blocks(query_full, length, packed, head_size) * inverse_root
            qkv_grad_scr[rows, at_query] = query_grad.astype(low)
    mixed = plane_scr[...] + matmul(heads_scr[...], output_ref[...])
    for group in range(groups):
        inner = (group // columns_each) * (rows_each * columns_each) + group % columns_each
        for part in range(row_parts):
            begin = group * length + part * rows_each
            put_tiles(
                seq_scr,
                pl.ds(part * part_rows + inner, rows_each, stride=columns_each),
                mixed[begin : begin + rows_each],
            )
    if direct:
        kept_ref[...] = get_tiles(seq_scr, slice(0, part_rows)).astype(low)
        sent_ref[...] = get_tiles(seq_scr, slice(part_rows, 2 * part_rows)).astype(low)
    else:
        mixed_ref[...] = get_tiles(seq_scr, slice(None)).astype(low)
    project_grad = contract_rows(qkv_grad_scr[...], normed_scr[...])
    output_grad = contract_rows(grad_low_scr[...], heads_scr[...])
    if not direct:
        first_grad_ref[...] = project_grad
        second_grad_ref[...] = output_grad
        return
    keep_ref, send_ref = first_grad_ref, second_grad_ref
    even = pair_ref[0] == 0
    project_each = project_grad.shape[0] // date_size
    output_each = output_grad.shape[0] // date_size
    half = (project_each + output_each) // 2
    lower = lax.broadcasted_iota(jnp.int32, (half, 128), 1) < 64
    for outer in range(date_size // 2):
        pair = []
        for part in (2 * outer, 2 * outer + 1):
            block = jnp.concatenate(
                [
                    project_grad[part * project_each : (part + 1) * project_each],
                    output_grad[part * output_each : (part + 1) * output_each],
                ],
                axis=0,
            )
            top, bottom = block[:half, 128:256], block[half:, 128:256]
            pair.append(
                (
                    (block[:, :128], jnp.where(lower, top, pltpu.roll(bottom, 64, 1))),
                    (block[:, 256:], jnp.where(lower, pltpu.roll(top, 64, 1), bottom)),
                )
            )
        for row_part in range(2):
            for first, one, two in zip((0, 2 * half), pair[0][row_part], pair[1][row_part]):
                place = (row_part, outer // 2, outer % 2, slice(first, first + one.shape[0]))
                keep_ref[place] = jnp.where(even, one, two).astype(low)
                send_ref[place] = jnp.where(even, two, one).astype(low)


def added(left, right):
    return (left.astype(wide) + right.astype(wide)).astype(low)


def halve_kernel(mid_ref, row_ref, kept_ref, came_ref, a_keep, a_send, b_keep, b_send):
    rows, outers, mids = kept_ref.shape[:3]
    mid, row = mid_ref[0], row_ref[0]
    for outer in range(outers // 2):
        for at in range(rows):
            a_keep[at, outer] = added(kept_ref[at, outer, mid], came_ref[at, outer, mid])
            a_send[at, outer] = added(kept_ref[at, outer, 1 - mid], came_ref[at, outer, 1 - mid])
        later = outer + outers // 2
        for at in range(mids):
            b_keep[outer, at] = added(kept_ref[row, later, at], came_ref[row, later, at])
            b_send[outer, at] = added(kept_ref[1 - row, later, at], came_ref[1 - row, later, at])


def halve_again_kernel(
    mid_ref, row_ref, a_kept, a_came, b_kept, b_came, a_keep, a_send, b_keep, b_send
):
    mid, row = mid_ref[0], row_ref[0]
    for outer in range(a_kept.shape[1]):
        a_keep[outer] = added(a_kept[row, outer], a_came[row, outer])
        a_send[outer] = added(a_kept[1 - row, outer], a_came[1 - row, outer])
        b_keep[outer] = added(b_kept[outer, mid], b_came[outer, mid])
        b_send[outer] = added(b_kept[outer, 1 - mid], b_came[outer, 1 - mid])


def spread_kernel(outer_ref, a_kept, a_came, b_kept, b_came, *refs):
    total = refs[-1]
    half = a_kept.shape[0]
    for outer in range(half):
        total[outer] = added(a_kept[outer], a_came[outer])
        total[half + outer] = added(b_kept[outer], b_came[outer])
    for step in range(2 * half):
        refs[step][...] = total[(outer_ref[0] + step) % (2 * half)]


def finish_kernel(project_each, row_ref, *refs):
    *terms, project_ref, output_ref = refs
    total = terms[0][...].astype(wide)
    for term in terms[1:]:
        total = total + term[...].astype(wide)
    whole = 2 * total.shape[0] // 3
    main = total[:whole]
    tail = total[whole:]
    swapped = pltpu.roll(tail, 64, 1)
    lower = lax.broadcasted_iota(jnp.int32, (whole, 128), 1) < 64
    tail_first = jnp.concatenate([tail, swapped], axis=0)
    turned = pltpu.roll(main, 64, 1)
    front = jnp.concatenate([main, tail_first[:, :64]], axis=1)
    back = jnp.concatenate([jnp.where(lower, tail_first, turned), turned[:, :64]], axis=1)
    owned = jnp.where(row_ref[0] == 0, front, back)
    project_ref[...] = owned[:project_each]
    output_ref[...] = owned[project_each:]


def body(
    row_size,
    date_size,
    tokens,
    clear_flags,
    date_numbers,
    decay_slopes,
    time_project,
    time_output,
    column_project,
    column_output,
    cotangent,
):
    date_local, row_local, column_count, width = tokens.shape
    head_count = decay_slopes.shape[0]
    head_size = width // head_count
    packed = max(1, 128 // head_size)
    local_patches = row_local * column_count
    patches_each = local_patches // date_size
    columns_each = column_count // row_size
    row_count = row_local * row_size
    date_count = date_local * date_size
    project_each = 3 * width // date_size
    output_each = width // date_size
    lane_each = width // row_size
    direct = (
        patches_each == column_count
        and column_count % 16 == 0
        and date_size % 8 == 0
        and row_size == 2
        and lane_each == 192
        and project_each % 8 == 0
        and output_each % 8 == 0
        and (project_each + output_each) % 32 == 0
    )
    token_rows = date_local * patches_each
    block_rows = -(-(token_rows + date_local) // 8) * 8
    tile_rows = (width // 128) * token_rows + -(-date_local // 8) * 8
    params = pltpu.CompilerParams(vmem_limit_bytes=vmem_limit)
    in_vmem = pl.BlockSpec(memory_space=pltpu.VMEM)
    in_smem = pl.BlockSpec(memory_space=pltpu.SMEM)
    swap = [(0, 1), (1, 0)]
    column_tokens = date_local * row_count * columns_each
    half_tokens = column_tokens // row_size
    if direct:
        outgoing = pl.pallas_call(
            pack_kernel,
            out_shape=jax.ShapeDtypeStruct((date_size, tile_rows, 128), low),
            in_specs=[pl.BlockSpec(memory_space=pl.ANY)] * 3,
            scratch_shapes=[
                pltpu.SMEM(date_numbers.shape, jnp.int32),
                pltpu.VMEM(tokens.shape, low),
                pltpu.VMEM(clear_flags.shape, jnp.int32),
                pltpu.SemaphoreType.DMA((3,)),
            ],
            compiler_params=params,
            name="pack_tokens",
        )(date_numbers, tokens, clear_flags)
        row_at = lax.axis_index("row")
        halves = cotangent.reshape(date_local, row_local, row_size, columns_each, width)
        leaving = lax.dynamic_index_in_dim(halves, 1 - row_at, 2, keepdims=False)
        other_grad = lax.ppermute(leaving, "row", swap)
    else:
        flags = jnp.transpose(
            clear_flags.reshape(date_local, date_size, patches_each), (1, 0, 2)
        ).astype(low)
        numbers = jnp.stack([date_numbers // 32, date_numbers % 32], axis=-1).astype(low)
        numbers = jnp.broadcast_to(numbers[None], (date_size, date_local, 2))
        info = jnp.concatenate([flags, numbers], axis=-1)
        info = jnp.pad(
            info, ((0, 0), (0, block_rows - token_rows - date_local), (0, width - patches_each - 2))
        )
        outgoing = jnp.transpose(
            tokens.reshape(date_local, date_size, patches_each, width), (1, 0, 2, 3)
        ).reshape(date_size, token_rows, width)
        outgoing = jnp.concatenate([outgoing, info], axis=1)
    incoming = lax.all_to_all(outgoing, dates, split_axis=0, concat_axis=0, tiled=True)

    if direct:
        grads_in = (
            row_at.reshape(1),
            cotangent.reshape(local_patches * date_local, width),
            other_grad.reshape(half_tokens, width),
        )
        in_specs = [in_smem] + [in_vmem] * 3
    else:
        grads_in = (
            lax.all_to_all(cotangent, "row", split_axis=2, concat_axis=1, tiled=True).reshape(
                column_tokens, width
            ),
        )
        in_specs = [in_vmem] * 2
    grad_low, heads_grad = pl.pallas_call(
        functools.partial(
            cotangent_kernel, (date_local, row_size, row_local, columns_each, direct)
        ),
        out_shape=(jax.ShapeDtypeStruct((column_tokens, width), low),) * 2,
        in_specs=in_specs,
        scratch_shapes=[pltpu.VMEM((width // 128, column_tokens, 128), wide)],
        compiler_params=params,
        name="cotangent_heads",
    )(*grads_in, column_output)

    time_tokens = date_count * patches_each
    hidden = pl.pallas_call(
        functools.partial(
            time_kernel,
            (
                date_size,
                date_local,
                patches_each,
                head_count,
                packed,
                columns_each if direct else patches_each,
            ),
        ),
        out_shape=jax.ShapeDtypeStruct((time_tokens, width), low),
        in_specs=[in_smem, in_vmem, in_vmem, in_vmem, pl.BlockSpec(memory_space=pl.ANY)],
        scratch_shapes=[
            pltpu.VMEM((width // 128, time_tokens, 128), wide),
            pltpu.VMEM((time_tokens, width), wide),
            pltpu.VMEM((time_tokens, 3 * width), low),
            pltpu.VMEM((time_tokens, width), low),
        ],
        compiler_params=params,
        name="time_attention",
    )(decay_slopes, incoming, time_project, time_output, heads_grad)

    if direct:
        parts = hidden.reshape(row_size * date_size, date_local * columns_each, width)
        plane = lax.all_to_all(parts, ("row", *dates), split_axis=0, concat_axis=0, tiled=True)
    else:
        parts = hidden.reshape(date_size, date_local, patches_each, width)
        back = lax.all_to_all(parts, dates, split_axis=0, concat_axis=0, tiled=True)
        back = jnp.transpose(back, (1, 0, 2, 3)).reshape(
            date_local, row_local, column_count, width
        )
        plane = lax.all_to_all(back, "row", split_axis=2, concat_axis=1, tiled=True)
    plane = plane.reshape(column_tokens, width)
    half_shape = jax.ShapeDtypeStruct((half_tokens, width), low)
    packed_rows = (project_each + output_each) * 3 // 2
    block = (packed_rows, 128)
    outers = date_size // 4
    if direct:
        half_grads = jax.ShapeDtypeStruct((row_size, outers, 2, *block), low)
        places = (row_at.reshape(1), lax.axis_index("pair").reshape(1))
        out_shape = (half_shape, half_shape, half_grads, half_grads)
        in_specs = [in_smem] * 2 + [in_vmem] * 5
    else:
        places = ()
        out_shape = (
            jax.ShapeDtypeStruct((column_tokens, width), low),
            jax.ShapeDtypeStruct((3 * width, width), wide),
            jax.ShapeDtypeStruct((width, width), wide),
        )
        in_specs = [in_vmem] * 5
    results = pl.pallas_call(
        functools.partial(
            column_kernel,
            (
                date_local,
                row_size,
                row_local,
                columns_each,
                head_count,
                packed,
                date_size,
                direct,
            ),
        ),
        out_shape=out_shape,
        in_specs=in_specs,
        scratch_shapes=[
            pltpu.VMEM((width // 128, column_tokens, 128), wide),
            pltpu.VMEM((column_tokens, width), wide),
            pltpu.VMEM((column_tokens, width), low),
            pltpu.VMEM((column_tokens, 3 * width), low),
            pltpu.VMEM((column_tokens, width), low),
            pltpu.VMEM((column_tokens, 3 * width), low),
        ],
        compiler_params=params,
        name="column_attention",
    )(*places, plane, grad_low, heads_grad, column_project, column_output)

    if direct:
        kept, sent, kept_grad, sent_grad = results
        arrived_grad = lax.ppermute(sent_grad, "pair", swap)
        arrived = lax.ppermute(sent, "row", swap)
        mid_one, row_one = lax.axis_index("mid").reshape(1), row_at.reshape(1)
        outer_one = lax.axis_index("outer").reshape(1)

        def shaped(*lead):
            return jax.ShapeDtypeStruct((*lead, *block), low)

        half = outers // 2
        a_kept, a_sent, b_kept, b_sent = pl.pallas_call(
            halve_kernel,
            out_shape=(shaped(2, half), shaped(2, half), shaped(half, 2), shaped(half, 2)),
            in_specs=[in_smem] * 2 + [in_vmem] * 2,
            compiler_params=params,
            name="halve_gradients",
        )(mid_one, row_one, kept_grad, arrived_grad)
        a_came = lax.ppermute(a_sent, "mid", swap)
        b_came = lax.ppermute(b_sent, "row", swap)
        a_kept, a_sent, b_kept, b_sent = pl.pallas_call(
            halve_again_kernel,
            out_shape=(shaped(half),) * 4,
            in_specs=[in_smem] * 2 + [in_vmem] * 4,
            compiler_params=params,
            name="halve_gradients_again",
        )(mid_one, row_one, a_kept, a_came, b_kept, b_came)
        a_came = lax.ppermute(a_sent, "row", swap)
        b_came = lax.ppermute(b_sent, "mid", swap)
        blocks = pl.pallas_call(
            spread_kernel,
            out_shape=(shaped(),) * outers,
            in_specs=[in_smem] + [in_vmem] * 4,
            scratch_shapes=[pltpu.VMEM((outers, *block), low)],
            compiler_params=params,
            name="spread_gradients",
        )(outer_one, a_kept, a_came, b_kept, b_came)
        terms = [blocks[0]]
        for step in range(1, outers):
            route = [(at, (at + step) % outers) for at in range(outers)]
            terms.append(lax.ppermute(blocks[step], "outer", route))
        owned_project, owned_output = pl.pallas_call(
            functools.partial(finish_kernel, project_each),
            out_shape=(
                jax.ShapeDtypeStruct((project_each, lane_each), wide),
                jax.ShapeDtypeStruct((output_each, lane_each), wide),
            ),
            in_specs=[in_smem] + [in_vmem] * outers,
            compiler_params=params,
            name="gradient_sum",
        )(row_one, *terms)
        quarter = (date_local, row_local, 1, columns_each, width)
        kept, arrived = kept.reshape(quarter), arrived.reshape(quarter)
        mixed = jnp.concatenate(
            [jnp.where(row_at == 0, kept, arrived), jnp.where(row_at == 0, arrived, kept)], axis=2
        )
    else:
        mixed, project_grad, output_grad = results
        grads = jnp.concatenate(
            [
                project_grad.reshape(date_size, project_each, row_size, lane_each),
                output_grad.reshape(date_size, output_each, row_size, lane_each),
            ],
            axis=1,
        ).astype(low)
        grads = jnp.transpose(grads, (2, 0, 1, 3)).reshape(
            row_size * date_size, project_each + output_each, lane_each
        )
        terms = lax.all_to_all(grads, ("row", *dates), split_axis=0, concat_axis=0, tiled=True)
        owned = jnp.sum(terms.astype(wide), axis=0)
        owned_project, owned_output = owned[:project_each], owned[project_each:]
        mixed = mixed.reshape(row_size, date_local, row_local, columns_each, width)
        mixed = lax.all_to_all(mixed, "row", split_axis=0, concat_axis=0, tiled=True)
        mixed = jnp.transpose(mixed, (1, 2, 0, 3, 4))
    mixed = mixed.reshape(date_local, row_local, column_count, width)
    return (mixed, jnp.transpose(owned_project), jnp.transpose(owned_output))


def solution(mesh):
    date_size, row_size = mesh.shape["date"], mesh.shape["row"]
    pair_size = 2 if date_size % 2 == 0 else 1
    mid_size = 2 if date_size % 4 == 0 else 1
    split = jax.sharding.Mesh(
        mesh.devices.reshape(-1, mid_size, pair_size, row_size), ("outer", "mid", "pair", "row")
    )
    return jax.shard_map(
        functools.partial(body, row_size, date_size),
        mesh=split,
        in_specs=(
            P(dates, "row", None, None),
            P(dates, "row", None),
            P(dates),
            P(),
            P(),
            P(),
            P(),
            P(),
            P(dates, "row", None, None),
        ),
        out_specs=(P(dates, "row", None, None), P("row", dates), P("row", dates)),
        check_vma=False,
    )
```

```python
import functools
import math

import jax
import jax.numpy as jnp
from jax import lax
from jax.experimental import pallas as pl
from jax.experimental.pallas import tpu as pltpu
from jax.sharding import PartitionSpec as P

epsilon = 1e-06
masked_score = -1e30
units_each = 12
dates = ("outer", "mid", "pair")
vmem_limit = 24 * 1024 * 1024
low = jnp.bfloat16
wide = jnp.float32


def rms_norm(values):
    factor = lax.rsqrt(jnp.mean(values * values, axis=-1, keepdims=True) + epsilon)
    return (values * factor).astype(low)


def matmul(left, right):
    return jnp.dot(left, right, preferred_element_type=wide)


def contract_rows(left, right):
    return lax.dot_general(left, right, (((0,), (0,)), ((), ())), preferred_element_type=wide)


def contract_last(left, right):
    return lax.dot_general(left, right, (((1,), (1,)), ((), ())), preferred_element_type=wide)


def block_mask(length, packed, head_size):
    shape = (packed * length, packed * head_size)
    rows = lax.broadcasted_iota(jnp.int32, shape, 0) // length
    lanes = lax.broadcasted_iota(jnp.int32, shape, 1) // head_size
    return jnp.where(rows == lanes, 1.0, 0.0).astype(low)


def spread(values, mask, packed):
    return jnp.concatenate([values] * packed, axis=0) * mask


def batches(groups, parts, each):
    units = [(group, part) for group in range(groups) for part in range(parts)]
    return [units[first : first + each] for first in range(0, len(units), each)]


def own_blocks(full, length, packed, head_size):
    lanes = lax.broadcasted_iota(jnp.int32, (length, packed * head_size), 1) // head_size
    out = full[:length]
    for head in range(1, packed):
        out = jnp.where(lanes == head, full[head * length : (head + 1) * length], out)
    return out


def softmax_first(scores):
    raised = jnp.exp(scores - jnp.max(scores, axis=0, keepdims=True))
    return raised * (1.0 / jnp.sum(raised, axis=0, keepdims=True))


def put_tiles(scratch, rows, values):
    tiles, _, lanes = scratch.shape
    for tile in range(tiles):
        scratch[tile, rows, :] = values[:, tile * lanes : (tile + 1) * lanes]


def get_tiles(scratch, rows):
    return jnp.concatenate([scratch[tile, rows, :] for tile in range(scratch.shape[0])], axis=-1)


def pack_kernel(
    numbers_ref, tokens_ref, flags_ref, out_ref, numbers_scr, tokens_scr, flags_scr, copied
):
    copies = [
        pltpu.make_async_copy(tokens_ref, tokens_scr, copied.at[0]),
        pltpu.make_async_copy(flags_ref, flags_scr, copied.at[1]),
        pltpu.make_async_copy(numbers_ref, numbers_scr, copied.at[2]),
    ]
    for copy in copies:
        copy.start()
    dates_each, parts, patches, width = tokens_ref.shape
    lanes = out_ref.shape[2]
    tiles = width // lanes
    spare = out_ref.shape[1] - tiles * dates_each * patches
    place = lax.broadcasted_iota(jnp.int32, (patches, lanes), 0)
    lane = lax.broadcasted_iota(jnp.int32, (patches, lanes), 1)
    place = jnp.where(place == lane, 1.0, 0.0).astype(low)
    lane = lax.broadcasted_iota(jnp.int32, (parts, lanes), 1)
    row = lax.broadcasted_iota(jnp.int32, (spare, lanes), 0)
    copies[1].wait()
    copies[2].wait()
    infos = []
    for date in range(dates_each):
        number = numbers_scr[date]
        upper = (number // 32).astype(wide)
        under = (number % 32).astype(wide)
        info = matmul(flags_scr[date].astype(wide).astype(low), place)
        info = jnp.where(lane == patches, upper, info)
        infos.append(jnp.where(lane == patches + 1, under, info))
    copies[0].wait()
    for part in range(parts):
        tokens = jnp.concatenate(
            [tokens_scr[date, part].astype(wide) for date in range(dates_each)], axis=0
        )
        extra = jnp.zeros((spare, lanes), wide)
        for date in range(dates_each):
            extra = jnp.where(row == date, infos[date][part : part + 1], extra)
        pieces = [tokens[:, tile * lanes : (tile + 1) * lanes] for tile in range(tiles)]
        out_ref[part] = jnp.concatenate(pieces + [extra], axis=0).astype(low)


def time_kernel(
    sizes,
    slopes_ref,
    block_ref,
    project_ref,
    output_ref,
    earlier_ref,
    out_ref,
    seq_scr,
    token_scr,
    qkv_scr,
    heads_scr,
    output_scr,
    copied,
):
    output_copy = pltpu.make_async_copy(output_ref, output_scr, copied)
    output_copy.start()
    sources, dates_each, groups, head_count, packed, columns_each = sizes
    width = project_ref.shape[0]
    tile_lanes = block_ref.shape[2]
    tiles = width // tile_lanes
    head_size = width // head_count
    lanes = packed * head_size
    length = sources * dates_each
    token_rows = dates_each * groups
    inverse_root = 1.0 / math.sqrt(head_size)
    info = []
    for source in range(sources):
        plane = block_ref[source].astype(wide)
        rows = slice(source * token_rows, (source + 1) * token_rows)
        for tile in range(tiles):
            at = slice(tile * token_rows, (tile + 1) * token_rows)
            if tiles == 1:
                put_tiles(seq_scr, rows, plane[at])
            else:
                seq_scr[tile, rows, :] = plane[at]
        info.append(plane[tiles * token_rows : tiles * token_rows + dates_each])
    info = jnp.concatenate(info, axis=0)
    for group in range(groups):
        token_scr[group * length : (group + 1) * length, :] = get_tiles(
            seq_scr, pl.ds(group, length, stride=groups)
        )
    tokens = token_scr[...]
    qkv_scr[...] = matmul(rms_norm(tokens), project_ref[...]).astype(low)
    numbers = info[:, groups : groups + 1] * 32.0 + info[:, groups + 1 : groups + 2]
    key_at = lax.broadcasted_iota(jnp.int32, (length, packed * length), 0)
    column_at = lax.broadcasted_iota(jnp.int32, (length, packed * length), 1)
    same_date = key_at == column_at % length
    query_numbers = jnp.sum(jnp.where(same_date, numbers, 0.0), axis=0, keepdims=True)
    gap_days = jnp.abs(numbers - query_numbers)
    head_at = column_at // length
    mask = block_mask(length, packed, head_size)
    biases = []
    for first in range(0, head_count, packed):
        slope = jnp.full((length, packed * length), slopes_ref[first], wide)
        for head in range(1, packed):
            slope = jnp.where(head_at == head, slopes_ref[first + head], slope)
        biases.append(-slope * gap_days)
    for units in batches(groups, head_count // packed, units_each):
        all_scores = []
        for group, part in units:
            rows = slice(group * length, (group + 1) * length)
            start = part * lanes
            query = qkv_scr[rows, start : start + lanes]
            key = qkv_scr[rows, width + start : width + start + lanes]
            all_scores.append(contract_last(key, spread(query, mask, packed)))
        all_weights = []
        for (group, part), scores in zip(units, all_scores):
            allowed = (info[:, group : group + 1] > 0) | same_date
            scores = jnp.where(allowed, scores * inverse_root + biases[part], masked_score)
            all_weights.append(softmax_first(scores).astype(low))
        all_heads = []
        for (group, part), weights in zip(units, all_weights):
            rows = slice(group * length, (group + 1) * length)
            start = 2 * width + part * lanes
            all_heads.append(contract_rows(weights, qkv_scr[rows, start : start + lanes]))
        for (group, part), full in zip(units, all_heads):
            rows = slice(group * length, (group + 1) * length)
            heads_scr[rows, part * lanes : (part + 1) * lanes] = own_blocks(
                full, length, packed, head_size
            ).astype(low)
    output_copy.wait()
    hidden = token_scr[...] + matmul(heads_scr[...], output_scr[...])
    for group in range(groups):
        first = (group // columns_each) * (length * columns_each) + group % columns_each
        put_tiles(
            seq_scr,
            pl.ds(first, length, stride=columns_each),
            hidden[group * length : (group + 1) * length],
        )
    out_ref[...] = get_tiles(seq_scr, slice(None)).astype(low)


def cotangent_kernel(sizes, *refs):
    dates_each, row_parts, rows_each, columns_each, direct = sizes
    output_ref, grad_low_ref, heads_grad_ref, grad_scr = refs[-4:]
    width = output_ref.shape[0]
    length = row_parts * rows_each
    groups = dates_each * columns_each
    part_rows = rows_each * groups
    if direct:
        row_ref, own_ref, other_ref = refs[:3]
        own = own_ref[...].astype(wide)
        own = own.reshape(dates_each * rows_each, row_parts, columns_each, width)
        own = jnp.where(row_ref[0] == 0, own[:, 0], own[:, 1]).reshape(part_rows, width)
        put_tiles(grad_scr, slice(0, part_rows), own)
        put_tiles(grad_scr, slice(part_rows, 2 * part_rows), other_ref[...].astype(wide))
    else:
        put_tiles(grad_scr, slice(None), refs[0][...].astype(wide))
    for group in range(groups):
        if direct:
            inner = (group // columns_each) * (rows_each * columns_each) + group % columns_each
            pieces = [
                get_tiles(
                    grad_scr, pl.ds(part * part_rows + inner, rows_each, stride=columns_each)
                )
                for part in range(row_parts)
            ]
            values = jnp.concatenate(pieces, axis=0)
        else:
            first = (group // columns_each) * (length * columns_each) + group % columns_each
            values = get_tiles(grad_scr, pl.ds(first, length, stride=columns_each))
        grad_low_ref[group * length : (group + 1) * length, :] = values.astype(low)
    heads_grad_ref[...] = contract_last(grad_low_ref[...], output_ref[...]).astype(low)


def column_kernel(sizes, *refs):
    dates_each, row_parts, rows_each, columns_each, head_count, packed, date_size, direct = sizes
    if direct:
        row_ref, pair_ref, *refs = refs
        kept_ref, sent_ref, first_grad_ref, second_grad_ref = refs[5:9]
    else:
        mixed_ref, first_grad_ref, second_grad_ref = refs[5:8]
    hidden_ref, grad_low_scr, heads_grad_scr, project_ref, output_ref = refs[:5]
    seq_scr, plane_scr, normed_scr, qkv_scr, heads_scr, qkv_grad_scr = refs[-6:]
    width = hidden_ref.shape[1]
    head_size = width // head_count
    lanes = packed * head_size
    length = row_parts * rows_each
    groups = dates_each * columns_each
    part_rows = rows_each * groups
    inverse_root = 1.0 / math.sqrt(head_size)
    if direct:
        for part in range(row_parts):
            source = pl.multiple_of(((row_ref[0] + part) % row_parts) * part_rows, part_rows)
            put_tiles(
                seq_scr,
                slice(part * part_rows, (part + 1) * part_rows),
                hidden_ref[pl.ds(source, part_rows), :].astype(wide),
            )
    else:
        put_tiles(seq_scr, slice(None), hidden_ref[...].astype(wide))
    for group in range(groups):
        rows = slice(group * length, (group + 1) * length)
        if direct:
            at = pl.ds(group, length, stride=groups)
        else:
            first = (group // columns_each) * (length * columns_each) + group % columns_each
            at = pl.ds(first, length, stride=columns_each)
        plane_scr[rows, :] = get_tiles(seq_scr, at)
    normed_scr[...] = rms_norm(plane_scr[...])
    qkv_scr[...] = matmul(normed_scr[...], project_ref[...]).astype(low)
    mask = block_mask(length, packed, head_size)
    for units in batches(groups, head_count // packed, units_each):
        places = []
        for group, part in units:
            start = part * lanes
            places.append(
                (
                    slice(group * length, (group + 1) * length),
                    slice(start, start + lanes),
                    slice(width + start, width + start + lanes),
                    slice(2 * width + start, 2 * width + start + lanes),
                )
            )
        all_scores = []
        for rows, at_query, at_key, at_value in places:
            query = spread(qkv_scr[rows, at_query], mask, packed)
            heads_grad = spread(heads_grad_scr[rows, at_query], mask, packed)
            all_scores.append(
                (
                    contract_last(qkv_scr[rows, at_key], query),
                    contract_last(qkv_scr[rows, at_value], heads_grad),
                )
            )
        all_weights = []
        for scores, product_grad in all_scores:
            weights = softmax_first(scores * inverse_root)
            score_grad = weights * (
                product_grad - jnp.sum(weights * product_grad, axis=0, keepdims=True)
            )
            all_weights.append((weights.astype(low), score_grad.astype(low)))
        all_full = []
        for (rows, at_query, at_key, at_value), (weights, score_low) in zip(places, all_weights):
            all_full.append(
                (
                    contract_rows(weights, qkv_scr[rows, at_value]),
                    contract_rows(score_low, qkv_scr[rows, at_key]),
                )
            )
            query = spread(qkv_scr[rows, at_query], mask, packed)
            heads_grad = spread(heads_grad_scr[rows, at_query], mask, packed)
            key_grad = matmul(score_low, query) * inverse_root
            qkv_grad_scr[rows, at_key] = key_grad.astype(low)
            qkv_grad_scr[rows, at_value] = matmul(weights, heads_grad).astype(low)
        for (rows, at_query, _, _), (heads_full, query_full) in zip(places, all_full):
            heads = own_blocks(heads_full, length, packed, head_size)
            heads_scr[rows, at_query] = heads.astype(low)
            query_grad = own_blocks(query_full, length, packed, head_size) * inverse_root
            qkv_grad_scr[rows, at_query] = query_grad.astype(low)
    mixed = plane_scr[...] + matmul(heads_scr[...], output_ref[...])
    for group in range(groups):
        inner = (group // columns_each) * (rows_each * columns_each) + group % columns_each
        for part in range(row_parts):
            begin = group * length + part * rows_each
            put_tiles(
                seq_scr,
                pl.ds(part * part_rows + inner, rows_each, stride=columns_each),
                mixed[begin : begin + rows_each],
            )
    if direct:
        kept_ref[...] = get_tiles(seq_scr, slice(0, part_rows)).astype(low)
        sent_ref[...] = get_tiles(seq_scr, slice(part_rows, 2 * part_rows)).astype(low)
    else:
        mixed_ref[...] = get_tiles(seq_scr, slice(None)).astype(low)
    project_grad = contract_rows(qkv_grad_scr[...], normed_scr[...])
    output_grad = contract_rows(grad_low_scr[...], heads_scr[...])
    if not direct:
        first_grad_ref[...] = project_grad
        second_grad_ref[...] = output_grad
        return
    keep_ref, send_ref = first_grad_ref, second_grad_ref
    even = pair_ref[0] == 0
    project_each = project_grad.shape[0] // date_size
    output_each = output_grad.shape[0] // date_size
    half = (project_each + output_each) // 2
    lower = lax.broadcasted_iota(jnp.int32, (half, 128), 1) < 64
    for outer in range(date_size // 2):
        pair = []
        for part in (2 * outer, 2 * outer + 1):
            block = jnp.concatenate(
                [
                    project_grad[part * project_each : (part + 1) * project_each],
                    output_grad[part * output_each : (part + 1) * output_each],
                ],
                axis=0,
            )
            top, bottom = block[:half, 128:256], block[half:, 128:256]
            pair.append(
                (
                    (block[:, :128], jnp.where(lower, top, pltpu.roll(bottom, 64, 1))),
                    (block[:, 256:], jnp.where(lower, pltpu.roll(top, 64, 1), bottom)),
                )
            )
        for row_part in range(2):
            for first, one, two in zip((0, 2 * half), pair[0][row_part], pair[1][row_part]):
                place = (row_part, outer // 2, outer % 2, slice(first, first + one.shape[0]))
                keep_ref[place] = jnp.where(even, one, two).astype(low)
                send_ref[place] = jnp.where(even, two, one).astype(low)


def added(left, right):
    return (left.astype(wide) + right.astype(wide)).astype(low)


def halve_kernel(mid_ref, row_ref, kept_ref, came_ref, a_keep, a_send, b_keep, b_send):
    rows, outers, mids = kept_ref.shape[:3]
    mid, row = mid_ref[0], row_ref[0]
    for outer in range(outers // 2):
        for at in range(rows):
            a_keep[at, outer] = added(kept_ref[at, outer, mid], came_ref[at, outer, mid])
            a_send[at, outer] = added(kept_ref[at, outer, 1 - mid], came_ref[at, outer, 1 - mid])
        later = outer + outers // 2
        for at in range(mids):
            b_keep[outer, at] = added(kept_ref[row, later, at], came_ref[row, later, at])
            b_send[outer, at] = added(kept_ref[1 - row, later, at], came_ref[1 - row, later, at])


def halve_again_kernel(
    mid_ref, row_ref, a_kept, a_came, b_kept, b_came, a_keep, a_send, b_keep, b_send
):
    mid, row = mid_ref[0], row_ref[0]
    for outer in range(a_kept.shape[1]):
        a_keep[outer] = added(a_kept[row, outer], a_came[row, outer])
        a_send[outer] = added(a_kept[1 - row, outer], a_came[1 - row, outer])
        b_keep[outer] = added(b_kept[outer, mid], b_came[outer, mid])
        b_send[outer] = added(b_kept[outer, 1 - mid], b_came[outer, 1 - mid])


def spread_kernel(outer_ref, a_kept, a_came, b_kept, b_came, *refs):
    total = refs[-1]
    half = a_kept.shape[0]
    for outer in range(half):
        total[outer] = added(a_kept[outer], a_came[outer])
        total[half + outer] = added(b_kept[outer], b_came[outer])
    for step in range(2 * half):
        refs[step][...] = total[(outer_ref[0] + step) % (2 * half)]


def finish_kernel(project_each, row_ref, *refs):
    *terms, project_ref, output_ref = refs
    total = terms[0][...].astype(wide)
    for term in terms[1:]:
        total = total + term[...].astype(wide)
    whole = 2 * total.shape[0] // 3
    main = total[:whole]
    tail = total[whole:]
    swapped = pltpu.roll(tail, 64, 1)
    lower = lax.broadcasted_iota(jnp.int32, (whole, 128), 1) < 64
    tail_first = jnp.concatenate([tail, swapped], axis=0)
    turned = pltpu.roll(main, 64, 1)
    front = jnp.concatenate([main, tail_first[:, :64]], axis=1)
    back = jnp.concatenate([jnp.where(lower, tail_first, turned), turned[:, :64]], axis=1)
    owned = jnp.where(row_ref[0] == 0, front, back)
    project_ref[...] = owned[:project_each]
    output_ref[...] = owned[project_each:]


def body(
    row_size,
    date_size,
    tokens,
    clear_flags,
    date_numbers,
    decay_slopes,
    time_project,
    time_output,
    column_project,
    column_output,
    cotangent,
):
    date_local, row_local, column_count, width = tokens.shape
    head_count = decay_slopes.shape[0]
    head_size = width // head_count
    packed = max(1, 128 // head_size)
    local_patches = row_local * column_count
    patches_each = local_patches // date_size
    columns_each = column_count // row_size
    row_count = row_local * row_size
    date_count = date_local * date_size
    project_each = 3 * width // date_size
    output_each = width // date_size
    lane_each = width // row_size
    direct = (
        patches_each == column_count
        and column_count % 16 == 0
        and date_size % 8 == 0
        and row_size == 2
        and lane_each == 192
        and project_each % 8 == 0
        and output_each % 8 == 0
        and (project_each + output_each) % 32 == 0
    )
    token_rows = date_local * patches_each
    block_rows = -(-(token_rows + date_local) // 8) * 8
    tile_rows = (width // 128) * token_rows + -(-date_local // 8) * 8
    params = pltpu.CompilerParams(vmem_limit_bytes=vmem_limit)
    in_vmem = pl.BlockSpec(memory_space=pltpu.VMEM)
    in_smem = pl.BlockSpec(memory_space=pltpu.SMEM)
    in_hbm = pl.BlockSpec(memory_space=pltpu.HBM)
    swap = [(0, 1), (1, 0)]
    column_tokens = date_local * row_count * columns_each
    half_tokens = column_tokens // row_size
    if direct:
        outgoing = pl.pallas_call(
            pack_kernel,
            out_shape=jax.ShapeDtypeStruct((date_size, tile_rows, 128), low),
            in_specs=[in_hbm] * 3,
            scratch_shapes=[
                pltpu.SMEM(date_numbers.shape, jnp.int32),
                pltpu.VMEM(tokens.shape, low),
                pltpu.VMEM(clear_flags.shape, jnp.int32),
                pltpu.SemaphoreType.DMA((3,)),
            ],
            compiler_params=params,
            name="pack_tokens",
        )(date_numbers, tokens, clear_flags)
        row_at = lax.axis_index("row")
        halves = cotangent.reshape(date_local, row_local, row_size, columns_each, width)
        leaving = lax.dynamic_index_in_dim(halves, 1 - row_at, 2, keepdims=False)
        other_grad = lax.ppermute(leaving, "row", swap)
    else:
        flags = jnp.transpose(
            clear_flags.reshape(date_local, date_size, patches_each), (1, 0, 2)
        ).astype(low)
        numbers = jnp.stack([date_numbers // 32, date_numbers % 32], axis=-1).astype(low)
        numbers = jnp.broadcast_to(numbers[None], (date_size, date_local, 2))
        info = jnp.concatenate([flags, numbers], axis=-1)
        info = jnp.pad(
            info, ((0, 0), (0, block_rows - token_rows - date_local), (0, width - patches_each - 2))
        )
        outgoing = jnp.transpose(
            tokens.reshape(date_local, date_size, patches_each, width), (1, 0, 2, 3)
        ).reshape(date_size, token_rows, width)
        outgoing = jnp.concatenate([outgoing, info], axis=1)
    incoming = lax.all_to_all(outgoing, dates, split_axis=0, concat_axis=0, tiled=True)

    if direct:
        grads_in = (
            row_at.reshape(1),
            cotangent.reshape(local_patches * date_local, width),
            other_grad.reshape(half_tokens, width),
        )
        in_specs = [in_smem] + [in_vmem] * 3
    else:
        grads_in = (
            lax.all_to_all(cotangent, "row", split_axis=2, concat_axis=1, tiled=True).reshape(
                column_tokens, width
            ),
        )
        in_specs = [in_vmem] * 2
    grad_low, heads_grad = pl.pallas_call(
        functools.partial(
            cotangent_kernel, (date_local, row_size, row_local, columns_each, direct)
        ),
        out_shape=(jax.ShapeDtypeStruct((column_tokens, width), low),) * 2,
        in_specs=in_specs,
        scratch_shapes=[pltpu.VMEM((width // 128, column_tokens, 128), wide)],
        compiler_params=params,
        name="cotangent_heads",
    )(*grads_in, column_output)

    time_tokens = date_count * patches_each
    hidden = pl.pallas_call(
        functools.partial(
            time_kernel,
            (
                date_size,
                date_local,
                patches_each,
                head_count,
                packed,
                columns_each if direct else patches_each,
            ),
        ),
        out_shape=jax.ShapeDtypeStruct((time_tokens, width), low),
        in_specs=[in_smem, in_vmem, in_vmem, in_hbm, pl.BlockSpec(memory_space=pl.ANY)],
        scratch_shapes=[
            pltpu.VMEM((width // 128, time_tokens, 128), wide),
            pltpu.VMEM((time_tokens, width), wide),
            pltpu.VMEM((time_tokens, 3 * width), low),
            pltpu.VMEM((time_tokens, width), low),
            pltpu.VMEM(time_output.shape, low),
            pltpu.SemaphoreType.DMA,
        ],
        compiler_params=params,
        name="time_attention",
    )(decay_slopes, incoming, time_project, time_output, heads_grad)

    if direct:
        parts = hidden.reshape(row_size * date_size, date_local * columns_each, width)
        plane = lax.all_to_all(parts, ("row", *dates), split_axis=0, concat_axis=0, tiled=True)
    else:
        parts = hidden.reshape(date_size, date_local, patches_each, width)
        back = lax.all_to_all(parts, dates, split_axis=0, concat_axis=0, tiled=True)
        back = jnp.transpose(back, (1, 0, 2, 3)).reshape(
            date_local, row_local, column_count, width
        )
        plane = lax.all_to_all(back, "row", split_axis=2, concat_axis=1, tiled=True)
    plane = plane.reshape(column_tokens, width)
    half_shape = jax.ShapeDtypeStruct((half_tokens, width), low)
    packed_rows = (project_each + output_each) * 3 // 2
    block = (packed_rows, 128)
    outers = date_size // 4
    if direct:
        half_grads = jax.ShapeDtypeStruct((row_size, outers, 2, *block), low)
        places = (row_at.reshape(1), lax.axis_index("pair").reshape(1))
        out_shape = (half_shape, half_shape, half_grads, half_grads)
        in_specs = [in_smem] * 2 + [in_vmem] * 5
    else:
        places = ()
        out_shape = (
            jax.ShapeDtypeStruct((column_tokens, width), low),
            jax.ShapeDtypeStruct((3 * width, width), wide),
            jax.ShapeDtypeStruct((width, width), wide),
        )
        in_specs = [in_vmem] * 5
    results = pl.pallas_call(
        functools.partial(
            column_kernel,
            (
                date_local,
                row_size,
                row_local,
                columns_each,
                head_count,
                packed,
                date_size,
                direct,
            ),
        ),
        out_shape=out_shape,
        in_specs=in_specs,
        scratch_shapes=[
            pltpu.VMEM((width // 128, column_tokens, 128), wide),
            pltpu.VMEM((column_tokens, width), wide),
            pltpu.VMEM((column_tokens, width), low),
            pltpu.VMEM((column_tokens, 3 * width), low),
            pltpu.VMEM((column_tokens, width), low),
            pltpu.VMEM((column_tokens, 3 * width), low),
        ],
        compiler_params=params,
        name="column_attention",
    )(*places, plane, grad_low, heads_grad, column_project, column_output)

    if direct:
        kept, sent, kept_grad, sent_grad = results
        arrived_grad = lax.ppermute(sent_grad, "pair", swap)
        arrived = lax.ppermute(sent, "row", swap)
        mid_one, row_one = lax.axis_index("mid").reshape(1), row_at.reshape(1)
        outer_one = lax.axis_index("outer").reshape(1)

        def shaped(*lead):
            return jax.ShapeDtypeStruct((*lead, *block), low)

        half = outers // 2
        a_kept, a_sent, b_kept, b_sent = pl.pallas_call(
            halve_kernel,
            out_shape=(shaped(2, half), shaped(2, half), shaped(half, 2), shaped(half, 2)),
            in_specs=[in_smem] * 2 + [in_vmem] * 2,
            compiler_params=params,
            name="halve_gradients",
        )(mid_one, row_one, kept_grad, arrived_grad)
        a_came = lax.ppermute(a_sent, "mid", swap)
        b_came = lax.ppermute(b_sent, "row", swap)
        a_kept, a_sent, b_kept, b_sent = pl.pallas_call(
            halve_again_kernel,
            out_shape=(shaped(half),) * 4,
            in_specs=[in_smem] * 2 + [in_vmem] * 4,
            compiler_params=params,
            name="halve_gradients_again",
        )(mid_one, row_one, a_kept, a_came, b_kept, b_came)
        a_came = lax.ppermute(a_sent, "row", swap)
        b_came = lax.ppermute(b_sent, "mid", swap)
        blocks = pl.pallas_call(
            spread_kernel,
            out_shape=(shaped(),) * outers,
            in_specs=[in_smem] + [in_vmem] * 4,
            scratch_shapes=[pltpu.VMEM((outers, *block), low)],
            compiler_params=params,
            name="spread_gradients",
        )(outer_one, a_kept, a_came, b_kept, b_came)
        terms = [blocks[0]]
        for step in range(1, outers):
            route = [(at, (at + step) % outers) for at in range(outers)]
            terms.append(lax.ppermute(blocks[step], "outer", route))
        owned_project, owned_output = pl.pallas_call(
            functools.partial(finish_kernel, project_each),
            out_shape=(
                jax.ShapeDtypeStruct((project_each, lane_each), wide),
                jax.ShapeDtypeStruct((output_each, lane_each), wide),
            ),
            in_specs=[in_smem] + [in_vmem] * outers,
            compiler_params=params,
            name="gradient_sum",
        )(row_one, *terms)
        quarter = (date_local, row_local, 1, columns_each, width)
        kept, arrived = kept.reshape(quarter), arrived.reshape(quarter)
        mixed = jnp.concatenate(
            [jnp.where(row_at == 0, kept, arrived), jnp.where(row_at == 0, arrived, kept)], axis=2
        )
    else:
        mixed, project_grad, output_grad = results
        grads = jnp.concatenate(
            [
                project_grad.reshape(date_size, project_each, row_size, lane_each),
                output_grad.reshape(date_size, output_each, row_size, lane_each),
            ],
            axis=1,
        ).astype(low)
        grads = jnp.transpose(grads, (2, 0, 1, 3)).reshape(
            row_size * date_size, project_each + output_each, lane_each
        )
        terms = lax.all_to_all(grads, ("row", *dates), split_axis=0, concat_axis=0, tiled=True)
        owned = jnp.sum(terms.astype(wide), axis=0)
        owned_project, owned_output = owned[:project_each], owned[project_each:]
        mixed = mixed.reshape(row_size, date_local, row_local, columns_each, width)
        mixed = lax.all_to_all(mixed, "row", split_axis=0, concat_axis=0, tiled=True)
        mixed = jnp.transpose(mixed, (1, 2, 0, 3, 4))
    mixed = mixed.reshape(date_local, row_local, column_count, width)
    return (mixed, jnp.transpose(owned_project), jnp.transpose(owned_output))


def solution(mesh):
    date_size, row_size = mesh.shape["date"], mesh.shape["row"]
    pair_size = 2 if date_size % 2 == 0 else 1
    mid_size = 2 if date_size % 4 == 0 else 1
    split = jax.sharding.Mesh(
        mesh.devices.reshape(-1, mid_size, pair_size, row_size), ("outer", "mid", "pair", "row")
    )
    return jax.shard_map(
        functools.partial(body, row_size, date_size),
        mesh=split,
        in_specs=(
            P(dates, "row", None, None),
            P(dates, "row", None),
            P(dates),
            P(),
            P(),
            P(),
            P(),
            P(),
            P(dates, "row", None, None),
        ),
        out_specs=(P(dates, "row", None, None), P("row", dates), P("row", dates)),
        check_vma=False,
    )
```

```python
import functools
import math

import jax
import jax.numpy as jnp
from jax import lax
from jax.experimental import pallas as pl
from jax.experimental.pallas import tpu as pltpu
from jax.sharding import PartitionSpec as P

epsilon = 1e-06
masked_score = -1e30
units_each = 24
dates = ("outer", "mid", "pair")
vmem_limit = 24 * 1024 * 1024
low = jnp.bfloat16
wide = jnp.float32


def rms_norm(values):
    factor = lax.rsqrt(jnp.mean(values * values, axis=-1, keepdims=True) + epsilon)
    return (values * factor).astype(low)


def matmul(left, right):
    return jnp.dot(left, right, preferred_element_type=wide)


def contract_rows(left, right):
    return lax.dot_general(left, right, (((0,), (0,)), ((), ())), preferred_element_type=wide)


def contract_last(left, right):
    return lax.dot_general(left, right, (((1,), (1,)), ((), ())), preferred_element_type=wide)


def block_mask(length, packed, head_size):
    shape = (packed * length, packed * head_size)
    rows = lax.broadcasted_iota(jnp.int32, shape, 0) // length
    lanes = lax.broadcasted_iota(jnp.int32, shape, 1) // head_size
    return jnp.where(rows == lanes, 1.0, 0.0).astype(low)


def spread(values, mask, packed):
    return jnp.concatenate([values] * packed, axis=0) * mask


def batches(groups, parts, each):
    units = [(group, part) for group in range(groups) for part in range(parts)]
    return [units[first : first + each] for first in range(0, len(units), each)]


def own_blocks(full, length, packed, head_size):
    lanes = lax.broadcasted_iota(jnp.int32, (length, packed * head_size), 1) // head_size
    out = full[:length]
    for head in range(1, packed):
        out = jnp.where(lanes == head, full[head * length : (head + 1) * length], out)
    return out


def softmax_first(scores):
    raised = jnp.exp(scores - jnp.max(scores, axis=0, keepdims=True))
    return raised * (1.0 / jnp.sum(raised, axis=0, keepdims=True))


def put_tiles(scratch, rows, values):
    tiles, _, lanes = scratch.shape
    for tile in range(tiles):
        scratch[tile, rows, :] = values[:, tile * lanes : (tile + 1) * lanes]


def get_tiles(scratch, rows):
    return jnp.concatenate([scratch[tile, rows, :] for tile in range(scratch.shape[0])], axis=-1)


def pack_kernel(
    numbers_ref, tokens_ref, flags_ref, out_ref, numbers_scr, tokens_scr, flags_scr, copied
):
    copies = [
        pltpu.make_async_copy(tokens_ref, tokens_scr, copied.at[0]),
        pltpu.make_async_copy(flags_ref, flags_scr, copied.at[1]),
        pltpu.make_async_copy(numbers_ref, numbers_scr, copied.at[2]),
    ]
    for copy in copies:
        copy.start()
    dates_each, parts, patches, width = tokens_ref.shape
    lanes = out_ref.shape[2]
    tiles = width // lanes
    spare = out_ref.shape[1] - tiles * dates_each * patches
    place = lax.broadcasted_iota(jnp.int32, (patches, lanes), 0)
    lane = lax.broadcasted_iota(jnp.int32, (patches, lanes), 1)
    place = jnp.where(place == lane, 1.0, 0.0).astype(low)
    lane = lax.broadcasted_iota(jnp.int32, (parts, lanes), 1)
    row = lax.broadcasted_iota(jnp.int32, (spare, lanes), 0)
    copies[1].wait()
    copies[2].wait()
    infos = []
    for date in range(dates_each):
        number = numbers_scr[date]
        upper = (number // 32).astype(wide)
        under = (number % 32).astype(wide)
        info = matmul(flags_scr[date].astype(wide).astype(low), place)
        info = jnp.where(lane == patches, upper, info)
        infos.append(jnp.where(lane == patches + 1, under, info))
    copies[0].wait()
    for part in range(parts):
        tokens = jnp.concatenate(
            [tokens_scr[date, part].astype(wide) for date in range(dates_each)], axis=0
        )
        extra = jnp.zeros((spare, lanes), wide)
        for date in range(dates_each):
            extra = jnp.where(row == date, infos[date][part : part + 1], extra)
        pieces = [tokens[:, tile * lanes : (tile + 1) * lanes] for tile in range(tiles)]
        out_ref[part] = jnp.concatenate(pieces + [extra], axis=0).astype(low)


def time_kernel(
    sizes,
    slopes_ref,
    block_ref,
    project_ref,
    output_ref,
    out_ref,
    seq_scr,
    token_scr,
    qkv_scr,
    heads_scr,
):
    sources, dates_each, groups, head_count, packed, columns_each = sizes
    width = project_ref.shape[0]
    tile_lanes = block_ref.shape[2]
    tiles = width // tile_lanes
    head_size = width // head_count
    lanes = packed * head_size
    length = sources * dates_each
    token_rows = dates_each * groups
    inverse_root = 1.0 / math.sqrt(head_size)
    info = []
    for source in range(sources):
        plane = block_ref[source].astype(wide)
        rows = slice(source * token_rows, (source + 1) * token_rows)
        for tile in range(tiles):
            at = slice(tile * token_rows, (tile + 1) * token_rows)
            if tiles == 1:
                put_tiles(seq_scr, rows, plane[at])
            else:
                seq_scr[tile, rows, :] = plane[at]
        info.append(plane[tiles * token_rows : tiles * token_rows + dates_each])
    info = jnp.concatenate(info, axis=0)
    for group in range(groups):
        token_scr[group * length : (group + 1) * length, :] = get_tiles(
            seq_scr, pl.ds(group, length, stride=groups)
        )
    tokens = token_scr[...]
    qkv_scr[...] = matmul(rms_norm(tokens), project_ref[...]).astype(low)
    numbers = info[:, groups : groups + 1] * 32.0 + info[:, groups + 1 : groups + 2]
    key_at = lax.broadcasted_iota(jnp.int32, (length, packed * length), 0)
    column_at = lax.broadcasted_iota(jnp.int32, (length, packed * length), 1)
    same_date = key_at == column_at % length
    query_numbers = jnp.sum(jnp.where(same_date, numbers, 0.0), axis=0, keepdims=True)
    gap_days = jnp.abs(numbers - query_numbers)
    head_at = column_at // length
    mask = block_mask(length, packed, head_size)
    biases = []
    for first in range(0, head_count, packed):
        slope = jnp.full((length, packed * length), slopes_ref[first], wide)
        for head in range(1, packed):
            slope = jnp.where(head_at == head, slopes_ref[first + head], slope)
        biases.append(-slope * gap_days)
    for units in batches(groups, head_count // packed, units_each):
        all_scores = []
        for group, part in units:
            rows = slice(group * length, (group + 1) * length)
            start = part * lanes
            query = qkv_scr[rows, start : start + lanes]
            key = qkv_scr[rows, width + start : width + start + lanes]
            all_scores.append(contract_last(key, spread(query, mask, packed)))
        all_weights = []
        for (group, part), scores in zip(units, all_scores):
            allowed = (info[:, group : group + 1] > 0) | same_date
            scores = jnp.where(allowed, scores * inverse_root + biases[part], masked_score)
            all_weights.append(softmax_first(scores).astype(low))
        all_heads = []
        for (group, part), weights in zip(units, all_weights):
            rows = slice(group * length, (group + 1) * length)
            start = 2 * width + part * lanes
            all_heads.append(contract_rows(weights, qkv_scr[rows, start : start + lanes]))
        for (group, part), full in zip(units, all_heads):
            rows = slice(group * length, (group + 1) * length)
            heads_scr[rows, part * lanes : (part + 1) * lanes] = own_blocks(
                full, length, packed, head_size
            ).astype(low)
    hidden = token_scr[...] + matmul(heads_scr[...], output_ref[...])
    for group in range(groups):
        first = (group // columns_each) * (length * columns_each) + group % columns_each
        put_tiles(
            seq_scr,
            pl.ds(first, length, stride=columns_each),
            hidden[group * length : (group + 1) * length],
        )
    out_ref[...] = get_tiles(seq_scr, slice(None)).astype(low)


def cotangent_kernel(sizes, *refs):
    dates_each, row_parts, rows_each, columns_each, direct = sizes
    output_ref, later_ref, grad_low_ref, heads_grad_ref, handed_ref, grad_scr = refs[-6:]
    handed_ref[...] = later_ref[...]
    width = output_ref.shape[0]
    length = row_parts * rows_each
    groups = dates_each * columns_each
    part_rows = rows_each * groups
    if direct:
        row_ref, own_ref, other_ref = refs[:3]
        own = own_ref[...].astype(wide)
        own = own.reshape(dates_each * rows_each, row_parts, columns_each, width)
        own = jnp.where(row_ref[0] == 0, own[:, 0], own[:, 1]).reshape(part_rows, width)
        put_tiles(grad_scr, slice(0, part_rows), own)
        put_tiles(grad_scr, slice(part_rows, 2 * part_rows), other_ref[...].astype(wide))
    else:
        put_tiles(grad_scr, slice(None), refs[0][...].astype(wide))
    for group in range(groups):
        if direct:
            inner = (group // columns_each) * (rows_each * columns_each) + group % columns_each
            pieces = [
                get_tiles(
                    grad_scr, pl.ds(part * part_rows + inner, rows_each, stride=columns_each)
                )
                for part in range(row_parts)
            ]
            values = jnp.concatenate(pieces, axis=0)
        else:
            first = (group // columns_each) * (length * columns_each) + group % columns_each
            values = get_tiles(grad_scr, pl.ds(first, length, stride=columns_each))
        grad_low_ref[group * length : (group + 1) * length, :] = values.astype(low)
    heads_grad_ref[...] = contract_last(grad_low_ref[...], output_ref[...]).astype(low)


def column_kernel(sizes, *refs):
    dates_each, row_parts, rows_each, columns_each, head_count, packed, date_size, direct = sizes
    if direct:
        row_ref, pair_ref, *refs = refs
        kept_ref, sent_ref, first_grad_ref, second_grad_ref = refs[5:9]
    else:
        mixed_ref, first_grad_ref, second_grad_ref = refs[5:8]
    hidden_ref, grad_low_scr, heads_grad_scr, project_ref, output_ref = refs[:5]
    seq_scr, plane_scr, normed_scr, qkv_scr, heads_scr, qkv_grad_scr = refs[-6:]
    width = hidden_ref.shape[1]
    head_size = width // head_count
    lanes = packed * head_size
    length = row_parts * rows_each
    groups = dates_each * columns_each
    part_rows = rows_each * groups
    inverse_root = 1.0 / math.sqrt(head_size)
    if direct:
        for part in range(row_parts):
            source = pl.multiple_of(((row_ref[0] + part) % row_parts) * part_rows, part_rows)
            put_tiles(
                seq_scr,
                slice(part * part_rows, (part + 1) * part_rows),
                hidden_ref[pl.ds(source, part_rows), :].astype(wide),
            )
    else:
        put_tiles(seq_scr, slice(None), hidden_ref[...].astype(wide))
    for group in range(groups):
        rows = slice(group * length, (group + 1) * length)
        if direct:
            at = pl.ds(group, length, stride=groups)
        else:
            first = (group // columns_each) * (length * columns_each) + group % columns_each
            at = pl.ds(first, length, stride=columns_each)
        plane_scr[rows, :] = get_tiles(seq_scr, at)
    normed_scr[...] = rms_norm(plane_scr[...])
    qkv_scr[...] = matmul(normed_scr[...], project_ref[...]).astype(low)
    mask = block_mask(length, packed, head_size)
    for units in batches(groups, head_count // packed, units_each):
        places = []
        for group, part in units:
            start = part * lanes
            places.append(
                (
                    slice(group * length, (group + 1) * length),
                    slice(start, start + lanes),
                    slice(width + start, width + start + lanes),
                    slice(2 * width + start, 2 * width + start + lanes),
                )
            )
        all_scores = []
        for rows, at_query, at_key, at_value in places:
            query = spread(qkv_scr[rows, at_query], mask, packed)
            heads_grad = spread(heads_grad_scr[rows, at_query], mask, packed)
            all_scores.append(
                (
                    contract_last(qkv_scr[rows, at_key], query),
                    contract_last(qkv_scr[rows, at_value], heads_grad),
                )
            )
        all_weights = []
        for scores, product_grad in all_scores:
            weights = softmax_first(scores * inverse_root)
            score_grad = weights * (
                product_grad - jnp.sum(weights * product_grad, axis=0, keepdims=True)
            )
            all_weights.append((weights.astype(low), score_grad.astype(low)))
        all_full = []
        for (rows, at_query, at_key, at_value), (weights, score_low) in zip(places, all_weights):
            all_full.append(
                (
                    contract_rows(weights, qkv_scr[rows, at_value]),
                    contract_rows(score_low, qkv_scr[rows, at_key]),
                )
            )
            query = spread(qkv_scr[rows, at_query], mask, packed)
            heads_grad = spread(heads_grad_scr[rows, at_query], mask, packed)
            key_grad = matmul(score_low, query) * inverse_root
            qkv_grad_scr[rows, at_key] = key_grad.astype(low)
            qkv_grad_scr[rows, at_value] = matmul(weights, heads_grad).astype(low)
        for (rows, at_query, _, _), (heads_full, query_full) in zip(places, all_full):
            heads = own_blocks(heads_full, length, packed, head_size)
            heads_scr[rows, at_query] = heads.astype(low)
            query_grad = own_blocks(query_full, length, packed, head_size) * inverse_root
            qkv_grad_scr[rows, at_query] = query_grad.astype(low)
    mixed = plane_scr[...] + matmul(heads_scr[...], output_ref[...])
    for group in range(groups):
        inner = (group // columns_each) * (rows_each * columns_each) + group % columns_each
        for part in range(row_parts):
            begin = group * length + part * rows_each
            put_tiles(
                seq_scr,
                pl.ds(part * part_rows + inner, rows_each, stride=columns_each),
                mixed[begin : begin + rows_each],
            )
    if direct:
        kept_ref[...] = get_tiles(seq_scr, slice(0, part_rows)).astype(low)
        sent_ref[...] = get_tiles(seq_scr, slice(part_rows, 2 * part_rows)).astype(low)
    else:
        mixed_ref[...] = get_tiles(seq_scr, slice(None)).astype(low)
    project_grad = contract_rows(qkv_grad_scr[...], normed_scr[...])
    output_grad = contract_rows(grad_low_scr[...], heads_scr[...])
    if not direct:
        first_grad_ref[...] = project_grad
        second_grad_ref[...] = output_grad
        return
    keep_ref, send_ref = first_grad_ref, second_grad_ref
    even = pair_ref[0] == 0
    project_each = project_grad.shape[0] // date_size
    output_each = output_grad.shape[0] // date_size
    half = (project_each + output_each) // 2
    lower = lax.broadcasted_iota(jnp.int32, (half, 128), 1) < 64
    for outer in range(date_size // 2):
        pair = []
        for part in (2 * outer, 2 * outer + 1):
            block = jnp.concatenate(
                [
                    project_grad[part * project_each : (part + 1) * project_each],
                    output_grad[part * output_each : (part + 1) * output_each],
                ],
                axis=0,
            )
            top, bottom = block[:half, 128:256], block[half:, 128:256]
            pair.append(
                (
                    (block[:, :128], jnp.where(lower, top, pltpu.roll(bottom, 64, 1))),
                    (block[:, 256:], jnp.where(lower, pltpu.roll(top, 64, 1), bottom)),
                )
            )
        for row_part in range(2):
            for first, one, two in zip((0, 2 * half), pair[0][row_part], pair[1][row_part]):
                place = (row_part, outer // 2, outer % 2, slice(first, first + one.shape[0]))
                keep_ref[place] = jnp.where(even, one, two).astype(low)
                send_ref[place] = jnp.where(even, two, one).astype(low)


def added(left, right):
    return (left.astype(wide) + right.astype(wide)).astype(low)


def halve_kernel(mid_ref, row_ref, kept_ref, came_ref, a_keep, a_send, b_keep, b_send):
    rows, outers, mids = kept_ref.shape[:3]
    mid, row = mid_ref[0], row_ref[0]
    for outer in range(outers // 2):
        for at in range(rows):
            a_keep[at, outer] = added(kept_ref[at, outer, mid], came_ref[at, outer, mid])
            a_send[at, outer] = added(kept_ref[at, outer, 1 - mid], came_ref[at, outer, 1 - mid])
        later = outer + outers // 2
        for at in range(mids):
            b_keep[outer, at] = added(kept_ref[row, later, at], came_ref[row, later, at])
            b_send[outer, at] = added(kept_ref[1 - row, later, at], came_ref[1 - row, later, at])


def halve_again_kernel(
    mid_ref, row_ref, a_kept, a_came, b_kept, b_came, a_keep, a_send, b_keep, b_send
):
    mid, row = mid_ref[0], row_ref[0]
    for outer in range(a_kept.shape[1]):
        a_keep[outer] = added(a_kept[row, outer], a_came[row, outer])
        a_send[outer] = added(a_kept[1 - row, outer], a_came[1 - row, outer])
        b_keep[outer] = added(b_kept[outer, mid], b_came[outer, mid])
        b_send[outer] = added(b_kept[outer, 1 - mid], b_came[outer, 1 - mid])


def spread_kernel(outer_ref, a_kept, a_came, b_kept, b_came, sent_ref, leave_ref, *refs):
    leave_ref[...] = sent_ref[...]
    total = refs[-1]
    half = a_kept.shape[0]
    for outer in range(half):
        total[outer] = added(a_kept[outer], a_came[outer])
        total[half + outer] = added(b_kept[outer], b_came[outer])
    for step in range(2 * half):
        refs[step][...] = total[(outer_ref[0] + step) % (2 * half)]


def finish_kernel(project_each, row_ref, *refs):
    *terms, project_ref, output_ref = refs
    total = terms[0][...].astype(wide)
    for term in terms[1:]:
        total = total + term[...].astype(wide)
    whole = 2 * total.shape[0] // 3
    main = total[:whole]
    tail = total[whole:]
    swapped = pltpu.roll(tail, 64, 1)
    lower = lax.broadcasted_iota(jnp.int32, (whole, 128), 1) < 64
    tail_first = jnp.concatenate([tail, swapped], axis=0)
    turned = pltpu.roll(main, 64, 1)
    front = jnp.concatenate([main, tail_first[:, :64]], axis=1)
    back = jnp.concatenate([jnp.where(lower, tail_first, turned), turned[:, :64]], axis=1)
    owned = jnp.where(row_ref[0] == 0, front, back)
    project_ref[...] = owned[:project_each]
    output_ref[...] = owned[project_each:]


def body(
    row_size,
    date_size,
    tokens,
    clear_flags,
    date_numbers,
    decay_slopes,
    time_project,
    time_output,
    column_project,
    column_output,
    cotangent,
):
    date_local, row_local, column_count, width = tokens.shape
    head_count = decay_slopes.shape[0]
    head_size = width // head_count
    packed = max(1, 128 // head_size)
    local_patches = row_local * column_count
    patches_each = local_patches // date_size
    columns_each = column_count // row_size
    row_count = row_local * row_size
    date_count = date_local * date_size
    project_each = 3 * width // date_size
    output_each = width // date_size
    lane_each = width // row_size
    direct = (
        patches_each == column_count
        and column_count % 16 == 0
        and date_size % 8 == 0
        and row_size == 2
        and lane_each == 192
        and project_each % 8 == 0
        and output_each % 8 == 0
        and (project_each + output_each) % 32 == 0
    )
    token_rows = date_local * patches_each
    block_rows = -(-(token_rows + date_local) // 8) * 8
    tile_rows = (width // 128) * token_rows + -(-date_local // 8) * 8
    params = pltpu.CompilerParams(vmem_limit_bytes=vmem_limit)
    in_vmem = pl.BlockSpec(memory_space=pltpu.VMEM)
    in_smem = pl.BlockSpec(memory_space=pltpu.SMEM)
    in_hbm = pl.BlockSpec(memory_space=pltpu.HBM)
    swap = [(0, 1), (1, 0)]
    column_tokens = date_local * row_count * columns_each
    half_tokens = column_tokens // row_size
    if direct:
        outgoing = pl.pallas_call(
            pack_kernel,
            out_shape=jax.ShapeDtypeStruct((date_size, tile_rows, 128), low),
            in_specs=[in_hbm] * 3,
            scratch_shapes=[
                pltpu.SMEM(date_numbers.shape, jnp.int32),
                pltpu.VMEM(tokens.shape, low),
                pltpu.VMEM(clear_flags.shape, jnp.int32),
                pltpu.SemaphoreType.DMA((3,)),
            ],
            name="pack_tokens",
        )(date_numbers, tokens, clear_flags)
        row_at = lax.axis_index("row")
        halves = cotangent.reshape(date_local, row_local, row_size, columns_each, width)
        leaving = lax.dynamic_index_in_dim(halves, 1 - row_at, 2, keepdims=False)
        other_grad = lax.ppermute(leaving, "row", swap)
    else:
        flags = jnp.transpose(
            clear_flags.reshape(date_local, date_size, patches_each), (1, 0, 2)
        ).astype(low)
        numbers = jnp.stack([date_numbers // 32, date_numbers % 32], axis=-1).astype(low)
        numbers = jnp.broadcast_to(numbers[None], (date_size, date_local, 2))
        info = jnp.concatenate([flags, numbers], axis=-1)
        info = jnp.pad(
            info, ((0, 0), (0, block_rows - token_rows - date_local), (0, width - patches_each - 2))
        )
        outgoing = jnp.transpose(
            tokens.reshape(date_local, date_size, patches_each, width), (1, 0, 2, 3)
        ).reshape(date_size, token_rows, width)
        outgoing = jnp.concatenate([outgoing, info], axis=1)
    incoming = lax.all_to_all(outgoing, dates, split_axis=0, concat_axis=0, tiled=True)

    if direct:
        grads_in = (
            row_at.reshape(1),
            cotangent.reshape(local_patches * date_local, width),
            other_grad.reshape(half_tokens, width),
        )
        in_specs = [in_smem] + [in_vmem] * 4
    else:
        grads_in = (
            lax.all_to_all(cotangent, "row", split_axis=2, concat_axis=1, tiled=True).reshape(
                column_tokens, width
            ),
        )
        in_specs = [in_vmem] * 3
    grad_low, heads_grad, time_output = pl.pallas_call(
        functools.partial(
            cotangent_kernel, (date_local, row_size, row_local, columns_each, direct)
        ),
        out_shape=(
            jax.ShapeDtypeStruct((column_tokens, width), low),
            jax.ShapeDtypeStruct((column_tokens, width), low),
            jax.ShapeDtypeStruct(time_output.shape, low),
        ),
        in_specs=in_specs,
        scratch_shapes=[pltpu.VMEM((width // 128, column_tokens, 128), wide)],
        compiler_params=params,
        name="cotangent_heads",
    )(*grads_in, column_output, time_output)

    time_tokens = date_count * patches_each
    hidden = pl.pallas_call(
        functools.partial(
            time_kernel,
            (
                date_size,
                date_local,
                patches_each,
                head_count,
                packed,
                columns_each if direct else patches_each,
            ),
        ),
        out_shape=jax.ShapeDtypeStruct((time_tokens, width), low),
        in_specs=[in_smem, in_vmem, in_vmem, in_vmem],
        scratch_shapes=[
            pltpu.VMEM((width // 128, time_tokens, 128), wide),
            pltpu.VMEM((time_tokens, width), wide),
            pltpu.VMEM((time_tokens, 3 * width), low),
            pltpu.VMEM((time_tokens, width), low),
        ],
        compiler_params=params,
        name="time_attention",
    )(decay_slopes, incoming, time_project, time_output)

    if direct:
        parts = hidden.reshape(row_size * date_size, date_local * columns_each, width)
        plane = lax.all_to_all(parts, ("row", *dates), split_axis=0, concat_axis=0, tiled=True)
    else:
        parts = hidden.reshape(date_size, date_local, patches_each, width)
        back = lax.all_to_all(parts, dates, split_axis=0, concat_axis=0, tiled=True)
        back = jnp.transpose(back, (1, 0, 2, 3)).reshape(
            date_local, row_local, column_count, width
        )
        plane = lax.all_to_all(back, "row", split_axis=2, concat_axis=1, tiled=True)
    plane = plane.reshape(column_tokens, width)
    half_shape = jax.ShapeDtypeStruct((half_tokens, width), low)
    packed_rows = (project_each + output_each) * 3 // 2
    block = (packed_rows, 128)
    outers = date_size // 4
    if direct:
        half_grads = jax.ShapeDtypeStruct((row_size, outers, 2, *block), low)
        places = (row_at.reshape(1), lax.axis_index("pair").reshape(1))
        out_shape = (half_shape, half_shape, half_grads, half_grads)
        in_specs = [in_smem] * 2 + [in_vmem] * 5
    else:
        places = ()
        out_shape = (
            jax.ShapeDtypeStruct((column_tokens, width), low),
            jax.ShapeDtypeStruct((3 * width, width), wide),
            jax.ShapeDtypeStruct((width, width), wide),
        )
        in_specs = [in_vmem] * 5
    results = pl.pallas_call(
        functools.partial(
            column_kernel,
            (
                date_local,
                row_size,
                row_local,
                columns_each,
                head_count,
                packed,
                date_size,
                direct,
            ),
        ),
        out_shape=out_shape,
        in_specs=in_specs,
        scratch_shapes=[
            pltpu.VMEM((width // 128, column_tokens, 128), wide),
            pltpu.VMEM((column_tokens, width), wide),
            pltpu.VMEM((column_tokens, width), low),
            pltpu.VMEM((column_tokens, 3 * width), low),
            pltpu.VMEM((column_tokens, width), low),
            pltpu.VMEM((column_tokens, 3 * width), low),
        ],
        compiler_params=params,
        name="column_attention",
    )(*places, plane, grad_low, heads_grad, column_project, column_output)

    if direct:
        kept, sent, kept_grad, sent_grad = results
        arrived_grad = lax.ppermute(sent_grad, "pair", swap)
        mid_one, row_one = lax.axis_index("mid").reshape(1), row_at.reshape(1)
        outer_one = lax.axis_index("outer").reshape(1)

        def shaped(*lead):
            return jax.ShapeDtypeStruct((*lead, *block), low)

        half = outers // 2
        a_kept, a_sent, b_kept, b_sent = pl.pallas_call(
            halve_kernel,
            out_shape=(shaped(2, half), shaped(2, half), shaped(half, 2), shaped(half, 2)),
            in_specs=[in_smem] * 2 + [in_vmem] * 2,
            compiler_params=params,
            name="halve_gradients",
        )(mid_one, row_one, kept_grad, arrived_grad)
        a_came = lax.ppermute(a_sent, "mid", swap)
        b_came = lax.ppermute(b_sent, "row", swap)
        a_kept, a_sent, b_kept, b_sent = pl.pallas_call(
            halve_again_kernel,
            out_shape=(shaped(half),) * 4,
            in_specs=[in_smem] * 2 + [in_vmem] * 4,
            compiler_params=params,
            name="halve_gradients_again",
        )(mid_one, row_one, a_kept, a_came, b_kept, b_came)
        a_came = lax.ppermute(a_sent, "row", swap)
        b_came = lax.ppermute(b_sent, "mid", swap)
        leaving, *blocks = pl.pallas_call(
            spread_kernel,
            out_shape=(half_shape, *(shaped(),) * outers),
            in_specs=[in_smem] + [in_vmem] * 5,
            scratch_shapes=[pltpu.VMEM((outers, *block), low)],
            compiler_params=params,
            name="spread_gradients",
        )(outer_one, a_kept, a_came, b_kept, b_came, sent)
        arrived = lax.ppermute(leaving, "row", swap)
        terms = [blocks[0]]
        for step in range(1, outers):
            route = [(at, (at + step) % outers) for at in range(outers)]
            terms.append(lax.ppermute(blocks[step], "outer", route))
        owned_project, owned_output = pl.pallas_call(
            functools.partial(finish_kernel, project_each),
            out_shape=(
                jax.ShapeDtypeStruct((project_each, lane_each), wide),
                jax.ShapeDtypeStruct((output_each, lane_each), wide),
            ),
            in_specs=[in_smem] + [in_vmem] * outers,
            compiler_params=params,
            name="gradient_sum",
        )(row_one, *terms)
        quarter = (date_local, row_local, 1, columns_each, width)
        kept, arrived = kept.reshape(quarter), arrived.reshape(quarter)
        mixed = jnp.concatenate(
            [jnp.where(row_at == 0, kept, arrived), jnp.where(row_at == 0, arrived, kept)], axis=2
        )
    else:
        mixed, project_grad, output_grad = results
        grads = jnp.concatenate(
            [
                project_grad.reshape(date_size, project_each, row_size, lane_each),
                output_grad.reshape(date_size, output_each, row_size, lane_each),
            ],
            axis=1,
        ).astype(low)
        grads = jnp.transpose(grads, (2, 0, 1, 3)).reshape(
            row_size * date_size, project_each + output_each, lane_each
        )
        terms = lax.all_to_all(grads, ("row", *dates), split_axis=0, concat_axis=0, tiled=True)
        owned = jnp.sum(terms.astype(wide), axis=0)
        owned_project, owned_output = owned[:project_each], owned[project_each:]
        mixed = mixed.reshape(row_size, date_local, row_local, columns_each, width)
        mixed = lax.all_to_all(mixed, "row", split_axis=0, concat_axis=0, tiled=True)
        mixed = jnp.transpose(mixed, (1, 2, 0, 3, 4))
    mixed = mixed.reshape(date_local, row_local, column_count, width)
    return (mixed, jnp.transpose(owned_project), jnp.transpose(owned_output))


def solution(mesh):
    date_size, row_size = mesh.shape["date"], mesh.shape["row"]
    pair_size = 2 if date_size % 2 == 0 else 1
    mid_size = 2 if date_size % 4 == 0 else 1
    split = jax.sharding.Mesh(
        mesh.devices.reshape(-1, mid_size, pair_size, row_size), ("outer", "mid", "pair", "row")
    )
    return jax.shard_map(
        functools.partial(body, row_size, date_size),
        mesh=split,
        in_specs=(
            P(dates, "row", None, None),
            P(dates, "row", None),
            P(dates),
            P(),
            P(),
            P(),
            P(),
            P(),
            P(dates, "row", None, None),
        ),
        out_specs=(P(dates, "row", None, None), P("row", dates), P("row", dates)),
        check_vma=False,
    )
```

```python
import functools
import math

import jax
import jax.numpy as jnp
from jax import lax
from jax.experimental import pallas as pl
from jax.experimental.pallas import tpu as pltpu
from jax.sharding import PartitionSpec as P

epsilon = 1e-06
masked_score = -1e30
units_each = 24
dates = ("outer", "mid", "pair")
vmem_limit = 24 * 1024 * 1024
low = jnp.bfloat16
wide = jnp.float32


def rms_norm(values):
    factor = lax.rsqrt(jnp.mean(values * values, axis=-1, keepdims=True) + epsilon)
    return (values * factor).astype(low)


def matmul(left, right):
    return jnp.dot(left, right, preferred_element_type=wide)


def contract_rows(left, right):
    return lax.dot_general(left, right, (((0,), (0,)), ((), ())), preferred_element_type=wide)


def contract_last(left, right):
    return lax.dot_general(left, right, (((1,), (1,)), ((), ())), preferred_element_type=wide)


def block_mask(length, packed, head_size):
    shape = (packed * length, packed * head_size)
    rows = lax.broadcasted_iota(jnp.int32, shape, 0) // length
    lanes = lax.broadcasted_iota(jnp.int32, shape, 1) // head_size
    return jnp.where(rows == lanes, 1.0, 0.0).astype(low)


def spread(values, mask, packed):
    return jnp.concatenate([values] * packed, axis=0) * mask


def batches(groups, parts, each):
    units = [(group, part) for group in range(groups) for part in range(parts)]
    return [units[first : first + each] for first in range(0, len(units), each)]


def own_blocks(full, length, packed, head_size):
    lanes = lax.broadcasted_iota(jnp.int32, (length, packed * head_size), 1) // head_size
    out = full[:length]
    for head in range(1, packed):
        out = jnp.where(lanes == head, full[head * length : (head + 1) * length], out)
    return out


def softmax_first(scores):
    raised = jnp.exp(scores - jnp.max(scores, axis=0, keepdims=True))
    return raised * (1.0 / jnp.sum(raised, axis=0, keepdims=True))


def put_tiles(scratch, rows, values):
    tiles, _, lanes = scratch.shape
    for tile in range(tiles):
        scratch[tile, rows, :] = values[:, tile * lanes : (tile + 1) * lanes]


def get_tiles(scratch, rows):
    return jnp.concatenate([scratch[tile, rows, :] for tile in range(scratch.shape[0])], axis=-1)


def pack_kernel(
    numbers_ref, tokens_ref, flags_ref, out_ref, numbers_scr, tokens_scr, flags_scr, copied
):
    copies = [
        pltpu.make_async_copy(tokens_ref, tokens_scr, copied.at[0]),
        pltpu.make_async_copy(flags_ref, flags_scr, copied.at[1]),
        pltpu.make_async_copy(numbers_ref, numbers_scr, copied.at[2]),
    ]
    for copy in copies:
        copy.start()
    dates_each, parts, patches, width = tokens_ref.shape
    lanes = out_ref.shape[2]
    tiles = width // lanes
    spare = out_ref.shape[1] - tiles * dates_each * patches
    place = lax.broadcasted_iota(jnp.int32, (patches, lanes), 0)
    lane = lax.broadcasted_iota(jnp.int32, (patches, lanes), 1)
    place = jnp.where(place == lane, 1.0, 0.0).astype(low)
    lane = lax.broadcasted_iota(jnp.int32, (parts, lanes), 1)
    row = lax.broadcasted_iota(jnp.int32, (spare, lanes), 0)
    copies[1].wait()
    copies[2].wait()
    infos = []
    for date in range(dates_each):
        number = numbers_scr[date]
        upper = (number // 32).astype(wide)
        under = (number % 32).astype(wide)
        info = matmul(flags_scr[date].astype(wide).astype(low), place)
        info = jnp.where(lane == patches, upper, info)
        infos.append(jnp.where(lane == patches + 1, under, info))
    copies[0].wait()
    for part in range(parts):
        tokens = jnp.concatenate(
            [tokens_scr[date, part].astype(wide) for date in range(dates_each)], axis=0
        )
        extra = jnp.zeros((spare, lanes), wide)
        for date in range(dates_each):
            extra = jnp.where(row == date, infos[date][part : part + 1], extra)
        pieces = [tokens[:, tile * lanes : (tile + 1) * lanes] for tile in range(tiles)]
        out_ref[part] = jnp.concatenate(pieces + [extra], axis=0).astype(low)


def time_kernel(
    sizes,
    slopes_ref,
    block_ref,
    project_ref,
    output_ref,
    out_ref,
    seq_scr,
    token_scr,
    qkv_scr,
    heads_scr,
):
    sources, dates_each, groups, head_count, packed, columns_each = sizes
    width = project_ref.shape[0]
    tile_lanes = block_ref.shape[2]
    tiles = width // tile_lanes
    head_size = width // head_count
    lanes = packed * head_size
    length = sources * dates_each
    token_rows = dates_each * groups
    inverse_root = 1.0 / math.sqrt(head_size)
    info = []
    for source in range(sources):
        plane = block_ref[source].astype(wide)
        rows = slice(source * token_rows, (source + 1) * token_rows)
        for tile in range(tiles):
            at = slice(tile * token_rows, (tile + 1) * token_rows)
            if tiles == 1:
                put_tiles(seq_scr, rows, plane[at])
            else:
                seq_scr[tile, rows, :] = plane[at]
        info.append(plane[tiles * token_rows : tiles * token_rows + dates_each])
    info = jnp.concatenate(info, axis=0)
    for group in range(groups):
        token_scr[group * length : (group + 1) * length, :] = get_tiles(
            seq_scr, pl.ds(group, length, stride=groups)
        )
    tokens = token_scr[...]
    qkv_scr[...] = matmul(rms_norm(tokens), project_ref[...]).astype(low)
    numbers = info[:, groups : groups + 1] * 32.0 + info[:, groups + 1 : groups + 2]
    key_at = lax.broadcasted_iota(jnp.int32, (length, packed * length), 0)
    column_at = lax.broadcasted_iota(jnp.int32, (length, packed * length), 1)
    same_date = key_at == column_at % length
    query_numbers = jnp.sum(jnp.where(same_date, numbers, 0.0), axis=0, keepdims=True)
    gap_days = jnp.abs(numbers - query_numbers)
    head_at = column_at // length
    mask = block_mask(length, packed, head_size)
    biases = []
    for first in range(0, head_count, packed):
        slope = jnp.full((length, packed * length), slopes_ref[first], wide)
        for head in range(1, packed):
            slope = jnp.where(head_at == head, slopes_ref[first + head], slope)
        biases.append(-slope * gap_days)
    for units in batches(groups, head_count // packed, units_each):
        all_scores = []
        for group, part in units:
            rows = slice(group * length, (group + 1) * length)
            start = part * lanes
            query = qkv_scr[rows, start : start + lanes]
            key = qkv_scr[rows, width + start : width + start + lanes]
            all_scores.append(contract_last(key, spread(query, mask, packed)))
        all_weights = []
        for (group, part), scores in zip(units, all_scores):
            allowed = (info[:, group : group + 1] > 0) | same_date
            scores = jnp.where(allowed, scores * inverse_root + biases[part], masked_score)
            all_weights.append(softmax_first(scores).astype(low))
        all_heads = []
        for (group, part), weights in zip(units, all_weights):
            rows = slice(group * length, (group + 1) * length)
            start = 2 * width + part * lanes
            all_heads.append(contract_rows(weights, qkv_scr[rows, start : start + lanes]))
        for (group, part), full in zip(units, all_heads):
            rows = slice(group * length, (group + 1) * length)
            heads_scr[rows, part * lanes : (part + 1) * lanes] = own_blocks(
                full, length, packed, head_size
            ).astype(low)
    hidden = token_scr[...] + matmul(heads_scr[...], output_ref[...])
    for group in range(groups):
        first = (group // columns_each) * (length * columns_each) + group % columns_each
        put_tiles(
            seq_scr,
            pl.ds(first, length, stride=columns_each),
            hidden[group * length : (group + 1) * length],
        )
    out_ref[...] = get_tiles(seq_scr, slice(None)).astype(low)


def cotangent_kernel(sizes, *refs):
    dates_each, row_parts, rows_each, columns_each, direct = sizes
    output_ref, slopes_ref, grad_low_ref, heads_grad_ref, handed_ref, grad_scr = refs[-6:]
    for head in range(slopes_ref.shape[0]):
        handed_ref[head] = slopes_ref[head]
    width = output_ref.shape[0]
    length = row_parts * rows_each
    groups = dates_each * columns_each
    part_rows = rows_each * groups
    if direct:
        row_ref, own_ref, other_ref = refs[:3]
        own = own_ref[...].astype(wide)
        own = own.reshape(dates_each * rows_each, row_parts, columns_each, width)
        own = jnp.where(row_ref[0] == 0, own[:, 0], own[:, 1]).reshape(part_rows, width)
        put_tiles(grad_scr, slice(0, part_rows), own)
        put_tiles(grad_scr, slice(part_rows, 2 * part_rows), other_ref[...].astype(wide))
    else:
        put_tiles(grad_scr, slice(None), refs[0][...].astype(wide))
    for group in range(groups):
        if direct:
            inner = (group // columns_each) * (rows_each * columns_each) + group % columns_each
            pieces = [
                get_tiles(
                    grad_scr, pl.ds(part * part_rows + inner, rows_each, stride=columns_each)
                )
                for part in range(row_parts)
            ]
            values = jnp.concatenate(pieces, axis=0)
        else:
            first = (group // columns_each) * (length * columns_each) + group % columns_each
            values = get_tiles(grad_scr, pl.ds(first, length, stride=columns_each))
        grad_low_ref[group * length : (group + 1) * length, :] = values.astype(low)
    heads_grad_ref[...] = contract_last(grad_low_ref[...], output_ref[...]).astype(low)


def load_planes(sizes, row_ref, hidden_ref, seq_scr, plane_scr):
    dates_each, row_parts, rows_each, columns_each, direct = sizes
    length = row_parts * rows_each
    groups = dates_each * columns_each
    part_rows = rows_each * groups
    if direct:
        for part in range(row_parts):
            source = pl.multiple_of(((row_ref[0] + part) % row_parts) * part_rows, part_rows)
            put_tiles(
                seq_scr,
                slice(part * part_rows, (part + 1) * part_rows),
                hidden_ref[pl.ds(source, part_rows), :].astype(wide),
            )
    else:
        put_tiles(seq_scr, slice(None), hidden_ref[...].astype(wide))
    for group in range(groups):
        rows = slice(group * length, (group + 1) * length)
        if direct:
            at = pl.ds(group, length, stride=groups)
        else:
            first = (group // columns_each) * (length * columns_each) + group % columns_each
            at = pl.ds(first, length, stride=columns_each)
        plane_scr[rows, :] = get_tiles(seq_scr, at)


def mixed_kernel(sizes, row_ref, hidden_ref, heads_ref, output_ref, *refs):
    dates_each, row_parts, rows_each, columns_each, direct = sizes
    *mixed_refs, seq_scr, plane_scr = refs
    length = row_parts * rows_each
    groups = dates_each * columns_each
    part_rows = rows_each * groups
    load_planes(sizes, row_ref, hidden_ref, seq_scr, plane_scr)
    mixed = plane_scr[...] + matmul(heads_ref[...], output_ref[...])
    for group in range(groups):
        inner = (group // columns_each) * (rows_each * columns_each) + group % columns_each
        for part in range(row_parts):
            begin = group * length + part * rows_each
            put_tiles(
                seq_scr,
                pl.ds(part * part_rows + inner, rows_each, stride=columns_each),
                mixed[begin : begin + rows_each],
            )
    if direct:
        kept_ref, sent_ref = mixed_refs
        kept_ref[...] = get_tiles(seq_scr, slice(0, part_rows)).astype(low)
        sent_ref[...] = get_tiles(seq_scr, slice(part_rows, 2 * part_rows)).astype(low)
    else:
        mixed_refs[0][...] = get_tiles(seq_scr, slice(None)).astype(low)


def column_kernel(
    sizes,
    row_ref,
    pair_ref,
    hidden_ref,
    grad_low_scr,
    heads_grad_scr,
    project_ref,
    heads_scr,
    first_grad_ref,
    second_grad_ref,
    seq_scr,
    plane_scr,
    normed_scr,
    qkv_scr,
    qkv_grad_scr,
):
    dates_each, row_parts, rows_each, columns_each, direct, head_count, packed, date_size = sizes
    width = hidden_ref.shape[1]
    head_size = width // head_count
    lanes = packed * head_size
    length = row_parts * rows_each
    groups = dates_each * columns_each
    inverse_root = 1.0 / math.sqrt(head_size)
    load_planes(sizes[:5], row_ref, hidden_ref, seq_scr, plane_scr)
    normed_scr[...] = rms_norm(plane_scr[...])
    qkv_scr[...] = matmul(normed_scr[...], project_ref[...]).astype(low)
    mask = block_mask(length, packed, head_size)
    for units in batches(groups, head_count // packed, units_each):
        places = []
        for group, part in units:
            start = part * lanes
            places.append(
                (
                    slice(group * length, (group + 1) * length),
                    slice(start, start + lanes),
                    slice(width + start, width + start + lanes),
                    slice(2 * width + start, 2 * width + start + lanes),
                )
            )
        all_scores = []
        for rows, at_query, at_key, at_value in places:
            query = spread(qkv_scr[rows, at_query], mask, packed)
            heads_grad = spread(heads_grad_scr[rows, at_query], mask, packed)
            all_scores.append(
                (
                    contract_last(qkv_scr[rows, at_key], query),
                    contract_last(qkv_scr[rows, at_value], heads_grad),
                )
            )
        all_weights = []
        for scores, product_grad in all_scores:
            weights = softmax_first(scores * inverse_root)
            score_grad = weights * (
                product_grad - jnp.sum(weights * product_grad, axis=0, keepdims=True)
            )
            all_weights.append((weights.astype(low), score_grad.astype(low)))
        all_full = []
        for (rows, at_query, at_key, at_value), (weights, score_low) in zip(places, all_weights):
            all_full.append(
                (
                    contract_rows(weights, qkv_scr[rows, at_value]),
                    contract_rows(score_low, qkv_scr[rows, at_key]),
                )
            )
            query = spread(qkv_scr[rows, at_query], mask, packed)
            heads_grad = spread(heads_grad_scr[rows, at_query], mask, packed)
            key_grad = matmul(score_low, query) * inverse_root
            qkv_grad_scr[rows, at_key] = key_grad.astype(low)
            qkv_grad_scr[rows, at_value] = matmul(weights, heads_grad).astype(low)
        for (rows, at_query, _, _), (heads_full, query_full) in zip(places, all_full):
            heads = own_blocks(heads_full, length, packed, head_size)
            heads_scr[rows, at_query] = heads.astype(low)
            query_grad = own_blocks(query_full, length, packed, head_size) * inverse_root
            qkv_grad_scr[rows, at_query] = query_grad.astype(low)
    project_grad = contract_rows(qkv_grad_scr[...], normed_scr[...])
    output_grad = contract_rows(grad_low_scr[...], heads_scr[...])
    if not direct:
        first_grad_ref[...] = project_grad
        second_grad_ref[...] = output_grad
        return
    keep_ref, send_ref = first_grad_ref, second_grad_ref
    even = pair_ref[0] == 0
    project_each = project_grad.shape[0] // date_size
    output_each = output_grad.shape[0] // date_size
    half = (project_each + output_each) // 2
    lower = lax.broadcasted_iota(jnp.int32, (half, 128), 1) < 64
    for outer in range(date_size // 2):
        pair = []
        for part in (2 * outer, 2 * outer + 1):
            block = jnp.concatenate(
                [
                    project_grad[part * project_each : (part + 1) * project_each],
                    output_grad[part * output_each : (part + 1) * output_each],
                ],
                axis=0,
            )
            top, bottom = block[:half, 128:256], block[half:, 128:256]
            pair.append(
                (
                    (block[:, :128], jnp.where(lower, top, pltpu.roll(bottom, 64, 1))),
                    (block[:, 256:], jnp.where(lower, pltpu.roll(top, 64, 1), bottom)),
                )
            )
        for row_part in range(2):
            for first, one, two in zip((0, 2 * half), pair[0][row_part], pair[1][row_part]):
                place = (row_part, outer, slice(first, first + one.shape[0]))
                keep_ref[place] = jnp.where(even, one, two).astype(low)
                send_ref[place] = jnp.where(even, two, one).astype(low)


def pair_kernel(row_ref, kept_ref, came_ref, sum_ref, handed_ref):
    handed_ref[0] = row_ref[0]
    sum_ref[...] = (kept_ref[...].astype(wide) + came_ref[...].astype(wide)).astype(low)


def finish_kernel(project_each, row_ref, terms_ref, project_ref, output_ref):
    total = terms_ref[0].astype(wide)
    for source in range(1, terms_ref.shape[0]):
        total = total + terms_ref[source].astype(wide)
    whole = 2 * total.shape[0] // 3
    main = total[:whole]
    tail = total[whole:]
    swapped = pltpu.roll(tail, 64, 1)
    lower = lax.broadcasted_iota(jnp.int32, (whole, 128), 1) < 64
    tail_first = jnp.concatenate([tail, swapped], axis=0)
    turned = pltpu.roll(main, 64, 1)
    front = jnp.concatenate([main, tail_first[:, :64]], axis=1)
    back = jnp.concatenate([jnp.where(lower, tail_first, turned), turned[:, :64]], axis=1)
    owned = jnp.where(row_ref[0] == 0, front, back)
    project_ref[...] = owned[:project_each]
    output_ref[...] = owned[project_each:]


def body(
    row_size,
    date_size,
    tokens,
    clear_flags,
    date_numbers,
    decay_slopes,
    time_project,
    time_output,
    column_project,
    column_output,
    cotangent,
):
    date_local, row_local, column_count, width = tokens.shape
    head_count = decay_slopes.shape[0]
    head_size = width // head_count
    packed = max(1, 128 // head_size)
    local_patches = row_local * column_count
    patches_each = local_patches // date_size
    columns_each = column_count // row_size
    row_count = row_local * row_size
    date_count = date_local * date_size
    project_each = 3 * width // date_size
    output_each = width // date_size
    lane_each = width // row_size
    direct = (
        patches_each == column_count
        and column_count % 16 == 0
        and date_size % 8 == 0
        and row_size == 2
        and lane_each == 192
        and project_each % 8 == 0
        and output_each % 8 == 0
        and (project_each + output_each) % 32 == 0
    )
    token_rows = date_local * patches_each
    block_rows = -(-(token_rows + date_local) // 8) * 8
    tile_rows = (width // 128) * token_rows + -(-date_local // 8) * 8
    params = pltpu.CompilerParams(vmem_limit_bytes=vmem_limit)
    in_vmem = pl.BlockSpec(memory_space=pltpu.VMEM)
    in_smem = pl.BlockSpec(memory_space=pltpu.SMEM)
    swap = [(0, 1), (1, 0)]
    column_tokens = date_local * row_count * columns_each
    half_tokens = column_tokens // row_size
    if direct:
        outgoing = pl.pallas_call(
            pack_kernel,
            out_shape=jax.ShapeDtypeStruct((date_size, tile_rows, 128), low),
            in_specs=[pl.BlockSpec(memory_space=pltpu.HBM)] * 3,
            scratch_shapes=[
                pltpu.SMEM(date_numbers.shape, jnp.int32),
                pltpu.VMEM(tokens.shape, low),
                pltpu.VMEM(clear_flags.shape, jnp.int32),
                pltpu.SemaphoreType.DMA((3,)),
            ],
            name="pack_tokens",
        )(date_numbers, tokens, clear_flags)
        row_at = lax.axis_index("row")
        halves = cotangent.reshape(date_local, row_local, row_size, columns_each, width)
        leaving = lax.dynamic_index_in_dim(halves, 1 - row_at, 2, keepdims=False)
        other_grad = lax.ppermute(leaving, "row", swap)
    else:
        flags = jnp.transpose(
            clear_flags.reshape(date_local, date_size, patches_each), (1, 0, 2)
        ).astype(low)
        numbers = jnp.stack([date_numbers // 32, date_numbers % 32], axis=-1).astype(low)
        numbers = jnp.broadcast_to(numbers[None], (date_size, date_local, 2))
        info = jnp.concatenate([flags, numbers], axis=-1)
        info = jnp.pad(
            info, ((0, 0), (0, block_rows - token_rows - date_local), (0, width - patches_each - 2))
        )
        outgoing = jnp.transpose(
            tokens.reshape(date_local, date_size, patches_each, width), (1, 0, 2, 3)
        ).reshape(date_size, token_rows, width)
        outgoing = jnp.concatenate([outgoing, info], axis=1)
    incoming = lax.all_to_all(outgoing, dates, split_axis=0, concat_axis=0, tiled=True)

    if direct:
        grads_in = (
            row_at.reshape(1),
            cotangent.reshape(local_patches * date_local, width),
            other_grad.reshape(half_tokens, width),
        )
        in_specs = [in_smem] + [in_vmem] * 3 + [in_smem]
    else:
        grads_in = (
            lax.all_to_all(cotangent, "row", split_axis=2, concat_axis=1, tiled=True).reshape(
                column_tokens, width
            ),
        )
        in_specs = [in_vmem] * 2 + [in_smem]
    grad_low, heads_grad, slopes = pl.pallas_call(
        functools.partial(
            cotangent_kernel, (date_local, row_size, row_local, columns_each, direct)
        ),
        out_shape=(
            jax.ShapeDtypeStruct((column_tokens, width), low),
            jax.ShapeDtypeStruct((column_tokens, width), low),
            jax.ShapeDtypeStruct(decay_slopes.shape, wide),
        ),
        in_specs=in_specs,
        out_specs=(in_vmem, in_vmem, in_smem),
        scratch_shapes=[pltpu.VMEM((width // 128, column_tokens, 128), wide)],
        name="cotangent_heads",
    )(*grads_in, column_output, decay_slopes)

    time_tokens = date_count * patches_each
    hidden = pl.pallas_call(
        functools.partial(
            time_kernel,
            (
                date_size,
                date_local,
                patches_each,
                head_count,
                packed,
                columns_each if direct else patches_each,
            ),
        ),
        out_shape=jax.ShapeDtypeStruct((time_tokens, width), low),
        in_specs=[in_smem, in_vmem, in_vmem, in_vmem],
        scratch_shapes=[
            pltpu.VMEM((width // 128, time_tokens, 128), wide),
            pltpu.VMEM((time_tokens, width), wide),
            pltpu.VMEM((time_tokens, 3 * width), low),
            pltpu.VMEM((time_tokens, width), low),
        ],
        compiler_params=params,
        name="time_attention",
    )(slopes, incoming, time_project, time_output)

    if direct:
        parts = hidden.reshape(row_size * date_size, date_local * columns_each, width)
        plane = lax.all_to_all(parts, ("row", *dates), split_axis=0, concat_axis=0, tiled=True)
    else:
        parts = hidden.reshape(date_size, date_local, patches_each, width)
        back = lax.all_to_all(parts, dates, split_axis=0, concat_axis=0, tiled=True)
        back = jnp.transpose(back, (1, 0, 2, 3)).reshape(
            date_local, row_local, column_count, width
        )
        plane = lax.all_to_all(back, "row", split_axis=2, concat_axis=1, tiled=True)
    plane = plane.reshape(column_tokens, width)
    half_shape = jax.ShapeDtypeStruct((half_tokens, width), low)
    packed_rows = (project_each + output_each) * 3 // 2
    row_one = lax.axis_index("row").reshape(1)
    pair_one = lax.axis_index("pair").reshape(1)
    sizes = (date_local, row_size, row_local, columns_each, direct)
    if direct:
        half_grads = jax.ShapeDtypeStruct((row_size, date_size // 2, packed_rows, 128), low)
        grad_shapes = (half_grads, half_grads)
        mixed_shapes = (half_shape, half_shape)
    else:
        grad_shapes = (
            jax.ShapeDtypeStruct((3 * width, width), wide),
            jax.ShapeDtypeStruct((width, width), wide),
        )
        mixed_shapes = (jax.ShapeDtypeStruct((column_tokens, width), low),)
    column_heads, first_grad, second_grad = pl.pallas_call(
        functools.partial(column_kernel, (*sizes, head_count, packed, date_size)),
        out_shape=(jax.ShapeDtypeStruct((column_tokens, width), low), *grad_shapes),
        in_specs=[in_smem] * 2 + [in_vmem] * 4,
        scratch_shapes=[
            pltpu.VMEM((width // 128, column_tokens, 128), wide),
            pltpu.VMEM((column_tokens, width), wide),
            pltpu.VMEM((column_tokens, width), low),
            pltpu.VMEM((column_tokens, 3 * width), low),
            pltpu.VMEM((column_tokens, 3 * width), low),
        ],
        compiler_params=params,
        name="column_attention",
    )(row_one, pair_one, plane, grad_low, heads_grad, column_project)
    after_one = row_one
    if direct:
        came = lax.ppermute(second_grad, "pair", swap)
        pair_sum, after_one = pl.pallas_call(
            pair_kernel,
            out_shape=(half_grads, jax.ShapeDtypeStruct((1,), jnp.int32)),
            in_specs=[in_smem] + [in_vmem] * 2,
            out_specs=(in_vmem, in_smem),
            compiler_params=params,
            name="pair_gradients",
        )(row_one, first_grad, came)
    mixed = pl.pallas_call(
        functools.partial(mixed_kernel, sizes),
        out_shape=mixed_shapes,
        in_specs=[in_smem] + [in_vmem] * 3,
        scratch_shapes=[
            pltpu.VMEM((width // 128, column_tokens, 128), wide),
            pltpu.VMEM((column_tokens, width), wide),
        ],
        compiler_params=params,
        name="mixed_tokens",
    )(after_one, plane, column_heads, column_output)

    if direct:
        terms = lax.all_to_all(
            pair_sum.reshape(row_size * date_size // 2, packed_rows, 128),
            ("row", "outer", "mid"),
            split_axis=0,
            concat_axis=0,
            tiled=True,
        )
        owned_project, owned_output = pl.pallas_call(
            functools.partial(finish_kernel, project_each),
            out_shape=(
                jax.ShapeDtypeStruct((project_each, lane_each), wide),
                jax.ShapeDtypeStruct((output_each, lane_each), wide),
            ),
            in_specs=[in_smem, in_vmem],
            compiler_params=params,
            name="gradient_sum",
        )(row_one, terms)
        kept, sent = mixed
        arrived = lax.ppermute(sent, "row", swap)
        quarter = (date_local, row_local, 1, columns_each, width)
        kept, arrived = kept.reshape(quarter), arrived.reshape(quarter)
        mixed = jnp.concatenate(
            [jnp.where(row_at == 0, kept, arrived), jnp.where(row_at == 0, arrived, kept)], axis=2
        )
    else:
        mixed = mixed[0]
        grads = jnp.concatenate(
            [
                first_grad.reshape(date_size, project_each, row_size, lane_each),
                second_grad.reshape(date_size, output_each, row_size, lane_each),
            ],
            axis=1,
        ).astype(low)
        grads = jnp.transpose(grads, (2, 0, 1, 3)).reshape(
            row_size * date_size, project_each + output_each, lane_each
        )
        terms = lax.all_to_all(grads, ("row", *dates), split_axis=0, concat_axis=0, tiled=True)
        owned = jnp.sum(terms.astype(wide), axis=0)
        owned_project, owned_output = owned[:project_each], owned[project_each:]
        mixed = mixed.reshape(row_size, date_local, row_local, columns_each, width)
        mixed = lax.all_to_all(mixed, "row", split_axis=0, concat_axis=0, tiled=True)
        mixed = jnp.transpose(mixed, (1, 2, 0, 3, 4))
    mixed = mixed.reshape(date_local, row_local, column_count, width)
    return (mixed, jnp.transpose(owned_project), jnp.transpose(owned_output))


def solution(mesh):
    date_size, row_size = mesh.shape["date"], mesh.shape["row"]
    pair_size = 2 if date_size % 2 == 0 else 1
    mid_size = 2 if date_size % 4 == 0 else 1
    split = jax.sharding.Mesh(
        mesh.devices.reshape(-1, mid_size, pair_size, row_size), ("outer", "mid", "pair", "row")
    )
    return jax.shard_map(
        functools.partial(body, row_size, date_size),
        mesh=split,
        in_specs=(
            P(dates, "row", None, None),
            P(dates, "row", None),
            P(dates),
            P(),
            P(),
            P(),
            P(),
            P(),
            P(dates, "row", None, None),
        ),
        out_specs=(P(dates, "row", None, None), P("row", dates), P("row", dates)),
        check_vma=False,
    )
```

```python
import functools
import math

import jax
import jax.numpy as jnp
from jax import lax
from jax.experimental import pallas as pl
from jax.experimental.pallas import tpu as pltpu
from jax.sharding import PartitionSpec as P

epsilon = 1e-06
masked_score = -1e30
units_each = 24
dates = ("outer", "mid", "pair")
vmem_limit = 24 * 1024 * 1024
low = jnp.bfloat16
wide = jnp.float32


def rms_norm(values):
    factor = lax.rsqrt(jnp.mean(values * values, axis=-1, keepdims=True) + epsilon)
    return (values * factor).astype(low)


def matmul(left, right):
    return jnp.dot(left, right, preferred_element_type=wide)


def contract_rows(left, right):
    return lax.dot_general(left, right, (((0,), (0,)), ((), ())), preferred_element_type=wide)


def contract_last(left, right):
    return lax.dot_general(left, right, (((1,), (1,)), ((), ())), preferred_element_type=wide)


def block_mask(length, packed, head_size):
    shape = (packed * length, packed * head_size)
    rows = lax.broadcasted_iota(jnp.int32, shape, 0) // length
    lanes = lax.broadcasted_iota(jnp.int32, shape, 1) // head_size
    return jnp.where(rows == lanes, 1.0, 0.0).astype(low)


def spread(values, mask, packed):
    return jnp.concatenate([values] * packed, axis=0) * mask


def batches(groups, parts, each):
    units = [(group, part) for group in range(groups) for part in range(parts)]
    return [units[first : first + each] for first in range(0, len(units), each)]


def own_blocks(full, length, packed, head_size):
    lanes = lax.broadcasted_iota(jnp.int32, (length, packed * head_size), 1) // head_size
    out = full[:length]
    for head in range(1, packed):
        out = jnp.where(lanes == head, full[head * length : (head + 1) * length], out)
    return out


def softmax_first(scores):
    raised = jnp.exp(scores - jnp.max(scores, axis=0, keepdims=True))
    return raised * (1.0 / jnp.sum(raised, axis=0, keepdims=True))


def put_tiles(scratch, rows, values):
    tiles, _, lanes = scratch.shape
    for tile in range(tiles):
        scratch[tile, rows, :] = values[:, tile * lanes : (tile + 1) * lanes]


def get_tiles(scratch, rows):
    return jnp.concatenate([scratch[tile, rows, :] for tile in range(scratch.shape[0])], axis=-1)


def pack_kernel(
    numbers_ref, tokens_ref, flags_ref, out_ref, numbers_scr, tokens_scr, flags_scr, copied
):
    copies = [
        pltpu.make_async_copy(tokens_ref, tokens_scr, copied.at[0]),
        pltpu.make_async_copy(flags_ref, flags_scr, copied.at[1]),
        pltpu.make_async_copy(numbers_ref, numbers_scr, copied.at[2]),
    ]
    for copy in copies:
        copy.start()
    dates_each, parts, patches, width = tokens_ref.shape
    lanes = out_ref.shape[2]
    tiles = width // lanes
    spare = out_ref.shape[1] - tiles * dates_each * patches
    place = lax.broadcasted_iota(jnp.int32, (patches, lanes), 0)
    lane = lax.broadcasted_iota(jnp.int32, (patches, lanes), 1)
    place = jnp.where(place == lane, 1.0, 0.0).astype(low)
    lane = lax.broadcasted_iota(jnp.int32, (parts, lanes), 1)
    row = lax.broadcasted_iota(jnp.int32, (spare, lanes), 0)
    copies[1].wait()
    copies[2].wait()
    infos = []
    for date in range(dates_each):
        number = numbers_scr[date]
        upper = (number // 32).astype(wide)
        under = (number % 32).astype(wide)
        info = matmul(flags_scr[date].astype(wide).astype(low), place)
        info = jnp.where(lane == patches, upper, info)
        infos.append(jnp.where(lane == patches + 1, under, info))
    copies[0].wait()
    for part in range(parts):
        tokens = jnp.concatenate(
            [tokens_scr[date, part].astype(wide) for date in range(dates_each)], axis=0
        )
        extra = jnp.zeros((spare, lanes), wide)
        for date in range(dates_each):
            extra = jnp.where(row == date, infos[date][part : part + 1], extra)
        pieces = [tokens[:, tile * lanes : (tile + 1) * lanes] for tile in range(tiles)]
        out_ref[part] = jnp.concatenate(pieces + [extra], axis=0).astype(low)


def time_kernel(
    sizes,
    slopes_ref,
    block_ref,
    project_ref,
    output_ref,
    earlier_ref,
    out_ref,
    after_ref,
    seq_scr,
    token_scr,
    qkv_scr,
    heads_scr,
):
    after_ref[0] = jnp.int32(0)
    sources, dates_each, groups, head_count, packed, columns_each = sizes
    width = project_ref.shape[0]
    tile_lanes = block_ref.shape[2]
    tiles = width // tile_lanes
    head_size = width // head_count
    lanes = packed * head_size
    length = sources * dates_each
    token_rows = dates_each * groups
    inverse_root = 1.0 / math.sqrt(head_size)
    info = []
    for source in range(sources):
        plane = block_ref[source].astype(wide)
        rows = slice(source * token_rows, (source + 1) * token_rows)
        for tile in range(tiles):
            at = slice(tile * token_rows, (tile + 1) * token_rows)
            if tiles == 1:
                put_tiles(seq_scr, rows, plane[at])
            else:
                seq_scr[tile, rows, :] = plane[at]
        info.append(plane[tiles * token_rows : tiles * token_rows + dates_each])
    info = jnp.concatenate(info, axis=0)
    for group in range(groups):
        token_scr[group * length : (group + 1) * length, :] = get_tiles(
            seq_scr, pl.ds(group, length, stride=groups)
        )
    tokens = token_scr[...]
    qkv_scr[...] = matmul(rms_norm(tokens), project_ref[...]).astype(low)
    numbers = info[:, groups : groups + 1] * 32.0 + info[:, groups + 1 : groups + 2]
    key_at = lax.broadcasted_iota(jnp.int32, (length, packed * length), 0)
    column_at = lax.broadcasted_iota(jnp.int32, (length, packed * length), 1)
    same_date = key_at == column_at % length
    query_numbers = jnp.sum(jnp.where(same_date, numbers, 0.0), axis=0, keepdims=True)
    gap_days = jnp.abs(numbers - query_numbers)
    head_at = column_at // length
    mask = block_mask(length, packed, head_size)
    biases = []
    for first in range(0, head_count, packed):
        slope = jnp.full((length, packed * length), slopes_ref[first], wide)
        for head in range(1, packed):
            slope = jnp.where(head_at == head, slopes_ref[first + head], slope)
        biases.append(-slope * gap_days)
    for units in batches(groups, head_count // packed, units_each):
        all_scores = []
        for group, part in units:
            rows = slice(group * length, (group + 1) * length)
            start = part * lanes
            query = qkv_scr[rows, start : start + lanes]
            key = qkv_scr[rows, width + start : width + start + lanes]
            all_scores.append(contract_last(key, spread(query, mask, packed)))
        all_weights = []
        for (group, part), scores in zip(units, all_scores):
            allowed = (info[:, group : group + 1] > 0) | same_date
            scores = jnp.where(allowed, scores * inverse_root + biases[part], masked_score)
            all_weights.append(softmax_first(scores).astype(low))
        all_heads = []
        for (group, part), weights in zip(units, all_weights):
            rows = slice(group * length, (group + 1) * length)
            start = 2 * width + part * lanes
            all_heads.append(contract_rows(weights, qkv_scr[rows, start : start + lanes]))
        for (group, part), full in zip(units, all_heads):
            rows = slice(group * length, (group + 1) * length)
            heads_scr[rows, part * lanes : (part + 1) * lanes] = own_blocks(
                full, length, packed, head_size
            ).astype(low)
    hidden = token_scr[...] + matmul(heads_scr[...], output_ref[...])
    for group in range(groups):
        first = (group // columns_each) * (length * columns_each) + group % columns_each
        put_tiles(
            seq_scr,
            pl.ds(first, length, stride=columns_each),
            hidden[group * length : (group + 1) * length],
        )
    out_ref[...] = get_tiles(seq_scr, slice(None)).astype(low)


def cotangent_kernel(sizes, *refs):
    dates_each, row_parts, rows_each, columns_each, direct = sizes
    output_ref, _, grad_low_ref, heads_grad_ref, grad_scr = refs[-5:]
    width = output_ref.shape[0]
    length = row_parts * rows_each
    groups = dates_each * columns_each
    part_rows = rows_each * groups
    if direct:
        row_ref, own_ref, other_ref = refs[:3]
        own = own_ref[...].astype(wide)
        own = own.reshape(dates_each * rows_each, row_parts, columns_each, width)
        own = jnp.where(row_ref[0] == 0, own[:, 0], own[:, 1]).reshape(part_rows, width)
        put_tiles(grad_scr, slice(0, part_rows), own)
        put_tiles(grad_scr, slice(part_rows, 2 * part_rows), other_ref[...].astype(wide))
    else:
        put_tiles(grad_scr, slice(None), refs[0][...].astype(wide))
    for group in range(groups):
        if direct:
            inner = (group // columns_each) * (rows_each * columns_each) + group % columns_each
            pieces = [
                get_tiles(
                    grad_scr, pl.ds(part * part_rows + inner, rows_each, stride=columns_each)
                )
                for part in range(row_parts)
            ]
            values = jnp.concatenate(pieces, axis=0)
        else:
            first = (group // columns_each) * (length * columns_each) + group % columns_each
            values = get_tiles(grad_scr, pl.ds(first, length, stride=columns_each))
        grad_low_ref[group * length : (group + 1) * length, :] = values.astype(low)
    heads_grad_ref[...] = contract_last(grad_low_ref[...], output_ref[...]).astype(low)


def load_planes(sizes, row_ref, hidden_ref, seq_scr, plane_scr):
    dates_each, row_parts, rows_each, columns_each, direct = sizes
    length = row_parts * rows_each
    groups = dates_each * columns_each
    part_rows = rows_each * groups
    if direct:
        for part in range(row_parts):
            source = pl.multiple_of(((row_ref[0] + part) % row_parts) * part_rows, part_rows)
            put_tiles(
                seq_scr,
                slice(part * part_rows, (part + 1) * part_rows),
                hidden_ref[pl.ds(source, part_rows), :].astype(wide),
            )
    else:
        put_tiles(seq_scr, slice(None), hidden_ref[...].astype(wide))
    for group in range(groups):
        rows = slice(group * length, (group + 1) * length)
        if direct:
            at = pl.ds(group, length, stride=groups)
        else:
            first = (group // columns_each) * (length * columns_each) + group % columns_each
            at = pl.ds(first, length, stride=columns_each)
        plane_scr[rows, :] = get_tiles(seq_scr, at)


def mixed_kernel(sizes, row_ref, hidden_ref, heads_ref, output_ref, *refs):
    dates_each, row_parts, rows_each, columns_each, direct = sizes
    *mixed_refs, seq_scr, plane_scr = refs
    length = row_parts * rows_each
    groups = dates_each * columns_each
    part_rows = rows_each * groups
    load_planes(sizes, row_ref, hidden_ref, seq_scr, plane_scr)
    mixed = plane_scr[...] + matmul(heads_ref[...], output_ref[...])
    for group in range(groups):
        inner = (group // columns_each) * (rows_each * columns_each) + group % columns_each
        for part in range(row_parts):
            begin = group * length + part * rows_each
            put_tiles(
                seq_scr,
                pl.ds(part * part_rows + inner, rows_each, stride=columns_each),
                mixed[begin : begin + rows_each],
            )
    if direct:
        kept_ref, sent_ref = mixed_refs
        kept_ref[...] = get_tiles(seq_scr, slice(0, part_rows)).astype(low)
        sent_ref[...] = get_tiles(seq_scr, slice(part_rows, 2 * part_rows)).astype(low)
    else:
        mixed_refs[0][...] = get_tiles(seq_scr, slice(None)).astype(low)


def column_kernel(
    sizes,
    row_ref,
    pair_ref,
    hidden_ref,
    grad_low_scr,
    heads_grad_scr,
    project_ref,
    heads_scr,
    first_grad_ref,
    second_grad_ref,
    seq_scr,
    plane_scr,
    normed_scr,
    qkv_scr,
    qkv_grad_scr,
):
    dates_each, row_parts, rows_each, columns_each, direct, head_count, packed, date_size = sizes
    width = hidden_ref.shape[1]
    head_size = width // head_count
    lanes = packed * head_size
    length = row_parts * rows_each
    groups = dates_each * columns_each
    inverse_root = 1.0 / math.sqrt(head_size)
    load_planes(sizes[:5], row_ref, hidden_ref, seq_scr, plane_scr)
    normed_scr[...] = rms_norm(plane_scr[...])
    qkv_scr[...] = matmul(normed_scr[...], project_ref[...]).astype(low)
    mask = block_mask(length, packed, head_size)
    for units in batches(groups, head_count // packed, units_each):
        places = []
        for group, part in units:
            start = part * lanes
            places.append(
                (
                    slice(group * length, (group + 1) * length),
                    slice(start, start + lanes),
                    slice(width + start, width + start + lanes),
                    slice(2 * width + start, 2 * width + start + lanes),
                )
            )
        all_scores = []
        for rows, at_query, at_key, at_value in places:
            query = spread(qkv_scr[rows, at_query], mask, packed)
            heads_grad = spread(heads_grad_scr[rows, at_query], mask, packed)
            all_scores.append(
                (
                    contract_last(qkv_scr[rows, at_key], query),
                    contract_last(qkv_scr[rows, at_value], heads_grad),
                )
            )
        all_weights = []
        for scores, product_grad in all_scores:
            weights = softmax_first(scores * inverse_root)
            score_grad = weights * (
                product_grad - jnp.sum(weights * product_grad, axis=0, keepdims=True)
            )
            all_weights.append((weights.astype(low), score_grad.astype(low)))
        all_full = []
        for (rows, at_query, at_key, at_value), (weights, score_low) in zip(places, all_weights):
            all_full.append(
                (
                    contract_rows(weights, qkv_scr[rows, at_value]),
                    contract_rows(score_low, qkv_scr[rows, at_key]),
                )
            )
            query = spread(qkv_scr[rows, at_query], mask, packed)
            heads_grad = spread(heads_grad_scr[rows, at_query], mask, packed)
            key_grad = matmul(score_low, query) * inverse_root
            qkv_grad_scr[rows, at_key] = key_grad.astype(low)
            qkv_grad_scr[rows, at_value] = matmul(weights, heads_grad).astype(low)
        for (rows, at_query, _, _), (heads_full, query_full) in zip(places, all_full):
            heads = own_blocks(heads_full, length, packed, head_size)
            heads_scr[rows, at_query] = heads.astype(low)
            query_grad = own_blocks(query_full, length, packed, head_size) * inverse_root
            qkv_grad_scr[rows, at_query] = query_grad.astype(low)
    project_grad = contract_rows(qkv_grad_scr[...], normed_scr[...])
    output_grad = contract_rows(grad_low_scr[...], heads_scr[...])
    if not direct:
        first_grad_ref[...] = project_grad
        second_grad_ref[...] = output_grad
        return
    keep_ref, send_ref = first_grad_ref, second_grad_ref
    even = pair_ref[0] == 0
    project_each = project_grad.shape[0] // date_size
    output_each = output_grad.shape[0] // date_size
    half = (project_each + output_each) // 2
    lower = lax.broadcasted_iota(jnp.int32, (half, 128), 1) < 64
    for outer in range(date_size // 2):
        pair = []
        for part in (2 * outer, 2 * outer + 1):
            block = jnp.concatenate(
                [
                    project_grad[part * project_each : (part + 1) * project_each],
                    output_grad[part * output_each : (part + 1) * output_each],
                ],
                axis=0,
            )
            top, bottom = block[:half, 128:256], block[half:, 128:256]
            pair.append(
                (
                    (block[:, :128], jnp.where(lower, top, pltpu.roll(bottom, 64, 1))),
                    (block[:, 256:], jnp.where(lower, pltpu.roll(top, 64, 1), bottom)),
                )
            )
        for row_part in range(2):
            for first, one, two in zip((0, 2 * half), pair[0][row_part], pair[1][row_part]):
                place = (row_part, outer, slice(first, first + one.shape[0]))
                keep_ref[place] = jnp.where(even, one, two).astype(low)
                send_ref[place] = jnp.where(even, two, one).astype(low)


def pair_kernel(
    row_ref, mid_ref, kept_ref, came_ref, own_ref, mid_out, row_out, both_out, handed_ref
):
    handed_ref[0] = row_ref[0]
    row, mid = row_ref[0], mid_ref[0]
    for outer in range(own_ref.shape[0]):
        for out_ref, row_at, mid_at in (
            (mid_out, row, 1 - mid),
            (row_out, 1 - row, mid),
            (both_out, 1 - row, 1 - mid),
            (own_ref, row, mid),
        ):
            place = (row_at, 2 * outer + mid_at)
            out_ref[outer] = (kept_ref[place].astype(wide) + came_ref[place].astype(wide)).astype(
                low
            )


def spread_kernel(outer_ref, own_ref, mid_ref, row_ref, both_ref, *refs):
    count = own_ref.shape[0]
    for step in range(count):
        at = (outer_ref[0] + step) % count
        total = own_ref[at].astype(wide) + mid_ref[at].astype(wide)
        total = total + (row_ref[at].astype(wide) + both_ref[at].astype(wide))
        refs[step][...] = total.astype(low)


def finish_kernel(project_each, row_ref, *refs):
    *terms, project_ref, output_ref = refs
    total = terms[0][...].astype(wide)
    for term in terms[1:]:
        total = total + term[...].astype(wide)
    whole = 2 * total.shape[0] // 3
    main = total[:whole]
    tail = total[whole:]
    swapped = pltpu.roll(tail, 64, 1)
    lower = lax.broadcasted_iota(jnp.int32, (whole, 128), 1) < 64
    tail_first = jnp.concatenate([tail, swapped], axis=0)
    turned = pltpu.roll(main, 64, 1)
    front = jnp.concatenate([main, tail_first[:, :64]], axis=1)
    back = jnp.concatenate([jnp.where(lower, tail_first, turned), turned[:, :64]], axis=1)
    owned = jnp.where(row_ref[0] == 0, front, back)
    project_ref[...] = owned[:project_each]
    output_ref[...] = owned[project_each:]


def body(
    row_size,
    date_size,
    tokens,
    clear_flags,
    date_numbers,
    decay_slopes,
    time_project,
    time_output,
    column_project,
    column_output,
    cotangent,
):
    date_local, row_local, column_count, width = tokens.shape
    head_count = decay_slopes.shape[0]
    head_size = width // head_count
    packed = max(1, 128 // head_size)
    local_patches = row_local * column_count
    patches_each = local_patches // date_size
    columns_each = column_count // row_size
    row_count = row_local * row_size
    date_count = date_local * date_size
    project_each = 3 * width // date_size
    output_each = width // date_size
    lane_each = width // row_size
    direct = (
        patches_each == column_count
        and column_count % 16 == 0
        and date_size % 8 == 0
        and row_size == 2
        and lane_each == 192
        and project_each % 8 == 0
        and output_each % 8 == 0
        and (project_each + output_each) % 32 == 0
    )
    token_rows = date_local * patches_each
    block_rows = -(-(token_rows + date_local) // 8) * 8
    tile_rows = (width // 128) * token_rows + -(-date_local // 8) * 8
    params = pltpu.CompilerParams(vmem_limit_bytes=vmem_limit)
    in_vmem = pl.BlockSpec(memory_space=pltpu.VMEM)
    in_smem = pl.BlockSpec(memory_space=pltpu.SMEM)
    swap = [(0, 1), (1, 0)]
    column_tokens = date_local * row_count * columns_each
    half_tokens = column_tokens // row_size
    if direct:
        outgoing = pl.pallas_call(
            pack_kernel,
            out_shape=jax.ShapeDtypeStruct((date_size, tile_rows, 128), low),
            in_specs=[pl.BlockSpec(memory_space=pltpu.HBM)] * 3,
            scratch_shapes=[
                pltpu.SMEM(date_numbers.shape, jnp.int32),
                pltpu.VMEM(tokens.shape, low),
                pltpu.VMEM(clear_flags.shape, jnp.int32),
                pltpu.SemaphoreType.DMA((3,)),
            ],
            name="pack_tokens",
        )(date_numbers, tokens, clear_flags)
        row_at = lax.axis_index("row")
        halves = cotangent.reshape(date_local, row_local, row_size, columns_each, width)
        leaving = lax.dynamic_index_in_dim(halves, 1 - row_at, 2, keepdims=False)
        other_grad = lax.ppermute(leaving, "row", swap)
    else:
        flags = jnp.transpose(
            clear_flags.reshape(date_local, date_size, patches_each), (1, 0, 2)
        ).astype(low)
        numbers = jnp.stack([date_numbers // 32, date_numbers % 32], axis=-1).astype(low)
        numbers = jnp.broadcast_to(numbers[None], (date_size, date_local, 2))
        info = jnp.concatenate([flags, numbers], axis=-1)
        info = jnp.pad(
            info, ((0, 0), (0, block_rows - token_rows - date_local), (0, width - patches_each - 2))
        )
        outgoing = jnp.transpose(
            tokens.reshape(date_local, date_size, patches_each, width), (1, 0, 2, 3)
        ).reshape(date_size, token_rows, width)
        outgoing = jnp.concatenate([outgoing, info], axis=1)
    incoming = lax.all_to_all(outgoing, dates, split_axis=0, concat_axis=0, tiled=True)

    if direct:
        grads_in = (
            row_at.reshape(1),
            cotangent.reshape(local_patches * date_local, width),
            other_grad.reshape(half_tokens, width),
        )
        in_specs = [in_smem] + [in_vmem] * 3 + [in_smem]
    else:
        grads_in = (
            lax.all_to_all(cotangent, "row", split_axis=2, concat_axis=1, tiled=True).reshape(
                column_tokens, width
            ),
        )
        in_specs = [in_vmem] * 2 + [in_smem]
    time_tokens = date_count * patches_each
    hidden, after_time = pl.pallas_call(
        functools.partial(
            time_kernel,
            (
                date_size,
                date_local,
                patches_each,
                head_count,
                packed,
                columns_each if direct else patches_each,
            ),
        ),
        out_shape=(
            jax.ShapeDtypeStruct((time_tokens, width), low),
            jax.ShapeDtypeStruct((1,), jnp.int32),
        ),
        in_specs=[in_smem, in_vmem, in_vmem, in_vmem, pl.BlockSpec(memory_space=pl.ANY)],
        out_specs=(in_vmem, in_smem),
        scratch_shapes=[
            pltpu.VMEM((width // 128, time_tokens, 128), wide),
            pltpu.VMEM((time_tokens, width), wide),
            pltpu.VMEM((time_tokens, 3 * width), low),
            pltpu.VMEM((time_tokens, width), low),
        ],
        compiler_params=params,
        name="time_attention",
    )(decay_slopes, incoming, time_project, time_output, grads_in[-1])

    grad_low, heads_grad = pl.pallas_call(
        functools.partial(
            cotangent_kernel, (date_local, row_size, row_local, columns_each, direct)
        ),
        out_shape=(
            jax.ShapeDtypeStruct((column_tokens, width), low),
            jax.ShapeDtypeStruct((column_tokens, width), low),
        ),
        in_specs=in_specs,
        scratch_shapes=[pltpu.VMEM((width // 128, column_tokens, 128), wide)],
        name="cotangent_heads",
    )(*grads_in, column_output, after_time)

    if direct:
        parts = hidden.reshape(row_size * date_size, date_local * columns_each, width)
        plane = lax.all_to_all(parts, ("row", *dates), split_axis=0, concat_axis=0, tiled=True)
    else:
        parts = hidden.reshape(date_size, date_local, patches_each, width)
        back = lax.all_to_all(parts, dates, split_axis=0, concat_axis=0, tiled=True)
        back = jnp.transpose(back, (1, 0, 2, 3)).reshape(
            date_local, row_local, column_count, width
        )
        plane = lax.all_to_all(back, "row", split_axis=2, concat_axis=1, tiled=True)
    plane = plane.reshape(column_tokens, width)
    half_shape = jax.ShapeDtypeStruct((half_tokens, width), low)
    packed_rows = (project_each + output_each) * 3 // 2
    row_one = lax.axis_index("row").reshape(1)
    pair_one = lax.axis_index("pair").reshape(1)
    sizes = (date_local, row_size, row_local, columns_each, direct)
    if direct:
        half_grads = jax.ShapeDtypeStruct((row_size, date_size // 2, packed_rows, 128), low)
        grad_shapes = (half_grads, half_grads)
        mixed_shapes = (half_shape, half_shape)
    else:
        grad_shapes = (
            jax.ShapeDtypeStruct((3 * width, width), wide),
            jax.ShapeDtypeStruct((width, width), wide),
        )
        mixed_shapes = (jax.ShapeDtypeStruct((column_tokens, width), low),)
    column_heads, first_grad, second_grad = pl.pallas_call(
        functools.partial(column_kernel, (*sizes, head_count, packed, date_size)),
        out_shape=(jax.ShapeDtypeStruct((column_tokens, width), low), *grad_shapes),
        in_specs=[in_smem] * 2 + [in_vmem] * 4,
        scratch_shapes=[
            pltpu.VMEM((width // 128, column_tokens, 128), wide),
            pltpu.VMEM((column_tokens, width), wide),
            pltpu.VMEM((column_tokens, width), low),
            pltpu.VMEM((column_tokens, 3 * width), low),
            pltpu.VMEM((column_tokens, 3 * width), low),
        ],
        compiler_params=params,
        name="column_attention",
    )(row_one, pair_one, plane, grad_low, heads_grad, column_project)
    after_one = row_one
    if direct:
        came = lax.ppermute(second_grad, "pair", swap)
        outers = date_size // 4
        block = jax.ShapeDtypeStruct((packed_rows, 128), low)
        blocks = jax.ShapeDtypeStruct((outers, packed_rows, 128), low)
        own_grad, mid_grad, row_grad, both_grad, after_one = pl.pallas_call(
            pair_kernel,
            out_shape=(blocks,) * 4 + (jax.ShapeDtypeStruct((1,), jnp.int32),),
            in_specs=[in_smem] * 2 + [in_vmem] * 2,
            out_specs=(in_vmem,) * 4 + (in_smem,),
            compiler_params=params,
            name="pair_gradients",
        )(row_one, lax.axis_index("mid").reshape(1), first_grad, came)
        both_grad = lax.ppermute(both_grad, ("mid", "row"), [(0, 3), (3, 0), (1, 2), (2, 1)])
        mid_grad = lax.ppermute(mid_grad, "mid", swap)
        row_grad = lax.ppermute(row_grad, "row", swap)
    mixed = pl.pallas_call(
        functools.partial(mixed_kernel, sizes),
        out_shape=mixed_shapes,
        in_specs=[in_smem] + [in_vmem] * 3,
        scratch_shapes=[
            pltpu.VMEM((width // 128, column_tokens, 128), wide),
            pltpu.VMEM((column_tokens, width), wide),
        ],
        compiler_params=params,
        name="mixed_tokens",
    )(after_one, plane, column_heads, column_output)

    if direct:
        steps = pl.pallas_call(
            spread_kernel,
            out_shape=(block,) * outers,
            in_specs=[in_smem] + [in_vmem] * 4,
            compiler_params=params,
            name="spread_gradients",
        )(lax.axis_index("outer").reshape(1), own_grad, mid_grad, row_grad, both_grad)
        terms = [steps[0]]
        for step in range(1, outers):
            route = [(at, (at + step) % outers) for at in range(outers)]
            terms.append(lax.ppermute(steps[step], "outer", route))
        owned_project, owned_output = pl.pallas_call(
            functools.partial(finish_kernel, project_each),
            out_shape=(
                jax.ShapeDtypeStruct((project_each, lane_each), wide),
                jax.ShapeDtypeStruct((output_each, lane_each), wide),
            ),
            in_specs=[in_smem] + [in_vmem] * outers,
            compiler_params=params,
            name="gradient_sum",
        )(row_one, *terms)
        kept, sent = mixed
        arrived = lax.ppermute(sent, "row", swap)
        quarter = (date_local, row_local, 1, columns_each, width)
        kept, arrived = kept.reshape(quarter), arrived.reshape(quarter)
        mixed = jnp.concatenate(
            [jnp.where(row_at == 0, kept, arrived), jnp.where(row_at == 0, arrived, kept)], axis=2
        )
    else:
        mixed = mixed[0]
        grads = jnp.concatenate(
            [
                first_grad.reshape(date_size, project_each, row_size, lane_each),
                second_grad.reshape(date_size, output_each, row_size, lane_each),
            ],
            axis=1,
        ).astype(low)
        grads = jnp.transpose(grads, (2, 0, 1, 3)).reshape(
            row_size * date_size, project_each + output_each, lane_each
        )
        terms = lax.all_to_all(grads, ("row", *dates), split_axis=0, concat_axis=0, tiled=True)
        owned = jnp.sum(terms.astype(wide), axis=0)
        owned_project, owned_output = owned[:project_each], owned[project_each:]
        mixed = mixed.reshape(row_size, date_local, row_local, columns_each, width)
        mixed = lax.all_to_all(mixed, "row", split_axis=0, concat_axis=0, tiled=True)
        mixed = jnp.transpose(mixed, (1, 2, 0, 3, 4))
    mixed = mixed.reshape(date_local, row_local, column_count, width)
    return (mixed, jnp.transpose(owned_project), jnp.transpose(owned_output))


def solution(mesh):
    date_size, row_size = mesh.shape["date"], mesh.shape["row"]
    pair_size = 2 if date_size % 2 == 0 else 1
    mid_size = 2 if date_size % 4 == 0 else 1
    split = jax.sharding.Mesh(
        mesh.devices.reshape(-1, mid_size, pair_size, row_size), ("outer", "mid", "pair", "row")
    )
    return jax.shard_map(
        functools.partial(body, row_size, date_size),
        mesh=split,
        in_specs=(
            P(dates, "row", None, None),
            P(dates, "row", None),
            P(dates),
            P(),
            P(),
            P(),
            P(),
            P(),
            P(dates, "row", None, None),
        ),
        out_specs=(P(dates, "row", None, None), P("row", dates), P("row", dates)),
        check_vma=False,
    )
```

```python
import functools
import math

import jax
import jax.numpy as jnp
from jax import lax
from jax.experimental import pallas as pl
from jax.experimental.pallas import tpu as pltpu
from jax.sharding import PartitionSpec as P

epsilon = 1e-06
masked_score = -1e30
units_each = 24
dates = ("outer", "mid", "pair")
vmem_limit = 24 * 1024 * 1024
low = jnp.bfloat16
wide = jnp.float32


def rms_norm(values):
    factor = lax.rsqrt(jnp.mean(values * values, axis=-1, keepdims=True) + epsilon)
    return (values * factor).astype(low)


def matmul(left, right):
    return jnp.dot(left, right, preferred_element_type=wide)


def contract_rows(left, right):
    return lax.dot_general(left, right, (((0,), (0,)), ((), ())), preferred_element_type=wide)


def contract_last(left, right):
    return lax.dot_general(left, right, (((1,), (1,)), ((), ())), preferred_element_type=wide)


def block_mask(length, packed, head_size):
    shape = (packed * length, packed * head_size)
    rows = lax.broadcasted_iota(jnp.int32, shape, 0) // length
    lanes = lax.broadcasted_iota(jnp.int32, shape, 1) // head_size
    return jnp.where(rows == lanes, 1.0, 0.0).astype(low)


def spread(values, mask, packed):
    return jnp.concatenate([values] * packed, axis=0) * mask


def batches(groups, parts, each):
    units = [(group, part) for group in range(groups) for part in range(parts)]
    return [units[first : first + each] for first in range(0, len(units), each)]


def own_blocks(full, length, packed, head_size):
    lanes = lax.broadcasted_iota(jnp.int32, (length, packed * head_size), 1) // head_size
    out = full[:length]
    for head in range(1, packed):
        out = jnp.where(lanes == head, full[head * length : (head + 1) * length], out)
    return out


def softmax_first(scores):
    raised = jnp.exp(scores - jnp.max(scores, axis=0, keepdims=True))
    return raised * (1.0 / jnp.sum(raised, axis=0, keepdims=True))


def put_tiles(scratch, rows, values):
    tiles, _, lanes = scratch.shape
    for tile in range(tiles):
        scratch[tile, rows, :] = values[:, tile * lanes : (tile + 1) * lanes]


def get_tiles(scratch, rows):
    return jnp.concatenate([scratch[tile, rows, :] for tile in range(scratch.shape[0])], axis=-1)


def pack_kernel(
    numbers_ref, tokens_ref, flags_ref, out_ref, numbers_scr, tokens_scr, flags_scr, copied
):
    copies = [
        pltpu.make_async_copy(tokens_ref, tokens_scr, copied.at[0]),
        pltpu.make_async_copy(flags_ref, flags_scr, copied.at[1]),
        pltpu.make_async_copy(numbers_ref, numbers_scr, copied.at[2]),
    ]
    for copy in copies:
        copy.start()
    dates_each, parts, patches, width = tokens_ref.shape
    lanes = out_ref.shape[2]
    tiles = width // lanes
    spare = out_ref.shape[1] - tiles * dates_each * patches
    place = lax.broadcasted_iota(jnp.int32, (patches, lanes), 0)
    lane = lax.broadcasted_iota(jnp.int32, (patches, lanes), 1)
    place = jnp.where(place == lane, 1.0, 0.0).astype(low)
    lane = lax.broadcasted_iota(jnp.int32, (parts, lanes), 1)
    row = lax.broadcasted_iota(jnp.int32, (spare, lanes), 0)
    copies[1].wait()
    copies[2].wait()
    infos = []
    for date in range(dates_each):
        number = numbers_scr[date]
        upper = (number // 32).astype(wide)
        under = (number % 32).astype(wide)
        info = matmul(flags_scr[date].astype(wide).astype(low), place)
        info = jnp.where(lane == patches, upper, info)
        infos.append(jnp.where(lane == patches + 1, under, info))
    copies[0].wait()
    for part in range(parts):
        tokens = jnp.concatenate(
            [tokens_scr[date, part].astype(wide) for date in range(dates_each)], axis=0
        )
        extra = jnp.zeros((spare, lanes), wide)
        for date in range(dates_each):
            extra = jnp.where(row == date, infos[date][part : part + 1], extra)
        pieces = [tokens[:, tile * lanes : (tile + 1) * lanes] for tile in range(tiles)]
        out_ref[part] = jnp.concatenate(pieces + [extra], axis=0).astype(low)


def time_kernel(
    sizes,
    slopes_ref,
    block_ref,
    project_ref,
    output_ref,
    earlier_ref,
    out_ref,
    after_ref,
    seq_scr,
    token_scr,
    qkv_scr,
    heads_scr,
):
    after_ref[0] = jnp.int32(0)
    sources, dates_each, groups, head_count, packed, columns_each = sizes
    width = project_ref.shape[0]
    tile_lanes = block_ref.shape[2]
    tiles = width // tile_lanes
    head_size = width // head_count
    lanes = packed * head_size
    length = sources * dates_each
    token_rows = dates_each * groups
    inverse_root = 1.0 / math.sqrt(head_size)
    info = []
    for source in range(sources):
        plane = block_ref[source].astype(wide)
        rows = slice(source * token_rows, (source + 1) * token_rows)
        for tile in range(tiles):
            at = slice(tile * token_rows, (tile + 1) * token_rows)
            if tiles == 1:
                put_tiles(seq_scr, rows, plane[at])
            else:
                seq_scr[tile, rows, :] = plane[at]
        info.append(plane[tiles * token_rows : tiles * token_rows + dates_each])
    info = jnp.concatenate(info, axis=0)
    for group in range(groups):
        token_scr[group * length : (group + 1) * length, :] = get_tiles(
            seq_scr, pl.ds(group, length, stride=groups)
        )
    tokens = token_scr[...]
    qkv_scr[...] = matmul(rms_norm(tokens), project_ref[...]).astype(low)
    numbers = info[:, groups : groups + 1] * 32.0 + info[:, groups + 1 : groups + 2]
    key_at = lax.broadcasted_iota(jnp.int32, (length, packed * length), 0)
    column_at = lax.broadcasted_iota(jnp.int32, (length, packed * length), 1)
    same_date = key_at == column_at % length
    query_numbers = jnp.sum(jnp.where(same_date, numbers, 0.0), axis=0, keepdims=True)
    gap_days = jnp.abs(numbers - query_numbers)
    head_at = column_at // length
    mask = block_mask(length, packed, head_size)
    biases = []
    for first in range(0, head_count, packed):
        slope = jnp.full((length, packed * length), slopes_ref[first], wide)
        for head in range(1, packed):
            slope = jnp.where(head_at == head, slopes_ref[first + head], slope)
        biases.append(-slope * gap_days)
    for units in batches(groups, head_count // packed, units_each):
        all_scores = []
        for group, part in units:
            rows = slice(group * length, (group + 1) * length)
            start = part * lanes
            query = qkv_scr[rows, start : start + lanes]
            key = qkv_scr[rows, width + start : width + start + lanes]
            all_scores.append(contract_last(key, spread(query, mask, packed)))
        all_weights = []
        for (group, part), scores in zip(units, all_scores):
            allowed = (info[:, group : group + 1] > 0) | same_date
            scores = jnp.where(allowed, scores * inverse_root + biases[part], masked_score)
            all_weights.append(softmax_first(scores).astype(low))
        all_heads = []
        for (group, part), weights in zip(units, all_weights):
            rows = slice(group * length, (group + 1) * length)
            start = 2 * width + part * lanes
            all_heads.append(contract_rows(weights, qkv_scr[rows, start : start + lanes]))
        for (group, part), full in zip(units, all_heads):
            rows = slice(group * length, (group + 1) * length)
            heads_scr[rows, part * lanes : (part + 1) * lanes] = own_blocks(
                full, length, packed, head_size
            ).astype(low)
    hidden = token_scr[...] + matmul(heads_scr[...], output_ref[...])
    for group in range(groups):
        first = (group // columns_each) * (length * columns_each) + group % columns_each
        put_tiles(
            seq_scr,
            pl.ds(first, length, stride=columns_each),
            hidden[group * length : (group + 1) * length],
        )
    out_ref[...] = get_tiles(seq_scr, slice(None)).astype(low)


def cotangent_kernel(sizes, *refs):
    dates_each, row_parts, rows_each, columns_each, direct = sizes
    output_ref, _, grad_low_ref, heads_grad_ref, grad_scr = refs[-5:]
    width = output_ref.shape[0]
    length = row_parts * rows_each
    groups = dates_each * columns_each
    part_rows = rows_each * groups
    if direct:
        row_ref, own_ref, other_ref = refs[:3]
        own = own_ref[...].astype(wide)
        own = own.reshape(dates_each * rows_each, row_parts, columns_each, width)
        own = jnp.where(row_ref[0] == 0, own[:, 0], own[:, 1]).reshape(part_rows, width)
        put_tiles(grad_scr, slice(0, part_rows), own)
        put_tiles(grad_scr, slice(part_rows, 2 * part_rows), other_ref[...].astype(wide))
    else:
        put_tiles(grad_scr, slice(None), refs[0][...].astype(wide))
    for group in range(groups):
        if direct:
            inner = (group // columns_each) * (rows_each * columns_each) + group % columns_each
            pieces = [
                get_tiles(
                    grad_scr, pl.ds(part * part_rows + inner, rows_each, stride=columns_each)
                )
                for part in range(row_parts)
            ]
            values = jnp.concatenate(pieces, axis=0)
        else:
            first = (group // columns_each) * (length * columns_each) + group % columns_each
            values = get_tiles(grad_scr, pl.ds(first, length, stride=columns_each))
        grad_low_ref[group * length : (group + 1) * length, :] = values.astype(low)
    heads_grad_ref[...] = contract_last(grad_low_ref[...], output_ref[...]).astype(low)


def load_planes(sizes, row_ref, hidden_ref, seq_scr, plane_scr):
    dates_each, row_parts, rows_each, columns_each, direct = sizes
    length = row_parts * rows_each
    groups = dates_each * columns_each
    part_rows = rows_each * groups
    if direct:
        for part in range(row_parts):
            source = pl.multiple_of(((row_ref[0] + part) % row_parts) * part_rows, part_rows)
            put_tiles(
                seq_scr,
                slice(part * part_rows, (part + 1) * part_rows),
                hidden_ref[pl.ds(source, part_rows), :].astype(wide),
            )
    else:
        put_tiles(seq_scr, slice(None), hidden_ref[...].astype(wide))
    for group in range(groups):
        rows = slice(group * length, (group + 1) * length)
        if direct:
            at = pl.ds(group, length, stride=groups)
        else:
            first = (group // columns_each) * (length * columns_each) + group % columns_each
            at = pl.ds(first, length, stride=columns_each)
        plane_scr[rows, :] = get_tiles(seq_scr, at)


def mixed_kernel(sizes, row_ref, hidden_ref, heads_ref, output_ref, *refs):
    dates_each, row_parts, rows_each, columns_each, direct = sizes
    *mixed_refs, seq_scr, plane_scr = refs
    length = row_parts * rows_each
    groups = dates_each * columns_each
    part_rows = rows_each * groups
    load_planes(sizes, row_ref, hidden_ref, seq_scr, plane_scr)
    mixed = plane_scr[...] + matmul(heads_ref[...], output_ref[...])
    for group in range(groups):
        inner = (group // columns_each) * (rows_each * columns_each) + group % columns_each
        for part in range(row_parts):
            begin = group * length + part * rows_each
            put_tiles(
                seq_scr,
                pl.ds(part * part_rows + inner, rows_each, stride=columns_each),
                mixed[begin : begin + rows_each],
            )
    if direct:
        kept_ref, sent_ref = mixed_refs
        kept_ref[...] = get_tiles(seq_scr, slice(0, part_rows)).astype(low)
        sent_ref[...] = get_tiles(seq_scr, slice(part_rows, 2 * part_rows)).astype(low)
    else:
        mixed_refs[0][...] = get_tiles(seq_scr, slice(None)).astype(low)


def column_kernel(
    sizes,
    row_ref,
    pair_ref,
    hidden_ref,
    grad_low_scr,
    heads_grad_scr,
    project_ref,
    heads_scr,
    first_grad_ref,
    second_grad_ref,
    seq_scr,
    plane_scr,
    normed_scr,
    qkv_scr,
    qkv_grad_scr,
):
    dates_each, row_parts, rows_each, columns_each, direct, head_count, packed, date_size = sizes
    width = hidden_ref.shape[1]
    head_size = width // head_count
    lanes = packed * head_size
    length = row_parts * rows_each
    groups = dates_each * columns_each
    inverse_root = 1.0 / math.sqrt(head_size)
    load_planes(sizes[:5], row_ref, hidden_ref, seq_scr, plane_scr)
    normed_scr[...] = rms_norm(plane_scr[...])
    qkv_scr[...] = matmul(normed_scr[...], project_ref[...]).astype(low)
    mask = block_mask(length, packed, head_size)
    for units in batches(groups, head_count // packed, units_each):
        places = []
        for group, part in units:
            start = part * lanes
            places.append(
                (
                    slice(group * length, (group + 1) * length),
                    slice(start, start + lanes),
                    slice(width + start, width + start + lanes),
                    slice(2 * width + start, 2 * width + start + lanes),
                )
            )
        all_scores = []
        for rows, at_query, at_key, at_value in places:
            query = spread(qkv_scr[rows, at_query], mask, packed)
            heads_grad = spread(heads_grad_scr[rows, at_query], mask, packed)
            all_scores.append(
                (
                    contract_last(qkv_scr[rows, at_key], query),
                    contract_last(qkv_scr[rows, at_value], heads_grad),
                )
            )
        all_weights = []
        for scores, product_grad in all_scores:
            weights = softmax_first(scores * inverse_root)
            score_grad = weights * (
                product_grad - jnp.sum(weights * product_grad, axis=0, keepdims=True)
            )
            all_weights.append((weights.astype(low), score_grad.astype(low)))
        all_full = []
        for (rows, at_query, at_key, at_value), (weights, score_low) in zip(places, all_weights):
            all_full.append(
                (
                    contract_rows(weights, qkv_scr[rows, at_value]),
                    contract_rows(score_low, qkv_scr[rows, at_key]),
                )
            )
            query = spread(qkv_scr[rows, at_query], mask, packed)
            heads_grad = spread(heads_grad_scr[rows, at_query], mask, packed)
            key_grad = matmul(score_low, query) * inverse_root
            qkv_grad_scr[rows, at_key] = key_grad.astype(low)
            qkv_grad_scr[rows, at_value] = matmul(weights, heads_grad).astype(low)
        for (rows, at_query, _, _), (heads_full, query_full) in zip(places, all_full):
            heads = own_blocks(heads_full, length, packed, head_size)
            heads_scr[rows, at_query] = heads.astype(low)
            query_grad = own_blocks(query_full, length, packed, head_size) * inverse_root
            qkv_grad_scr[rows, at_query] = query_grad.astype(low)
    project_grad = contract_rows(qkv_grad_scr[...], normed_scr[...])
    output_grad = contract_rows(grad_low_scr[...], heads_scr[...])
    if not direct:
        first_grad_ref[...] = project_grad
        second_grad_ref[...] = output_grad
        return
    keep_ref, send_ref = first_grad_ref, second_grad_ref
    even = pair_ref[0] == 0
    project_each = project_grad.shape[0] // date_size
    output_each = output_grad.shape[0] // date_size
    half = (project_each + output_each) // 2
    lower = lax.broadcasted_iota(jnp.int32, (half, 128), 1) < 64
    for outer in range(date_size // 2):
        pair = []
        for part in (2 * outer, 2 * outer + 1):
            block = jnp.concatenate(
                [
                    project_grad[part * project_each : (part + 1) * project_each],
                    output_grad[part * output_each : (part + 1) * output_each],
                ],
                axis=0,
            )
            top, bottom = block[:half, 128:256], block[half:, 128:256]
            pair.append(
                (
                    (block[:, :128], jnp.where(lower, top, pltpu.roll(bottom, 64, 1))),
                    (block[:, 256:], jnp.where(lower, pltpu.roll(top, 64, 1), bottom)),
                )
            )
        for row_part in range(2):
            for first, one, two in zip((0, 2 * half), pair[0][row_part], pair[1][row_part]):
                place = (row_part, outer, slice(first, first + one.shape[0]))
                keep_ref[place] = jnp.where(even, one, two).astype(low)
                send_ref[place] = jnp.where(even, two, one).astype(low)


def pair_kernel(
    row_ref, mid_ref, kept_ref, came_ref, own_ref, mid_out, row_out, both_out, handed_ref
):
    handed_ref[0] = row_ref[0]
    row, mid = row_ref[0], mid_ref[0]
    for outer in range(own_ref.shape[0]):
        for out_ref, row_at, mid_at in (
            (mid_out, row, 1 - mid),
            (row_out, 1 - row, mid),
            (both_out, 1 - row, 1 - mid),
            (own_ref, row, mid),
        ):
            place = (row_at, 2 * outer + mid_at)
            out_ref[outer] = (kept_ref[place].astype(wide) + came_ref[place].astype(wide)).astype(
                low
            )


def spread_kernel(outer_ref, own_ref, mid_ref, row_ref, both_ref, sent_ref, leave_ref, *refs):
    leave_ref[...] = sent_ref[...]
    count = own_ref.shape[0]
    for step in range(count):
        at = (outer_ref[0] + step) % count
        total = own_ref[at].astype(wide) + mid_ref[at].astype(wide)
        total = total + (row_ref[at].astype(wide) + both_ref[at].astype(wide))
        refs[step][...] = total.astype(low)


def finish_kernel(project_each, row_ref, *refs):
    *terms, project_ref, output_ref = refs
    total = terms[0][...].astype(wide)
    for term in terms[1:]:
        total = total + term[...].astype(wide)
    whole = 2 * total.shape[0] // 3
    main = total[:whole]
    tail = total[whole:]
    swapped = pltpu.roll(tail, 64, 1)
    lower = lax.broadcasted_iota(jnp.int32, (whole, 128), 1) < 64
    tail_first = jnp.concatenate([tail, swapped], axis=0)
    turned = pltpu.roll(main, 64, 1)
    front = jnp.concatenate([main, tail_first[:, :64]], axis=1)
    back = jnp.concatenate([jnp.where(lower, tail_first, turned), turned[:, :64]], axis=1)
    owned = jnp.where(row_ref[0] == 0, front, back)
    project_ref[...] = owned[:project_each]
    output_ref[...] = owned[project_each:]


def body(
    row_size,
    date_size,
    tokens,
    clear_flags,
    date_numbers,
    decay_slopes,
    time_project,
    time_output,
    column_project,
    column_output,
    cotangent,
):
    date_local, row_local, column_count, width = tokens.shape
    head_count = decay_slopes.shape[0]
    head_size = width // head_count
    packed = max(1, 128 // head_size)
    local_patches = row_local * column_count
    patches_each = local_patches // date_size
    columns_each = column_count // row_size
    row_count = row_local * row_size
    date_count = date_local * date_size
    project_each = 3 * width // date_size
    output_each = width // date_size
    lane_each = width // row_size
    direct = (
        patches_each == column_count
        and column_count % 16 == 0
        and date_size % 8 == 0
        and row_size == 2
        and lane_each == 192
        and project_each % 8 == 0
        and output_each % 8 == 0
        and (project_each + output_each) % 32 == 0
    )
    token_rows = date_local * patches_each
    block_rows = -(-(token_rows + date_local) // 8) * 8
    tile_rows = (width // 128) * token_rows + -(-date_local // 8) * 8
    params = pltpu.CompilerParams(vmem_limit_bytes=vmem_limit)
    in_vmem = pl.BlockSpec(memory_space=pltpu.VMEM)
    in_smem = pl.BlockSpec(memory_space=pltpu.SMEM)
    swap = [(0, 1), (1, 0)]
    column_tokens = date_local * row_count * columns_each
    half_tokens = column_tokens // row_size
    if direct:
        outgoing = pl.pallas_call(
            pack_kernel,
            out_shape=jax.ShapeDtypeStruct((date_size, tile_rows, 128), low),
            in_specs=[pl.BlockSpec(memory_space=pltpu.HBM)] * 3,
            scratch_shapes=[
                pltpu.SMEM(date_numbers.shape, jnp.int32),
                pltpu.VMEM(tokens.shape, low),
                pltpu.VMEM(clear_flags.shape, jnp.int32),
                pltpu.SemaphoreType.DMA((3,)),
            ],
            name="pack_tokens",
        )(date_numbers, tokens, clear_flags)
        row_at = lax.axis_index("row")
        halves = cotangent.reshape(date_local, row_local, row_size, columns_each, width)
        leaving = lax.dynamic_index_in_dim(halves, 1 - row_at, 2, keepdims=False)
        other_grad = lax.ppermute(leaving, "row", swap)
    else:
        flags = jnp.transpose(
            clear_flags.reshape(date_local, date_size, patches_each), (1, 0, 2)
        ).astype(low)
        numbers = jnp.stack([date_numbers // 32, date_numbers % 32], axis=-1).astype(low)
        numbers = jnp.broadcast_to(numbers[None], (date_size, date_local, 2))
        info = jnp.concatenate([flags, numbers], axis=-1)
        info = jnp.pad(
            info, ((0, 0), (0, block_rows - token_rows - date_local), (0, width - patches_each - 2))
        )
        outgoing = jnp.transpose(
            tokens.reshape(date_local, date_size, patches_each, width), (1, 0, 2, 3)
        ).reshape(date_size, token_rows, width)
        outgoing = jnp.concatenate([outgoing, info], axis=1)
    incoming = lax.all_to_all(outgoing, dates, split_axis=0, concat_axis=0, tiled=True)

    if direct:
        grads_in = (
            row_at.reshape(1),
            cotangent.reshape(local_patches * date_local, width),
            other_grad.reshape(half_tokens, width),
        )
        in_specs = [in_smem] + [in_vmem] * 3 + [in_smem]
    else:
        grads_in = (
            lax.all_to_all(cotangent, "row", split_axis=2, concat_axis=1, tiled=True).reshape(
                column_tokens, width
            ),
        )
        in_specs = [in_vmem] * 2 + [in_smem]
    time_tokens = date_count * patches_each
    hidden, after_time = pl.pallas_call(
        functools.partial(
            time_kernel,
            (
                date_size,
                date_local,
                patches_each,
                head_count,
                packed,
                columns_each if direct else patches_each,
            ),
        ),
        out_shape=(
            jax.ShapeDtypeStruct((time_tokens, width), low),
            jax.ShapeDtypeStruct((1,), jnp.int32),
        ),
        in_specs=[in_smem, in_vmem, in_vmem, in_vmem, pl.BlockSpec(memory_space=pl.ANY)],
        out_specs=(in_vmem, in_smem),
        scratch_shapes=[
            pltpu.VMEM((width // 128, time_tokens, 128), wide),
            pltpu.VMEM((time_tokens, width), wide),
            pltpu.VMEM((time_tokens, 3 * width), low),
            pltpu.VMEM((time_tokens, width), low),
        ],
        compiler_params=params,
        name="time_attention",
    )(decay_slopes, incoming, time_project, time_output, grads_in[-1])

    grad_low, heads_grad = pl.pallas_call(
        functools.partial(
            cotangent_kernel, (date_local, row_size, row_local, columns_each, direct)
        ),
        out_shape=(
            jax.ShapeDtypeStruct((column_tokens, width), low),
            jax.ShapeDtypeStruct((column_tokens, width), low),
        ),
        in_specs=in_specs,
        scratch_shapes=[pltpu.VMEM((width // 128, column_tokens, 128), wide)],
        compiler_params=params,
        name="cotangent_heads",
    )(*grads_in, column_output, after_time)

    if direct:
        parts = hidden.reshape(row_size * date_size, date_local * columns_each, width)
        plane = lax.all_to_all(parts, ("row", *dates), split_axis=0, concat_axis=0, tiled=True)
    else:
        parts = hidden.reshape(date_size, date_local, patches_each, width)
        back = lax.all_to_all(parts, dates, split_axis=0, concat_axis=0, tiled=True)
        back = jnp.transpose(back, (1, 0, 2, 3)).reshape(
            date_local, row_local, column_count, width
        )
        plane = lax.all_to_all(back, "row", split_axis=2, concat_axis=1, tiled=True)
    plane = plane.reshape(column_tokens, width)
    half_shape = jax.ShapeDtypeStruct((half_tokens, width), low)
    packed_rows = (project_each + output_each) * 3 // 2
    row_one = lax.axis_index("row").reshape(1)
    pair_one = lax.axis_index("pair").reshape(1)
    sizes = (date_local, row_size, row_local, columns_each, direct)
    if direct:
        half_grads = jax.ShapeDtypeStruct((row_size, date_size // 2, packed_rows, 128), low)
        grad_shapes = (half_grads, half_grads)
        mixed_shapes = (half_shape, half_shape)
    else:
        grad_shapes = (
            jax.ShapeDtypeStruct((3 * width, width), wide),
            jax.ShapeDtypeStruct((width, width), wide),
        )
        mixed_shapes = (jax.ShapeDtypeStruct((column_tokens, width), low),)
    column_heads, first_grad, second_grad = pl.pallas_call(
        functools.partial(column_kernel, (*sizes, head_count, packed, date_size)),
        out_shape=(jax.ShapeDtypeStruct((column_tokens, width), low), *grad_shapes),
        in_specs=[in_smem] * 2 + [in_vmem] * 4,
        scratch_shapes=[
            pltpu.VMEM((width // 128, column_tokens, 128), wide),
            pltpu.VMEM((column_tokens, width), wide),
            pltpu.VMEM((column_tokens, width), low),
            pltpu.VMEM((column_tokens, 3 * width), low),
            pltpu.VMEM((column_tokens, 3 * width), low),
        ],
        compiler_params=params,
        name="column_attention",
    )(row_one, pair_one, plane, grad_low, heads_grad, column_project)
    after_one = row_one
    if direct:
        came = lax.ppermute(second_grad, "pair", swap)
        outers = date_size // 4
        block = jax.ShapeDtypeStruct((packed_rows, 128), low)
        blocks = jax.ShapeDtypeStruct((outers, packed_rows, 128), low)
        own_grad, mid_grad, row_grad, both_grad, after_one = pl.pallas_call(
            pair_kernel,
            out_shape=(blocks,) * 4 + (jax.ShapeDtypeStruct((1,), jnp.int32),),
            in_specs=[in_smem] * 2 + [in_vmem] * 2,
            out_specs=(in_vmem,) * 4 + (in_smem,),
            compiler_params=params,
            name="pair_gradients",
        )(row_one, lax.axis_index("mid").reshape(1), first_grad, came)
        both_grad = lax.ppermute(both_grad, ("mid", "row"), [(0, 3), (3, 0), (1, 2), (2, 1)])
        mid_grad = lax.ppermute(mid_grad, "mid", swap)
        row_grad = lax.ppermute(row_grad, "row", swap)
    mixed = pl.pallas_call(
        functools.partial(mixed_kernel, sizes),
        out_shape=mixed_shapes,
        in_specs=[in_smem] + [in_vmem] * 3,
        scratch_shapes=[
            pltpu.VMEM((width // 128, column_tokens, 128), wide),
            pltpu.VMEM((column_tokens, width), wide),
        ],
        compiler_params=params,
        name="mixed_tokens",
    )(after_one, plane, column_heads, column_output)

    if direct:
        kept, sent = mixed
        leaving, *steps = pl.pallas_call(
            spread_kernel,
            out_shape=(half_shape,) + (block,) * outers,
            in_specs=[in_smem] + [in_vmem] * 5,
            compiler_params=params,
            name="spread_gradients",
        )(lax.axis_index("outer").reshape(1), own_grad, mid_grad, row_grad, both_grad, sent)
        terms = [steps[0]]
        for step in range(1, outers):
            route = [(at, (at + step) % outers) for at in range(outers)]
            terms.append(lax.ppermute(steps[step], "outer", route))
        owned_project, owned_output = pl.pallas_call(
            functools.partial(finish_kernel, project_each),
            out_shape=(
                jax.ShapeDtypeStruct((project_each, lane_each), wide),
                jax.ShapeDtypeStruct((output_each, lane_each), wide),
            ),
            in_specs=[in_smem] + [in_vmem] * outers,
            compiler_params=params,
            name="gradient_sum",
        )(row_one, *terms)
        arrived = lax.ppermute(leaving, "row", swap)
        quarter = (date_local, row_local, 1, columns_each, width)
        kept, arrived = kept.reshape(quarter), arrived.reshape(quarter)
        mixed = jnp.concatenate(
            [jnp.where(row_at == 0, kept, arrived), jnp.where(row_at == 0, arrived, kept)], axis=2
        )
    else:
        mixed = mixed[0]
        grads = jnp.concatenate(
            [
                first_grad.reshape(date_size, project_each, row_size, lane_each),
                second_grad.reshape(date_size, output_each, row_size, lane_each),
            ],
            axis=1,
        ).astype(low)
        grads = jnp.transpose(grads, (2, 0, 1, 3)).reshape(
            row_size * date_size, project_each + output_each, lane_each
        )
        terms = lax.all_to_all(grads, ("row", *dates), split_axis=0, concat_axis=0, tiled=True)
        owned = jnp.sum(terms.astype(wide), axis=0)
        owned_project, owned_output = owned[:project_each], owned[project_each:]
        mixed = mixed.reshape(row_size, date_local, row_local, columns_each, width)
        mixed = lax.all_to_all(mixed, "row", split_axis=0, concat_axis=0, tiled=True)
        mixed = jnp.transpose(mixed, (1, 2, 0, 3, 4))
    mixed = mixed.reshape(date_local, row_local, column_count, width)
    return (mixed, jnp.transpose(owned_project), jnp.transpose(owned_output))


def solution(mesh):
    date_size, row_size = mesh.shape["date"], mesh.shape["row"]
    pair_size = 2 if date_size % 2 == 0 else 1
    mid_size = 2 if date_size % 4 == 0 else 1
    split = jax.sharding.Mesh(
        mesh.devices.reshape(-1, mid_size, pair_size, row_size), ("outer", "mid", "pair", "row")
    )
    return jax.shard_map(
        functools.partial(body, row_size, date_size),
        mesh=split,
        in_specs=(
            P(dates, "row", None, None),
            P(dates, "row", None),
            P(dates),
            P(),
            P(),
            P(),
            P(),
            P(),
            P(dates, "row", None, None),
        ),
        out_specs=(P(dates, "row", None, None), P("row", dates), P("row", dates)),
        check_vma=False,
    )
```

```python
import functools
import math

import jax
import jax.numpy as jnp
from jax import lax
from jax.experimental import pallas as pl
from jax.experimental.pallas import tpu as pltpu
from jax.sharding import PartitionSpec as P

epsilon = 1e-06
masked_score = -1e30
time_units = 48
column_units = 24
dates = ("outer", "mid", "pair")
vmem_limit = 12 * 1024 * 1024
low = jnp.bfloat16
wide = jnp.float32


def rms_norm(values):
    factor = lax.rsqrt(jnp.mean(values * values, axis=-1, keepdims=True) + epsilon)
    return (values * factor).astype(low)


def matmul(left, right):
    return jnp.dot(left, right, preferred_element_type=wide)


def contract_rows(left, right):
    return lax.dot_general(left, right, (((0,), (0,)), ((), ())), preferred_element_type=wide)


def contract_last(left, right):
    return lax.dot_general(left, right, (((1,), (1,)), ((), ())), preferred_element_type=wide)


def block_mask(length, packed, head_size):
    shape = (packed * length, packed * head_size)
    rows = lax.broadcasted_iota(jnp.int32, shape, 0) // length
    lanes = lax.broadcasted_iota(jnp.int32, shape, 1) // head_size
    return jnp.where(rows == lanes, 1.0, 0.0).astype(low)


def spread(values, mask, packed):
    return jnp.concatenate([values] * packed, axis=0) * mask


def batches(groups, parts, each):
    units = [(group, part) for group in range(groups) for part in range(parts)]
    return [units[first : first + each] for first in range(0, len(units), each)]


def own_blocks(full, length, packed, head_size):
    lanes = lax.broadcasted_iota(jnp.int32, (length, packed * head_size), 1) // head_size
    out = full[:length]
    for head in range(1, packed):
        out = jnp.where(lanes == head, full[head * length : (head + 1) * length], out)
    return out


def softmax_first(scores):
    raised = jnp.exp(scores - jnp.max(scores, axis=0, keepdims=True))
    return raised * (1.0 / jnp.sum(raised, axis=0, keepdims=True))


def put_tiles(scratch, rows, values):
    tiles, _, lanes = scratch.shape
    for tile in range(tiles):
        scratch[tile, rows, :] = values[:, tile * lanes : (tile + 1) * lanes]


def get_tiles(scratch, rows):
    return jnp.concatenate([scratch[tile, rows, :] for tile in range(scratch.shape[0])], axis=-1)


def pack_kernel(
    numbers_ref,
    tokens_ref,
    flags_ref,
    out_ref,
    numbers_scr,
    tokens_scr,
    flags_scr,
    out_scr,
    small_copied,
    came,
    left,
):
    dates_each, parts, patches, width = tokens_ref.shape
    chunks = came.shape[0]
    each = parts // chunks
    small = [
        pltpu.make_async_copy(flags_ref, flags_scr, small_copied.at[0]),
        pltpu.make_async_copy(numbers_ref, numbers_scr, small_copied.at[1]),
    ]
    arrivals, departures = [], []
    for chunk in range(chunks):
        at = pl.ds(chunk * each, each)
        arrivals.append(
            pltpu.make_async_copy(tokens_ref.at[:, at], tokens_scr.at[:, at], came.at[chunk])
        )
        departures.append(pltpu.make_async_copy(out_scr.at[at], out_ref.at[at], left.at[chunk]))
    for copy in small + arrivals:
        copy.start()
    lanes = out_ref.shape[2]
    tiles = width // lanes
    spare = out_ref.shape[1] - tiles * dates_each * patches
    place = lax.broadcasted_iota(jnp.int32, (patches, lanes), 0)
    lane = lax.broadcasted_iota(jnp.int32, (patches, lanes), 1)
    place = jnp.where(place == lane, 1.0, 0.0).astype(low)
    lane = lax.broadcasted_iota(jnp.int32, (parts, lanes), 1)
    row = lax.broadcasted_iota(jnp.int32, (spare, lanes), 0)
    for copy in small:
        copy.wait()
    infos = []
    for date in range(dates_each):
        number = numbers_scr[date]
        upper = (number // 32).astype(wide)
        under = (number % 32).astype(wide)
        info = matmul(flags_scr[date].astype(wide).astype(low), place)
        info = jnp.where(lane == patches, upper, info)
        infos.append(jnp.where(lane == patches + 1, under, info))
    for chunk in range(chunks):
        arrivals[chunk].wait()
        for part in range(chunk * each, (chunk + 1) * each):
            tokens = jnp.concatenate(
                [tokens_scr[date, part].astype(wide) for date in range(dates_each)], axis=0
            )
            extra = jnp.zeros((spare, lanes), wide)
            for date in range(dates_each):
                extra = jnp.where(row == date, infos[date][part : part + 1], extra)
            pieces = [tokens[:, tile * lanes : (tile + 1) * lanes] for tile in range(tiles)]
            out_scr[part] = jnp.concatenate(pieces + [extra], axis=0).astype(low)
        departures[chunk].start()
    for copy in departures:
        copy.wait()


def time_kernel(
    sizes,
    slopes_ref,
    block_ref,
    project_ref,
    output_ref,
    earlier_ref,
    out_ref,
    after_ref,
    seq_scr,
    token_scr,
    qkv_scr,
    heads_scr,
):
    after_ref[0] = jnp.int32(0)
    sources, dates_each, groups, head_count, packed, columns_each = sizes
    width = project_ref.shape[0]
    tile_lanes = block_ref.shape[2]
    tiles = width // tile_lanes
    head_size = width // head_count
    lanes = packed * head_size
    length = sources * dates_each
    token_rows = dates_each * groups
    inverse_root = 1.0 / math.sqrt(head_size)
    info = []
    for source in range(sources):
        plane = block_ref[source].astype(wide)
        rows = slice(source * token_rows, (source + 1) * token_rows)
        for tile in range(tiles):
            at = slice(tile * token_rows, (tile + 1) * token_rows)
            if tiles == 1:
                put_tiles(seq_scr, rows, plane[at])
            else:
                seq_scr[tile, rows, :] = plane[at]
        info.append(plane[tiles * token_rows : tiles * token_rows + dates_each])
    info = jnp.concatenate(info, axis=0)
    for group in range(groups):
        token_scr[group * length : (group + 1) * length, :] = get_tiles(
            seq_scr, pl.ds(group, length, stride=groups)
        )
    tokens = token_scr[...]
    qkv_scr[...] = matmul(rms_norm(tokens), project_ref[...]).astype(low)
    numbers = info[:, groups : groups + 1] * 32.0 + info[:, groups + 1 : groups + 2]
    key_at = lax.broadcasted_iota(jnp.int32, (length, packed * length), 0)
    column_at = lax.broadcasted_iota(jnp.int32, (length, packed * length), 1)
    same_date = key_at == column_at % length
    query_numbers = jnp.sum(jnp.where(same_date, numbers, 0.0), axis=0, keepdims=True)
    gap_days = jnp.abs(numbers - query_numbers)
    head_at = column_at // length
    mask = block_mask(length, packed, head_size)
    biases = []
    for first in range(0, head_count, packed):
        slope = jnp.full((length, packed * length), slopes_ref[first], wide)
        for head in range(1, packed):
            slope = jnp.where(head_at == head, slopes_ref[first + head], slope)
        biases.append(-slope * gap_days)
    for units in batches(groups, head_count // packed, time_units):
        all_scores = []
        for group, part in units:
            rows = slice(group * length, (group + 1) * length)
            start = part * lanes
            query = qkv_scr[rows, start : start + lanes]
            key = qkv_scr[rows, width + start : width + start + lanes]
            all_scores.append(contract_last(key, spread(query, mask, packed)))
        all_weights = []
        for (group, part), scores in zip(units, all_scores):
            allowed = (info[:, group : group + 1] > 0) | same_date
            scores = jnp.where(allowed, scores * inverse_root + biases[part], masked_score)
            all_weights.append(softmax_first(scores).astype(low))
        all_heads = []
        for (group, part), weights in zip(units, all_weights):
            rows = slice(group * length, (group + 1) * length)
            start = 2 * width + part * lanes
            all_heads.append(contract_rows(weights, qkv_scr[rows, start : start + lanes]))
        for (group, part), full in zip(units, all_heads):
            rows = slice(group * length, (group + 1) * length)
            heads_scr[rows, part * lanes : (part + 1) * lanes] = own_blocks(
                full, length, packed, head_size
            ).astype(low)
    hidden = token_scr[...] + matmul(heads_scr[...], output_ref[...])
    for group in range(groups):
        first = (group // columns_each) * (length * columns_each) + group % columns_each
        put_tiles(
            seq_scr,
            pl.ds(first, length, stride=columns_each),
            hidden[group * length : (group + 1) * length],
        )
    out_ref[...] = get_tiles(seq_scr, slice(None)).astype(low)


def cotangent_kernel(sizes, *refs):
    dates_each, row_parts, rows_each, columns_each, direct = sizes
    output_ref, _, grad_low_ref, heads_grad_ref, grad_scr = refs[-5:]
    width = output_ref.shape[0]
    length = row_parts * rows_each
    groups = dates_each * columns_each
    part_rows = rows_each * groups
    if direct:
        row_ref, own_ref, other_ref = refs[:3]
        own = own_ref[...].astype(wide)
        own = own.reshape(dates_each * rows_each, row_parts, columns_each, width)
        own = jnp.where(row_ref[0] == 0, own[:, 0], own[:, 1]).reshape(part_rows, width)
        put_tiles(grad_scr, slice(0, part_rows), own)
        put_tiles(grad_scr, slice(part_rows, 2 * part_rows), other_ref[...].astype(wide))
    else:
        put_tiles(grad_scr, slice(None), refs[0][...].astype(wide))
    for group in range(groups):
        if direct:
            inner = (group // columns_each) * (rows_each * columns_each) + group % columns_each
            pieces = [
                get_tiles(
                    grad_scr, pl.ds(part * part_rows + inner, rows_each, stride=columns_each)
                )
                for part in range(row_parts)
            ]
            values = jnp.concatenate(pieces, axis=0)
        else:
            first = (group // columns_each) * (length * columns_each) + group % columns_each
            values = get_tiles(grad_scr, pl.ds(first, length, stride=columns_each))
        grad_low_ref[group * length : (group + 1) * length, :] = values.astype(low)
    heads_grad_ref[...] = contract_last(grad_low_ref[...], output_ref[...]).astype(low)


def load_planes(sizes, row_ref, hidden_ref, seq_scr, plane_scr):
    dates_each, row_parts, rows_each, columns_each, direct = sizes
    length = row_parts * rows_each
    groups = dates_each * columns_each
    part_rows = rows_each * groups
    if direct:
        for part in range(row_parts):
            source = pl.multiple_of(((row_ref[0] + part) % row_parts) * part_rows, part_rows)
            put_tiles(
                seq_scr,
                slice(part * part_rows, (part + 1) * part_rows),
                hidden_ref[pl.ds(source, part_rows), :].astype(wide),
            )
    else:
        put_tiles(seq_scr, slice(None), hidden_ref[...].astype(wide))
    for group in range(groups):
        rows = slice(group * length, (group + 1) * length)
        if direct:
            at = pl.ds(group, length, stride=groups)
        else:
            first = (group // columns_each) * (length * columns_each) + group % columns_each
            at = pl.ds(first, length, stride=columns_each)
        plane_scr[rows, :] = get_tiles(seq_scr, at)


def mixed_kernel(sizes, row_ref, hidden_ref, heads_ref, output_ref, *refs):
    dates_each, row_parts, rows_each, columns_each, direct = sizes
    *mixed_refs, seq_scr, plane_scr = refs
    length = row_parts * rows_each
    groups = dates_each * columns_each
    part_rows = rows_each * groups
    load_planes(sizes, row_ref, hidden_ref, seq_scr, plane_scr)
    mixed = plane_scr[...] + matmul(heads_ref[...], output_ref[...])
    for group in range(groups):
        inner = (group // columns_each) * (rows_each * columns_each) + group % columns_each
        for part in range(row_parts):
            begin = group * length + part * rows_each
            put_tiles(
                seq_scr,
                pl.ds(part * part_rows + inner, rows_each, stride=columns_each),
                mixed[begin : begin + rows_each],
            )
    if direct:
        kept_ref, sent_ref = mixed_refs
        kept_ref[...] = get_tiles(seq_scr, slice(0, part_rows)).astype(low)
        sent_ref[...] = get_tiles(seq_scr, slice(part_rows, 2 * part_rows)).astype(low)
    else:
        mixed_refs[0][...] = get_tiles(seq_scr, slice(None)).astype(low)


def column_kernel(
    sizes,
    row_ref,
    pair_ref,
    hidden_ref,
    grad_low_scr,
    heads_grad_scr,
    project_ref,
    heads_scr,
    first_grad_ref,
    second_grad_ref,
    seq_scr,
    plane_scr,
    normed_scr,
    qkv_scr,
    qkv_grad_scr,
):
    dates_each, row_parts, rows_each, columns_each, direct, head_count, packed, date_size = sizes
    width = hidden_ref.shape[1]
    head_size = width // head_count
    lanes = packed * head_size
    length = row_parts * rows_each
    groups = dates_each * columns_each
    inverse_root = 1.0 / math.sqrt(head_size)
    load_planes(sizes[:5], row_ref, hidden_ref, seq_scr, plane_scr)
    normed_scr[...] = rms_norm(plane_scr[...])
    qkv_scr[...] = matmul(normed_scr[...], project_ref[...]).astype(low)
    mask = block_mask(length, packed, head_size)
    for units in batches(groups, head_count // packed, column_units):
        places = []
        for group, part in units:
            start = part * lanes
            places.append(
                (
                    slice(group * length, (group + 1) * length),
                    slice(start, start + lanes),
                    slice(width + start, width + start + lanes),
                    slice(2 * width + start, 2 * width + start + lanes),
                )
            )
        all_scores = []
        for rows, at_query, at_key, at_value in places:
            query = spread(qkv_scr[rows, at_query], mask, packed)
            heads_grad = spread(heads_grad_scr[rows, at_query], mask, packed)
            all_scores.append(
                (
                    contract_last(qkv_scr[rows, at_key], query),
                    contract_last(qkv_scr[rows, at_value], heads_grad),
                )
            )
        all_weights = []
        for scores, product_grad in all_scores:
            weights = softmax_first(scores * inverse_root)
            score_grad = weights * (
                product_grad - jnp.sum(weights * product_grad, axis=0, keepdims=True)
            )
            all_weights.append((weights.astype(low), score_grad.astype(low)))
        all_full = []
        for (rows, at_query, at_key, at_value), (weights, score_low) in zip(places, all_weights):
            all_full.append(
                (
                    contract_rows(weights, qkv_scr[rows, at_value]),
                    contract_rows(score_low, qkv_scr[rows, at_key]),
                )
            )
            query = spread(qkv_scr[rows, at_query], mask, packed)
            heads_grad = spread(heads_grad_scr[rows, at_query], mask, packed)
            key_grad = matmul(score_low, query) * inverse_root
            qkv_grad_scr[rows, at_key] = key_grad.astype(low)
            qkv_grad_scr[rows, at_value] = matmul(weights, heads_grad).astype(low)
        for (rows, at_query, _, _), (heads_full, query_full) in zip(places, all_full):
            heads = own_blocks(heads_full, length, packed, head_size)
            heads_scr[rows, at_query] = heads.astype(low)
            query_grad = own_blocks(query_full, length, packed, head_size) * inverse_root
            qkv_grad_scr[rows, at_query] = query_grad.astype(low)
    project_grad = contract_rows(qkv_grad_scr[...], normed_scr[...])
    output_grad = contract_rows(grad_low_scr[...], heads_scr[...])
    if not direct:
        first_grad_ref[...] = project_grad
        second_grad_ref[...] = output_grad
        return
    keep_ref, send_ref = first_grad_ref, second_grad_ref
    even = pair_ref[0] == 0
    project_each = project_grad.shape[0] // date_size
    output_each = output_grad.shape[0] // date_size
    half = (project_each + output_each) // 2
    lower = lax.broadcasted_iota(jnp.int32, (half, 128), 1) < 64
    for outer in range(date_size // 2):
        pair = []
        for part in (2 * outer, 2 * outer + 1):
            block = jnp.concatenate(
                [
                    project_grad[part * project_each : (part + 1) * project_each],
                    output_grad[part * output_each : (part + 1) * output_each],
                ],
                axis=0,
            )
            top, bottom = block[:half, 128:256], block[half:, 128:256]
            pair.append(
                (
                    (block[:, :128], jnp.where(lower, top, pltpu.roll(bottom, 64, 1))),
                    (block[:, 256:], jnp.where(lower, pltpu.roll(top, 64, 1), bottom)),
                )
            )
        for row_part in range(2):
            for first, one, two in zip((0, 2 * half), pair[0][row_part], pair[1][row_part]):
                place = (row_part, outer, slice(first, first + one.shape[0]))
                keep_ref[place] = jnp.where(even, one, two).astype(low)
                send_ref[place] = jnp.where(even, two, one).astype(low)


def pair_kernel(
    row_ref, mid_ref, kept_ref, came_ref, own_ref, mid_out, row_out, both_out, handed_ref
):
    handed_ref[0] = row_ref[0]
    row, mid = row_ref[0], mid_ref[0]
    for outer in range(own_ref.shape[0]):
        for out_ref, row_at, mid_at in (
            (mid_out, row, 1 - mid),
            (row_out, 1 - row, mid),
            (both_out, 1 - row, 1 - mid),
            (own_ref, row, mid),
        ):
            place = (row_at, 2 * outer + mid_at)
            out_ref[outer] = (kept_ref[place].astype(wide) + came_ref[place].astype(wide)).astype(
                low
            )


def spread_kernel(outer_ref, own_ref, mid_ref, row_ref, both_ref, sent_ref, leave_ref, *refs):
    leave_ref[...] = sent_ref[...]
    count = own_ref.shape[0]
    for step in range(count):
        at = (outer_ref[0] + step) % count
        total = own_ref[at].astype(wide) + mid_ref[at].astype(wide)
        total = total + (row_ref[at].astype(wide) + both_ref[at].astype(wide))
        refs[step][...] = total.astype(low)


def finish_kernel(project_each, row_ref, *refs):
    *terms, _, project_ref, output_ref = refs
    total = terms[0][...].astype(wide)
    for term in terms[1:]:
        total = total + term[...].astype(wide)
    whole = 2 * total.shape[0] // 3
    main = total[:whole]
    tail = total[whole:]
    swapped = pltpu.roll(tail, 64, 1)
    lower = lax.broadcasted_iota(jnp.int32, (whole, 128), 1) < 64
    tail_first = jnp.concatenate([tail, swapped], axis=0)
    turned = pltpu.roll(main, 64, 1)
    front = jnp.concatenate([main, tail_first[:, :64]], axis=1)
    back = jnp.concatenate([jnp.where(lower, tail_first, turned), turned[:, :64]], axis=1)
    owned = jnp.where(row_ref[0] == 0, front, back)
    project_ref[...] = owned[:project_each]
    output_ref[...] = owned[project_each:]


def body(
    row_size,
    date_size,
    tokens,
    clear_flags,
    date_numbers,
    decay_slopes,
    time_project,
    time_output,
    column_project,
    column_output,
    cotangent,
):
    date_local, row_local, column_count, width = tokens.shape
    head_count = decay_slopes.shape[0]
    head_size = width // head_count
    packed = max(1, 128 // head_size)
    local_patches = row_local * column_count
    patches_each = local_patches // date_size
    columns_each = column_count // row_size
    row_count = row_local * row_size
    date_count = date_local * date_size
    project_each = 3 * width // date_size
    output_each = width // date_size
    lane_each = width // row_size
    direct = (
        patches_each == column_count
        and column_count % 16 == 0
        and date_size % 8 == 0
        and row_size == 2
        and lane_each == 192
        and project_each % 8 == 0
        and output_each % 8 == 0
        and (project_each + output_each) % 32 == 0
    )
    token_rows = date_local * patches_each
    block_rows = -(-(token_rows + date_local) // 8) * 8
    tile_rows = (width // 128) * token_rows + -(-date_local // 8) * 8
    params = pltpu.CompilerParams(vmem_limit_bytes=vmem_limit)
    in_vmem = pl.BlockSpec(memory_space=pltpu.VMEM)
    in_smem = pl.BlockSpec(memory_space=pltpu.SMEM)
    swap = [(0, 1), (1, 0)]
    column_tokens = date_local * row_count * columns_each
    half_tokens = column_tokens // row_size
    if direct:
        outgoing = pl.pallas_call(
            pack_kernel,
            out_shape=jax.ShapeDtypeStruct((date_size, tile_rows, 128), low),
            in_specs=[pl.BlockSpec(memory_space=pltpu.HBM)] * 3,
            out_specs=pl.BlockSpec(memory_space=pltpu.HBM),
            scratch_shapes=[
                pltpu.SMEM(date_numbers.shape, jnp.int32),
                pltpu.VMEM(tokens.shape, low),
                pltpu.VMEM(clear_flags.shape, jnp.int32),
                pltpu.VMEM((date_size, tile_rows, 128), low),
                pltpu.SemaphoreType.DMA((2,)),
                pltpu.SemaphoreType.DMA((4,)),
                pltpu.SemaphoreType.DMA((4,)),
            ],
            name="pack_tokens",
        )(date_numbers, tokens, clear_flags)
        row_at = lax.axis_index("row")
        halves = cotangent.reshape(date_local, row_local, row_size, columns_each, width)
        leaving = lax.dynamic_index_in_dim(halves, 1 - row_at, 2, keepdims=False)
        other_grad = lax.ppermute(leaving, "row", swap)
    else:
        flags = jnp.transpose(
            clear_flags.reshape(date_local, date_size, patches_each), (1, 0, 2)
        ).astype(low)
        numbers = jnp.stack([date_numbers // 32, date_numbers % 32], axis=-1).astype(low)
        numbers = jnp.broadcast_to(numbers[None], (date_size, date_local, 2))
        info = jnp.concatenate([flags, numbers], axis=-1)
        info = jnp.pad(
            info, ((0, 0), (0, block_rows - token_rows - date_local), (0, width - patches_each - 2))
        )
        outgoing = jnp.transpose(
            tokens.reshape(date_local, date_size, patches_each, width), (1, 0, 2, 3)
        ).reshape(date_size, token_rows, width)
        outgoing = jnp.concatenate([outgoing, info], axis=1)
    incoming = lax.all_to_all(outgoing, dates, split_axis=0, concat_axis=0, tiled=True)

    if direct:
        grads_in = (
            row_at.reshape(1),
            cotangent.reshape(local_patches * date_local, width),
            other_grad.reshape(half_tokens, width),
        )
        in_specs = [in_smem] + [in_vmem] * 3 + [in_smem]
    else:
        grads_in = (
            lax.all_to_all(cotangent, "row", split_axis=2, concat_axis=1, tiled=True).reshape(
                column_tokens, width
            ),
        )
        in_specs = [in_vmem] * 2 + [in_smem]
    time_tokens = date_count * patches_each
    hidden, after_time = pl.pallas_call(
        functools.partial(
            time_kernel,
            (
                date_size,
                date_local,
                patches_each,
                head_count,
                packed,
                columns_each if direct else patches_each,
            ),
        ),
        out_shape=(
            jax.ShapeDtypeStruct((time_tokens, width), low),
            jax.ShapeDtypeStruct((1,), jnp.int32),
        ),
        in_specs=[in_smem, in_vmem, in_vmem, in_vmem, pl.BlockSpec(memory_space=pl.ANY)],
        out_specs=(in_vmem, in_smem),
        scratch_shapes=[
            pltpu.VMEM((width // 128, time_tokens, 128), wide),
            pltpu.VMEM((time_tokens, width), wide),
            pltpu.VMEM((time_tokens, 3 * width), low),
            pltpu.VMEM((time_tokens, width), low),
        ],
        compiler_params=params,
        name="time_attention",
    )(decay_slopes, incoming, time_project, time_output, grads_in[-1])

    grad_low, heads_grad = pl.pallas_call(
        functools.partial(
            cotangent_kernel, (date_local, row_size, row_local, columns_each, direct)
        ),
        out_shape=(
            jax.ShapeDtypeStruct((column_tokens, width), low),
            jax.ShapeDtypeStruct((column_tokens, width), low),
        ),
        in_specs=in_specs,
        scratch_shapes=[pltpu.VMEM((width // 128, column_tokens, 128), wide)],
        compiler_params=params,
        name="cotangent_heads",
    )(*grads_in, column_output, after_time)

    if direct:
        parts = hidden.reshape(row_size * date_size, date_local * columns_each, width)
        plane = lax.all_to_all(parts, ("row", *dates), split_axis=0, concat_axis=0, tiled=True)
    else:
        parts = hidden.reshape(date_size, date_local, patches_each, width)
        back = lax.all_to_all(parts, dates, split_axis=0, concat_axis=0, tiled=True)
        back = jnp.transpose(back, (1, 0, 2, 3)).reshape(
            date_local, row_local, column_count, width
        )
        plane = lax.all_to_all(back, "row", split_axis=2, concat_axis=1, tiled=True)
    plane = plane.reshape(column_tokens, width)
    half_shape = jax.ShapeDtypeStruct((half_tokens, width), low)
    packed_rows = (project_each + output_each) * 3 // 2
    row_one = lax.axis_index("row").reshape(1)
    pair_one = lax.axis_index("pair").reshape(1)
    sizes = (date_local, row_size, row_local, columns_each, direct)
    if direct:
        half_grads = jax.ShapeDtypeStruct((row_size, date_size // 2, packed_rows, 128), low)
        grad_shapes = (half_grads, half_grads)
        mixed_shapes = (half_shape, half_shape)
    else:
        grad_shapes = (
            jax.ShapeDtypeStruct((3 * width, width), wide),
            jax.ShapeDtypeStruct((width, width), wide),
        )
        mixed_shapes = (jax.ShapeDtypeStruct((column_tokens, width), low),)
    column_heads, first_grad, second_grad = pl.pallas_call(
        functools.partial(column_kernel, (*sizes, head_count, packed, date_size)),
        out_shape=(jax.ShapeDtypeStruct((column_tokens, width), low), *grad_shapes),
        in_specs=[in_smem] * 2 + [in_vmem] * 4,
        scratch_shapes=[
            pltpu.VMEM((width // 128, column_tokens, 128), wide),
            pltpu.VMEM((column_tokens, width), wide),
            pltpu.VMEM((column_tokens, width), low),
            pltpu.VMEM((column_tokens, 3 * width), low),
            pltpu.VMEM((column_tokens, 3 * width), low),
        ],
        compiler_params=params,
        name="column_attention",
    )(row_one, pair_one, plane, grad_low, heads_grad, column_project)
    after_one = row_one
    if direct:
        came = lax.ppermute(second_grad, "pair", swap)
        outers = date_size // 4
        block = jax.ShapeDtypeStruct((packed_rows, 128), low)
        blocks = jax.ShapeDtypeStruct((outers, packed_rows, 128), low)
        own_grad, mid_grad, row_grad, both_grad, after_one = pl.pallas_call(
            pair_kernel,
            out_shape=(blocks,) * 4 + (jax.ShapeDtypeStruct((1,), jnp.int32),),
            in_specs=[in_smem] * 2 + [in_vmem] * 2,
            out_specs=(in_vmem,) * 4 + (in_smem,),
            compiler_params=params,
            name="pair_gradients",
        )(row_one, lax.axis_index("mid").reshape(1), first_grad, came)
        both_grad = lax.ppermute(both_grad, ("mid", "row"), [(0, 3), (3, 0), (1, 2), (2, 1)])
        mid_grad = lax.ppermute(mid_grad, "mid", swap)
        row_grad = lax.ppermute(row_grad, "row", swap)
    mixed = pl.pallas_call(
        functools.partial(mixed_kernel, sizes),
        out_shape=mixed_shapes,
        in_specs=[in_smem] + [in_vmem] * 3,
        scratch_shapes=[
            pltpu.VMEM((width // 128, column_tokens, 128), wide),
            pltpu.VMEM((column_tokens, width), wide),
        ],
        compiler_params=params,
        name="mixed_tokens",
    )(after_one, plane, column_heads, column_output)

    if direct:
        kept, sent = mixed
        leaving, *steps = pl.pallas_call(
            spread_kernel,
            out_shape=(half_shape,) + (block,) * outers,
            in_specs=[in_smem] + [in_vmem] * 5,
            compiler_params=params,
            name="spread_gradients",
        )(lax.axis_index("outer").reshape(1), own_grad, mid_grad, row_grad, both_grad, sent)
        terms = [steps[0]]
        for step in range(1, outers):
            route = [(at, (at + step) % outers) for at in range(outers)]
            terms.append(lax.ppermute(steps[step], "outer", route))
        arrived = lax.ppermute(leaving, "row", swap)
        quarter = (date_local, row_local, 1, columns_each, width)
        kept, arrived = kept.reshape(quarter), arrived.reshape(quarter)
        mixed = jnp.concatenate(
            [jnp.where(row_at == 0, kept, arrived), jnp.where(row_at == 0, arrived, kept)], axis=2
        )
        owned_project, owned_output = pl.pallas_call(
            functools.partial(finish_kernel, project_each),
            out_shape=(
                jax.ShapeDtypeStruct((project_each, lane_each), wide),
                jax.ShapeDtypeStruct((output_each, lane_each), wide),
            ),
            in_specs=[in_smem] + [in_vmem] * outers + [pl.BlockSpec(memory_space=pl.ANY)],
            compiler_params=params,
            name="gradient_sum",
        )(row_one, *terms, mixed)
    else:
        mixed = mixed[0]
        grads = jnp.concatenate(
            [
                first_grad.reshape(date_size, project_each, row_size, lane_each),
                second_grad.reshape(date_size, output_each, row_size, lane_each),
            ],
            axis=1,
        ).astype(low)
        grads = jnp.transpose(grads, (2, 0, 1, 3)).reshape(
            row_size * date_size, project_each + output_each, lane_each
        )
        terms = lax.all_to_all(grads, ("row", *dates), split_axis=0, concat_axis=0, tiled=True)
        owned = jnp.sum(terms.astype(wide), axis=0)
        owned_project, owned_output = owned[:project_each], owned[project_each:]
        mixed = mixed.reshape(row_size, date_local, row_local, columns_each, width)
        mixed = lax.all_to_all(mixed, "row", split_axis=0, concat_axis=0, tiled=True)
        mixed = jnp.transpose(mixed, (1, 2, 0, 3, 4))
    mixed = mixed.reshape(date_local, row_local, column_count, width)
    return (mixed, jnp.transpose(owned_project), jnp.transpose(owned_output))


def solution(mesh):
    date_size, row_size = mesh.shape["date"], mesh.shape["row"]
    pair_size = 2 if date_size % 2 == 0 else 1
    mid_size = 2 if date_size % 4 == 0 else 1
    split = jax.sharding.Mesh(
        mesh.devices.reshape(-1, mid_size, pair_size, row_size), ("outer", "mid", "pair", "row")
    )
    return jax.shard_map(
        functools.partial(body, row_size, date_size),
        mesh=split,
        in_specs=(
            P(dates, "row", None, None),
            P(dates, "row", None),
            P(dates),
            P(),
            P(),
            P(),
            P(),
            P(),
            P(dates, "row", None, None),
        ),
        out_specs=(P(dates, "row", None, None), P("row", dates), P("row", dates)),
        check_vma=False,
    )
```

```python
import functools
import math

import jax
import jax.numpy as jnp
from jax import lax
from jax.experimental import pallas as pl
from jax.experimental.pallas import tpu as pltpu
from jax.sharding import PartitionSpec as P

epsilon = 1e-06
masked_score = -1e30
time_units = 48
column_units = 24
dates = ("outer", "mid", "pair")
vmem_limit = 12 * 1024 * 1024
low = jnp.bfloat16
wide = jnp.float32


def rms_norm(values):
    factor = lax.rsqrt(jnp.mean(values * values, axis=-1, keepdims=True) + epsilon)
    return (values * factor).astype(low)


def matmul(left, right):
    return jnp.dot(left, right, preferred_element_type=wide)


def contract_rows(left, right):
    return lax.dot_general(left, right, (((0,), (0,)), ((), ())), preferred_element_type=wide)


def contract_last(left, right):
    return lax.dot_general(left, right, (((1,), (1,)), ((), ())), preferred_element_type=wide)


def block_mask(length, packed, head_size):
    shape = (packed * length, packed * head_size)
    rows = lax.broadcasted_iota(jnp.int32, shape, 0) // length
    lanes = lax.broadcasted_iota(jnp.int32, shape, 1) // head_size
    return jnp.where(rows == lanes, 1.0, 0.0).astype(low)


def spread(values, mask, packed):
    return jnp.concatenate([values] * packed, axis=0) * mask


def batches(groups, parts, each):
    units = [(group, part) for group in range(groups) for part in range(parts)]
    return [units[first : first + each] for first in range(0, len(units), each)]


def own_blocks(full, length, packed, head_size):
    lanes = lax.broadcasted_iota(jnp.int32, (length, packed * head_size), 1) // head_size
    out = full[:length]
    for head in range(1, packed):
        out = jnp.where(lanes == head, full[head * length : (head + 1) * length], out)
    return out


def softmax_first(scores):
    raised = jnp.exp(scores - jnp.max(scores, axis=0, keepdims=True))
    return raised * (1.0 / jnp.sum(raised, axis=0, keepdims=True))


def put_tiles(scratch, rows, values):
    tiles, _, lanes = scratch.shape
    for tile in range(tiles):
        scratch[tile, rows, :] = values[:, tile * lanes : (tile + 1) * lanes]


def get_tiles(scratch, rows):
    return jnp.concatenate([scratch[tile, rows, :] for tile in range(scratch.shape[0])], axis=-1)


def pack_kernel(
    numbers_ref,
    tokens_ref,
    flags_ref,
    out_ref,
    numbers_scr,
    tokens_scr,
    flags_scr,
    out_scr,
    small_copied,
    came,
    left,
):
    dates_each, parts, patches, width = tokens_ref.shape
    chunks = came.shape[0]
    each = parts // chunks
    small = [
        pltpu.make_async_copy(flags_ref, flags_scr, small_copied.at[0]),
        pltpu.make_async_copy(numbers_ref, numbers_scr, small_copied.at[1]),
    ]
    arrivals, departures = [], []
    for chunk in range(chunks):
        at = pl.ds(chunk * each, each)
        arrivals.append(
            pltpu.make_async_copy(tokens_ref.at[:, at], tokens_scr.at[:, at], came.at[chunk])
        )
        departures.append(pltpu.make_async_copy(out_scr.at[at], out_ref.at[at], left.at[chunk]))
    for copy in small + arrivals:
        copy.start()
    lanes = out_ref.shape[2]
    tiles = width // lanes
    spare = out_ref.shape[1] - tiles * dates_each * patches
    place = lax.broadcasted_iota(jnp.int32, (patches, lanes), 0)
    lane = lax.broadcasted_iota(jnp.int32, (patches, lanes), 1)
    place = jnp.where(place == lane, 1.0, 0.0).astype(low)
    lane = lax.broadcasted_iota(jnp.int32, (parts, lanes), 1)
    row = lax.broadcasted_iota(jnp.int32, (spare, lanes), 0)
    for copy in small:
        copy.wait()
    infos = []
    for date in range(dates_each):
        number = numbers_scr[date]
        upper = (number // 32).astype(wide)
        under = (number % 32).astype(wide)
        info = matmul(flags_scr[date].astype(wide).astype(low), place)
        info = jnp.where(lane == patches, upper, info)
        infos.append(jnp.where(lane == patches + 1, under, info))
    for chunk in range(chunks):
        arrivals[chunk].wait()
        for part in range(chunk * each, (chunk + 1) * each):
            tokens = jnp.concatenate(
                [tokens_scr[date, part].astype(wide) for date in range(dates_each)], axis=0
            )
            extra = jnp.zeros((spare, lanes), wide)
            for date in range(dates_each):
                extra = jnp.where(row == date, infos[date][part : part + 1], extra)
            pieces = [tokens[:, tile * lanes : (tile + 1) * lanes] for tile in range(tiles)]
            out_scr[part] = jnp.concatenate(pieces + [extra], axis=0).astype(low)
        departures[chunk].start()
    for copy in departures:
        copy.wait()


def time_kernel(
    sizes,
    slopes_ref,
    block_ref,
    project_ref,
    output_ref,
    earlier_ref,
    out_ref,
    seq_scr,
    token_scr,
    qkv_scr,
    heads_scr,
):
    sources, dates_each, groups, head_count, packed, columns_each = sizes
    width = project_ref.shape[0]
    tile_lanes = block_ref.shape[2]
    tiles = width // tile_lanes
    head_size = width // head_count
    lanes = packed * head_size
    length = sources * dates_each
    token_rows = dates_each * groups
    inverse_root = 1.0 / math.sqrt(head_size)
    info = []
    for source in range(sources):
        plane = block_ref[source].astype(wide)
        rows = slice(source * token_rows, (source + 1) * token_rows)
        for tile in range(tiles):
            at = slice(tile * token_rows, (tile + 1) * token_rows)
            if tiles == 1:
                put_tiles(seq_scr, rows, plane[at])
            else:
                seq_scr[tile, rows, :] = plane[at]
        info.append(plane[tiles * token_rows : tiles * token_rows + dates_each])
    info = jnp.concatenate(info, axis=0)
    for group in range(groups):
        token_scr[group * length : (group + 1) * length, :] = get_tiles(
            seq_scr, pl.ds(group, length, stride=groups)
        )
    tokens = token_scr[...]
    qkv_scr[...] = matmul(rms_norm(tokens), project_ref[...]).astype(low)
    numbers = info[:, groups : groups + 1] * 32.0 + info[:, groups + 1 : groups + 2]
    key_at = lax.broadcasted_iota(jnp.int32, (length, packed * length), 0)
    column_at = lax.broadcasted_iota(jnp.int32, (length, packed * length), 1)
    same_date = key_at == column_at % length
    query_numbers = jnp.sum(jnp.where(same_date, numbers, 0.0), axis=0, keepdims=True)
    gap_days = jnp.abs(numbers - query_numbers)
    head_at = column_at // length
    mask = block_mask(length, packed, head_size)
    biases = []
    for first in range(0, head_count, packed):
        slope = jnp.full((length, packed * length), slopes_ref[first], wide)
        for head in range(1, packed):
            slope = jnp.where(head_at == head, slopes_ref[first + head], slope)
        biases.append(-slope * gap_days)
    for units in batches(groups, head_count // packed, time_units):
        all_scores = []
        for group, part in units:
            rows = slice(group * length, (group + 1) * length)
            start = part * lanes
            query = qkv_scr[rows, start : start + lanes]
            key = qkv_scr[rows, width + start : width + start + lanes]
            all_scores.append(contract_last(key, spread(query, mask, packed)))
        all_weights = []
        for (group, part), scores in zip(units, all_scores):
            allowed = (info[:, group : group + 1] > 0) | same_date
            scores = jnp.where(allowed, scores * inverse_root + biases[part], masked_score)
            all_weights.append(softmax_first(scores).astype(low))
        all_heads = []
        for (group, part), weights in zip(units, all_weights):
            rows = slice(group * length, (group + 1) * length)
            start = 2 * width + part * lanes
            all_heads.append(contract_rows(weights, qkv_scr[rows, start : start + lanes]))
        for (group, part), full in zip(units, all_heads):
            rows = slice(group * length, (group + 1) * length)
            heads_scr[rows, part * lanes : (part + 1) * lanes] = own_blocks(
                full, length, packed, head_size
            ).astype(low)
    hidden = token_scr[...] + matmul(heads_scr[...], output_ref[...])
    for group in range(groups):
        first = (group // columns_each) * (length * columns_each) + group % columns_each
        put_tiles(
            seq_scr,
            pl.ds(first, length, stride=columns_each),
            hidden[group * length : (group + 1) * length],
        )
    out_ref[...] = get_tiles(seq_scr, slice(None)).astype(low)


def cotangent_kernel(sizes, *refs):
    dates_each, row_parts, rows_each, columns_each, direct = sizes
    output_ref, _, grad_low_ref, heads_grad_ref, grad_scr = refs[-5:]
    width = output_ref.shape[0]
    length = row_parts * rows_each
    groups = dates_each * columns_each
    part_rows = rows_each * groups
    if direct:
        row_ref, own_ref, other_ref = refs[:3]
        own = own_ref[...].astype(wide)
        own = own.reshape(dates_each * rows_each, row_parts, columns_each, width)
        own = jnp.where(row_ref[0] == 0, own[:, 0], own[:, 1]).reshape(part_rows, width)
        put_tiles(grad_scr, slice(0, part_rows), own)
        put_tiles(grad_scr, slice(part_rows, 2 * part_rows), other_ref[...].astype(wide))
    else:
        put_tiles(grad_scr, slice(None), refs[0][...].astype(wide))
    for group in range(groups):
        if direct:
            inner = (group // columns_each) * (rows_each * columns_each) + group % columns_each
            pieces = [
                get_tiles(
                    grad_scr, pl.ds(part * part_rows + inner, rows_each, stride=columns_each)
                )
                for part in range(row_parts)
            ]
            values = jnp.concatenate(pieces, axis=0)
        else:
            first = (group // columns_each) * (length * columns_each) + group % columns_each
            values = get_tiles(grad_scr, pl.ds(first, length, stride=columns_each))
        grad_low_ref[group * length : (group + 1) * length, :] = values.astype(low)
    heads_grad_ref[...] = contract_last(grad_low_ref[...], output_ref[...]).astype(low)


def load_planes(sizes, row_ref, hidden_ref, seq_scr, plane_scr):
    dates_each, row_parts, rows_each, columns_each, direct = sizes
    length = row_parts * rows_each
    groups = dates_each * columns_each
    part_rows = rows_each * groups
    if direct:
        for part in range(row_parts):
            source = pl.multiple_of(((row_ref[0] + part) % row_parts) * part_rows, part_rows)
            put_tiles(
                seq_scr,
                slice(part * part_rows, (part + 1) * part_rows),
                hidden_ref[pl.ds(source, part_rows), :].astype(wide),
            )
    else:
        put_tiles(seq_scr, slice(None), hidden_ref[...].astype(wide))
    for group in range(groups):
        rows = slice(group * length, (group + 1) * length)
        if direct:
            at = pl.ds(group, length, stride=groups)
        else:
            first = (group // columns_each) * (length * columns_each) + group % columns_each
            at = pl.ds(first, length, stride=columns_each)
        plane_scr[rows, :] = get_tiles(seq_scr, at)


def mixed_kernel(sizes, row_ref, hidden_ref, heads_ref, output_ref, _, *refs):
    dates_each, row_parts, rows_each, columns_each, direct = sizes
    *mixed_refs, seq_scr, plane_scr = refs
    length = row_parts * rows_each
    groups = dates_each * columns_each
    part_rows = rows_each * groups
    load_planes(sizes, row_ref, hidden_ref, seq_scr, plane_scr)
    mixed = plane_scr[...] + matmul(heads_ref[...], output_ref[...])
    for group in range(groups):
        inner = (group // columns_each) * (rows_each * columns_each) + group % columns_each
        for part in range(row_parts):
            begin = group * length + part * rows_each
            put_tiles(
                seq_scr,
                pl.ds(part * part_rows + inner, rows_each, stride=columns_each),
                mixed[begin : begin + rows_each],
            )
    if direct:
        kept_ref, sent_ref = mixed_refs
        kept_ref[...] = get_tiles(seq_scr, slice(0, part_rows)).astype(low)
        sent_ref[...] = get_tiles(seq_scr, slice(part_rows, 2 * part_rows)).astype(low)
    else:
        mixed_refs[0][...] = get_tiles(seq_scr, slice(None)).astype(low)


def column_kernel(
    sizes,
    row_ref,
    pair_ref,
    hidden_ref,
    grad_low_scr,
    heads_grad_scr,
    project_ref,
    heads_scr,
    first_grad_ref,
    second_grad_ref,
    seq_scr,
    plane_scr,
    normed_scr,
    qkv_scr,
    qkv_grad_scr,
):
    dates_each, row_parts, rows_each, columns_each, direct, head_count, packed, date_size = sizes
    width = hidden_ref.shape[1]
    head_size = width // head_count
    lanes = packed * head_size
    length = row_parts * rows_each
    groups = dates_each * columns_each
    inverse_root = 1.0 / math.sqrt(head_size)
    load_planes(sizes[:5], row_ref, hidden_ref, seq_scr, plane_scr)
    normed_scr[...] = rms_norm(plane_scr[...])
    qkv_scr[...] = matmul(normed_scr[...], project_ref[...]).astype(low)
    mask = block_mask(length, packed, head_size)
    for units in batches(groups, head_count // packed, column_units):
        places = []
        for group, part in units:
            start = part * lanes
            places.append(
                (
                    slice(group * length, (group + 1) * length),
                    slice(start, start + lanes),
                    slice(width + start, width + start + lanes),
                    slice(2 * width + start, 2 * width + start + lanes),
                )
            )
        all_scores = []
        for rows, at_query, at_key, at_value in places:
            query = spread(qkv_scr[rows, at_query], mask, packed)
            heads_grad = spread(heads_grad_scr[rows, at_query], mask, packed)
            all_scores.append(
                (
                    contract_last(qkv_scr[rows, at_key], query),
                    contract_last(qkv_scr[rows, at_value], heads_grad),
                )
            )
        all_weights = []
        for scores, product_grad in all_scores:
            weights = softmax_first(scores * inverse_root)
            score_grad = weights * (
                product_grad - jnp.sum(weights * product_grad, axis=0, keepdims=True)
            )
            all_weights.append((weights.astype(low), score_grad.astype(low)))
        all_full = []
        for (rows, at_query, at_key, at_value), (weights, score_low) in zip(places, all_weights):
            all_full.append(
                (
                    contract_rows(weights, qkv_scr[rows, at_value]),
                    contract_rows(score_low, qkv_scr[rows, at_key]),
                )
            )
            query = spread(qkv_scr[rows, at_query], mask, packed)
            heads_grad = spread(heads_grad_scr[rows, at_query], mask, packed)
            key_grad = matmul(score_low, query) * inverse_root
            qkv_grad_scr[rows, at_key] = key_grad.astype(low)
            qkv_grad_scr[rows, at_value] = matmul(weights, heads_grad).astype(low)
        for (rows, at_query, _, _), (heads_full, query_full) in zip(places, all_full):
            heads = own_blocks(heads_full, length, packed, head_size)
            heads_scr[rows, at_query] = heads.astype(low)
            query_grad = own_blocks(query_full, length, packed, head_size) * inverse_root
            qkv_grad_scr[rows, at_query] = query_grad.astype(low)
    project_grad = contract_rows(qkv_grad_scr[...], normed_scr[...])
    output_grad = contract_rows(grad_low_scr[...], heads_scr[...])
    if not direct:
        first_grad_ref[...] = project_grad
        second_grad_ref[...] = output_grad
        return
    keep_ref, send_ref = first_grad_ref, second_grad_ref
    even = pair_ref[0] == 0
    project_each = project_grad.shape[0] // date_size
    output_each = output_grad.shape[0] // date_size
    half = (project_each + output_each) // 2
    lower = lax.broadcasted_iota(jnp.int32, (half, 128), 1) < 64
    for outer in range(date_size // 2):
        pair = []
        for part in (2 * outer, 2 * outer + 1):
            block = jnp.concatenate(
                [
                    project_grad[part * project_each : (part + 1) * project_each],
                    output_grad[part * output_each : (part + 1) * output_each],
                ],
                axis=0,
            )
            top, bottom = block[:half, 128:256], block[half:, 128:256]
            pair.append(
                (
                    (block[:, :128], jnp.where(lower, top, pltpu.roll(bottom, 64, 1))),
                    (block[:, 256:], jnp.where(lower, pltpu.roll(top, 64, 1), bottom)),
                )
            )
        for row_part in range(2):
            for first, one, two in zip((0, 2 * half), pair[0][row_part], pair[1][row_part]):
                place = (row_part, outer, slice(first, first + one.shape[0]))
                keep_ref[place] = jnp.where(even, one, two).astype(low)
                send_ref[place] = jnp.where(even, two, one).astype(low)


def pair_kernel(row_ref, mid_ref, kept_ref, came_ref, own_ref, mid_out, row_out, both_out):
    row, mid = row_ref[0], mid_ref[0]
    for outer in range(own_ref.shape[0]):
        for out_ref, row_at, mid_at in (
            (mid_out, row, 1 - mid),
            (row_out, 1 - row, mid),
            (both_out, 1 - row, 1 - mid),
            (own_ref, row, mid),
        ):
            place = (row_at, 2 * outer + mid_at)
            out_ref[outer] = (kept_ref[place].astype(wide) + came_ref[place].astype(wide)).astype(
                low
            )


def spread_kernel(outer_ref, own_ref, mid_ref, row_ref, both_ref, sent_ref, leave_ref, *refs):
    leave_ref[...] = sent_ref[...]
    count = own_ref.shape[0]
    for step in range(count):
        at = (outer_ref[0] + step) % count
        total = own_ref[at].astype(wide) + mid_ref[at].astype(wide)
        total = total + (row_ref[at].astype(wide) + both_ref[at].astype(wide))
        refs[step][...] = total.astype(low)


def finish_kernel(project_each, row_ref, *refs):
    *terms, _, project_ref, output_ref = refs
    total = terms[0][...].astype(wide)
    for term in terms[1:]:
        total = total + term[...].astype(wide)
    whole = 2 * total.shape[0] // 3
    main = total[:whole]
    tail = total[whole:]
    swapped = pltpu.roll(tail, 64, 1)
    lower = lax.broadcasted_iota(jnp.int32, (whole, 128), 1) < 64
    tail_first = jnp.concatenate([tail, swapped], axis=0)
    turned = pltpu.roll(main, 64, 1)
    front = jnp.concatenate([main, tail_first[:, :64]], axis=1)
    back = jnp.concatenate([jnp.where(lower, tail_first, turned), turned[:, :64]], axis=1)
    owned = jnp.where(row_ref[0] == 0, front, back)
    project_ref[...] = owned[:project_each]
    output_ref[...] = owned[project_each:]


def body(
    row_size,
    date_size,
    tokens,
    clear_flags,
    date_numbers,
    decay_slopes,
    time_project,
    time_output,
    column_project,
    column_output,
    cotangent,
):
    date_local, row_local, column_count, width = tokens.shape
    head_count = decay_slopes.shape[0]
    head_size = width // head_count
    packed = max(1, 128 // head_size)
    local_patches = row_local * column_count
    patches_each = local_patches // date_size
    columns_each = column_count // row_size
    row_count = row_local * row_size
    date_count = date_local * date_size
    project_each = 3 * width // date_size
    output_each = width // date_size
    lane_each = width // row_size
    direct = (
        patches_each == column_count
        and column_count % 16 == 0
        and date_size % 8 == 0
        and row_size == 2
        and lane_each == 192
        and project_each % 8 == 0
        and output_each % 8 == 0
        and (project_each + output_each) % 32 == 0
    )
    token_rows = date_local * patches_each
    block_rows = -(-(token_rows + date_local) // 8) * 8
    tile_rows = (width // 128) * token_rows + -(-date_local // 8) * 8
    params = pltpu.CompilerParams(vmem_limit_bytes=vmem_limit)
    in_vmem = pl.BlockSpec(memory_space=pltpu.VMEM)
    in_smem = pl.BlockSpec(memory_space=pltpu.SMEM)
    in_any = pl.BlockSpec(memory_space=pl.ANY)
    swap = [(0, 1), (1, 0)]
    column_tokens = date_local * row_count * columns_each
    half_tokens = column_tokens // row_size
    if direct:
        outgoing = pl.pallas_call(
            pack_kernel,
            out_shape=jax.ShapeDtypeStruct((date_size, tile_rows, 128), low),
            in_specs=[pl.BlockSpec(memory_space=pltpu.HBM)] * 3,
            out_specs=pl.BlockSpec(memory_space=pltpu.HBM),
            scratch_shapes=[
                pltpu.SMEM(date_numbers.shape, jnp.int32),
                pltpu.VMEM(tokens.shape, low),
                pltpu.VMEM(clear_flags.shape, jnp.int32),
                pltpu.VMEM((date_size, tile_rows, 128), low),
                pltpu.SemaphoreType.DMA((2,)),
                pltpu.SemaphoreType.DMA((4,)),
                pltpu.SemaphoreType.DMA((4,)),
            ],
            name="pack_tokens",
        )(date_numbers, tokens, clear_flags)
        row_at = lax.axis_index("row")
        halves = cotangent.reshape(date_local, row_local, row_size, columns_each, width)
        leaving = lax.dynamic_index_in_dim(halves, 1 - row_at, 2, keepdims=False)
        other_grad = lax.ppermute(leaving, "row", swap)
    else:
        flags = jnp.transpose(
            clear_flags.reshape(date_local, date_size, patches_each), (1, 0, 2)
        ).astype(low)
        numbers = jnp.stack([date_numbers // 32, date_numbers % 32], axis=-1).astype(low)
        numbers = jnp.broadcast_to(numbers[None], (date_size, date_local, 2))
        info = jnp.concatenate([flags, numbers], axis=-1)
        info = jnp.pad(
            info, ((0, 0), (0, block_rows - token_rows - date_local), (0, width - patches_each - 2))
        )
        outgoing = jnp.transpose(
            tokens.reshape(date_local, date_size, patches_each, width), (1, 0, 2, 3)
        ).reshape(date_size, token_rows, width)
        outgoing = jnp.concatenate([outgoing, info], axis=1)
    incoming = lax.all_to_all(outgoing, dates, split_axis=0, concat_axis=0, tiled=True)

    if direct:
        grads_in = (
            row_at.reshape(1),
            cotangent.reshape(local_patches * date_local, width),
            other_grad.reshape(half_tokens, width),
        )
        in_specs = [in_smem] + [in_vmem] * 3 + [in_any]
    else:
        grads_in = (
            lax.all_to_all(cotangent, "row", split_axis=2, concat_axis=1, tiled=True).reshape(
                column_tokens, width
            ),
        )
        in_specs = [in_vmem] * 2 + [in_any]
    time_tokens = date_count * patches_each
    hidden = pl.pallas_call(
        functools.partial(
            time_kernel,
            (
                date_size,
                date_local,
                patches_each,
                head_count,
                packed,
                columns_each if direct else patches_each,
            ),
        ),
        out_shape=jax.ShapeDtypeStruct((time_tokens, width), low),
        in_specs=[in_smem, in_vmem, in_vmem, in_vmem, in_any],
        scratch_shapes=[
            pltpu.VMEM((width // 128, time_tokens, 128), wide),
            pltpu.VMEM((time_tokens, width), wide),
            pltpu.VMEM((time_tokens, 3 * width), low),
            pltpu.VMEM((time_tokens, width), low),
        ],
        compiler_params=params,
        name="time_attention",
    )(decay_slopes, incoming, time_project, time_output, grads_in[-1])

    grad_low, heads_grad = pl.pallas_call(
        functools.partial(
            cotangent_kernel, (date_local, row_size, row_local, columns_each, direct)
        ),
        out_shape=(
            jax.ShapeDtypeStruct((column_tokens, width), low),
            jax.ShapeDtypeStruct((column_tokens, width), low),
        ),
        in_specs=in_specs,
        scratch_shapes=[pltpu.VMEM((width // 128, column_tokens, 128), wide)],
        compiler_params=params,
        name="cotangent_heads",
    )(*grads_in, column_output, hidden)

    if direct:
        parts = hidden.reshape(row_size * date_size, date_local * columns_each, width)
        plane = lax.all_to_all(parts, ("row", *dates), split_axis=0, concat_axis=0, tiled=True)
    else:
        parts = hidden.reshape(date_size, date_local, patches_each, width)
        back = lax.all_to_all(parts, dates, split_axis=0, concat_axis=0, tiled=True)
        back = jnp.transpose(back, (1, 0, 2, 3)).reshape(
            date_local, row_local, column_count, width
        )
        plane = lax.all_to_all(back, "row", split_axis=2, concat_axis=1, tiled=True)
    plane = plane.reshape(column_tokens, width)
    half_shape = jax.ShapeDtypeStruct((half_tokens, width), low)
    packed_rows = (project_each + output_each) * 3 // 2
    row_one = lax.axis_index("row").reshape(1)
    pair_one = lax.axis_index("pair").reshape(1)
    sizes = (date_local, row_size, row_local, columns_each, direct)
    if direct:
        half_grads = jax.ShapeDtypeStruct((row_size, date_size // 2, packed_rows, 128), low)
        grad_shapes = (half_grads, half_grads)
        mixed_shapes = (half_shape, half_shape)
    else:
        grad_shapes = (
            jax.ShapeDtypeStruct((3 * width, width), wide),
            jax.ShapeDtypeStruct((width, width), wide),
        )
        mixed_shapes = (jax.ShapeDtypeStruct((column_tokens, width), low),)
    column_heads, first_grad, second_grad = pl.pallas_call(
        functools.partial(column_kernel, (*sizes, head_count, packed, date_size)),
        out_shape=(jax.ShapeDtypeStruct((column_tokens, width), low), *grad_shapes),
        in_specs=[in_smem] * 2 + [in_vmem] * 4,
        input_output_aliases={4: 0},
        scratch_shapes=[
            pltpu.VMEM((width // 128, column_tokens, 128), wide),
            pltpu.VMEM((column_tokens, width), wide),
            pltpu.VMEM((column_tokens, width), low),
            pltpu.VMEM((column_tokens, 3 * width), low),
            pltpu.VMEM((column_tokens, 3 * width), low),
        ],
        compiler_params=params,
        name="column_attention",
    )(row_one, pair_one, plane, grad_low, heads_grad, column_project)
    own_grad = first_grad
    if direct:
        came = lax.ppermute(second_grad, "pair", swap)
        outers = date_size // 4
        block = jax.ShapeDtypeStruct((packed_rows, 128), low)
        blocks = jax.ShapeDtypeStruct((outers, packed_rows, 128), low)
        own_grad, mid_grad, row_grad, both_grad = pl.pallas_call(
            pair_kernel,
            out_shape=(blocks,) * 4,
            in_specs=[in_smem] * 2 + [in_vmem] * 2,
            out_specs=(in_vmem,) * 4,
            compiler_params=params,
            name="pair_gradients",
        )(row_one, lax.axis_index("mid").reshape(1), first_grad, came)
        both_grad = lax.ppermute(both_grad, ("mid", "row"), [(0, 3), (3, 0), (1, 2), (2, 1)])
        mid_grad = lax.ppermute(mid_grad, "mid", swap)
        row_grad = lax.ppermute(row_grad, "row", swap)
    mixed = pl.pallas_call(
        functools.partial(mixed_kernel, sizes),
        out_shape=mixed_shapes,
        in_specs=[in_smem] + [in_vmem] * 3 + [in_any],
        scratch_shapes=[
            pltpu.VMEM((width // 128, column_tokens, 128), wide),
            pltpu.VMEM((column_tokens, width), wide),
        ],
        compiler_params=params,
        name="mixed_tokens",
    )(row_one, plane, column_heads, column_output, own_grad)

    if direct:
        kept, sent = mixed
        leaving, *steps = pl.pallas_call(
            spread_kernel,
            out_shape=(half_shape,) + (block,) * outers,
            in_specs=[in_smem] + [in_vmem] * 5,
            compiler_params=params,
            name="spread_gradients",
        )(lax.axis_index("outer").reshape(1), own_grad, mid_grad, row_grad, both_grad, sent)
        terms = [steps[0]]
        for step in range(1, outers):
            route = [(at, (at + step) % outers) for at in range(outers)]
            terms.append(lax.ppermute(steps[step], "outer", route))
        arrived = lax.ppermute(leaving, "row", swap)
        quarter = (date_local, row_local, 1, columns_each, width)
        kept, arrived = kept.reshape(quarter), arrived.reshape(quarter)
        mixed = jnp.concatenate(
            [jnp.where(row_at == 0, kept, arrived), jnp.where(row_at == 0, arrived, kept)], axis=2
        )
        owned_project, owned_output = pl.pallas_call(
            functools.partial(finish_kernel, project_each),
            out_shape=(
                jax.ShapeDtypeStruct((project_each, lane_each), wide),
                jax.ShapeDtypeStruct((output_each, lane_each), wide),
            ),
            in_specs=[in_smem] + [in_vmem] * outers + [in_any],
            compiler_params=params,
            name="gradient_sum",
        )(row_one, *terms, mixed)
    else:
        mixed = mixed[0]
        grads = jnp.concatenate(
            [
                first_grad.reshape(date_size, project_each, row_size, lane_each),
                second_grad.reshape(date_size, output_each, row_size, lane_each),
            ],
            axis=1,
        ).astype(low)
        grads = jnp.transpose(grads, (2, 0, 1, 3)).reshape(
            row_size * date_size, project_each + output_each, lane_each
        )
        terms = lax.all_to_all(grads, ("row", *dates), split_axis=0, concat_axis=0, tiled=True)
        owned = jnp.sum(terms.astype(wide), axis=0)
        owned_project, owned_output = owned[:project_each], owned[project_each:]
        mixed = mixed.reshape(row_size, date_local, row_local, columns_each, width)
        mixed = lax.all_to_all(mixed, "row", split_axis=0, concat_axis=0, tiled=True)
        mixed = jnp.transpose(mixed, (1, 2, 0, 3, 4))
    mixed = mixed.reshape(date_local, row_local, column_count, width)
    return (mixed, jnp.transpose(owned_project), jnp.transpose(owned_output))


def solution(mesh):
    date_size, row_size = mesh.shape["date"], mesh.shape["row"]
    pair_size = 2 if date_size % 2 == 0 else 1
    mid_size = 2 if date_size % 4 == 0 else 1
    split = jax.sharding.Mesh(
        mesh.devices.reshape(-1, mid_size, pair_size, row_size), ("outer", "mid", "pair", "row")
    )
    return jax.shard_map(
        functools.partial(body, row_size, date_size),
        mesh=split,
        in_specs=(
            P(dates, "row", None, None),
            P(dates, "row", None),
            P(dates),
            P(),
            P(),
            P(),
            P(),
            P(),
            P(dates, "row", None, None),
        ),
        out_specs=(P(dates, "row", None, None), P("row", dates), P("row", dates)),
        check_vma=False,
    )
```

```python
import functools
import math

import jax
import jax.numpy as jnp
from jax import lax
from jax.experimental import pallas as pl
from jax.experimental.pallas import tpu as pltpu
from jax.sharding import PartitionSpec as P

epsilon = 1e-06
masked_score = -1e30
time_units = 48
column_units = 24
dates = ("outer", "mid", "pair")
vmem_limit = 12 * 1024 * 1024
low = jnp.bfloat16
wide = jnp.float32


def rms_norm(values):
    factor = lax.rsqrt(jnp.mean(values * values, axis=-1, keepdims=True) + epsilon)
    return (values * factor).astype(low)


def matmul(left, right):
    return jnp.dot(left, right, preferred_element_type=wide)


def contract_rows(left, right):
    return lax.dot_general(left, right, (((0,), (0,)), ((), ())), preferred_element_type=wide)


def contract_last(left, right):
    return lax.dot_general(left, right, (((1,), (1,)), ((), ())), preferred_element_type=wide)


def block_mask(length, packed, head_size):
    shape = (packed * length, packed * head_size)
    rows = lax.broadcasted_iota(jnp.int32, shape, 0) // length
    lanes = lax.broadcasted_iota(jnp.int32, shape, 1) // head_size
    return jnp.where(rows == lanes, 1.0, 0.0).astype(low)


def spread(values, mask, packed):
    return jnp.concatenate([values] * packed, axis=0) * mask


def batches(groups, parts, each):
    units = [(group, part) for group in range(groups) for part in range(parts)]
    return [units[first : first + each] for first in range(0, len(units), each)]


def own_blocks(full, length, packed, head_size):
    lanes = lax.broadcasted_iota(jnp.int32, (length, packed * head_size), 1) // head_size
    out = full[:length]
    for head in range(1, packed):
        out = jnp.where(lanes == head, full[head * length : (head + 1) * length], out)
    return out


def softmax_first(scores):
    raised = jnp.exp(scores - jnp.max(scores, axis=0, keepdims=True))
    return raised * (1.0 / jnp.sum(raised, axis=0, keepdims=True))


def put_tiles(scratch, rows, values):
    tiles, _, lanes = scratch.shape
    for tile in range(tiles):
        scratch[tile, rows, :] = values[:, tile * lanes : (tile + 1) * lanes]


def get_tiles(scratch, rows):
    return jnp.concatenate([scratch[tile, rows, :] for tile in range(scratch.shape[0])], axis=-1)


def pack_kernel(
    numbers_ref,
    tokens_ref,
    flags_ref,
    out_ref,
    numbers_scr,
    tokens_scr,
    flags_scr,
    out_scr,
    small_copied,
    came,
    left,
):
    dates_each, parts, patches, width = tokens_ref.shape
    chunks = came.shape[0]
    each = parts // chunks
    small = [
        pltpu.make_async_copy(flags_ref, flags_scr, small_copied.at[0]),
        pltpu.make_async_copy(numbers_ref, numbers_scr, small_copied.at[1]),
    ]
    arrivals, departures = [], []
    for chunk in range(chunks):
        at = pl.ds(chunk * each, each)
        arrivals.append(
            pltpu.make_async_copy(tokens_ref.at[:, at], tokens_scr.at[:, at], came.at[chunk])
        )
        departures.append(pltpu.make_async_copy(out_scr.at[at], out_ref.at[at], left.at[chunk]))
    for copy in small + arrivals:
        copy.start()
    lanes = out_ref.shape[2]
    tiles = width // lanes
    spare = out_ref.shape[1] - tiles * dates_each * patches
    place = lax.broadcasted_iota(jnp.int32, (patches, lanes), 0)
    lane = lax.broadcasted_iota(jnp.int32, (patches, lanes), 1)
    place = jnp.where(place == lane, 1.0, 0.0).astype(low)
    lane = lax.broadcasted_iota(jnp.int32, (parts, lanes), 1)
    row = lax.broadcasted_iota(jnp.int32, (spare, lanes), 0)
    for copy in small:
        copy.wait()
    infos = []
    for date in range(dates_each):
        number = numbers_scr[date]
        upper = (number // 32).astype(wide)
        under = (number % 32).astype(wide)
        info = matmul(flags_scr[date].astype(wide).astype(low), place)
        info = jnp.where(lane == patches, upper, info)
        infos.append(jnp.where(lane == patches + 1, under, info))
    for chunk in range(chunks):
        arrivals[chunk].wait()
        for part in range(chunk * each, (chunk + 1) * each):
            tokens = jnp.concatenate(
                [tokens_scr[date, part].astype(wide) for date in range(dates_each)], axis=0
            )
            extra = jnp.zeros((spare, lanes), wide)
            for date in range(dates_each):
                extra = jnp.where(row == date, infos[date][part : part + 1], extra)
            pieces = [tokens[:, tile * lanes : (tile + 1) * lanes] for tile in range(tiles)]
            out_scr[part] = jnp.concatenate(pieces + [extra], axis=0).astype(low)
        departures[chunk].start()
    for copy in departures:
        copy.wait()


def time_kernel(
    sizes,
    slopes_ref,
    block_ref,
    project_ref,
    output_ref,
    earlier_ref,
    out_ref,
    seq_scr,
    token_scr,
    qkv_scr,
    heads_scr,
    out_scr,
    left,
):
    sources, dates_each, groups, head_count, packed, columns_each = sizes
    width = project_ref.shape[0]
    tile_lanes = block_ref.shape[2]
    tiles = width // tile_lanes
    head_size = width // head_count
    lanes = packed * head_size
    length = sources * dates_each
    token_rows = dates_each * groups
    inverse_root = 1.0 / math.sqrt(head_size)
    info = []
    for source in range(sources):
        plane = block_ref[source].astype(wide)
        rows = slice(source * token_rows, (source + 1) * token_rows)
        for tile in range(tiles):
            at = slice(tile * token_rows, (tile + 1) * token_rows)
            if tiles == 1:
                put_tiles(seq_scr, rows, plane[at])
            else:
                seq_scr[tile, rows, :] = plane[at]
        info.append(plane[tiles * token_rows : tiles * token_rows + dates_each])
    info = jnp.concatenate(info, axis=0)
    for group in range(groups):
        token_scr[group * length : (group + 1) * length, :] = get_tiles(
            seq_scr, pl.ds(group, length, stride=groups)
        )
    tokens = token_scr[...]
    qkv_scr[...] = matmul(rms_norm(tokens), project_ref[...]).astype(low)
    numbers = info[:, groups : groups + 1] * 32.0 + info[:, groups + 1 : groups + 2]
    key_at = lax.broadcasted_iota(jnp.int32, (length, packed * length), 0)
    column_at = lax.broadcasted_iota(jnp.int32, (length, packed * length), 1)
    same_date = key_at == column_at % length
    query_numbers = jnp.sum(jnp.where(same_date, numbers, 0.0), axis=0, keepdims=True)
    gap_days = jnp.abs(numbers - query_numbers)
    head_at = column_at // length
    mask = block_mask(length, packed, head_size)
    biases = []
    for first in range(0, head_count, packed):
        slope = jnp.full((length, packed * length), slopes_ref[first], wide)
        for head in range(1, packed):
            slope = jnp.where(head_at == head, slopes_ref[first + head], slope)
        biases.append(-slope * gap_days)
    for units in batches(groups, head_count // packed, time_units):
        all_scores = []
        for group, part in units:
            rows = slice(group * length, (group + 1) * length)
            start = part * lanes
            query = qkv_scr[rows, start : start + lanes]
            key = qkv_scr[rows, width + start : width + start + lanes]
            all_scores.append(contract_last(key, spread(query, mask, packed)))
        all_weights = []
        for (group, part), scores in zip(units, all_scores):
            allowed = (info[:, group : group + 1] > 0) | same_date
            scores = jnp.where(allowed, scores * inverse_root + biases[part], masked_score)
            all_weights.append(softmax_first(scores).astype(low))
        all_heads = []
        for (group, part), weights in zip(units, all_weights):
            rows = slice(group * length, (group + 1) * length)
            start = 2 * width + part * lanes
            all_heads.append(contract_rows(weights, qkv_scr[rows, start : start + lanes]))
        for (group, part), full in zip(units, all_heads):
            rows = slice(group * length, (group + 1) * length)
            heads_scr[rows, part * lanes : (part + 1) * lanes] = own_blocks(
                full, length, packed, head_size
            ).astype(low)
    copies = []
    chunk_rows = columns_each * length
    for chunk in range(groups // columns_each):
        rows = slice(chunk * chunk_rows, (chunk + 1) * chunk_rows)
        hidden = token_scr[rows, :] + matmul(heads_scr[rows, :], output_ref[...])
        for column in range(columns_each):
            put_tiles(
                seq_scr,
                pl.ds(chunk * chunk_rows + column, length, stride=columns_each),
                hidden[column * length : (column + 1) * length],
            )
        out_scr[rows, :] = get_tiles(seq_scr, rows).astype(low)
        at = pl.ds(chunk * chunk_rows, chunk_rows)
        copies.append(pltpu.make_async_copy(out_scr.at[at], out_ref.at[at], left.at[chunk]))
        copies[-1].start()
    for copy in copies:
        copy.wait()


def cotangent_kernel(sizes, *refs):
    dates_each, row_parts, rows_each, columns_each, direct = sizes
    output_ref, _, grad_low_ref, heads_grad_ref, grad_scr = refs[-5:]
    width = output_ref.shape[0]
    length = row_parts * rows_each
    groups = dates_each * columns_each
    part_rows = rows_each * groups
    if direct:
        row_ref, own_ref, other_ref = refs[:3]
        own = own_ref[...].astype(wide)
        own = own.reshape(dates_each * rows_each, row_parts, columns_each, width)
        own = jnp.where(row_ref[0] == 0, own[:, 0], own[:, 1]).reshape(part_rows, width)
        put_tiles(grad_scr, slice(0, part_rows), own)
        put_tiles(grad_scr, slice(part_rows, 2 * part_rows), other_ref[...].astype(wide))
    else:
        put_tiles(grad_scr, slice(None), refs[0][...].astype(wide))
    for group in range(groups):
        if direct:
            inner = (group // columns_each) * (rows_each * columns_each) + group % columns_each
            pieces = [
                get_tiles(
                    grad_scr, pl.ds(part * part_rows + inner, rows_each, stride=columns_each)
                )
                for part in range(row_parts)
            ]
            values = jnp.concatenate(pieces, axis=0)
        else:
            first = (group // columns_each) * (length * columns_each) + group % columns_each
            values = get_tiles(grad_scr, pl.ds(first, length, stride=columns_each))
        grad_low_ref[group * length : (group + 1) * length, :] = values.astype(low)
    heads_grad_ref[...] = contract_last(grad_low_ref[...], output_ref[...]).astype(low)


def load_planes(sizes, row_ref, hidden_ref, seq_scr, plane_scr):
    dates_each, row_parts, rows_each, columns_each, direct = sizes
    length = row_parts * rows_each
    groups = dates_each * columns_each
    part_rows = rows_each * groups
    if direct:
        for part in range(row_parts):
            source = pl.multiple_of(((row_ref[0] + part) % row_parts) * part_rows, part_rows)
            put_tiles(
                seq_scr,
                slice(part * part_rows, (part + 1) * part_rows),
                hidden_ref[pl.ds(source, part_rows), :].astype(wide),
            )
    else:
        put_tiles(seq_scr, slice(None), hidden_ref[...].astype(wide))
    for group in range(groups):
        rows = slice(group * length, (group + 1) * length)
        if direct:
            at = pl.ds(group, length, stride=groups)
        else:
            first = (group // columns_each) * (length * columns_each) + group % columns_each
            at = pl.ds(first, length, stride=columns_each)
        plane_scr[rows, :] = get_tiles(seq_scr, at)


def mixed_kernel(sizes, row_ref, hidden_ref, heads_ref, output_ref, _, *refs):
    dates_each, row_parts, rows_each, columns_each, direct = sizes
    *mixed_refs, seq_scr, plane_scr = refs
    length = row_parts * rows_each
    groups = dates_each * columns_each
    part_rows = rows_each * groups
    load_planes(sizes, row_ref, hidden_ref, seq_scr, plane_scr)
    mixed = plane_scr[...] + matmul(heads_ref[...], output_ref[...])
    for group in range(groups):
        inner = (group // columns_each) * (rows_each * columns_each) + group % columns_each
        for part in range(row_parts):
            begin = group * length + part * rows_each
            put_tiles(
                seq_scr,
                pl.ds(part * part_rows + inner, rows_each, stride=columns_each),
                mixed[begin : begin + rows_each],
            )
    if direct:
        kept_ref, sent_ref = mixed_refs
        kept_ref[...] = get_tiles(seq_scr, slice(0, part_rows)).astype(low)
        sent_ref[...] = get_tiles(seq_scr, slice(part_rows, 2 * part_rows)).astype(low)
    else:
        mixed_refs[0][...] = get_tiles(seq_scr, slice(None)).astype(low)


def column_kernel(
    sizes,
    row_ref,
    pair_ref,
    hidden_ref,
    grad_low_scr,
    heads_grad_scr,
    project_ref,
    heads_scr,
    first_grad_ref,
    second_grad_ref,
    seq_scr,
    plane_scr,
    normed_scr,
    qkv_scr,
    qkv_grad_scr,
):
    dates_each, row_parts, rows_each, columns_each, direct, head_count, packed, date_size = sizes
    width = hidden_ref.shape[1]
    head_size = width // head_count
    lanes = packed * head_size
    length = row_parts * rows_each
    groups = dates_each * columns_each
    inverse_root = 1.0 / math.sqrt(head_size)
    load_planes(sizes[:5], row_ref, hidden_ref, seq_scr, plane_scr)
    normed_scr[...] = rms_norm(plane_scr[...])
    qkv_scr[...] = matmul(normed_scr[...], project_ref[...]).astype(low)
    mask = block_mask(length, packed, head_size)
    for units in batches(groups, head_count // packed, column_units):
        places = []
        for group, part in units:
            start = part * lanes
            places.append(
                (
                    slice(group * length, (group + 1) * length),
                    slice(start, start + lanes),
                    slice(width + start, width + start + lanes),
                    slice(2 * width + start, 2 * width + start + lanes),
                )
            )
        all_scores = []
        for rows, at_query, at_key, at_value in places:
            query = spread(qkv_scr[rows, at_query], mask, packed)
            heads_grad = spread(heads_grad_scr[rows, at_query], mask, packed)
            all_scores.append(
                (
                    contract_last(qkv_scr[rows, at_key], query),
                    contract_last(qkv_scr[rows, at_value], heads_grad),
                )
            )
        all_weights = []
        for scores, product_grad in all_scores:
            weights = softmax_first(scores * inverse_root)
            score_grad = weights * (
                product_grad - jnp.sum(weights * product_grad, axis=0, keepdims=True)
            )
            all_weights.append((weights.astype(low), score_grad.astype(low)))
        all_full = []
        for (rows, at_query, at_key, at_value), (weights, score_low) in zip(places, all_weights):
            all_full.append(
                (
                    contract_rows(weights, qkv_scr[rows, at_value]),
                    contract_rows(score_low, qkv_scr[rows, at_key]),
                )
            )
            query = spread(qkv_scr[rows, at_query], mask, packed)
            heads_grad = spread(heads_grad_scr[rows, at_query], mask, packed)
            key_grad = matmul(score_low, query) * inverse_root
            qkv_grad_scr[rows, at_key] = key_grad.astype(low)
            qkv_grad_scr[rows, at_value] = matmul(weights, heads_grad).astype(low)
        for (rows, at_query, _, _), (heads_full, query_full) in zip(places, all_full):
            heads = own_blocks(heads_full, length, packed, head_size)
            heads_scr[rows, at_query] = heads.astype(low)
            query_grad = own_blocks(query_full, length, packed, head_size) * inverse_root
            qkv_grad_scr[rows, at_query] = query_grad.astype(low)
    project_grad = contract_rows(qkv_grad_scr[...], normed_scr[...])
    output_grad = contract_rows(grad_low_scr[...], heads_scr[...])
    if not direct:
        first_grad_ref[...] = project_grad
        second_grad_ref[...] = output_grad
        return
    keep_ref, send_ref = first_grad_ref, second_grad_ref
    even = pair_ref[0] == 0
    project_each = project_grad.shape[0] // date_size
    output_each = output_grad.shape[0] // date_size
    half = (project_each + output_each) // 2
    lower = lax.broadcasted_iota(jnp.int32, (half, 128), 1) < 64
    for outer in range(date_size // 2):
        pair = []
        for part in (2 * outer, 2 * outer + 1):
            block = jnp.concatenate(
                [
                    project_grad[part * project_each : (part + 1) * project_each],
                    output_grad[part * output_each : (part + 1) * output_each],
                ],
                axis=0,
            )
            top, bottom = block[:half, 128:256], block[half:, 128:256]
            pair.append(
                (
                    (block[:, :128], jnp.where(lower, top, pltpu.roll(bottom, 64, 1))),
                    (block[:, 256:], jnp.where(lower, pltpu.roll(top, 64, 1), bottom)),
                )
            )
        for row_part in range(2):
            for first, one, two in zip((0, 2 * half), pair[0][row_part], pair[1][row_part]):
                place = (row_part, outer, slice(first, first + one.shape[0]))
                keep_ref[place] = jnp.where(even, one, two).astype(low)
                send_ref[place] = jnp.where(even, two, one).astype(low)


def pair_kernel(row_ref, mid_ref, kept_ref, came_ref, own_ref, mid_out, row_out, both_out):
    row, mid = row_ref[0], mid_ref[0]
    for outer in range(own_ref.shape[0]):
        for out_ref, row_at, mid_at in (
            (mid_out, row, 1 - mid),
            (row_out, 1 - row, mid),
            (both_out, 1 - row, 1 - mid),
            (own_ref, row, mid),
        ):
            place = (row_at, 2 * outer + mid_at)
            out_ref[outer] = (kept_ref[place].astype(wide) + came_ref[place].astype(wide)).astype(
                low
            )


def spread_kernel(outer_ref, own_ref, mid_ref, row_ref, both_ref, sent_ref, leave_ref, *refs):
    leave_ref[...] = sent_ref[...]
    count = own_ref.shape[0]
    for step in range(count):
        at = outer_ref[0] ^ step
        total = own_ref[at].astype(wide) + mid_ref[at].astype(wide)
        total = total + (row_ref[at].astype(wide) + both_ref[at].astype(wide))
        refs[step][...] = total.astype(low)


def finish_kernel(project_each, row_ref, *refs):
    *terms, _, project_ref, output_ref = refs
    total = terms[0][...].astype(wide)
    for term in terms[1:]:
        total = total + term[...].astype(wide)
    whole = 2 * total.shape[0] // 3
    main = total[:whole]
    tail = total[whole:]
    swapped = pltpu.roll(tail, 64, 1)
    lower = lax.broadcasted_iota(jnp.int32, (whole, 128), 1) < 64
    tail_first = jnp.concatenate([tail, swapped], axis=0)
    turned = pltpu.roll(main, 64, 1)
    front = jnp.concatenate([main, tail_first[:, :64]], axis=1)
    back = jnp.concatenate([jnp.where(lower, tail_first, turned), turned[:, :64]], axis=1)
    owned = jnp.where(row_ref[0] == 0, front, back)
    project_ref[...] = owned[:project_each]
    output_ref[...] = owned[project_each:]


def body(
    row_size,
    date_size,
    tokens,
    clear_flags,
    date_numbers,
    decay_slopes,
    time_project,
    time_output,
    column_project,
    column_output,
    cotangent,
):
    date_local, row_local, column_count, width = tokens.shape
    head_count = decay_slopes.shape[0]
    head_size = width // head_count
    packed = max(1, 128 // head_size)
    local_patches = row_local * column_count
    patches_each = local_patches // date_size
    columns_each = column_count // row_size
    row_count = row_local * row_size
    date_count = date_local * date_size
    project_each = 3 * width // date_size
    output_each = width // date_size
    lane_each = width // row_size
    direct = (
        patches_each == column_count
        and column_count % 16 == 0
        and date_size % 8 == 0
        and date_size & (date_size - 1) == 0
        and row_size == 2
        and lane_each == 192
        and project_each % 8 == 0
        and output_each % 8 == 0
        and (project_each + output_each) % 32 == 0
    )
    token_rows = date_local * patches_each
    block_rows = -(-(token_rows + date_local) // 8) * 8
    tile_rows = (width // 128) * token_rows + -(-date_local // 8) * 8
    params = pltpu.CompilerParams(vmem_limit_bytes=vmem_limit)
    in_vmem = pl.BlockSpec(memory_space=pltpu.VMEM)
    in_smem = pl.BlockSpec(memory_space=pltpu.SMEM)
    in_any = pl.BlockSpec(memory_space=pl.ANY)
    swap = [(0, 1), (1, 0)]
    column_tokens = date_local * row_count * columns_each
    half_tokens = column_tokens // row_size
    if direct:
        outgoing = pl.pallas_call(
            pack_kernel,
            out_shape=jax.ShapeDtypeStruct((date_size, tile_rows, 128), low),
            in_specs=[pl.BlockSpec(memory_space=pltpu.HBM)] * 3,
            out_specs=pl.BlockSpec(memory_space=pltpu.HBM),
            scratch_shapes=[
                pltpu.SMEM(date_numbers.shape, jnp.int32),
                pltpu.VMEM(tokens.shape, low),
                pltpu.VMEM(clear_flags.shape, jnp.int32),
                pltpu.VMEM((date_size, tile_rows, 128), low),
                pltpu.SemaphoreType.DMA((2,)),
                pltpu.SemaphoreType.DMA((4,)),
                pltpu.SemaphoreType.DMA((4,)),
            ],
            name="pack_tokens",
        )(date_numbers, tokens, clear_flags)
        row_at = lax.axis_index("row")
        halves = cotangent.reshape(date_local, row_local, row_size, columns_each, width)
        leaving = lax.dynamic_index_in_dim(halves, 1 - row_at, 2, keepdims=False)
        other_grad = lax.ppermute(leaving, "row", swap)
    else:
        flags = jnp.transpose(
            clear_flags.reshape(date_local, date_size, patches_each), (1, 0, 2)
        ).astype(low)
        numbers = jnp.stack([date_numbers // 32, date_numbers % 32], axis=-1).astype(low)
        numbers = jnp.broadcast_to(numbers[None], (date_size, date_local, 2))
        info = jnp.concatenate([flags, numbers], axis=-1)
        info = jnp.pad(
            info, ((0, 0), (0, block_rows - token_rows - date_local), (0, width - patches_each - 2))
        )
        outgoing = jnp.transpose(
            tokens.reshape(date_local, date_size, patches_each, width), (1, 0, 2, 3)
        ).reshape(date_size, token_rows, width)
        outgoing = jnp.concatenate([outgoing, info], axis=1)
    incoming = lax.all_to_all(outgoing, dates, split_axis=0, concat_axis=0, tiled=True)

    if direct:
        grads_in = (
            row_at.reshape(1),
            cotangent.reshape(local_patches * date_local, width),
            other_grad.reshape(half_tokens, width),
        )
        in_specs = [in_smem] + [in_vmem] * 3 + [in_any]
    else:
        grads_in = (
            lax.all_to_all(cotangent, "row", split_axis=2, concat_axis=1, tiled=True).reshape(
                column_tokens, width
            ),
        )
        in_specs = [in_vmem] * 2 + [in_any]
    time_tokens = date_count * patches_each
    hidden = pl.pallas_call(
        functools.partial(
            time_kernel,
            (
                date_size,
                date_local,
                patches_each,
                head_count,
                packed,
                columns_each if direct else patches_each,
            ),
        ),
        out_shape=jax.ShapeDtypeStruct((time_tokens, width), low),
        in_specs=[in_smem, in_vmem, in_vmem, in_vmem, in_any],
        out_specs=pl.BlockSpec(memory_space=pltpu.HBM),
        scratch_shapes=[
            pltpu.VMEM((width // 128, time_tokens, 128), wide),
            pltpu.VMEM((time_tokens, width), wide),
            pltpu.VMEM((time_tokens, 3 * width), low),
            pltpu.VMEM((time_tokens, width), low),
            pltpu.VMEM((time_tokens, width), low),
            pltpu.SemaphoreType.DMA((patches_each // (columns_each if direct else patches_each),)),
        ],
        compiler_params=params,
        name="time_attention",
    )(decay_slopes, incoming, time_project, time_output, grads_in[-1])

    grad_low, heads_grad = pl.pallas_call(
        functools.partial(
            cotangent_kernel, (date_local, row_size, row_local, columns_each, direct)
        ),
        out_shape=(
            jax.ShapeDtypeStruct((column_tokens, width), low),
            jax.ShapeDtypeStruct((column_tokens, width), low),
        ),
        in_specs=in_specs,
        scratch_shapes=[pltpu.VMEM((width // 128, column_tokens, 128), wide)],
        compiler_params=params,
        name="cotangent_heads",
    )(*grads_in, column_output, hidden)

    if direct:
        parts = hidden.reshape(row_size * date_size, date_local * columns_each, width)
        plane = lax.all_to_all(parts, ("row", *dates), split_axis=0, concat_axis=0, tiled=True)
    else:
        parts = hidden.reshape(date_size, date_local, patches_each, width)
        back = lax.all_to_all(parts, dates, split_axis=0, concat_axis=0, tiled=True)
        back = jnp.transpose(back, (1, 0, 2, 3)).reshape(
            date_local, row_local, column_count, width
        )
        plane = lax.all_to_all(back, "row", split_axis=2, concat_axis=1, tiled=True)
    plane = plane.reshape(column_tokens, width)
    half_shape = jax.ShapeDtypeStruct((half_tokens, width), low)
    packed_rows = (project_each + output_each) * 3 // 2
    row_one = lax.axis_index("row").reshape(1)
    pair_one = lax.axis_index("pair").reshape(1)
    sizes = (date_local, row_size, row_local, columns_each, direct)
    if direct:
        half_grads = jax.ShapeDtypeStruct((row_size, date_size // 2, packed_rows, 128), low)
        grad_shapes = (half_grads, half_grads)
        mixed_shapes = (half_shape, half_shape)
    else:
        grad_shapes = (
            jax.ShapeDtypeStruct((3 * width, width), wide),
            jax.ShapeDtypeStruct((width, width), wide),
        )
        mixed_shapes = (jax.ShapeDtypeStruct((column_tokens, width), low),)
    column_heads, first_grad, second_grad = pl.pallas_call(
        functools.partial(column_kernel, (*sizes, head_count, packed, date_size)),
        out_shape=(jax.ShapeDtypeStruct((column_tokens, width), low), *grad_shapes),
        in_specs=[in_smem] * 2 + [in_vmem] * 4,
        input_output_aliases={4: 0},
        scratch_shapes=[
            pltpu.VMEM((width // 128, column_tokens, 128), wide),
            pltpu.VMEM((column_tokens, width), wide),
            pltpu.VMEM((column_tokens, width), low),
            pltpu.VMEM((column_tokens, 3 * width), low),
            pltpu.VMEM((column_tokens, 3 * width), low),
        ],
        compiler_params=params,
        name="column_attention",
    )(row_one, pair_one, plane, grad_low, heads_grad, column_project)
    own_grad = first_grad
    if direct:
        came = lax.ppermute(second_grad, "pair", swap)
        outers = date_size // 4
        block = jax.ShapeDtypeStruct((packed_rows, 128), low)
        blocks = jax.ShapeDtypeStruct((outers, packed_rows, 128), low)
        own_grad, mid_grad, row_grad, both_grad = pl.pallas_call(
            pair_kernel,
            out_shape=(blocks,) * 4,
            in_specs=[in_smem] * 2 + [in_vmem] * 2,
            out_specs=(in_vmem,) * 4,
            compiler_params=params,
            name="pair_gradients",
        )(row_one, lax.axis_index("mid").reshape(1), first_grad, came)
        both_grad = lax.ppermute(both_grad, ("mid", "row"), [(0, 3), (3, 0), (1, 2), (2, 1)])
        mid_grad = lax.ppermute(mid_grad, "mid", swap)
        row_grad = lax.ppermute(row_grad, "row", swap)
    mixed = pl.pallas_call(
        functools.partial(mixed_kernel, sizes),
        out_shape=mixed_shapes,
        in_specs=[in_smem] + [in_vmem] * 3 + [in_any],
        scratch_shapes=[
            pltpu.VMEM((width // 128, column_tokens, 128), wide),
            pltpu.VMEM((column_tokens, width), wide),
        ],
        compiler_params=params,
        name="mixed_tokens",
    )(row_one, plane, column_heads, column_output, own_grad)

    if direct:
        kept, sent = mixed
        leaving, *steps = pl.pallas_call(
            spread_kernel,
            out_shape=(half_shape,) + (block,) * outers,
            in_specs=[in_smem] + [in_vmem] * 5,
            compiler_params=params,
            name="spread_gradients",
        )(lax.axis_index("outer").reshape(1), own_grad, mid_grad, row_grad, both_grad, sent)
        terms = [steps[0]]
        for step in range(1, outers):
            route = [(at, at ^ step) for at in range(outers)]
            terms.append(lax.ppermute(steps[step], "outer", route))
        arrived = lax.ppermute(leaving, "row", swap)
        quarter = (date_local, row_local, 1, columns_each, width)
        kept, arrived = kept.reshape(quarter), arrived.reshape(quarter)
        mixed = jnp.concatenate(
            [jnp.where(row_at == 0, kept, arrived), jnp.where(row_at == 0, arrived, kept)], axis=2
        )
        owned_project, owned_output = pl.pallas_call(
            functools.partial(finish_kernel, project_each),
            out_shape=(
                jax.ShapeDtypeStruct((project_each, lane_each), wide),
                jax.ShapeDtypeStruct((output_each, lane_each), wide),
            ),
            in_specs=[in_smem] + [in_vmem] * outers + [in_any],
            compiler_params=params,
            name="gradient_sum",
        )(row_one, *terms, mixed)
    else:
        mixed = mixed[0]
        grads = jnp.concatenate(
            [
                first_grad.reshape(date_size, project_each, row_size, lane_each),
                second_grad.reshape(date_size, output_each, row_size, lane_each),
            ],
            axis=1,
        ).astype(low)
        grads = jnp.transpose(grads, (2, 0, 1, 3)).reshape(
            row_size * date_size, project_each + output_each, lane_each
        )
        terms = lax.all_to_all(grads, ("row", *dates), split_axis=0, concat_axis=0, tiled=True)
        owned = jnp.sum(terms.astype(wide), axis=0)
        owned_project, owned_output = owned[:project_each], owned[project_each:]
        mixed = mixed.reshape(row_size, date_local, row_local, columns_each, width)
        mixed = lax.all_to_all(mixed, "row", split_axis=0, concat_axis=0, tiled=True)
        mixed = jnp.transpose(mixed, (1, 2, 0, 3, 4))
    mixed = mixed.reshape(date_local, row_local, column_count, width)
    return (mixed, jnp.transpose(owned_project), jnp.transpose(owned_output))


def solution(mesh):
    date_size, row_size = mesh.shape["date"], mesh.shape["row"]
    pair_size = 2 if date_size % 2 == 0 else 1
    mid_size = 2 if date_size % 4 == 0 else 1
    split = jax.sharding.Mesh(
        mesh.devices.reshape(-1, mid_size, pair_size, row_size), ("outer", "mid", "pair", "row")
    )
    return jax.shard_map(
        functools.partial(body, row_size, date_size),
        mesh=split,
        in_specs=(
            P(dates, "row", None, None),
            P(dates, "row", None),
            P(dates),
            P(),
            P(),
            P(),
            P(),
            P(),
            P(dates, "row", None, None),
        ),
        out_specs=(P(dates, "row", None, None), P("row", dates), P("row", dates)),
        check_vma=False,
    )
```

```python
import functools
import math

import jax
import jax.numpy as jnp
from jax import lax
from jax.experimental import pallas as pl
from jax.experimental.pallas import tpu as pltpu
from jax.sharding import PartitionSpec as P

epsilon = 1e-06
masked_score = -1e30
time_units = 48
column_units = 24
dates = ("outer", "mid", "pair")
vmem_limit = 12 * 1024 * 1024
low = jnp.bfloat16
wide = jnp.float32


def rms_norm(values):
    factor = lax.rsqrt(jnp.mean(values * values, axis=-1, keepdims=True) + epsilon)
    return (values * factor).astype(low)


def matmul(left, right):
    return jnp.dot(left, right, preferred_element_type=wide)


def contract_rows(left, right):
    return lax.dot_general(left, right, (((0,), (0,)), ((), ())), preferred_element_type=wide)


def contract_last(left, right):
    return lax.dot_general(left, right, (((1,), (1,)), ((), ())), preferred_element_type=wide)


def block_mask(length, packed, head_size):
    shape = (packed * length, packed * head_size)
    rows = lax.broadcasted_iota(jnp.int32, shape, 0) // length
    lanes = lax.broadcasted_iota(jnp.int32, shape, 1) // head_size
    return jnp.where(rows == lanes, 1.0, 0.0).astype(low)


def spread(values, mask, packed):
    return jnp.concatenate([values] * packed, axis=0) * mask


def batches(groups, parts, each):
    units = [(group, part) for group in range(groups) for part in range(parts)]
    return [units[first : first + each] for first in range(0, len(units), each)]


def own_blocks(full, length, packed, head_size):
    lanes = lax.broadcasted_iota(jnp.int32, (length, packed * head_size), 1) // head_size
    out = full[:length]
    for head in range(1, packed):
        out = jnp.where(lanes == head, full[head * length : (head + 1) * length], out)
    return out


def softmax_first(scores):
    raised = jnp.exp(scores - jnp.max(scores, axis=0, keepdims=True))
    return raised * (1.0 / jnp.sum(raised, axis=0, keepdims=True))


def put_tiles(scratch, rows, values):
    tiles, _, lanes = scratch.shape
    for tile in range(tiles):
        scratch[tile, rows, :] = values[:, tile * lanes : (tile + 1) * lanes]


def get_tiles(scratch, rows):
    return jnp.concatenate([scratch[tile, rows, :] for tile in range(scratch.shape[0])], axis=-1)


def pack_kernel(
    numbers_ref,
    tokens_ref,
    flags_ref,
    out_ref,
    numbers_scr,
    tokens_scr,
    flags_scr,
    out_scr,
    small_copied,
    came,
    left,
):
    dates_each, parts, patches, width = tokens_ref.shape
    chunks = came.shape[0]
    each = parts // chunks
    small = [
        pltpu.make_async_copy(flags_ref, flags_scr, small_copied.at[0]),
        pltpu.make_async_copy(numbers_ref, numbers_scr, small_copied.at[1]),
    ]
    arrivals, departures = [], []
    for chunk in range(chunks):
        at = pl.ds(chunk * each, each)
        arrivals.append(
            pltpu.make_async_copy(tokens_ref.at[:, at], tokens_scr.at[:, at], came.at[chunk])
        )
        departures.append(pltpu.make_async_copy(out_scr.at[at], out_ref.at[at], left.at[chunk]))
    for copy in small + arrivals:
        copy.start()
    lanes = out_ref.shape[2]
    tiles = width // lanes
    spare = out_ref.shape[1] - tiles * dates_each * patches
    place = lax.broadcasted_iota(jnp.int32, (patches, lanes), 0)
    lane = lax.broadcasted_iota(jnp.int32, (patches, lanes), 1)
    place = jnp.where(place == lane, 1.0, 0.0).astype(low)
    lane = lax.broadcasted_iota(jnp.int32, (parts, lanes), 1)
    row = lax.broadcasted_iota(jnp.int32, (spare, lanes), 0)
    for copy in small:
        copy.wait()
    infos = []
    for date in range(dates_each):
        number = numbers_scr[date]
        upper = (number // 32).astype(wide)
        under = (number % 32).astype(wide)
        info = matmul(flags_scr[date].astype(wide).astype(low), place)
        info = jnp.where(lane == patches, upper, info)
        infos.append(jnp.where(lane == patches + 1, under, info))
    for chunk in range(chunks):
        arrivals[chunk].wait()
        for part in range(chunk * each, (chunk + 1) * each):
            tokens = jnp.concatenate(
                [tokens_scr[date, part].astype(wide) for date in range(dates_each)], axis=0
            )
            extra = jnp.zeros((spare, lanes), wide)
            for date in range(dates_each):
                extra = jnp.where(row == date, infos[date][part : part + 1], extra)
            pieces = [tokens[:, tile * lanes : (tile + 1) * lanes] for tile in range(tiles)]
            out_scr[part] = jnp.concatenate(pieces + [extra], axis=0).astype(low)
        departures[chunk].start()
    for copy in departures:
        copy.wait()


def time_kernel(
    sizes,
    slopes_ref,
    block_ref,
    project_ref,
    output_ref,
    earlier_ref,
    out_ref,
    seq_scr,
    token_scr,
    qkv_scr,
    heads_scr,
):
    sources, dates_each, groups, head_count, packed, columns_each = sizes
    width = project_ref.shape[0]
    tile_lanes = block_ref.shape[2]
    tiles = width // tile_lanes
    head_size = width // head_count
    lanes = packed * head_size
    length = sources * dates_each
    token_rows = dates_each * groups
    inverse_root = 1.0 / math.sqrt(head_size)
    info = []
    for source in range(sources):
        plane = block_ref[source].astype(wide)
        rows = slice(source * token_rows, (source + 1) * token_rows)
        for tile in range(tiles):
            at = slice(tile * token_rows, (tile + 1) * token_rows)
            if tiles == 1:
                put_tiles(seq_scr, rows, plane[at])
            else:
                seq_scr[tile, rows, :] = plane[at]
        info.append(plane[tiles * token_rows : tiles * token_rows + dates_each])
    info = jnp.concatenate(info, axis=0)
    for group in range(groups):
        token_scr[group * length : (group + 1) * length, :] = get_tiles(
            seq_scr, pl.ds(group, length, stride=groups)
        )
    tokens = token_scr[...]
    qkv_scr[...] = matmul(rms_norm(tokens), project_ref[...]).astype(low)
    numbers = info[:, groups : groups + 1] * 32.0 + info[:, groups + 1 : groups + 2]
    key_at = lax.broadcasted_iota(jnp.int32, (length, packed * length), 0)
    column_at = lax.broadcasted_iota(jnp.int32, (length, packed * length), 1)
    same_date = key_at == column_at % length
    query_numbers = jnp.sum(jnp.where(same_date, numbers, 0.0), axis=0, keepdims=True)
    gap_days = jnp.abs(numbers - query_numbers)
    head_at = column_at // length
    mask = block_mask(length, packed, head_size)
    biases = []
    for first in range(0, head_count, packed):
        slope = jnp.full((length, packed * length), slopes_ref[first], wide)
        for head in range(1, packed):
            slope = jnp.where(head_at == head, slopes_ref[first + head], slope)
        biases.append(-slope * gap_days)
    for units in batches(groups, head_count // packed, time_units):
        all_scores = []
        for group, part in units:
            rows = slice(group * length, (group + 1) * length)
            start = part * lanes
            query = qkv_scr[rows, start : start + lanes]
            key = qkv_scr[rows, width + start : width + start + lanes]
            all_scores.append(contract_last(key, spread(query, mask, packed)))
        all_weights = []
        for (group, part), scores in zip(units, all_scores):
            allowed = (info[:, group : group + 1] > 0) | same_date
            scores = jnp.where(allowed, scores * inverse_root + biases[part], masked_score)
            all_weights.append(softmax_first(scores).astype(low))
        all_heads = []
        for (group, part), weights in zip(units, all_weights):
            rows = slice(group * length, (group + 1) * length)
            start = 2 * width + part * lanes
            all_heads.append(contract_rows(weights, qkv_scr[rows, start : start + lanes]))
        for (group, part), full in zip(units, all_heads):
            rows = slice(group * length, (group + 1) * length)
            heads_scr[rows, part * lanes : (part + 1) * lanes] = own_blocks(
                full, length, packed, head_size
            ).astype(low)
    hidden = token_scr[...] + matmul(heads_scr[...], output_ref[...])
    for group in range(groups):
        first = (group // columns_each) * (length * columns_each) + group % columns_each
        put_tiles(
            seq_scr,
            pl.ds(first, length, stride=columns_each),
            hidden[group * length : (group + 1) * length],
        )
    out_ref[...] = get_tiles(seq_scr, slice(None)).astype(low)


def cotangent_kernel(sizes, *refs):
    dates_each, row_parts, rows_each, columns_each, direct = sizes
    output_ref, _, grad_low_ref, heads_grad_ref, grad_scr = refs[-5:]
    width = output_ref.shape[0]
    length = row_parts * rows_each
    groups = dates_each * columns_each
    part_rows = rows_each * groups
    if direct:
        row_ref, own_ref, other_ref = refs[:3]
        own = own_ref[...].astype(wide)
        own = own.reshape(dates_each * rows_each, row_parts, columns_each, width)
        own = jnp.where(row_ref[0] == 0, own[:, 0], own[:, 1]).reshape(part_rows, width)
        put_tiles(grad_scr, slice(0, part_rows), own)
        put_tiles(grad_scr, slice(part_rows, 2 * part_rows), other_ref[...].astype(wide))
    else:
        put_tiles(grad_scr, slice(None), refs[0][...].astype(wide))
    for group in range(groups):
        if direct:
            inner = (group // columns_each) * (rows_each * columns_each) + group % columns_each
            pieces = [
                get_tiles(
                    grad_scr, pl.ds(part * part_rows + inner, rows_each, stride=columns_each)
                )
                for part in range(row_parts)
            ]
            values = jnp.concatenate(pieces, axis=0)
        else:
            first = (group // columns_each) * (length * columns_each) + group % columns_each
            values = get_tiles(grad_scr, pl.ds(first, length, stride=columns_each))
        grad_low_ref[group * length : (group + 1) * length, :] = values.astype(low)
    heads_grad_ref[...] = contract_last(grad_low_ref[...], output_ref[...]).astype(low)


def load_planes(sizes, row_ref, hidden_ref, seq_scr, plane_scr):
    dates_each, row_parts, rows_each, columns_each, direct = sizes
    length = row_parts * rows_each
    groups = dates_each * columns_each
    part_rows = rows_each * groups
    if direct:
        for part in range(row_parts):
            source = pl.multiple_of(((row_ref[0] + part) % row_parts) * part_rows, part_rows)
            put_tiles(
                seq_scr,
                slice(part * part_rows, (part + 1) * part_rows),
                hidden_ref[pl.ds(source, part_rows), :].astype(wide),
            )
    else:
        put_tiles(seq_scr, slice(None), hidden_ref[...].astype(wide))
    for group in range(groups):
        rows = slice(group * length, (group + 1) * length)
        if direct:
            at = pl.ds(group, length, stride=groups)
        else:
            first = (group // columns_each) * (length * columns_each) + group % columns_each
            at = pl.ds(first, length, stride=columns_each)
        plane_scr[rows, :] = get_tiles(seq_scr, at)


def mixed_kernel(sizes, row_ref, hidden_ref, heads_ref, output_ref, _, *refs):
    dates_each, row_parts, rows_each, columns_each, direct = sizes
    *mixed_refs, seq_scr, plane_scr = refs
    length = row_parts * rows_each
    groups = dates_each * columns_each
    part_rows = rows_each * groups
    load_planes(sizes, row_ref, hidden_ref, seq_scr, plane_scr)
    mixed = plane_scr[...] + matmul(heads_ref[...], output_ref[...])
    for group in range(groups):
        inner = (group // columns_each) * (rows_each * columns_each) + group % columns_each
        for part in range(row_parts):
            begin = group * length + part * rows_each
            put_tiles(
                seq_scr,
                pl.ds(part * part_rows + inner, rows_each, stride=columns_each),
                mixed[begin : begin + rows_each],
            )
    if direct:
        kept_ref, sent_ref = mixed_refs
        kept_ref[...] = get_tiles(seq_scr, slice(0, part_rows)).astype(low)
        sent_ref[...] = get_tiles(seq_scr, slice(part_rows, 2 * part_rows)).astype(low)
    else:
        mixed_refs[0][...] = get_tiles(seq_scr, slice(None)).astype(low)


def column_kernel(
    sizes,
    row_ref,
    pair_ref,
    hidden_ref,
    grad_low_scr,
    heads_grad_scr,
    project_ref,
    heads_scr,
    first_grad_ref,
    second_grad_ref,
    seq_scr,
    plane_scr,
    normed_scr,
    qkv_scr,
    qkv_grad_scr,
):
    dates_each, row_parts, rows_each, columns_each, direct, head_count, packed, date_size = sizes
    width = hidden_ref.shape[1]
    head_size = width // head_count
    lanes = packed * head_size
    length = row_parts * rows_each
    groups = dates_each * columns_each
    inverse_root = 1.0 / math.sqrt(head_size)
    load_planes(sizes[:5], row_ref, hidden_ref, seq_scr, plane_scr)
    normed_scr[...] = rms_norm(plane_scr[...])
    qkv_scr[...] = matmul(normed_scr[...], project_ref[...]).astype(low)
    mask = block_mask(length, packed, head_size)
    for units in batches(groups, head_count // packed, column_units):
        places = []
        for group, part in units:
            start = part * lanes
            places.append(
                (
                    slice(group * length, (group + 1) * length),
                    slice(start, start + lanes),
                    slice(width + start, width + start + lanes),
                    slice(2 * width + start, 2 * width + start + lanes),
                )
            )
        all_scores = []
        for rows, at_query, at_key, at_value in places:
            query = spread(qkv_scr[rows, at_query], mask, packed)
            heads_grad = spread(heads_grad_scr[rows, at_query], mask, packed)
            all_scores.append(
                (
                    contract_last(qkv_scr[rows, at_key], query),
                    contract_last(qkv_scr[rows, at_value], heads_grad),
                )
            )
        all_weights = []
        for scores, product_grad in all_scores:
            weights = softmax_first(scores * inverse_root)
            score_grad = weights * (
                product_grad - jnp.sum(weights * product_grad, axis=0, keepdims=True)
            )
            all_weights.append((weights.astype(low), score_grad.astype(low)))
        all_full = []
        for (rows, at_query, at_key, at_value), (weights, score_low) in zip(places, all_weights):
            all_full.append(
                (
                    contract_rows(weights, qkv_scr[rows, at_value]),
                    contract_rows(score_low, qkv_scr[rows, at_key]),
                )
            )
            query = spread(qkv_scr[rows, at_query], mask, packed)
            heads_grad = spread(heads_grad_scr[rows, at_query], mask, packed)
            key_grad = matmul(score_low, query) * inverse_root
            qkv_grad_scr[rows, at_key] = key_grad.astype(low)
            qkv_grad_scr[rows, at_value] = matmul(weights, heads_grad).astype(low)
        for (rows, at_query, _, _), (heads_full, query_full) in zip(places, all_full):
            heads = own_blocks(heads_full, length, packed, head_size)
            heads_scr[rows, at_query] = heads.astype(low)
            query_grad = own_blocks(query_full, length, packed, head_size) * inverse_root
            qkv_grad_scr[rows, at_query] = query_grad.astype(low)
    project_grad = contract_rows(qkv_grad_scr[...], normed_scr[...])
    output_grad = contract_rows(grad_low_scr[...], heads_scr[...])
    if not direct:
        first_grad_ref[...] = project_grad
        second_grad_ref[...] = output_grad
        return
    keep_ref, send_ref = first_grad_ref, second_grad_ref
    even = pair_ref[0] == 0
    project_each = project_grad.shape[0] // date_size
    output_each = output_grad.shape[0] // date_size
    half = (project_each + output_each) // 2
    lower = lax.broadcasted_iota(jnp.int32, (half, 128), 1) < 64
    for outer in range(date_size // 2):
        pair = []
        for part in (2 * outer, 2 * outer + 1):
            block = jnp.concatenate(
                [
                    project_grad[part * project_each : (part + 1) * project_each],
                    output_grad[part * output_each : (part + 1) * output_each],
                ],
                axis=0,
            )
            top, bottom = block[:half, 128:256], block[half:, 128:256]
            pair.append(
                (
                    (block[:, :128], jnp.where(lower, top, pltpu.roll(bottom, 64, 1))),
                    (block[:, 256:], jnp.where(lower, pltpu.roll(top, 64, 1), bottom)),
                )
            )
        for row_part in range(2):
            for first, one, two in zip((0, 2 * half), pair[0][row_part], pair[1][row_part]):
                place = (row_part, outer, slice(first, first + one.shape[0]))
                keep_ref[place] = jnp.where(even, one, two).astype(low)
                send_ref[place] = jnp.where(even, two, one).astype(low)


def pair_kernel(row_ref, mid_ref, kept_ref, came_ref, own_ref, mid_out, row_out, both_out):
    row, mid = row_ref[0], mid_ref[0]
    for outer in range(own_ref.shape[0]):
        for out_ref, row_at, mid_at in (
            (mid_out, row, 1 - mid),
            (row_out, 1 - row, mid),
            (both_out, 1 - row, 1 - mid),
            (own_ref, row, mid),
        ):
            place = (row_at, 2 * outer + mid_at)
            out_ref[outer] = (kept_ref[place].astype(wide) + came_ref[place].astype(wide)).astype(
                low
            )


def spread_kernel(outer_ref, own_ref, row_ref, both_ref, mid_ref, sent_ref, leave_ref, *refs):
    leave_ref[...] = sent_ref[...]
    count = own_ref.shape[0]
    for step in range(count):
        at = outer_ref[0] ^ step
        total = own_ref[at].astype(wide) + mid_ref[at].astype(wide)
        total = total + (row_ref[at].astype(wide) + both_ref[at].astype(wide))
        refs[step][...] = total.astype(low)


def finish_kernel(project_each, row_ref, *refs):
    *terms, _, project_ref, output_ref = refs
    total = terms[0][...].astype(wide)
    for term in terms[1:]:
        total = total + term[...].astype(wide)
    whole = 2 * total.shape[0] // 3
    main = total[:whole]
    tail = total[whole:]
    swapped = pltpu.roll(tail, 64, 1)
    lower = lax.broadcasted_iota(jnp.int32, (whole, 128), 1) < 64
    tail_first = jnp.concatenate([tail, swapped], axis=0)
    turned = pltpu.roll(main, 64, 1)
    front = jnp.concatenate([main, tail_first[:, :64]], axis=1)
    back = jnp.concatenate([jnp.where(lower, tail_first, turned), turned[:, :64]], axis=1)
    owned = jnp.where(row_ref[0] == 0, front, back)
    project_ref[...] = owned[:project_each]
    output_ref[...] = owned[project_each:]


def body(
    row_size,
    date_size,
    tokens,
    clear_flags,
    date_numbers,
    decay_slopes,
    time_project,
    time_output,
    column_project,
    column_output,
    cotangent,
):
    date_local, row_local, column_count, width = tokens.shape
    head_count = decay_slopes.shape[0]
    head_size = width // head_count
    packed = max(1, 128 // head_size)
    local_patches = row_local * column_count
    patches_each = local_patches // date_size
    columns_each = column_count // row_size
    row_count = row_local * row_size
    date_count = date_local * date_size
    project_each = 3 * width // date_size
    output_each = width // date_size
    lane_each = width // row_size
    direct = (
        patches_each == column_count
        and column_count % 16 == 0
        and date_size % 8 == 0
        and date_size & (date_size - 1) == 0
        and row_size == 2
        and lane_each == 192
        and project_each % 8 == 0
        and output_each % 8 == 0
        and (project_each + output_each) % 32 == 0
    )
    token_rows = date_local * patches_each
    block_rows = -(-(token_rows + date_local) // 8) * 8
    tile_rows = (width // 128) * token_rows + -(-date_local // 8) * 8
    params = pltpu.CompilerParams(vmem_limit_bytes=vmem_limit)
    in_vmem = pl.BlockSpec(memory_space=pltpu.VMEM)
    in_smem = pl.BlockSpec(memory_space=pltpu.SMEM)
    in_any = pl.BlockSpec(memory_space=pl.ANY)
    swap = [(0, 1), (1, 0)]
    column_tokens = date_local * row_count * columns_each
    half_tokens = column_tokens // row_size
    if direct:
        outgoing = pl.pallas_call(
            pack_kernel,
            out_shape=jax.ShapeDtypeStruct((date_size, tile_rows, 128), low),
            in_specs=[pl.BlockSpec(memory_space=pltpu.HBM)] * 3,
            out_specs=pl.BlockSpec(memory_space=pltpu.HBM),
            scratch_shapes=[
                pltpu.SMEM(date_numbers.shape, jnp.int32),
                pltpu.VMEM(tokens.shape, low),
                pltpu.VMEM(clear_flags.shape, jnp.int32),
                pltpu.VMEM((date_size, tile_rows, 128), low),
                pltpu.SemaphoreType.DMA((2,)),
                pltpu.SemaphoreType.DMA((4,)),
                pltpu.SemaphoreType.DMA((4,)),
            ],
            name="pack_tokens",
        )(date_numbers, tokens, clear_flags)
        row_at = lax.axis_index("row")
        halves = cotangent.reshape(date_local, row_local, row_size, columns_each, width)
        leaving = lax.dynamic_index_in_dim(halves, 1 - row_at, 2, keepdims=False)
        other_grad = lax.ppermute(leaving, "row", swap)
    else:
        flags = jnp.transpose(
            clear_flags.reshape(date_local, date_size, patches_each), (1, 0, 2)
        ).astype(low)
        numbers = jnp.stack([date_numbers // 32, date_numbers % 32], axis=-1).astype(low)
        numbers = jnp.broadcast_to(numbers[None], (date_size, date_local, 2))
        info = jnp.concatenate([flags, numbers], axis=-1)
        info = jnp.pad(
            info, ((0, 0), (0, block_rows - token_rows - date_local), (0, width - patches_each - 2))
        )
        outgoing = jnp.transpose(
            tokens.reshape(date_local, date_size, patches_each, width), (1, 0, 2, 3)
        ).reshape(date_size, token_rows, width)
        outgoing = jnp.concatenate([outgoing, info], axis=1)
    incoming = lax.all_to_all(outgoing, dates, split_axis=0, concat_axis=0, tiled=True)

    if direct:
        grads_in = (
            row_at.reshape(1),
            cotangent.reshape(local_patches * date_local, width),
            other_grad.reshape(half_tokens, width),
        )
        in_specs = [in_smem] + [in_vmem] * 3 + [in_any]
    else:
        grads_in = (
            lax.all_to_all(cotangent, "row", split_axis=2, concat_axis=1, tiled=True).reshape(
                column_tokens, width
            ),
        )
        in_specs = [in_vmem] * 2 + [in_any]
    time_tokens = date_count * patches_each
    hidden = pl.pallas_call(
        functools.partial(
            time_kernel,
            (
                date_size,
                date_local,
                patches_each,
                head_count,
                packed,
                columns_each if direct else patches_each,
            ),
        ),
        out_shape=jax.ShapeDtypeStruct((time_tokens, width), low),
        in_specs=[in_smem, in_vmem, in_vmem, in_vmem, in_any],
        scratch_shapes=[
            pltpu.VMEM((width // 128, time_tokens, 128), wide),
            pltpu.VMEM((time_tokens, width), wide),
            pltpu.VMEM((time_tokens, 3 * width), low),
            pltpu.VMEM((time_tokens, width), low),
        ],
        compiler_params=params,
        name="time_attention",
    )(decay_slopes, incoming, time_project, time_output, grads_in[-1])

    grad_low, heads_grad = pl.pallas_call(
        functools.partial(
            cotangent_kernel, (date_local, row_size, row_local, columns_each, direct)
        ),
        out_shape=(
            jax.ShapeDtypeStruct((column_tokens, width), low),
            jax.ShapeDtypeStruct((column_tokens, width), low),
        ),
        in_specs=in_specs,
        scratch_shapes=[pltpu.VMEM((width // 128, column_tokens, 128), wide)],
        compiler_params=params,
        name="cotangent_heads",
    )(*grads_in, column_output, hidden)

    if direct:
        parts = hidden.reshape(row_size * date_size, date_local * columns_each, width)
        plane = lax.all_to_all(parts, ("row", *dates), split_axis=0, concat_axis=0, tiled=True)
    else:
        parts = hidden.reshape(date_size, date_local, patches_each, width)
        back = lax.all_to_all(parts, dates, split_axis=0, concat_axis=0, tiled=True)
        back = jnp.transpose(back, (1, 0, 2, 3)).reshape(
            date_local, row_local, column_count, width
        )
        plane = lax.all_to_all(back, "row", split_axis=2, concat_axis=1, tiled=True)
    plane = plane.reshape(column_tokens, width)
    half_shape = jax.ShapeDtypeStruct((half_tokens, width), low)
    packed_rows = (project_each + output_each) * 3 // 2
    row_one = lax.axis_index("row").reshape(1)
    pair_one = lax.axis_index("pair").reshape(1)
    sizes = (date_local, row_size, row_local, columns_each, direct)
    if direct:
        half_grads = jax.ShapeDtypeStruct((row_size, date_size // 2, packed_rows, 128), low)
        grad_shapes = (half_grads, half_grads)
        mixed_shapes = (half_shape, half_shape)
    else:
        grad_shapes = (
            jax.ShapeDtypeStruct((3 * width, width), wide),
            jax.ShapeDtypeStruct((width, width), wide),
        )
        mixed_shapes = (jax.ShapeDtypeStruct((column_tokens, width), low),)
    column_heads, first_grad, second_grad = pl.pallas_call(
        functools.partial(column_kernel, (*sizes, head_count, packed, date_size)),
        out_shape=(jax.ShapeDtypeStruct((column_tokens, width), low), *grad_shapes),
        in_specs=[in_smem] * 2 + [in_vmem] * 4,
        input_output_aliases={4: 0},
        scratch_shapes=[
            pltpu.VMEM((width // 128, column_tokens, 128), wide),
            pltpu.VMEM((column_tokens, width), wide),
            pltpu.VMEM((column_tokens, width), low),
            pltpu.VMEM((column_tokens, 3 * width), low),
            pltpu.VMEM((column_tokens, 3 * width), low),
        ],
        compiler_params=params,
        name="column_attention",
    )(row_one, pair_one, plane, grad_low, heads_grad, column_project)
    own_grad = first_grad
    if direct:
        came = lax.ppermute(second_grad, "pair", swap)
        outers = date_size // 4
        block = jax.ShapeDtypeStruct((packed_rows, 128), low)
        blocks = jax.ShapeDtypeStruct((outers, packed_rows, 128), low)
        own_grad, mid_grad, row_grad, both_grad = pl.pallas_call(
            pair_kernel,
            out_shape=(blocks,) * 4,
            in_specs=[in_smem] * 2 + [in_vmem] * 2,
            out_specs=(in_vmem,) * 4,
            compiler_params=params,
            name="pair_gradients",
        )(row_one, lax.axis_index("mid").reshape(1), first_grad, came)
        row_grad = lax.ppermute(row_grad, "row", swap)
        both_grad = lax.ppermute(both_grad, ("mid", "row"), [(0, 3), (3, 0), (1, 2), (2, 1)])
        mid_grad = lax.ppermute(mid_grad, "mid", swap)
    mixed = pl.pallas_call(
        functools.partial(mixed_kernel, sizes),
        out_shape=mixed_shapes,
        in_specs=[in_smem] + [in_vmem] * 3 + [in_any],
        scratch_shapes=[
            pltpu.VMEM((width // 128, column_tokens, 128), wide),
            pltpu.VMEM((column_tokens, width), wide),
        ],
        compiler_params=params,
        name="mixed_tokens",
    )(row_one, plane, column_heads, column_output, own_grad)

    if direct:
        kept, sent = mixed
        leaving, *steps = pl.pallas_call(
            spread_kernel,
            out_shape=(half_shape,) + (block,) * outers,
            in_specs=[in_smem] + [in_vmem] * 5,
            compiler_params=params,
            name="spread_gradients",
        )(lax.axis_index("outer").reshape(1), own_grad, row_grad, both_grad, mid_grad, sent)
        terms = [steps[0]]
        for step in range(outers - 1, 0, -1):
            route = [(at, at ^ step) for at in range(outers)]
            terms.append(lax.ppermute(steps[step], "outer", route))
        arrived = lax.ppermute(leaving, "row", swap)
        quarter = (date_local, row_local, 1, columns_each, width)
        kept, arrived = kept.reshape(quarter), arrived.reshape(quarter)
        mixed = jnp.concatenate(
            [jnp.where(row_at == 0, kept, arrived), jnp.where(row_at == 0, arrived, kept)], axis=2
        )
        owned_project, owned_output = pl.pallas_call(
            functools.partial(finish_kernel, project_each),
            out_shape=(
                jax.ShapeDtypeStruct((project_each, lane_each), wide),
                jax.ShapeDtypeStruct((output_each, lane_each), wide),
            ),
            in_specs=[in_smem] + [in_vmem] * outers + [in_any],
            compiler_params=params,
            name="gradient_sum",
        )(row_one, *terms, mixed)
    else:
        mixed = mixed[0]
        grads = jnp.concatenate(
            [
                first_grad.reshape(date_size, project_each, row_size, lane_each),
                second_grad.reshape(date_size, output_each, row_size, lane_each),
            ],
            axis=1,
        ).astype(low)
        grads = jnp.transpose(grads, (2, 0, 1, 3)).reshape(
            row_size * date_size, project_each + output_each, lane_each
        )
        terms = lax.all_to_all(grads, ("row", *dates), split_axis=0, concat_axis=0, tiled=True)
        owned = jnp.sum(terms.astype(wide), axis=0)
        owned_project, owned_output = owned[:project_each], owned[project_each:]
        mixed = mixed.reshape(row_size, date_local, row_local, columns_each, width)
        mixed = lax.all_to_all(mixed, "row", split_axis=0, concat_axis=0, tiled=True)
        mixed = jnp.transpose(mixed, (1, 2, 0, 3, 4))
    mixed = mixed.reshape(date_local, row_local, column_count, width)
    return (mixed, jnp.transpose(owned_project), jnp.transpose(owned_output))


def solution(mesh):
    date_size, row_size = mesh.shape["date"], mesh.shape["row"]
    pair_size = 2 if date_size % 2 == 0 else 1
    mid_size = 2 if date_size % 4 == 0 else 1
    split = jax.sharding.Mesh(
        mesh.devices.reshape(-1, mid_size, pair_size, row_size), ("outer", "mid", "pair", "row")
    )
    return jax.shard_map(
        functools.partial(body, row_size, date_size),
        mesh=split,
        in_specs=(
            P(dates, "row", None, None),
            P(dates, "row", None),
            P(dates),
            P(),
            P(),
            P(),
            P(),
            P(),
            P(dates, "row", None, None),
        ),
        out_specs=(P(dates, "row", None, None), P("row", dates), P("row", dates)),
        check_vma=False,
    )
```

```python
import functools
import math

import jax
import jax.numpy as jnp
from jax import lax
from jax.experimental import pallas as pl
from jax.experimental.pallas import tpu as pltpu
from jax.sharding import PartitionSpec as P

epsilon = 1e-06
masked_score = -1e30
time_units = 48
column_units = 48
dates = ("outer", "mid", "pair")
vmem_limit = 12 * 1024 * 1024
low = jnp.bfloat16
wide = jnp.float32


def rms_norm(values):
    factor = lax.rsqrt(jnp.mean(values * values, axis=-1, keepdims=True) + epsilon)
    return (values * factor).astype(low)


def matmul(left, right):
    return jnp.dot(left, right, preferred_element_type=wide)


def contract_rows(left, right):
    return lax.dot_general(left, right, (((0,), (0,)), ((), ())), preferred_element_type=wide)


def contract_last(left, right):
    return lax.dot_general(left, right, (((1,), (1,)), ((), ())), preferred_element_type=wide)


def block_mask(length, packed, head_size):
    shape = (packed * length, packed * head_size)
    rows = lax.broadcasted_iota(jnp.int32, shape, 0) // length
    lanes = lax.broadcasted_iota(jnp.int32, shape, 1) // head_size
    return jnp.where(rows == lanes, 1.0, 0.0).astype(low)


def spread(values, mask, packed):
    return jnp.concatenate([values] * packed, axis=0) * mask


def batches(groups, parts, each):
    units = [(group, part) for group in range(groups) for part in range(parts)]
    return [units[first : first + each] for first in range(0, len(units), each)]


def own_blocks(full, length, packed, head_size):
    lanes = lax.broadcasted_iota(jnp.int32, (length, packed * head_size), 1) // head_size
    out = full[:length]
    for head in range(1, packed):
        out = jnp.where(lanes == head, full[head * length : (head + 1) * length], out)
    return out


def softmax_first(scores):
    raised = jnp.exp(scores - jnp.max(scores, axis=0, keepdims=True))
    return raised * (1.0 / jnp.sum(raised, axis=0, keepdims=True))


def put_tiles(scratch, rows, values):
    tiles, _, lanes = scratch.shape
    for tile in range(tiles):
        scratch[tile, rows, :] = values[:, tile * lanes : (tile + 1) * lanes]


def get_tiles(scratch, rows):
    return jnp.concatenate([scratch[tile, rows, :] for tile in range(scratch.shape[0])], axis=-1)


def pack_kernel(
    numbers_ref,
    tokens_ref,
    flags_ref,
    out_ref,
    numbers_scr,
    tokens_scr,
    flags_scr,
    out_scr,
    small_copied,
    came,
    left,
):
    dates_each, parts, patches, width = tokens_ref.shape
    chunks = came.shape[0]
    each = parts // chunks
    small = [
        pltpu.make_async_copy(flags_ref, flags_scr, small_copied.at[0]),
        pltpu.make_async_copy(numbers_ref, numbers_scr, small_copied.at[1]),
    ]
    arrivals, departures = [], []
    for chunk in range(chunks):
        at = pl.ds(chunk * each, each)
        arrivals.append(
            pltpu.make_async_copy(tokens_ref.at[:, at], tokens_scr.at[:, at], came.at[chunk])
        )
        departures.append(pltpu.make_async_copy(out_scr.at[at], out_ref.at[at], left.at[chunk]))
    for copy in small + arrivals:
        copy.start()
    lanes = out_ref.shape[2]
    tiles = width // lanes
    spare = out_ref.shape[1] - tiles * dates_each * patches
    place = lax.broadcasted_iota(jnp.int32, (patches, lanes), 0)
    lane = lax.broadcasted_iota(jnp.int32, (patches, lanes), 1)
    place = jnp.where(place == lane, 1.0, 0.0).astype(low)
    lane = lax.broadcasted_iota(jnp.int32, (parts, lanes), 1)
    row = lax.broadcasted_iota(jnp.int32, (spare, lanes), 0)
    for copy in small:
        copy.wait()
    infos = []
    for date in range(dates_each):
        number = numbers_scr[date]
        upper = (number // 32).astype(wide)
        under = (number % 32).astype(wide)
        info = matmul(flags_scr[date].astype(wide).astype(low), place)
        info = jnp.where(lane == patches, upper, info)
        infos.append(jnp.where(lane == patches + 1, under, info))
    for chunk in range(chunks):
        arrivals[chunk].wait()
        for part in range(chunk * each, (chunk + 1) * each):
            tokens = jnp.concatenate(
                [tokens_scr[date, part].astype(wide) for date in range(dates_each)], axis=0
            )
            extra = jnp.zeros((spare, lanes), wide)
            for date in range(dates_each):
                extra = jnp.where(row == date, infos[date][part : part + 1], extra)
            pieces = [tokens[:, tile * lanes : (tile + 1) * lanes] for tile in range(tiles)]
            out_scr[part] = jnp.concatenate(pieces + [extra], axis=0).astype(low)
        departures[chunk].start()
    for copy in departures:
        copy.wait()


def time_kernel(
    sizes,
    slopes_ref,
    block_ref,
    project_ref,
    output_ref,
    earlier_ref,
    out_ref,
    seq_scr,
    token_scr,
    qkv_scr,
    heads_scr,
):
    sources, dates_each, groups, head_count, packed, columns_each = sizes
    width = project_ref.shape[0]
    tile_lanes = block_ref.shape[2]
    tiles = width // tile_lanes
    head_size = width // head_count
    lanes = packed * head_size
    length = sources * dates_each
    token_rows = dates_each * groups
    inverse_root = 1.0 / math.sqrt(head_size)
    info = []
    for source in range(sources):
        plane = block_ref[source].astype(wide)
        rows = slice(source * token_rows, (source + 1) * token_rows)
        for tile in range(tiles):
            at = slice(tile * token_rows, (tile + 1) * token_rows)
            if tiles == 1:
                put_tiles(seq_scr, rows, plane[at])
            else:
                seq_scr[tile, rows, :] = plane[at]
        info.append(plane[tiles * token_rows : tiles * token_rows + dates_each])
    info = jnp.concatenate(info, axis=0)
    for group in range(groups):
        token_scr[group * length : (group + 1) * length, :] = get_tiles(
            seq_scr, pl.ds(group, length, stride=groups)
        )
    tokens = token_scr[...]
    qkv_scr[...] = matmul(rms_norm(tokens), project_ref[...]).astype(low)
    numbers = info[:, groups : groups + 1] * 32.0 + info[:, groups + 1 : groups + 2]
    key_at = lax.broadcasted_iota(jnp.int32, (length, packed * length), 0)
    column_at = lax.broadcasted_iota(jnp.int32, (length, packed * length), 1)
    same_date = key_at == column_at % length
    query_numbers = jnp.sum(jnp.where(same_date, numbers, 0.0), axis=0, keepdims=True)
    gap_days = jnp.abs(numbers - query_numbers)
    head_at = column_at // length
    mask = block_mask(length, packed, head_size)
    biases = []
    for first in range(0, head_count, packed):
        slope = jnp.full((length, packed * length), slopes_ref[first], wide)
        for head in range(1, packed):
            slope = jnp.where(head_at == head, slopes_ref[first + head], slope)
        biases.append(-slope * gap_days)
    for units in batches(groups, head_count // packed, time_units):
        all_scores = []
        for group, part in units:
            rows = slice(group * length, (group + 1) * length)
            start = part * lanes
            query = qkv_scr[rows, start : start + lanes]
            key = qkv_scr[rows, width + start : width + start + lanes]
            all_scores.append(contract_last(key, spread(query, mask, packed)))
        all_weights = []
        for (group, part), scores in zip(units, all_scores):
            allowed = (info[:, group : group + 1] > 0) | same_date
            scores = jnp.where(allowed, scores * inverse_root + biases[part], masked_score)
            all_weights.append(softmax_first(scores).astype(low))
        all_heads = []
        for (group, part), weights in zip(units, all_weights):
            rows = slice(group * length, (group + 1) * length)
            start = 2 * width + part * lanes
            all_heads.append(contract_rows(weights, qkv_scr[rows, start : start + lanes]))
        for (group, part), full in zip(units, all_heads):
            rows = slice(group * length, (group + 1) * length)
            heads_scr[rows, part * lanes : (part + 1) * lanes] = own_blocks(
                full, length, packed, head_size
            ).astype(low)
    hidden = token_scr[...] + matmul(heads_scr[...], output_ref[...])
    for group in range(groups):
        first = (group // columns_each) * (length * columns_each) + group % columns_each
        put_tiles(
            seq_scr,
            pl.ds(first, length, stride=columns_each),
            hidden[group * length : (group + 1) * length],
        )
    out_ref[...] = get_tiles(seq_scr, slice(None)).astype(low)


def cotangent_kernel(sizes, *refs):
    dates_each, row_parts, rows_each, columns_each, direct = sizes
    output_ref, _, grad_low_ref, heads_grad_ref, grad_scr = refs[-5:]
    width = output_ref.shape[0]
    length = row_parts * rows_each
    groups = dates_each * columns_each
    part_rows = rows_each * groups
    if direct:
        row_ref, own_ref, other_ref = refs[:3]
        own = own_ref[...].astype(wide)
        own = own.reshape(dates_each * rows_each, row_parts, columns_each, width)
        own = jnp.where(row_ref[0] == 0, own[:, 0], own[:, 1]).reshape(part_rows, width)
        put_tiles(grad_scr, slice(0, part_rows), own)
        put_tiles(grad_scr, slice(part_rows, 2 * part_rows), other_ref[...].astype(wide))
    else:
        put_tiles(grad_scr, slice(None), refs[0][...].astype(wide))
    for group in range(groups):
        if direct:
            inner = (group // columns_each) * (rows_each * columns_each) + group % columns_each
            pieces = [
                get_tiles(
                    grad_scr, pl.ds(part * part_rows + inner, rows_each, stride=columns_each)
                )
                for part in range(row_parts)
            ]
            values = jnp.concatenate(pieces, axis=0)
        else:
            first = (group // columns_each) * (length * columns_each) + group % columns_each
            values = get_tiles(grad_scr, pl.ds(first, length, stride=columns_each))
        grad_low_ref[group * length : (group + 1) * length, :] = values.astype(low)
    heads_grad_ref[...] = contract_last(grad_low_ref[...], output_ref[...]).astype(low)


def load_planes(sizes, row_ref, hidden_ref, seq_scr, plane_scr):
    dates_each, row_parts, rows_each, columns_each, direct = sizes
    length = row_parts * rows_each
    groups = dates_each * columns_each
    part_rows = rows_each * groups
    if direct:
        for part in range(row_parts):
            source = pl.multiple_of(((row_ref[0] + part) % row_parts) * part_rows, part_rows)
            put_tiles(
                seq_scr,
                slice(part * part_rows, (part + 1) * part_rows),
                hidden_ref[pl.ds(source, part_rows), :].astype(wide),
            )
    else:
        put_tiles(seq_scr, slice(None), hidden_ref[...].astype(wide))
    for group in range(groups):
        rows = slice(group * length, (group + 1) * length)
        if direct:
            at = pl.ds(group, length, stride=groups)
        else:
            first = (group // columns_each) * (length * columns_each) + group % columns_each
            at = pl.ds(first, length, stride=columns_each)
        plane_scr[rows, :] = get_tiles(seq_scr, at)


def mixed_kernel(sizes, row_ref, hidden_ref, heads_ref, output_ref, _, *refs):
    dates_each, row_parts, rows_each, columns_each, direct = sizes
    *mixed_refs, seq_scr, plane_scr = refs
    length = row_parts * rows_each
    groups = dates_each * columns_each
    part_rows = rows_each * groups
    load_planes(sizes, row_ref, hidden_ref, seq_scr, plane_scr)
    mixed = plane_scr[...] + matmul(heads_ref[...], output_ref[...])
    for group in range(groups):
        inner = (group // columns_each) * (rows_each * columns_each) + group % columns_each
        for part in range(row_parts):
            begin = group * length + part * rows_each
            put_tiles(
                seq_scr,
                pl.ds(part * part_rows + inner, rows_each, stride=columns_each),
                mixed[begin : begin + rows_each],
            )
    if direct:
        kept_ref, sent_ref = mixed_refs
        kept_ref[...] = get_tiles(seq_scr, slice(0, part_rows)).astype(low)
        sent_ref[...] = get_tiles(seq_scr, slice(part_rows, 2 * part_rows)).astype(low)
    else:
        mixed_refs[0][...] = get_tiles(seq_scr, slice(None)).astype(low)


def column_kernel(
    sizes,
    row_ref,
    pair_ref,
    hidden_ref,
    grad_low_scr,
    heads_grad_scr,
    project_ref,
    heads_scr,
    first_grad_ref,
    second_grad_ref,
    seq_scr,
    plane_scr,
    normed_scr,
    qkv_scr,
    qkv_grad_scr,
):
    dates_each, row_parts, rows_each, columns_each, direct, head_count, packed, date_size = sizes
    width = hidden_ref.shape[1]
    head_size = width // head_count
    lanes = packed * head_size
    length = row_parts * rows_each
    groups = dates_each * columns_each
    inverse_root = 1.0 / math.sqrt(head_size)
    load_planes(sizes[:5], row_ref, hidden_ref, seq_scr, plane_scr)
    normed_scr[...] = rms_norm(plane_scr[...])
    qkv_scr[...] = matmul(normed_scr[...], project_ref[...]).astype(low)
    mask = block_mask(length, packed, head_size)
    for units in batches(groups, head_count // packed, column_units):
        places = []
        for group, part in units:
            start = part * lanes
            places.append(
                (
                    slice(group * length, (group + 1) * length),
                    slice(start, start + lanes),
                    slice(width + start, width + start + lanes),
                    slice(2 * width + start, 2 * width + start + lanes),
                )
            )
        all_scores = []
        for rows, at_query, at_key, at_value in places:
            query = spread(qkv_scr[rows, at_query], mask, packed)
            heads_grad = spread(heads_grad_scr[rows, at_query], mask, packed)
            all_scores.append(
                (
                    contract_last(qkv_scr[rows, at_key], query),
                    contract_last(qkv_scr[rows, at_value], heads_grad),
                )
            )
        all_weights = []
        for scores, product_grad in all_scores:
            weights = softmax_first(scores * inverse_root)
            score_grad = weights * (
                product_grad - jnp.sum(weights * product_grad, axis=0, keepdims=True)
            )
            all_weights.append((weights.astype(low), score_grad.astype(low)))
        all_full = []
        for (rows, at_query, at_key, at_value), (weights, score_low) in zip(places, all_weights):
            all_full.append(
                (
                    contract_rows(weights, qkv_scr[rows, at_value]),
                    contract_rows(score_low, qkv_scr[rows, at_key]),
                )
            )
            query = spread(qkv_scr[rows, at_query], mask, packed)
            heads_grad = spread(heads_grad_scr[rows, at_query], mask, packed)
            key_grad = matmul(score_low, query) * inverse_root
            qkv_grad_scr[rows, at_key] = key_grad.astype(low)
            qkv_grad_scr[rows, at_value] = matmul(weights, heads_grad).astype(low)
        for (rows, at_query, _, _), (heads_full, query_full) in zip(places, all_full):
            heads = own_blocks(heads_full, length, packed, head_size)
            heads_scr[rows, at_query] = heads.astype(low)
            query_grad = own_blocks(query_full, length, packed, head_size) * inverse_root
            qkv_grad_scr[rows, at_query] = query_grad.astype(low)
    project_grad = contract_rows(qkv_grad_scr[...], normed_scr[...])
    output_grad = contract_rows(grad_low_scr[...], heads_scr[...])
    if not direct:
        first_grad_ref[...] = project_grad
        second_grad_ref[...] = output_grad
        return
    keep_ref, send_ref = first_grad_ref, second_grad_ref
    even = pair_ref[0] == 0
    project_each = project_grad.shape[0] // date_size
    output_each = output_grad.shape[0] // date_size
    half = (project_each + output_each) // 2
    lower = lax.broadcasted_iota(jnp.int32, (half, 128), 1) < 64
    for outer in range(date_size // 2):
        pair = []
        for part in (2 * outer, 2 * outer + 1):
            block = jnp.concatenate(
                [
                    project_grad[part * project_each : (part + 1) * project_each],
                    output_grad[part * output_each : (part + 1) * output_each],
                ],
                axis=0,
            )
            top, bottom = block[:half, 128:256], block[half:, 128:256]
            pair.append(
                (
                    (block[:, :128], jnp.where(lower, top, pltpu.roll(bottom, 64, 1))),
                    (block[:, 256:], jnp.where(lower, pltpu.roll(top, 64, 1), bottom)),
                )
            )
        for row_part in range(2):
            for first, one, two in zip((0, 2 * half), pair[0][row_part], pair[1][row_part]):
                place = (row_part, outer, slice(first, first + one.shape[0]))
                keep_ref[place] = jnp.where(even, one, two).astype(low)
                send_ref[place] = jnp.where(even, two, one).astype(low)


def pair_kernel(row_ref, mid_ref, kept_ref, came_ref, own_ref, mid_out, row_out, both_out):
    row, mid = row_ref[0], mid_ref[0]
    for outer in range(own_ref.shape[0]):
        for out_ref, row_at, mid_at in (
            (mid_out, row, 1 - mid),
            (row_out, 1 - row, mid),
            (both_out, 1 - row, 1 - mid),
            (own_ref, row, mid),
        ):
            place = (row_at, 2 * outer + mid_at)
            out_ref[outer] = (kept_ref[place].astype(wide) + came_ref[place].astype(wide)).astype(
                low
            )


def spread_kernel(outer_ref, own_ref, mid_ref, row_ref, both_ref, sent_ref, leave_ref, *refs):
    leave_ref[...] = sent_ref[...]
    count = own_ref.shape[0]
    for step in range(count):
        at = (outer_ref[0] + step) % count
        total = own_ref[at].astype(wide) + mid_ref[at].astype(wide)
        total = total + (row_ref[at].astype(wide) + both_ref[at].astype(wide))
        refs[step][...] = total.astype(low)


def finish_kernel(project_each, row_ref, *refs):
    *terms, _, project_ref, output_ref = refs
    total = terms[0][...].astype(wide)
    for term in terms[1:]:
        total = total + term[...].astype(wide)
    whole = 2 * total.shape[0] // 3
    main = total[:whole]
    tail = total[whole:]
    swapped = pltpu.roll(tail, 64, 1)
    lower = lax.broadcasted_iota(jnp.int32, (whole, 128), 1) < 64
    tail_first = jnp.concatenate([tail, swapped], axis=0)
    turned = pltpu.roll(main, 64, 1)
    front = jnp.concatenate([main, tail_first[:, :64]], axis=1)
    back = jnp.concatenate([jnp.where(lower, tail_first, turned), turned[:, :64]], axis=1)
    owned = jnp.where(row_ref[0] == 0, front, back)
    project_ref[...] = owned[:project_each]
    output_ref[...] = owned[project_each:]


def body(
    row_size,
    date_size,
    tokens,
    clear_flags,
    date_numbers,
    decay_slopes,
    time_project,
    time_output,
    column_project,
    column_output,
    cotangent,
):
    date_local, row_local, column_count, width = tokens.shape
    head_count = decay_slopes.shape[0]
    head_size = width // head_count
    packed = max(1, 128 // head_size)
    local_patches = row_local * column_count
    patches_each = local_patches // date_size
    columns_each = column_count // row_size
    row_count = row_local * row_size
    date_count = date_local * date_size
    project_each = 3 * width // date_size
    output_each = width // date_size
    lane_each = width // row_size
    direct = (
        patches_each == column_count
        and column_count % 16 == 0
        and date_size % 8 == 0
        and row_size == 2
        and lane_each == 192
        and project_each % 8 == 0
        and output_each % 8 == 0
        and (project_each + output_each) % 32 == 0
    )
    token_rows = date_local * patches_each
    block_rows = -(-(token_rows + date_local) // 8) * 8
    tile_rows = (width // 128) * token_rows + -(-date_local // 8) * 8
    params = pltpu.CompilerParams(vmem_limit_bytes=vmem_limit)
    in_vmem = pl.BlockSpec(memory_space=pltpu.VMEM)
    in_smem = pl.BlockSpec(memory_space=pltpu.SMEM)
    in_any = pl.BlockSpec(memory_space=pl.ANY)
    swap = [(0, 1), (1, 0)]
    column_tokens = date_local * row_count * columns_each
    half_tokens = column_tokens // row_size
    if direct:
        outgoing = pl.pallas_call(
            pack_kernel,
            out_shape=jax.ShapeDtypeStruct((date_size, tile_rows, 128), low),
            in_specs=[pl.BlockSpec(memory_space=pltpu.HBM)] * 3,
            out_specs=pl.BlockSpec(memory_space=pltpu.HBM),
            scratch_shapes=[
                pltpu.SMEM(date_numbers.shape, jnp.int32),
                pltpu.VMEM(tokens.shape, low),
                pltpu.VMEM(clear_flags.shape, jnp.int32),
                pltpu.VMEM((date_size, tile_rows, 128), low),
                pltpu.SemaphoreType.DMA((2,)),
                pltpu.SemaphoreType.DMA((4,)),
                pltpu.SemaphoreType.DMA((4,)),
            ],
            name="pack_tokens",
        )(date_numbers, tokens, clear_flags)
        row_at = lax.axis_index("row")
        halves = cotangent.reshape(date_local, row_local, row_size, columns_each, width)
        leaving = lax.dynamic_index_in_dim(halves, 1 - row_at, 2, keepdims=False)
        other_grad = lax.ppermute(leaving, "row", swap)
    else:
        flags = jnp.transpose(
            clear_flags.reshape(date_local, date_size, patches_each), (1, 0, 2)
        ).astype(low)
        numbers = jnp.stack([date_numbers // 32, date_numbers % 32], axis=-1).astype(low)
        numbers = jnp.broadcast_to(numbers[None], (date_size, date_local, 2))
        info = jnp.concatenate([flags, numbers], axis=-1)
        info = jnp.pad(
            info, ((0, 0), (0, block_rows - token_rows - date_local), (0, width - patches_each - 2))
        )
        outgoing = jnp.transpose(
            tokens.reshape(date_local, date_size, patches_each, width), (1, 0, 2, 3)
        ).reshape(date_size, token_rows, width)
        outgoing = jnp.concatenate([outgoing, info], axis=1)
    incoming = lax.all_to_all(outgoing, dates, split_axis=0, concat_axis=0, tiled=True)

    if direct:
        grads_in = (
            row_at.reshape(1),
            cotangent.reshape(local_patches * date_local, width),
            other_grad.reshape(half_tokens, width),
        )
        in_specs = [in_smem] + [in_vmem] * 3 + [in_any]
    else:
        grads_in = (
            lax.all_to_all(cotangent, "row", split_axis=2, concat_axis=1, tiled=True).reshape(
                column_tokens, width
            ),
        )
        in_specs = [in_vmem] * 2 + [in_any]
    time_tokens = date_count * patches_each
    hidden = pl.pallas_call(
        functools.partial(
            time_kernel,
            (
                date_size,
                date_local,
                patches_each,
                head_count,
                packed,
                columns_each if direct else patches_each,
            ),
        ),
        out_shape=jax.ShapeDtypeStruct((time_tokens, width), low),
        in_specs=[in_smem, in_vmem, in_vmem, in_vmem, in_any],
        scratch_shapes=[
            pltpu.VMEM((width // 128, time_tokens, 128), wide),
            pltpu.VMEM((time_tokens, width), wide),
            pltpu.VMEM((time_tokens, 3 * width), low),
            pltpu.VMEM((time_tokens, width), low),
        ],
        compiler_params=params,
        name="time_attention",
    )(decay_slopes, incoming, time_project, time_output, grads_in[-1])

    grad_low, heads_grad = pl.pallas_call(
        functools.partial(
            cotangent_kernel, (date_local, row_size, row_local, columns_each, direct)
        ),
        out_shape=(
            jax.ShapeDtypeStruct((column_tokens, width), low),
            jax.ShapeDtypeStruct((column_tokens, width), low),
        ),
        in_specs=in_specs,
        scratch_shapes=[pltpu.VMEM((width // 128, column_tokens, 128), wide)],
        compiler_params=params,
        name="cotangent_heads",
    )(*grads_in, column_output, hidden)

    if direct:
        parts = hidden.reshape(row_size * date_size, date_local * columns_each, width)
        plane = lax.all_to_all(parts, ("row", *dates), split_axis=0, concat_axis=0, tiled=True)
    else:
        parts = hidden.reshape(date_size, date_local, patches_each, width)
        back = lax.all_to_all(parts, dates, split_axis=0, concat_axis=0, tiled=True)
        back = jnp.transpose(back, (1, 0, 2, 3)).reshape(
            date_local, row_local, column_count, width
        )
        plane = lax.all_to_all(back, "row", split_axis=2, concat_axis=1, tiled=True)
    plane = plane.reshape(column_tokens, width)
    half_shape = jax.ShapeDtypeStruct((half_tokens, width), low)
    packed_rows = (project_each + output_each) * 3 // 2
    row_one = lax.axis_index("row").reshape(1)
    pair_one = lax.axis_index("pair").reshape(1)
    sizes = (date_local, row_size, row_local, columns_each, direct)
    if direct:
        half_grads = jax.ShapeDtypeStruct((row_size, date_size // 2, packed_rows, 128), low)
        grad_shapes = (half_grads, half_grads)
        mixed_shapes = (half_shape, half_shape)
    else:
        grad_shapes = (
            jax.ShapeDtypeStruct((3 * width, width), wide),
            jax.ShapeDtypeStruct((width, width), wide),
        )
        mixed_shapes = (jax.ShapeDtypeStruct((column_tokens, width), low),)
    column_heads, first_grad, second_grad = pl.pallas_call(
        functools.partial(column_kernel, (*sizes, head_count, packed, date_size)),
        out_shape=(jax.ShapeDtypeStruct((column_tokens, width), low), *grad_shapes),
        in_specs=[in_smem] * 2 + [in_vmem] * 4,
        input_output_aliases={4: 0},
        scratch_shapes=[
            pltpu.VMEM((width // 128, column_tokens, 128), wide),
            pltpu.VMEM((column_tokens, width), wide),
            pltpu.VMEM((column_tokens, width), low),
            pltpu.VMEM((column_tokens, 3 * width), low),
            pltpu.VMEM((column_tokens, 3 * width), low),
        ],
        compiler_params=params,
        name="column_attention",
    )(row_one, pair_one, plane, grad_low, heads_grad, column_project)
    own_grad = first_grad
    if direct:
        came = lax.ppermute(second_grad, "pair", swap)
        outers = date_size // 4
        block = jax.ShapeDtypeStruct((packed_rows, 128), low)
        blocks = jax.ShapeDtypeStruct((outers, packed_rows, 128), low)
        own_grad, mid_grad, row_grad, both_grad = pl.pallas_call(
            pair_kernel,
            out_shape=(blocks,) * 4,
            in_specs=[in_smem] * 2 + [in_vmem] * 2,
            out_specs=(in_vmem,) * 4,
            compiler_params=params,
            name="pair_gradients",
        )(row_one, lax.axis_index("mid").reshape(1), first_grad, came)
        both_grad = lax.ppermute(both_grad, ("mid", "row"), [(0, 3), (3, 0), (1, 2), (2, 1)])
        mid_grad = lax.ppermute(mid_grad, "mid", swap)
        row_grad = lax.ppermute(row_grad, "row", swap)
    mixed = pl.pallas_call(
        functools.partial(mixed_kernel, sizes),
        out_shape=mixed_shapes,
        in_specs=[in_smem] + [in_vmem] * 3 + [in_any],
        scratch_shapes=[
            pltpu.VMEM((width // 128, column_tokens, 128), wide),
            pltpu.VMEM((column_tokens, width), wide),
        ],
        compiler_params=params,
        name="mixed_tokens",
    )(row_one, plane, column_heads, column_output, own_grad)

    if direct:
        kept, sent = mixed
        leaving, *steps = pl.pallas_call(
            spread_kernel,
            out_shape=(half_shape,) + (block,) * outers,
            in_specs=[in_smem] + [in_vmem] * 5,
            compiler_params=params,
            name="spread_gradients",
        )(lax.axis_index("outer").reshape(1), own_grad, mid_grad, row_grad, both_grad, sent)
        terms = [steps[0]]
        for step in range(1, outers):
            route = [(at, (at + step) % outers) for at in range(outers)]
            terms.append(lax.ppermute(steps[step], "outer", route))
        arrived = lax.ppermute(leaving, "row", swap)
        quarter = (date_local, row_local, 1, columns_each, width)
        kept, arrived = kept.reshape(quarter), arrived.reshape(quarter)
        mixed = jnp.concatenate(
            [jnp.where(row_at == 0, kept, arrived), jnp.where(row_at == 0, arrived, kept)], axis=2
        )
        owned_project, owned_output = pl.pallas_call(
            functools.partial(finish_kernel, project_each),
            out_shape=(
                jax.ShapeDtypeStruct((project_each, lane_each), wide),
                jax.ShapeDtypeStruct((output_each, lane_each), wide),
            ),
            in_specs=[in_smem] + [in_vmem] * outers + [in_any],
            compiler_params=params,
            name="gradient_sum",
        )(row_one, *terms, mixed)
    else:
        mixed = mixed[0]
        grads = jnp.concatenate(
            [
                first_grad.reshape(date_size, project_each, row_size, lane_each),
                second_grad.reshape(date_size, output_each, row_size, lane_each),
            ],
            axis=1,
        ).astype(low)
        grads = jnp.transpose(grads, (2, 0, 1, 3)).reshape(
            row_size * date_size, project_each + output_each, lane_each
        )
        terms = lax.all_to_all(grads, ("row", *dates), split_axis=0, concat_axis=0, tiled=True)
        owned = jnp.sum(terms.astype(wide), axis=0)
        owned_project, owned_output = owned[:project_each], owned[project_each:]
        mixed = mixed.reshape(row_size, date_local, row_local, columns_each, width)
        mixed = lax.all_to_all(mixed, "row", split_axis=0, concat_axis=0, tiled=True)
        mixed = jnp.transpose(mixed, (1, 2, 0, 3, 4))
    mixed = mixed.reshape(date_local, row_local, column_count, width)
    return (mixed, jnp.transpose(owned_project), jnp.transpose(owned_output))


def solution(mesh):
    date_size, row_size = mesh.shape["date"], mesh.shape["row"]
    pair_size = 2 if date_size % 2 == 0 else 1
    mid_size = 2 if date_size % 4 == 0 else 1
    split = jax.sharding.Mesh(
        mesh.devices.reshape(-1, mid_size, pair_size, row_size), ("outer", "mid", "pair", "row")
    )
    return jax.shard_map(
        functools.partial(body, row_size, date_size),
        mesh=split,
        in_specs=(
            P(dates, "row", None, None),
            P(dates, "row", None),
            P(dates),
            P(),
            P(),
            P(),
            P(),
            P(),
            P(dates, "row", None, None),
        ),
        out_specs=(P(dates, "row", None, None), P("row", dates), P("row", dates)),
        check_vma=False,
    )
```

```python
import functools
import math

import jax
import jax.numpy as jnp
from jax import lax
from jax.experimental import pallas as pl
from jax.experimental.pallas import tpu as pltpu
from jax.sharding import PartitionSpec as P

epsilon = 1e-06
masked_score = -1e30
time_units = 48
column_units = 24
dates = ("outer", "mid", "pair")
vmem_limit = 12 * 1024 * 1024
low = jnp.bfloat16
wide = jnp.float32


def rms_norm(values):
    factor = lax.rsqrt(jnp.mean(values * values, axis=-1, keepdims=True) + epsilon)
    return (values * factor).astype(low)


def matmul(left, right):
    return jnp.dot(left, right, preferred_element_type=wide)


def contract_rows(left, right):
    return lax.dot_general(left, right, (((0,), (0,)), ((), ())), preferred_element_type=wide)


def contract_last(left, right):
    return lax.dot_general(left, right, (((1,), (1,)), ((), ())), preferred_element_type=wide)


def block_mask(length, packed, head_size):
    shape = (packed * length, packed * head_size)
    rows = lax.broadcasted_iota(jnp.int32, shape, 0) // length
    lanes = lax.broadcasted_iota(jnp.int32, shape, 1) // head_size
    return jnp.where(rows == lanes, 1.0, 0.0).astype(low)


def spread(values, mask, packed):
    return jnp.concatenate([values] * packed, axis=0) * mask


def batches(groups, parts, each):
    units = [(group, part) for group in range(groups) for part in range(parts)]
    return [units[first : first + each] for first in range(0, len(units), each)]


def own_blocks(full, length, packed, head_size):
    lanes = lax.broadcasted_iota(jnp.int32, (length, packed * head_size), 1) // head_size
    out = full[:length]
    for head in range(1, packed):
        out = jnp.where(lanes == head, full[head * length : (head + 1) * length], out)
    return out


def softmax_first(scores):
    raised = jnp.exp(scores - jnp.max(scores, axis=0, keepdims=True))
    return raised * (1.0 / jnp.sum(raised, axis=0, keepdims=True))


def put_tiles(scratch, rows, values):
    tiles, _, lanes = scratch.shape
    for tile in range(tiles):
        scratch[tile, rows, :] = values[:, tile * lanes : (tile + 1) * lanes]


def get_tiles(scratch, rows):
    return jnp.concatenate([scratch[tile, rows, :] for tile in range(scratch.shape[0])], axis=-1)


def pack_kernel(
    numbers_ref,
    tokens_ref,
    flags_ref,
    out_ref,
    numbers_scr,
    tokens_scr,
    flags_scr,
    out_scr,
    small_copied,
    came,
    left,
):
    dates_each, parts, patches, width = tokens_ref.shape
    chunks = came.shape[0]
    each = parts // chunks
    small = [
        pltpu.make_async_copy(flags_ref, flags_scr, small_copied.at[0]),
        pltpu.make_async_copy(numbers_ref, numbers_scr, small_copied.at[1]),
    ]
    arrivals, departures = [], []
    for chunk in range(chunks):
        at = pl.ds(chunk * each, each)
        arrivals.append(
            pltpu.make_async_copy(tokens_ref.at[:, at], tokens_scr.at[:, at], came.at[chunk])
        )
        departures.append(pltpu.make_async_copy(out_scr.at[at], out_ref.at[at], left.at[chunk]))
    for copy in small + arrivals:
        copy.start()
    lanes = out_ref.shape[2]
    tiles = width // lanes
    spare = out_ref.shape[1] - tiles * dates_each * patches
    place = lax.broadcasted_iota(jnp.int32, (patches, lanes), 0)
    lane = lax.broadcasted_iota(jnp.int32, (patches, lanes), 1)
    place = jnp.where(place == lane, 1.0, 0.0).astype(low)
    lane = lax.broadcasted_iota(jnp.int32, (parts, lanes), 1)
    row = lax.broadcasted_iota(jnp.int32, (spare, lanes), 0)
    for copy in small:
        copy.wait()
    infos = []
    for date in range(dates_each):
        number = numbers_scr[date]
        upper = (number // 32).astype(wide)
        under = (number % 32).astype(wide)
        info = matmul(flags_scr[date].astype(wide).astype(low), place)
        info = jnp.where(lane == patches, upper, info)
        infos.append(jnp.where(lane == patches + 1, under, info))
    for chunk in range(chunks):
        arrivals[chunk].wait()
        for part in range(chunk * each, (chunk + 1) * each):
            tokens = jnp.concatenate(
                [tokens_scr[date, part].astype(wide) for date in range(dates_each)], axis=0
            )
            extra = jnp.zeros((spare, lanes), wide)
            for date in range(dates_each):
                extra = jnp.where(row == date, infos[date][part : part + 1], extra)
            pieces = [tokens[:, tile * lanes : (tile + 1) * lanes] for tile in range(tiles)]
            out_scr[part] = jnp.concatenate(pieces + [extra], axis=0).astype(low)
        departures[chunk].start()
    for copy in departures:
        copy.wait()


def time_kernel(
    sizes,
    slopes_ref,
    block_ref,
    project_ref,
    output_ref,
    earlier_ref,
    out_ref,
    seq_scr,
    token_scr,
    qkv_scr,
    heads_scr,
):
    sources, dates_each, groups, head_count, packed, columns_each = sizes
    width = project_ref.shape[0]
    tile_lanes = block_ref.shape[2]
    tiles = width // tile_lanes
    head_size = width // head_count
    lanes = packed * head_size
    length = sources * dates_each
    token_rows = dates_each * groups
    inverse_root = 1.0 / math.sqrt(head_size)
    info = []
    for source in range(sources):
        plane = block_ref[source].astype(wide)
        rows = slice(source * token_rows, (source + 1) * token_rows)
        for tile in range(tiles):
            at = slice(tile * token_rows, (tile + 1) * token_rows)
            if tiles == 1:
                put_tiles(seq_scr, rows, plane[at])
            else:
                seq_scr[tile, rows, :] = plane[at]
        info.append(plane[tiles * token_rows : tiles * token_rows + dates_each])
    info = jnp.concatenate(info, axis=0)
    for group in range(groups):
        token_scr[group * length : (group + 1) * length, :] = get_tiles(
            seq_scr, pl.ds(group, length, stride=groups)
        )
    tokens = token_scr[...]
    qkv_scr[...] = matmul(rms_norm(tokens), project_ref[...]).astype(low)
    numbers = info[:, groups : groups + 1] * 32.0 + info[:, groups + 1 : groups + 2]
    key_at = lax.broadcasted_iota(jnp.int32, (length, packed * length), 0)
    column_at = lax.broadcasted_iota(jnp.int32, (length, packed * length), 1)
    same_date = key_at == column_at % length
    query_numbers = jnp.sum(jnp.where(same_date, numbers, 0.0), axis=0, keepdims=True)
    gap_days = jnp.abs(numbers - query_numbers)
    head_at = column_at // length
    mask = block_mask(length, packed, head_size)
    biases = []
    for first in range(0, head_count, packed):
        slope = jnp.full((length, packed * length), slopes_ref[first], wide)
        for head in range(1, packed):
            slope = jnp.where(head_at == head, slopes_ref[first + head], slope)
        biases.append(-slope * gap_days)
    for units in batches(groups, head_count // packed, time_units):
        all_scores = []
        for group, part in units:
            rows = slice(group * length, (group + 1) * length)
            start = part * lanes
            query = qkv_scr[rows, start : start + lanes]
            key = qkv_scr[rows, width + start : width + start + lanes]
            all_scores.append(contract_last(key, spread(query, mask, packed)))
        all_weights = []
        for (group, part), scores in zip(units, all_scores):
            allowed = (info[:, group : group + 1] > 0) | same_date
            scores = jnp.where(allowed, scores * inverse_root + biases[part], masked_score)
            all_weights.append(softmax_first(scores).astype(low))
        all_heads = []
        for (group, part), weights in zip(units, all_weights):
            rows = slice(group * length, (group + 1) * length)
            start = 2 * width + part * lanes
            all_heads.append(contract_rows(weights, qkv_scr[rows, start : start + lanes]))
        for (group, part), full in zip(units, all_heads):
            rows = slice(group * length, (group + 1) * length)
            heads_scr[rows, part * lanes : (part + 1) * lanes] = own_blocks(
                full, length, packed, head_size
            ).astype(low)
    hidden = token_scr[...] + matmul(heads_scr[...], output_ref[...])
    for group in range(groups):
        first = (group // columns_each) * (length * columns_each) + group % columns_each
        put_tiles(
            seq_scr,
            pl.ds(first, length, stride=columns_each),
            hidden[group * length : (group + 1) * length],
        )
    out_ref[...] = get_tiles(seq_scr, slice(None)).astype(low)


def cotangent_kernel(sizes, *refs):
    dates_each, row_parts, rows_each, columns_each, direct = sizes
    output_ref, _, grad_low_ref, heads_grad_ref, grad_scr = refs[-5:]
    width = output_ref.shape[0]
    length = row_parts * rows_each
    groups = dates_each * columns_each
    part_rows = rows_each * groups
    if direct:
        row_ref, own_ref, other_ref = refs[:3]
        own = own_ref[...].astype(wide)
        own = own.reshape(dates_each * rows_each, row_parts, columns_each, width)
        own = jnp.where(row_ref[0] == 0, own[:, 0], own[:, 1]).reshape(part_rows, width)
        put_tiles(grad_scr, slice(0, part_rows), own)
        put_tiles(grad_scr, slice(part_rows, 2 * part_rows), other_ref[...].astype(wide))
    else:
        put_tiles(grad_scr, slice(None), refs[0][...].astype(wide))
    for group in range(groups):
        if direct:
            inner = (group // columns_each) * (rows_each * columns_each) + group % columns_each
            pieces = [
                get_tiles(
                    grad_scr, pl.ds(part * part_rows + inner, rows_each, stride=columns_each)
                )
                for part in range(row_parts)
            ]
            values = jnp.concatenate(pieces, axis=0)
        else:
            first = (group // columns_each) * (length * columns_each) + group % columns_each
            values = get_tiles(grad_scr, pl.ds(first, length, stride=columns_each))
        grad_low_ref[group * length : (group + 1) * length, :] = values.astype(low)
    heads_grad_ref[...] = contract_last(grad_low_ref[...], output_ref[...]).astype(low)


def load_planes(sizes, row_ref, hidden_ref, seq_scr, plane_scr):
    dates_each, row_parts, rows_each, columns_each, direct = sizes
    length = row_parts * rows_each
    groups = dates_each * columns_each
    part_rows = rows_each * groups
    if direct:
        for part in range(row_parts):
            source = pl.multiple_of(((row_ref[0] + part) % row_parts) * part_rows, part_rows)
            put_tiles(
                seq_scr,
                slice(part * part_rows, (part + 1) * part_rows),
                hidden_ref[pl.ds(source, part_rows), :].astype(wide),
            )
    else:
        put_tiles(seq_scr, slice(None), hidden_ref[...].astype(wide))
    for group in range(groups):
        rows = slice(group * length, (group + 1) * length)
        if direct:
            at = pl.ds(group, length, stride=groups)
        else:
            first = (group // columns_each) * (length * columns_each) + group % columns_each
            at = pl.ds(first, length, stride=columns_each)
        plane_scr[rows, :] = get_tiles(seq_scr, at)


def mixed_kernel(sizes, row_ref, hidden_ref, heads_ref, output_ref, _, *refs):
    dates_each, row_parts, rows_each, columns_each, direct = sizes
    *mixed_refs, seq_scr, plane_scr = refs
    length = row_parts * rows_each
    groups = dates_each * columns_each
    part_rows = rows_each * groups
    load_planes(sizes, row_ref, hidden_ref, seq_scr, plane_scr)
    mixed = plane_scr[...] + matmul(heads_ref[...], output_ref[...])
    for group in range(groups):
        inner = (group // columns_each) * (rows_each * columns_each) + group % columns_each
        for part in range(row_parts):
            begin = group * length + part * rows_each
            put_tiles(
                seq_scr,
                pl.ds(part * part_rows + inner, rows_each, stride=columns_each),
                mixed[begin : begin + rows_each],
            )
    if direct:
        kept_ref, sent_ref = mixed_refs
        kept_ref[...] = get_tiles(seq_scr, slice(0, part_rows)).astype(low)
        sent_ref[...] = get_tiles(seq_scr, slice(part_rows, 2 * part_rows)).astype(low)
    else:
        mixed_refs[0][...] = get_tiles(seq_scr, slice(None)).astype(low)


def column_kernel(
    sizes,
    row_ref,
    pair_ref,
    hidden_ref,
    grad_low_scr,
    heads_grad_scr,
    project_ref,
    heads_scr,
    first_grad_ref,
    second_grad_ref,
    seq_scr,
    plane_scr,
    normed_scr,
    qkv_scr,
    qkv_grad_scr,
):
    dates_each, row_parts, rows_each, columns_each, direct, head_count, packed, date_size = sizes
    width = hidden_ref.shape[1]
    head_size = width // head_count
    lanes = packed * head_size
    length = row_parts * rows_each
    groups = dates_each * columns_each
    inverse_root = 1.0 / math.sqrt(head_size)
    load_planes(sizes[:5], row_ref, hidden_ref, seq_scr, plane_scr)
    normed_scr[...] = rms_norm(plane_scr[...])
    qkv_scr[...] = matmul(normed_scr[...], project_ref[...]).astype(low)
    mask = block_mask(length, packed, head_size)
    for units in batches(groups, head_count // packed, column_units):
        places = []
        for group, part in units:
            start = part * lanes
            places.append(
                (
                    slice(group * length, (group + 1) * length),
                    slice(start, start + lanes),
                    slice(width + start, width + start + lanes),
                    slice(2 * width + start, 2 * width + start + lanes),
                )
            )
        all_scores = []
        for rows, at_query, at_key, at_value in places:
            query = spread(qkv_scr[rows, at_query], mask, packed)
            heads_grad = spread(heads_grad_scr[rows, at_query], mask, packed)
            all_scores.append(
                (
                    contract_last(qkv_scr[rows, at_key], query),
                    contract_last(qkv_scr[rows, at_value], heads_grad),
                )
            )
        all_weights = []
        for scores, product_grad in all_scores:
            weights = softmax_first(scores * inverse_root)
            score_grad = weights * (
                product_grad - jnp.sum(weights * product_grad, axis=0, keepdims=True)
            )
            all_weights.append((weights.astype(low), score_grad.astype(low)))
        all_full = []
        for (rows, at_query, at_key, at_value), (weights, score_low) in zip(places, all_weights):
            all_full.append(
                (
                    contract_rows(weights, qkv_scr[rows, at_value]),
                    contract_rows(score_low, qkv_scr[rows, at_key]),
                )
            )
            query = spread(qkv_scr[rows, at_query], mask, packed)
            heads_grad = spread(heads_grad_scr[rows, at_query], mask, packed)
            key_grad = matmul(score_low, query) * inverse_root
            qkv_grad_scr[rows, at_key] = key_grad.astype(low)
            qkv_grad_scr[rows, at_value] = matmul(weights, heads_grad).astype(low)
        for (rows, at_query, _, _), (heads_full, query_full) in zip(places, all_full):
            heads = own_blocks(heads_full, length, packed, head_size)
            heads_scr[rows, at_query] = heads.astype(low)
            query_grad = own_blocks(query_full, length, packed, head_size) * inverse_root
            qkv_grad_scr[rows, at_query] = query_grad.astype(low)
    project_grad = contract_rows(qkv_grad_scr[...], normed_scr[...])
    output_grad = contract_rows(grad_low_scr[...], heads_scr[...])
    if not direct:
        first_grad_ref[...] = project_grad
        second_grad_ref[...] = output_grad
        return
    keep_ref, send_ref = first_grad_ref, second_grad_ref
    even = pair_ref[0] == 0
    project_each = project_grad.shape[0] // date_size
    output_each = output_grad.shape[0] // date_size
    half = (project_each + output_each) // 2
    lower = lax.broadcasted_iota(jnp.int32, (half, 128), 1) < 64
    for outer in range(date_size // 2):
        pair = []
        for part in (2 * outer, 2 * outer + 1):
            block = jnp.concatenate(
                [
                    project_grad[part * project_each : (part + 1) * project_each],
                    output_grad[part * output_each : (part + 1) * output_each],
                ],
                axis=0,
            )
            top, bottom = block[:half, 128:256], block[half:, 128:256]
            pair.append(
                (
                    (block[:, :128], jnp.where(lower, top, pltpu.roll(bottom, 64, 1))),
                    (block[:, 256:], jnp.where(lower, pltpu.roll(top, 64, 1), bottom)),
                )
            )
        for row_part in range(2):
            for first, one, two in zip((0, 2 * half), pair[0][row_part], pair[1][row_part]):
                place = (row_part, outer, slice(first, first + one.shape[0]))
                keep_ref[place] = jnp.where(even, one, two).astype(low)
                send_ref[place] = jnp.where(even, two, one).astype(low)


def pair_kernel(row_ref, mid_ref, kept_ref, came_ref, own_ref, mid_out, row_out, both_out):
    row, mid = row_ref[0], mid_ref[0]
    for outer in range(own_ref.shape[0]):
        for out_ref, row_at, mid_at in (
            (mid_out, row, 1 - mid),
            (row_out, 1 - row, mid),
            (both_out, 1 - row, 1 - mid),
            (own_ref, row, mid),
        ):
            place = (row_at, 2 * outer + mid_at)
            out_ref[outer] = (kept_ref[place].astype(wide) + came_ref[place].astype(wide)).astype(
                low
            )


def spread_kernel(outer_ref, own_ref, mid_ref, row_ref, both_ref, sent_ref, leave_ref, *refs):
    leave_ref[...] = sent_ref[...]
    count = own_ref.shape[0]
    for step in range(count):
        at = (outer_ref[0] + step) % count
        total = own_ref[at].astype(wide) + mid_ref[at].astype(wide)
        total = total + (row_ref[at].astype(wide) + both_ref[at].astype(wide))
        refs[step][...] = total.astype(low)


def finish_kernel(project_each, row_ref, *refs):
    *terms, _, project_ref, output_ref = refs
    total = terms[0][...].astype(wide)
    for term in terms[1:]:
        total = total + term[...].astype(wide)
    whole = 2 * total.shape[0] // 3
    main = total[:whole]
    tail = total[whole:]
    swapped = pltpu.roll(tail, 64, 1)
    lower = lax.broadcasted_iota(jnp.int32, (whole, 128), 1) < 64
    tail_first = jnp.concatenate([tail, swapped], axis=0)
    turned = pltpu.roll(main, 64, 1)
    front = jnp.concatenate([main, tail_first[:, :64]], axis=1)
    back = jnp.concatenate([jnp.where(lower, tail_first, turned), turned[:, :64]], axis=1)
    owned = jnp.where(row_ref[0] == 0, front, back)
    project_ref[...] = owned[:project_each]
    output_ref[...] = owned[project_each:]


def body(
    row_size,
    date_size,
    tokens,
    clear_flags,
    date_numbers,
    decay_slopes,
    time_project,
    time_output,
    column_project,
    column_output,
    cotangent,
):
    date_local, row_local, column_count, width = tokens.shape
    head_count = decay_slopes.shape[0]
    head_size = width // head_count
    packed = max(1, 128 // head_size)
    local_patches = row_local * column_count
    patches_each = local_patches // date_size
    columns_each = column_count // row_size
    row_count = row_local * row_size
    date_count = date_local * date_size
    project_each = 3 * width // date_size
    output_each = width // date_size
    lane_each = width // row_size
    direct = (
        patches_each == column_count
        and column_count % 16 == 0
        and date_size % 8 == 0
        and row_size == 2
        and lane_each == 192
        and project_each % 8 == 0
        and output_each % 8 == 0
        and (project_each + output_each) % 32 == 0
    )
    token_rows = date_local * patches_each
    block_rows = -(-(token_rows + date_local) // 8) * 8
    tile_rows = (width // 128) * token_rows + -(-date_local // 8) * 8
    params = pltpu.CompilerParams(vmem_limit_bytes=vmem_limit)
    in_vmem = pl.BlockSpec(memory_space=pltpu.VMEM)
    in_smem = pl.BlockSpec(memory_space=pltpu.SMEM)
    in_any = pl.BlockSpec(memory_space=pl.ANY)
    swap = [(0, 1), (1, 0)]
    column_tokens = date_local * row_count * columns_each
    half_tokens = column_tokens // row_size
    if direct:
        outgoing = pl.pallas_call(
            pack_kernel,
            out_shape=jax.ShapeDtypeStruct((date_size, tile_rows, 128), low),
            in_specs=[pl.BlockSpec(memory_space=pltpu.HBM)] * 3,
            out_specs=pl.BlockSpec(memory_space=pltpu.HBM),
            scratch_shapes=[
                pltpu.SMEM(date_numbers.shape, jnp.int32),
                pltpu.VMEM(tokens.shape, low),
                pltpu.VMEM(clear_flags.shape, jnp.int32),
                pltpu.VMEM((date_size, tile_rows, 128), low),
                pltpu.SemaphoreType.DMA((2,)),
                pltpu.SemaphoreType.DMA((4,)),
                pltpu.SemaphoreType.DMA((4,)),
            ],
            name="pack_tokens",
        )(date_numbers, tokens, clear_flags)
        row_at = lax.axis_index("row")
        halves = cotangent.reshape(date_local, row_local, row_size, columns_each, width)
        leaving = lax.dynamic_index_in_dim(halves, 1 - row_at, 2, keepdims=False)
        other_grad = lax.ppermute(leaving, "row", swap)
    else:
        flags = jnp.transpose(
            clear_flags.reshape(date_local, date_size, patches_each), (1, 0, 2)
        ).astype(low)
        numbers = jnp.stack([date_numbers // 32, date_numbers % 32], axis=-1).astype(low)
        numbers = jnp.broadcast_to(numbers[None], (date_size, date_local, 2))
        info = jnp.concatenate([flags, numbers], axis=-1)
        info = jnp.pad(
            info, ((0, 0), (0, block_rows - token_rows - date_local), (0, width - patches_each - 2))
        )
        outgoing = jnp.transpose(
            tokens.reshape(date_local, date_size, patches_each, width), (1, 0, 2, 3)
        ).reshape(date_size, token_rows, width)
        outgoing = jnp.concatenate([outgoing, info], axis=1)
    incoming = lax.all_to_all(outgoing, dates, split_axis=0, concat_axis=0, tiled=True)

    if direct:
        grads_in = (
            row_at.reshape(1),
            cotangent.reshape(local_patches * date_local, width),
            other_grad.reshape(half_tokens, width),
        )
        in_specs = [in_smem] + [in_vmem] * 3 + [in_any]
    else:
        grads_in = (
            lax.all_to_all(cotangent, "row", split_axis=2, concat_axis=1, tiled=True).reshape(
                column_tokens, width
            ),
        )
        in_specs = [in_vmem] * 2 + [in_any]
    time_tokens = date_count * patches_each
    hidden = pl.pallas_call(
        functools.partial(
            time_kernel,
            (
                date_size,
                date_local,
                patches_each,
                head_count,
                packed,
                columns_each if direct else patches_each,
            ),
        ),
        out_shape=jax.ShapeDtypeStruct((time_tokens, width), low),
        in_specs=[in_smem, in_vmem, in_vmem, in_vmem, in_any],
        scratch_shapes=[
            pltpu.VMEM((width // 128, time_tokens, 128), wide),
            pltpu.VMEM((time_tokens, width), wide),
            pltpu.VMEM((time_tokens, 3 * width), low),
            pltpu.VMEM((time_tokens, width), low),
        ],
        compiler_params=params,
        name="time_attention",
    )(decay_slopes, incoming, time_project, time_output, grads_in[-1])

    grad_low, heads_grad = pl.pallas_call(
        functools.partial(
            cotangent_kernel, (date_local, row_size, row_local, columns_each, direct)
        ),
        out_shape=(
            jax.ShapeDtypeStruct((column_tokens, width), low),
            jax.ShapeDtypeStruct((column_tokens, width), low),
        ),
        in_specs=in_specs,
        scratch_shapes=[pltpu.VMEM((width // 128, column_tokens, 128), wide)],
        compiler_params=params,
        name="cotangent_heads",
    )(*grads_in, column_output, hidden)

    if direct:
        parts = hidden.reshape(row_size * date_size, date_local * columns_each, width)
        plane = lax.all_to_all(parts, ("row", *dates), split_axis=0, concat_axis=0, tiled=True)
    else:
        parts = hidden.reshape(date_size, date_local, patches_each, width)
        back = lax.all_to_all(parts, dates, split_axis=0, concat_axis=0, tiled=True)
        back = jnp.transpose(back, (1, 0, 2, 3)).reshape(
            date_local, row_local, column_count, width
        )
        plane = lax.all_to_all(back, "row", split_axis=2, concat_axis=1, tiled=True)
    plane = plane.reshape(column_tokens, width)
    half_shape = jax.ShapeDtypeStruct((half_tokens, width), low)
    packed_rows = (project_each + output_each) * 3 // 2
    row_one = lax.axis_index("row").reshape(1)
    pair_one = lax.axis_index("pair").reshape(1)
    sizes = (date_local, row_size, row_local, columns_each, direct)
    if direct:
        half_grads = jax.ShapeDtypeStruct((row_size, date_size // 2, packed_rows, 128), low)
        grad_shapes = (half_grads, half_grads)
        mixed_shapes = (half_shape, half_shape)
    else:
        grad_shapes = (
            jax.ShapeDtypeStruct((3 * width, width), wide),
            jax.ShapeDtypeStruct((width, width), wide),
        )
        mixed_shapes = (jax.ShapeDtypeStruct((column_tokens, width), low),)
    column_heads, first_grad, second_grad = pl.pallas_call(
        functools.partial(column_kernel, (*sizes, head_count, packed, date_size)),
        out_shape=(jax.ShapeDtypeStruct((column_tokens, width), low), *grad_shapes),
        in_specs=[in_smem] * 2 + [in_vmem] * 4,
        input_output_aliases={4: 0},
        scratch_shapes=[
            pltpu.VMEM((width // 128, column_tokens, 128), wide),
            pltpu.VMEM((column_tokens, width), wide),
            pltpu.VMEM((column_tokens, width), low),
            pltpu.VMEM((column_tokens, 3 * width), low),
            pltpu.VMEM((column_tokens, 3 * width), low),
        ],
        compiler_params=params,
        name="column_attention",
    )(row_one, pair_one, plane, grad_low, heads_grad, column_project)
    own_grad = first_grad
    if direct:
        came = lax.ppermute(second_grad, "pair", swap)
        outers = date_size // 4
        block = jax.ShapeDtypeStruct((packed_rows, 128), low)
        blocks = jax.ShapeDtypeStruct((outers, packed_rows, 128), low)
        own_grad, mid_grad, row_grad, both_grad = pl.pallas_call(
            pair_kernel,
            out_shape=(blocks,) * 4,
            in_specs=[in_smem] * 2 + [in_vmem] * 2,
            out_specs=(in_vmem,) * 4,
            compiler_params=params,
            name="pair_gradients",
        )(row_one, lax.axis_index("mid").reshape(1), first_grad, came)
        both_grad = lax.ppermute(both_grad, ("mid", "row"), [(0, 3), (3, 0), (1, 2), (2, 1)])
        mid_grad = lax.ppermute(mid_grad, "mid", swap)
        row_grad = lax.ppermute(row_grad, "row", swap)
    mixed = pl.pallas_call(
        functools.partial(mixed_kernel, sizes),
        out_shape=mixed_shapes,
        in_specs=[in_smem] + [in_vmem] * 3 + [in_any],
        scratch_shapes=[
            pltpu.VMEM((width // 128, column_tokens, 128), wide),
            pltpu.VMEM((column_tokens, width), wide),
        ],
        compiler_params=params,
        name="mixed_tokens",
    )(row_one, plane, column_heads, column_output, own_grad)

    if direct:
        kept, sent = mixed
        leaving, *steps = pl.pallas_call(
            spread_kernel,
            out_shape=(half_shape,) + (block,) * outers,
            in_specs=[in_smem] + [in_vmem] * 5,
            compiler_params=params,
            name="spread_gradients",
        )(lax.axis_index("outer").reshape(1), own_grad, mid_grad, row_grad, both_grad, sent)
        terms = [steps[0]]
        for step in sorted(range(1, outers), key=lambda step: abs(step - outers // 2)):
            route = [(at, (at + step) % outers) for at in range(outers)]
            terms.append(lax.ppermute(steps[step], "outer", route))
        arrived = lax.ppermute(leaving, "row", swap)
        quarter = (date_local, row_local, 1, columns_each, width)
        kept, arrived = kept.reshape(quarter), arrived.reshape(quarter)
        mixed = jnp.concatenate(
            [jnp.where(row_at == 0, kept, arrived), jnp.where(row_at == 0, arrived, kept)], axis=2
        )
        owned_project, owned_output = pl.pallas_call(
            functools.partial(finish_kernel, project_each),
            out_shape=(
                jax.ShapeDtypeStruct((project_each, lane_each), wide),
                jax.ShapeDtypeStruct((output_each, lane_each), wide),
            ),
            in_specs=[in_smem] + [in_vmem] * outers + [in_any],
            compiler_params=params,
            name="gradient_sum",
        )(row_one, *terms, mixed)
    else:
        mixed = mixed[0]
        grads = jnp.concatenate(
            [
                first_grad.reshape(date_size, project_each, row_size, lane_each),
                second_grad.reshape(date_size, output_each, row_size, lane_each),
            ],
            axis=1,
        ).astype(low)
        grads = jnp.transpose(grads, (2, 0, 1, 3)).reshape(
            row_size * date_size, project_each + output_each, lane_each
        )
        terms = lax.all_to_all(grads, ("row", *dates), split_axis=0, concat_axis=0, tiled=True)
        owned = jnp.sum(terms.astype(wide), axis=0)
        owned_project, owned_output = owned[:project_each], owned[project_each:]
        mixed = mixed.reshape(row_size, date_local, row_local, columns_each, width)
        mixed = lax.all_to_all(mixed, "row", split_axis=0, concat_axis=0, tiled=True)
        mixed = jnp.transpose(mixed, (1, 2, 0, 3, 4))
    mixed = mixed.reshape(date_local, row_local, column_count, width)
    return (mixed, jnp.transpose(owned_project), jnp.transpose(owned_output))


def solution(mesh):
    date_size, row_size = mesh.shape["date"], mesh.shape["row"]
    pair_size = 2 if date_size % 2 == 0 else 1
    mid_size = 2 if date_size % 4 == 0 else 1
    split = jax.sharding.Mesh(
        mesh.devices.reshape(-1, mid_size, pair_size, row_size), ("outer", "mid", "pair", "row")
    )
    return jax.shard_map(
        functools.partial(body, row_size, date_size),
        mesh=split,
        in_specs=(
            P(dates, "row", None, None),
            P(dates, "row", None),
            P(dates),
            P(),
            P(),
            P(),
            P(),
            P(),
            P(dates, "row", None, None),
        ),
        out_specs=(P(dates, "row", None, None), P("row", dates), P("row", dates)),
        check_vma=False,
    )
```
